32 devices in a mesh: expert: 8 (over z, x), shard: 4 (over y, core).
Axes of the slice: x: 2, y: 2, z: 4, core: 2. Of those that a mesh axis runs over, the one named last changes fastest.
Arguments:
- tokens: bfloat16 [8192, 2048], P(('expert', 'shard')), may hold values from -16 to 16
- cotangent: bfloat16 [8192, 2048], P(('expert', 'shard')), may hold values from -6 to 6
- segments: int32 [32, 256], P(('expert', 'shard')), may hold values from 0 to 2, never falling along the last dimension, each value on 1 to 160 neighbouring positions
- routes: int32 [8192, 8], P(('expert', 'shard')), may hold values from 0 to 15, as said below
- tile_counts: int32 [16], replicated, may hold values from 8 to 16
- norm_one: bfloat16 [2048], P('shard'), may hold values from 0.25 to 1.75
- norm_query: bfloat16 [2048], P('shard'), may hold values from 0.25 to 1.75
- norm_key: bfloat16 [2048], P('shard'), may hold values from 0.25 to 1.75
- norm_two: bfloat16 [2048], P('shard'), may hold values from 0.25 to 1.75
- qkv_weight: bfloat16 [2048, 6144], P('shard'), may hold values from -0.125 to 0.125
- out_weight: bfloat16 [2048, 2048], P('shard'), may hold values from -0.5 to 0.5
- router_weight: bfloat16 [2048, 16], P('shard'), may hold values from -0.125 to 0.125
- gate_up_weight: bfloat16 [16, 2048, 2048], P('expert'), may hold values from -0.125 to 0.125
- down_weight: bfloat16 [16, 1024, 2048], P('expert'), may hold values from -1 to 1
Outputs:
- block_out: bfloat16 [8192, 2048], P(('expert', 'shard'))
- grad_tokens: float32 [8192, 2048], P(('expert', 'shard'))
- grad_norm_one: float32 [2048], P('shard')
- grad_norm_query: float32 [2048], P('shard')
- grad_norm_key: float32 [2048], P('shard')
- grad_norm_two: float32 [2048], P('shard')
- grad_qkv_weight: float32 [2048, 6144], P('shard')
- grad_out_weight: float32 [2048, 2048], P('shard')
- grad_router_weight: float32 [2048, 16], P('shard')
- grad_gate_up_weight: float32 [16, 2048, 2048], P('expert', 'shard')
- grad_down_weight: float32 [16, 1024, 2048], P('expert', None, 'shard')
The draws below stay inside these ranges and needn't reach their ends.
Inputs may be any that keep to these rules, and one draw needn't show every extreme that they name: `routes`: each row names 8 different experts. In every sequence one expert, the same for all sequences, is named by 192 rows or more, and its tile count is 16. `segments`: segment numbers start at 0 in every sequence.
All inputs are finite; a program needn't handle non-finite values.
Results may differ from the reference program's by a relative error of at most 0.015.
Values may be sent and summed in bfloat16 or wider, within the bound.
A program may use at most 320 MiB of HBM per device.

```python
import math
import jax
import jax.numpy as jnp
import numpy as np
from jax import lax

D = 2048
HEADS = 16
HEAD_DIM = 128
FF = 1024
TOP = 8
TILE = 8
TOK_DEV = 256
EXPERTS = 16
MAXT = 16
CAP = 128
SEQS = 32
TOKENS = 8192


def favoured_expert(key):
    return jax.random.randint(jax.random.fold_in(key, 11), (), 0, EXPERTS)


def draw_routes(key, part):
    favoured = favoured_expert(key)
    noise_key = jax.random.fold_in(key, 21)
    order_key = jax.random.fold_in(key, 22)
    bias_key = jax.random.fold_in(key, 23)
    raw_scores = jax.random.randint(noise_key, (TOKENS, EXPERTS), 0, 65536)
    expert_bias = jax.random.randint(bias_key, (EXPERTS,), 0, 32768)
    ordering_draws = jax.random.randint(order_key, (SEQS, TOK_DEV), 0, 1 << 20)
    unique_draws = ordering_draws * TOK_DEV + jnp.arange(TOK_DEV, dtype=jnp.int32)[None, :]
    sort_order = jnp.argsort(unique_draws, axis=1)
    token_ranks = jnp.argsort(sort_order, axis=1)
    boosted = (token_ranks < 3 * TOK_DEV // 4).reshape(TOKENS)
    is_favoured = jnp.arange(EXPERTS, dtype=jnp.int32)[None, :] == favoured
    combined = raw_scores + expert_bias[None, :] + jnp.where(is_favoured & boosted[:, None], 1 << 20, 0)
    unique_total = combined * EXPERTS + jnp.arange(EXPERTS, dtype=jnp.int32)[None, :]
    return lax.top_k(unique_total, TOP)[1].astype(jnp.int32)


def draw_tile_counts(key, part):
    favoured = favoured_expert(key)
    drawn = jax.random.randint(jax.random.fold_in(key, 31), (EXPERTS,), MAXT // 2, MAXT + 1)
    return jnp.where(jnp.arange(EXPERTS, dtype=jnp.int32) == favoured, MAXT, drawn).astype(jnp.int32)


def draw_tokens(key, part):
    row_key = jax.random.fold_in(key, 51)
    column_key = jax.random.fold_in(key, 52)
    base_key = jax.random.fold_in(key, 53)
    row_scale = jnp.exp(jax.random.uniform(row_key, (TOKENS, 1), jnp.float32, jnp.log(0.5), jnp.log(2.0)))
    column_scale = jnp.exp(jax.random.uniform(column_key, (1, D), jnp.float32, jnp.log(0.5), jnp.log(2.0)))
    values = row_scale * column_scale * jnp.clip(jax.random.normal(base_key, (TOKENS, D), jnp.float32), -4.0, 4.0)
    return values.astype(jnp.bfloat16)


def level_of(stream_key, dims, split, smallest, high):
    factor_of, own = 1.0, jax.random.fold_in(stream_key, 6)
    for dim, blocks in split:
        heights = jnp.exp(jax.random.uniform(jax.random.fold_in(own, dim), (blocks,), jnp.float32, smallest / len(split), high / len(split)))
        factor_of = factor_of * jnp.repeat(heights, dims[dim] // blocks).reshape([-1 if axis == dim else 1 for axis in range(len(dims))])
    return factor_of


def profile(count, total, bound, slope):
    weights = [(1 << 20) // math.isqrt(grade ** slope) + 1 for grade in range(2, count + 1)]
    spare, holding = total - bound - (count - 1), [1] * (count - 1)
    while spare > 0:
        candidates = [i for i in range(count - 1) if holding[i] < bound]
        pool, remaining = sum([weights[i] for i in candidates]), spare
        for i in candidates:
            addition = min(bound - holding[i], max(1, remaining * weights[i] // pool), spare)
            holding[i] = holding[i] + addition
            spare = spare - addition
    return np.array([bound] + holding)


def uneven(key, count, total, most, slope):
    if count == 2:
        one = jax.random.randint(key, (), max(1, total - most), min(most, total - 1) + 1)
        return jnp.stack([one, total - one])
    tallies = jnp.asarray(profile(count, total, most, slope), jnp.int32)
    pairs = (count - 1) // 2
    source_of, sink = tallies[1:1 + 2 * pairs:2], tallies[2:2 + 2 * pairs:2]
    margin = jnp.minimum(source_of - 1, most - sink)
    passed = jax.random.randint(jax.random.fold_in(key, 1), (pairs,), 0, 1 << 20) % (margin + 1)
    tallies = tallies.at[1:1 + 2 * pairs:2].set(source_of - passed).at[2:2 + 2 * pairs:2].set(sink + passed)
    return tallies[jax.random.permutation(jax.random.fold_in(key, 2), count)]


def scatter_about(stream_key, dims, deviation, bound, cuts=(), held_as=jnp.bfloat16):
    array = jax.random.normal(stream_key, dims, jnp.float32) * deviation
    if len(cuts) > 0:
        array = level_of(stream_key, dims, cuts, -0.22, 0.18) * array
    return jnp.clip(array, min=-bound, max=bound).astype(held_as)


def setup_inputs(seed: int = 0) -> dict:
    key_of = jax.random.split(jax.random.key(seed), 15)
    tokens = draw_tokens(jax.random.fold_in(key_of[14], 71), 0)
    cotangent = scatter_about(key_of[1], (TOKENS, D), 1.0, 6.0, ((0, 32),))
    segments = jax.vmap(lambda own: jnp.searchsorted(jnp.cumsum(uneven(own, 3, TOK_DEV, TOK_DEV * 5 // 8, 0)), jnp.arange(TOK_DEV), side="right"))(jax.random.split(key_of[2], SEQS)).reshape((SEQS, TOK_DEV)).astype(jnp.int32)
    routes = draw_routes(jax.random.fold_in(key_of[14], 71), 0)
    tile_counts = draw_tile_counts(jax.random.fold_in(key_of[14], 71), 0)
    norm_one = jnp.clip(1.0 + 0.15 * jax.random.normal(key_of[5], (D,), jnp.float32), 0.25, 1.75).astype(jnp.bfloat16)
    norm_query = jnp.clip(1.0 + 0.15 * jax.random.normal(key_of[6], (D,), jnp.float32), 0.25, 1.75).astype(jnp.bfloat16)
    norm_key = jnp.clip(1.0 + 0.15 * jax.random.normal(key_of[7], (D,), jnp.float32), 0.25, 1.75).astype(jnp.bfloat16)
    norm_two = jnp.clip(1.0 + 0.15 * jax.random.normal(key_of[8], (D,), jnp.float32), 0.25, 1.75).astype(jnp.bfloat16)
    qkv_weight = scatter_about(key_of[9], (D, 3 * D), D ** -0.5, 0.125, ((0, 4),))
    out_weight = scatter_about(key_of[10], (D, D), (D // 16) ** -0.5, 0.5, ((0, 4),))
    router_weight = scatter_about(key_of[11], (D, EXPERTS), D ** -0.5, 0.125, ((0, 4),))
    gate_up_weight = scatter_about(key_of[12], (EXPERTS, D, 2 * FF), D ** -0.5, 0.125, ((0, 8),))
    down_weight = scatter_about(key_of[13], (EXPERTS, FF, D), (max(1, FF * TOP // (EXPERTS * EXPERTS))) ** -0.5, 1.0, ((0, 8),))
    return dict(tokens=tokens, cotangent=cotangent, segments=segments, routes=routes, tile_counts=tile_counts, norm_one=norm_one, norm_query=norm_query, norm_key=norm_key, norm_two=norm_two, qkv_weight=qkv_weight, out_weight=out_weight, router_weight=router_weight, gate_up_weight=gate_up_weight, down_weight=down_weight)


@jax.custom_vjp
def low(v):
    return lax.optimization_barrier(v.astype(jnp.bfloat16)).astype(jnp.float32)

@jax.custom_vjp
def low_back(v):
    return v

def low_keep(v):
    return (low(v), None)

def low_pass(kept, grad):
    return (grad,)

def back_keep(v):
    return (v, None)

def back_low(kept, grad):
    return (low(grad),)
low.defvjp(low_keep, low_pass)
low_back.defvjp(back_keep, back_low)
epsilon = 1e-05
rope_base = 10000.0
highest = lax.Precision.HIGHEST

def rms_scale(values, scale_gain):
    return values * lax.rsqrt(lax.optimization_barrier(jnp.mean(values * values, axis=-1, keepdims=True)) + epsilon) * scale_gain

def rotary_tables(length):
    half_dim = HEAD_DIM // 2
    position = jnp.arange(length, dtype=jnp.float32)[:, None]
    frequency = rope_base ** (-jnp.arange(half_dim, dtype=jnp.float32) * 2.0 / HEAD_DIM)
    angles = position * frequency[None, :]
    angles = jnp.concatenate([angles, angles], axis=-1)
    return (jnp.cos(angles)[:, None, :], jnp.sin(angles)[:, None, :])

def rotate(vectors, cosine, sine_table):
    half_dim = vectors.shape[-1] // 2
    turned = jnp.concatenate([-vectors[..., half_dim:], vectors[..., :half_dim]], axis=-1)
    return vectors * cosine + turned * sine_table

def query_key(raw_query, raw_key, query_gain, key_gain, cosine, sine_table):
    length = raw_query.shape[0]
    queries = rms_scale(raw_query, query_gain).reshape(length, HEADS, HEAD_DIM)
    keys_rot = rms_scale(raw_key, key_gain).reshape(length, HEADS, HEAD_DIM)
    return (rotate(queries, cosine, sine_table), rotate(keys_rot, cosine, sine_table))

def swiglu(gate_up):
    half_dim = gate_up.shape[-1] // 2
    gate_part = gate_up[..., :half_dim]
    return gate_part / (1.0 + jnp.exp(-gate_part)) * gate_up[..., half_dim:]

def softmax_rows(logits):
    largest = lax.optimization_barrier(jnp.max(logits, axis=-1, keepdims=True))
    raised = jnp.exp(logits - largest)
    return raised / lax.optimization_barrier(jnp.sum(raised, axis=-1, keepdims=True))

def sequence_layer(weights, tokens_in, segment, route_rows, tile_counts):
    norm_one, norm_query, norm_key, norm_two, qkv_weight, out_weight, router_weight, gate_up_weight, down_weight = weights
    length = tokens_in.shape[0]
    hidden_one = low(rms_scale(tokens_in, norm_one))
    projected = low_back(jnp.dot(hidden_one, qkv_weight, precision=highest))
    cosine, sine_table = rotary_tables(length)
    queries, keys_rot = query_key(projected[:, :D], projected[:, D:2 * D], norm_query, norm_key, cosine, sine_table)
    queries = low(queries)
    keys_rot = low(keys_rot)
    values_all = low(projected[:, 2 * D:]).reshape(length, HEADS, HEAD_DIM)
    scores = low_back(jnp.einsum('qhd,khd->hqk', queries, keys_rot, precision=highest) * HEAD_DIM ** (-0.5))
    position = jnp.arange(length, dtype=jnp.int32)
    allowed = (position[:, None] >= position[None, :]) & (segment[:, None] == segment[None, :])
    probs_low = low(softmax_rows(jnp.where(allowed[None], scores, -1e+30)))
    attended = jnp.einsum('hqk,khd->qhd', probs_low, values_all, precision=highest).reshape(length, D)
    attended = low(low_back(attended))
    branch = low_back(jnp.dot(attended, out_weight, precision=highest))
    middle = tokens_in + branch
    hidden_two = low(rms_scale(middle, norm_two))
    router = softmax_rows(low_back(jnp.dot(hidden_two, router_weight, precision=highest)))
    flat_expert = route_rows.reshape(-1).astype(jnp.int32)
    pair_count = flat_expert.shape[0]
    chosen = (flat_expert[:, None] == jnp.arange(EXPERTS, dtype=jnp.int32)[None, :]).astype(jnp.int32)
    before = (jnp.cumsum(chosen, axis=0) - chosen).astype(jnp.int32)
    rank_pair = lax.optimization_barrier(jnp.sum(before * chosen, axis=1)).astype(jnp.int32)
    kept_pair = rank_pair < tile_counts[flat_expert] * TILE
    slot_index = jnp.where(kept_pair, flat_expert * CAP + rank_pair, EXPERTS * CAP).astype(jnp.int32)
    slot_pair = jnp.full((EXPERTS * CAP,), pair_count, jnp.int32).at[slot_index].set(jnp.arange(pair_count, dtype=jnp.int32), mode='drop')
    slot_token = (slot_pair // TOP).astype(jnp.int32)
    padded = jnp.concatenate([hidden_two, jnp.zeros((1, D), jnp.float32)], axis=0)
    expert_rows = low_back(padded[slot_token]).reshape(EXPERTS, CAP, D)
    gate_up = low_back(jnp.einsum('ecd,edf->ecf', expert_rows, gate_up_weight, precision=highest))
    activated = low(swiglu(gate_up))
    expert_out = jnp.einsum('ecf,efd->ecd', activated, down_weight, precision=highest)
    expert_out = low(low_back(expert_out)).reshape(EXPERTS * CAP, D)
    padded_out = jnp.concatenate([expert_out, jnp.zeros((1, D), jnp.float32)], axis=0)
    pair_out = padded_out[slot_index].reshape(length, TOP, D)
    pair_prob = jnp.take_along_axis(router, route_rows, axis=1) * kept_pair.reshape(length, TOP).astype(jnp.float32)
    mixture = lax.optimization_barrier(jnp.sum(pair_prob[:, :, None] * pair_out, axis=1))
    return middle + mixture

def reference(tokens, cotangent, segments, routes, tile_counts, norm_one, norm_query, norm_key, norm_two, qkv_weight, out_weight, router_weight, gate_up_weight, down_weight):
    weights = tuple((member.astype(jnp.float32) for member in (norm_one, norm_query, norm_key, norm_two, qkv_weight, out_weight, router_weight, gate_up_weight, down_weight)))
    inputs = tokens.astype(jnp.float32).reshape(SEQS, TOK_DEV, D)
    upstream = cotangent.astype(jnp.float32).reshape(SEQS, TOK_DEV, D)
    route_rows = routes.reshape(SEQS, TOK_DEV, TOP)
    checked = jax.checkpoint(sequence_layer)

    def whole_layer(inputs_all, weights_all):

        def one_sequence(carried):
            return checked(weights_all, carried[0], carried[1], carried[2], tile_counts)
        return lax.map(one_sequence, (inputs_all, segments, route_rows))
    result, pullback = jax.vjp(whole_layer, inputs, weights)
    grad_inputs, grad_weights = pullback(upstream)
    return (result.reshape(TOKENS, D).astype(jnp.bfloat16), grad_inputs.reshape(TOKENS, D), grad_weights[0], grad_weights[1], grad_weights[2], grad_weights[3], grad_weights[4], grad_weights[5], grad_weights[6], grad_weights[7], grad_weights[8])
```

```python
import jax
import jax.numpy as jnp
from jax import lax
from jax.sharding import PartitionSpec as P

HEADS = 16
HEAD_DIM = 128
TOP = 8
TILE = 8


epsilon = 1e-05
rope_base = 10000.0


def rms_scale(values, scale_gain):
    return (
        values * lax.rsqrt(jnp.mean(values * values, axis=-1, keepdims=True) + epsilon) * scale_gain
    )


def rotary_tables(length):
    half_dim = HEAD_DIM // 2
    position = jnp.arange(length, dtype=jnp.float32)[:, None]
    frequency = rope_base ** (-jnp.arange(half_dim, dtype=jnp.float32) * 2.0 / HEAD_DIM)
    angles = position * frequency[None, :]
    angles = jnp.concatenate([angles, angles], axis=-1)
    return (jnp.cos(angles)[:, None, :], jnp.sin(angles)[:, None, :])


def rotate(vectors, cosine, sine_table):
    half_dim = vectors.shape[-1] // 2
    turned = jnp.concatenate([-vectors[..., half_dim:], vectors[..., :half_dim]], axis=-1)
    return vectors * cosine + turned * sine_table


def query_key(raw_query, raw_key, query_gain, key_gain, cosine, sine_table):
    length = raw_query.shape[0]
    queries = rms_scale(raw_query, query_gain).reshape(length, HEADS, HEAD_DIM)
    keys_rot = rms_scale(raw_key, key_gain).reshape(length, HEADS, HEAD_DIM)
    return (rotate(queries, cosine, sine_table), rotate(keys_rot, cosine, sine_table))


def swiglu(gate_up):
    half_dim = gate_up.shape[-1] // 2
    gate_part = gate_up[..., :half_dim]
    return gate_part / (1.0 + jnp.exp(-gate_part)) * gate_up[..., half_dim:]


def softmax_rows(logits):
    largest = jnp.max(logits, axis=-1, keepdims=True)
    raised = jnp.exp(logits - largest)
    return raised / jnp.sum(raised, axis=-1, keepdims=True)


def z_size(expert_group):
    return 4 if expert_group % 4 == 0 else 1


def shift(values, expert_group, dz, dx):
    z_all = z_size(expert_group)
    x_all = expert_group // z_all
    pairs = [
        (i, ((i // x_all + dz) % z_all) * x_all + (i % x_all + dx) % x_all)
        for i in range(expert_group)
    ]
    return lax.ppermute(values, "expert", pairs)


def gather_expert(block, expert_group):
    z_all = z_size(expert_group)
    x_all = expert_group // z_all
    rows = [block] + [shift(block, expert_group, dz, 0) for dz in range(1, z_all)]
    return [
        rows[dz] if dx == 0 else shift(rows[dz], expert_group, 0, dx)
        for dz in range(z_all)
        for dx in range(x_all)
    ]


def reduce_expert(parts, expert_group):
    z_all = z_size(expert_group)
    x_all = expert_group // z_all
    rows = []
    for dz in range(z_all):
        total = parts[dz * x_all].astype(jnp.float32)
        for dx in range(1, x_all):
            total = total + shift(parts[dz * x_all + dx], expert_group, 0, -dx).astype(jnp.float32)
        rows.append(total)
    total = rows[0]
    for dz in range(1, z_all):
        total = total + shift(
            rows[dz].astype(jnp.bfloat16), expert_group, -dz, 0
        ).astype(jnp.float32)
    return total


def relative_sources(expert_group):
    z_all = z_size(expert_group)
    x_all = expert_group // z_all
    me = lax.axis_index("expert")
    order = jnp.arange(expert_group, dtype=jnp.int32)
    return ((me // x_all - order // x_all) % z_all) * x_all + (me % x_all - order % x_all) % x_all


def body(
    tokens,
    cotangent,
    segments,
    routes,
    tile_counts,
    norm_one,
    norm_query,
    norm_key,
    norm_two,
    qkv_weight,
    out_weight,
    router_weight,
    gate_up_weight,
    down_weight,
):
    f32, bf16 = jnp.float32, jnp.bfloat16
    length, model_width = tokens.shape
    experts_all = tile_counts.shape[0]
    local_experts = gate_up_weight.shape[0]
    expert_group = lax.axis_size("expert")
    shard_group = lax.axis_size("shard")
    capacity = length * TOP // (experts_all * TILE) * TILE
    score_scale = HEAD_DIM ** (-0.5)
    own_expert = lax.axis_index("expert")
    own_shard = lax.axis_index("shard")
    sources = relative_sources(expert_group)

    def gather(values, axis):
        return lax.all_gather(values, axis, axis=0, tiled=True)

    qkv_full = gather(qkv_weight, "shard")
    out_full = gather(out_weight, "shard")
    router_full = gather(router_weight, "shard")
    gains = lax.all_gather(
        jnp.stack([norm_one, norm_query, norm_key, norm_two]), "shard", axis=1, tiled=True
    ).astype(f32)
    gain_one, gain_query, gain_key, gain_two = gains[0], gains[1], gains[2], gains[3]

    expert_ids = jnp.arange(experts_all, dtype=jnp.int32)
    chosen = jnp.any(routes[:, :, None] == expert_ids[None, None, :], axis=1)
    position = jnp.arange(length, dtype=jnp.int32)
    earlier = (position[:, None] > position[None, :]).astype(bf16)
    rank = jnp.dot(earlier, chosen.astype(bf16), preferred_element_type=f32)
    kept = chosen & (rank < (tile_counts * TILE).astype(f32)[None, :])
    place = jnp.where(kept, rank, -1.0)
    place_all = lax.all_gather(place, "expert", axis=0, tiled=False)[sources]
    place_own = lax.dynamic_slice_in_dim(
        place_all, own_expert * local_experts, local_experts, axis=2
    )
    place_own = place_own.transpose(0, 2, 1)
    slots = jnp.arange(capacity, dtype=jnp.int32).astype(f32)
    one_hot = place_own[:, :, None, :] == slots[None, None, :, None]
    one_hot_low = one_hot.astype(bf16)
    upstream_all = jnp.stack(gather_expert(cotangent, expert_group))

    inputs = tokens.astype(f32)
    scaled_one, first_pull = jax.vjp(rms_scale, inputs, gain_one)
    hidden_one = scaled_one.astype(bf16)
    hidden_one_columns = lax.all_to_all(
        hidden_one, "shard", split_axis=1, concat_axis=0, tiled=True
    )
    projected = jnp.dot(hidden_one, qkv_full, preferred_element_type=f32)
    cosine, sine_table = rotary_tables(length)

    def query_key_local(raw_query, raw_key, query_gain, key_gain):
        return query_key(raw_query, raw_key, query_gain, key_gain, cosine, sine_table)

    rotated, rotary_pull = jax.vjp(
        query_key_local,
        projected[:, :model_width],
        projected[:, model_width : 2 * model_width],
        gain_query,
        gain_key,
    )
    query_low = rotated[0].astype(bf16)
    key_low = rotated[1].astype(bf16)
    value_low = projected[:, 2 * model_width :].astype(bf16).reshape(length, HEADS, HEAD_DIM)
    allowed = (position[:, None] >= position[None, :]) & (
        segments[0][:, None] == segments[0][None, :]
    )
    masked = jnp.where(
        allowed[None],
        jnp.einsum("qhd,khd->hqk", query_low, key_low, preferred_element_type=f32) * score_scale,
        -1e30,
    )
    probs = softmax_rows(masked)
    probs_low = probs.astype(bf16)
    attended_low = (
        jnp.einsum("hqk,khd->qhd", probs_low, value_low, preferred_element_type=f32)
        .reshape(length, model_width)
        .astype(bf16)
    )
    attended_columns = lax.all_to_all(
        attended_low, "shard", split_axis=1, concat_axis=0, tiled=True
    )
    middle = inputs + jnp.dot(attended_low, out_full, preferred_element_type=f32)
    scaled_two, second_pull = jax.vjp(rms_scale, middle, gain_two)
    hidden_two = scaled_two.astype(bf16)
    hidden_all = jnp.stack(gather_expert(hidden_two, expert_group))
    router = softmax_rows(jnp.dot(hidden_two, router_full, preferred_element_type=f32))
    prob = jnp.where(kept, router, 0.0)
    prob_all = lax.all_gather(prob, "expert", axis=0, tiled=False)[sources]
    prob_own = lax.dynamic_slice_in_dim(
        prob_all, own_expert * local_experts, local_experts, axis=2
    ).transpose(0, 2, 1)

    expert_rows = jnp.einsum(
        "sect,std->escd", one_hot_low, hidden_all, preferred_element_type=f32
    ).astype(bf16)
    row_count = expert_group * capacity
    expert_rows = expert_rows.reshape(local_experts, row_count, model_width)
    gate_up = jnp.einsum("erd,edf->erf", expert_rows, gate_up_weight, preferred_element_type=f32)
    activated_full, swiglu_pull = jax.vjp(swiglu, gate_up)
    activated = activated_full.astype(bf16)
    expert_out = jnp.einsum(
        "erf,efd->erd", activated, down_weight, preferred_element_type=f32
    ).astype(bf16)
    weighted = jnp.where(one_hot, prob_own[:, :, None, :], 0.0)
    weighted_high = weighted.astype(bf16)
    weighted_low = (weighted - weighted_high.astype(f32)).astype(bf16)
    out_rows = expert_out.reshape(local_experts, expert_group, capacity, model_width)
    mixture_parts = (
        jnp.einsum("sect,escd->std", weighted_high, out_rows, preferred_element_type=f32)
        + jnp.einsum("sect,escd->std", weighted_low, out_rows, preferred_element_type=f32)
    ).astype(bf16)
    mixture = reduce_expert([mixture_parts[i] for i in range(expert_group)], expert_group)
    block_out = (middle + mixture).astype(bf16)

    prob_rows = jnp.sum(weighted, axis=3).transpose(1, 0, 2).reshape(local_experts, row_count)
    upstream_rows = jnp.einsum(
        "sect,std->escd", one_hot_low, upstream_all, preferred_element_type=f32
    ).reshape(local_experts, row_count, model_width)
    grad_expert = (prob_rows[:, :, None] * upstream_rows).astype(bf16)
    grad_prob_rows = jnp.sum(upstream_rows * expert_out.astype(f32), axis=-1).reshape(
        local_experts, expert_group, capacity
    )
    grad_router_parts = jnp.sum(
        jnp.where(one_hot, grad_prob_rows.transpose(1, 0, 2)[:, :, :, None], 0.0), axis=2
    )
    back = jnp.zeros((expert_group, local_experts, length), f32).at[sources].set(grad_router_parts)
    grad_router = lax.all_to_all(back, "expert", split_axis=0, concat_axis=0, tiled=True)
    grad_router = grad_router.reshape(experts_all, length).T
    grad_activated = jnp.einsum("erd,efd->erf", grad_expert, down_weight, preferred_element_type=f32)
    grad_gate_up_low = swiglu_pull(grad_activated)[0].astype(bf16)
    grad_row = jnp.einsum(
        "erf,edf->erd", grad_gate_up_low, gate_up_weight, preferred_element_type=f32
    ).astype(bf16)
    grad_hidden_parts = jnp.einsum(
        "sect,escd->std",
        one_hot_low,
        grad_row.reshape(local_experts, expert_group, capacity, model_width),
        preferred_element_type=f32,
    ).astype(bf16)
    grad_rows_sum = reduce_expert([grad_hidden_parts[i] for i in range(expert_group)], expert_group)
    grad_down_full = jnp.einsum("erf,erd->efd", activated, grad_expert, preferred_element_type=f32)
    grad_gate_up_full = jnp.einsum(
        "erd,erf->edf", expert_rows, grad_gate_up_low, preferred_element_type=f32
    )
    grad_gate_up_weight = lax.psum_scatter(
        grad_gate_up_full.astype(bf16), "shard", scatter_dimension=1, tiled=True
    ).astype(f32)
    grad_down_weight = lax.psum_scatter(
        grad_down_full.astype(bf16), "shard", scatter_dimension=2, tiled=True
    ).astype(f32)

    upstream = cotangent.astype(f32)
    grad_logits = (
        router * (grad_router - jnp.sum(router * grad_router, axis=-1, keepdims=True))
    ).astype(bf16)
    grad_hidden_two = grad_rows_sum + jnp.einsum(
        "te,de->td", grad_logits, router_full, preferred_element_type=f32
    )
    grad_middle_norm, grad_gain_two = second_pull(grad_hidden_two)
    grad_middle = upstream + grad_middle_norm
    grad_branch_low = grad_middle.astype(bf16)
    grad_attended_low = (
        jnp.einsum("te,de->td", grad_branch_low, out_full, preferred_element_type=f32)
        .astype(bf16)
        .reshape(length, HEADS, HEAD_DIM)
    )
    grad_probs = jnp.einsum(
        "qhd,khd->hqk", grad_attended_low, value_low, preferred_element_type=f32
    )
    grad_scores_low = (
        probs * (grad_probs - jnp.sum(probs * grad_probs, axis=-1, keepdims=True))
    ).astype(bf16)
    grad_queries = (
        jnp.einsum("hqk,khd->qhd", grad_scores_low, key_low, preferred_element_type=f32)
        * score_scale
    )
    grad_keys = (
        jnp.einsum("hqk,qhd->khd", grad_scores_low, query_low, preferred_element_type=f32)
        * score_scale
    )
    grad_values = jnp.einsum(
        "hqk,qhd->khd", probs_low, grad_attended_low, preferred_element_type=f32
    )
    grad_raw_query, grad_raw_key, grad_gain_query, grad_gain_key = rotary_pull(
        (grad_queries, grad_keys)
    )
    grad_projected_low = jnp.concatenate(
        [grad_raw_query, grad_raw_key, grad_values.reshape(length, model_width)], axis=-1
    ).astype(bf16)
    grad_hidden_one = jnp.einsum(
        "te,de->td", grad_projected_low, qkv_full, preferred_element_type=f32
    )
    grad_inputs_norm, grad_gain_one = first_pull(grad_hidden_one)
    grad_tokens = grad_middle + grad_inputs_norm

    def over_sequences(columns, grads):
        part = jnp.einsum("td,te->de", columns, gather(grads, "shard"), preferred_element_type=f32)
        return lax.psum(part.astype(bf16), "expert").astype(f32)

    grad_out_weight = over_sequences(attended_columns, grad_branch_low)
    grad_qkv_weight = over_sequences(hidden_one_columns, grad_projected_low)
    grad_router_part = jnp.einsum(
        "td,te->ed", hidden_two, grad_logits, preferred_element_type=f32
    )
    small = jnp.concatenate(
        [
            grad_router_part,
            jnp.stack([grad_gain_one, grad_gain_query, grad_gain_key, grad_gain_two]),
        ],
        axis=0,
    )
    small = lax.psum(small, ("expert", "shard"))
    width = norm_one.shape[0]
    small = lax.dynamic_slice_in_dim(small, own_shard * width, width, axis=1)
    return (
        block_out,
        grad_tokens,
        small[experts_all],
        small[experts_all + 1],
        small[experts_all + 2],
        small[experts_all + 3],
        grad_qkv_weight,
        grad_out_weight,
        small[:experts_all].T,
        grad_gate_up_weight,
        grad_down_weight,
    )


def solution(mesh):
    return jax.shard_map(
        body,
        mesh=mesh,
        in_specs=(
            P(("expert", "shard"), None),
            P(("expert", "shard"), None),
            P(("expert", "shard"), None),
            P(("expert", "shard"), None),
            P(),
            P("shard"),
            P("shard"),
            P("shard"),
            P("shard"),
            P("shard", None),
            P("shard", None),
            P("shard", None),
            P("expert", None, None),
            P("expert", None, None),
        ),
        out_specs=(
            P(("expert", "shard"), None),
            P(("expert", "shard"), None),
            P("shard"),
            P("shard"),
            P("shard"),
            P("shard"),
            P("shard", None),
            P("shard", None),
            P("shard", None),
            P("expert", "shard", None),
            P("expert", None, "shard"),
        ),
        check_vma=False,
    )
```

```python
import functools

import jax
import jax.numpy as jnp
from jax import lax
from jax.experimental import pallas as pl
from jax.experimental.pallas import tpu as pltpu
from jax.sharding import PartitionSpec as P

HEADS = 16
HEAD_DIM = 128
TOP = 8
TILE = 8


epsilon = 1e-05
rope_base = 10000.0


def rms_scale(values, scale_gain):
    return (
        values * lax.rsqrt(jnp.mean(values * values, axis=-1, keepdims=True) + epsilon) * scale_gain
    )


def rotary_tables(length):
    half_dim = HEAD_DIM // 2
    position = jnp.arange(length, dtype=jnp.float32)[:, None]
    frequency = rope_base ** (-jnp.arange(half_dim, dtype=jnp.float32) * 2.0 / HEAD_DIM)
    angles = position * frequency[None, :]
    angles = jnp.concatenate([angles, angles], axis=-1)
    return (jnp.cos(angles)[:, None, :], jnp.sin(angles)[:, None, :])


def rotate(vectors, cosine, sine_table):
    half_dim = vectors.shape[-1] // 2
    turned = jnp.concatenate([-vectors[..., half_dim:], vectors[..., :half_dim]], axis=-1)
    return vectors * cosine + turned * sine_table


def query_key(raw_query, raw_key, query_gain, key_gain, cosine, sine_table):
    length = raw_query.shape[0]
    queries = rms_scale(raw_query, query_gain).reshape(length, HEADS, HEAD_DIM)
    keys_rot = rms_scale(raw_key, key_gain).reshape(length, HEADS, HEAD_DIM)
    return (rotate(queries, cosine, sine_table), rotate(keys_rot, cosine, sine_table))


def swiglu(gate_up):
    half_dim = gate_up.shape[-1] // 2
    gate_part = gate_up[..., :half_dim]
    return gate_part / (1.0 + jnp.exp(-gate_part)) * gate_up[..., half_dim:]


def softmax_rows(logits):
    largest = jnp.max(logits, axis=-1, keepdims=True)
    raised = jnp.exp(logits - largest)
    return raised / jnp.sum(raised, axis=-1, keepdims=True)


def z_size(expert_group):
    return 4 if expert_group % 4 == 0 else 1


def shift(values, expert_group, dz, dx):
    z_all = z_size(expert_group)
    x_all = expert_group // z_all
    pairs = [
        (i, ((i // x_all + dz) % z_all) * x_all + (i % x_all + dx) % x_all)
        for i in range(expert_group)
    ]
    return lax.ppermute(values, "expert", pairs)


def gather_expert(block, expert_group):
    z_all = z_size(expert_group)
    x_all = expert_group // z_all
    rows = [block] + [shift(block, expert_group, dz, 0) for dz in range(1, z_all)]
    return [
        rows[dz] if dx == 0 else shift(rows[dz], expert_group, 0, dx)
        for dz in range(z_all)
        for dx in range(x_all)
    ]


def reduce_expert(parts, expert_group):
    z_all = z_size(expert_group)
    x_all = expert_group // z_all
    rows = []
    for dz in range(z_all):
        total = parts[dz * x_all].astype(jnp.float32)
        for dx in range(1, x_all):
            total = total + shift(parts[dz * x_all + dx], expert_group, 0, -dx).astype(jnp.float32)
        rows.append(total)
    total = rows[0]
    for dz in range(1, z_all):
        total = total + shift(
            rows[dz].astype(jnp.bfloat16), expert_group, -dz, 0
        ).astype(jnp.float32)
    return total


def relative_sources(expert_group):
    z_all = z_size(expert_group)
    x_all = expert_group // z_all
    me = lax.axis_index("expert")
    order = jnp.arange(expert_group, dtype=jnp.int32)
    return ((me // x_all - order // x_all) % z_all) * x_all + (me % x_all - order % x_all) % x_all


def shard_shift(values, shard_group, dy, flip):
    y_all = shard_group // 2
    pairs = [(i, ((i // 2 + dy) % y_all) * 2 + (i % 2 + flip) % 2) for i in range(shard_group)]
    return lax.ppermute(values, "shard", pairs)


def gather_shard(block, shard_group):
    found = []
    for dy in range(shard_group // 2):
        straight = block if dy == 0 else shard_shift(block, shard_group, dy, 0)
        found += [straight, shard_shift(straight, shard_group, 0, 1)]
    return found


def own_columns(values, shard_group):
    me = lax.axis_index("shard")
    y_all = shard_group // 2
    width = values.shape[1] // shard_group
    found = []
    for dy in range(y_all):
        for flip in range(2):
            there = ((me // 2 + dy) % y_all) * 2 + (me % 2 + flip) % 2
            piece = lax.dynamic_slice_in_dim(values, there * width, width, axis=1)
            found.append(piece if dy + flip == 0 else shard_shift(piece, shard_group, dy, flip))
    return jnp.concatenate(found, axis=0)


def tail_kernel(dims, grads_ref, columns_ref, out_ref, gall, xsend, xrecv, zsend, zrecv, acc, fin, *sems):
    steps, width, x_all, z_all, y_all, lag = dims
    (y_s, y_r, core_s, core_r, fwd_s, fwd_r, x_s, x_r, z_s, z_r, zb_s, zb_r, xb_s, xb_r) = sems
    f32, bf16 = jnp.float32, jnp.bfloat16
    length = grads_ref.shape[0]
    rows = columns_ref.shape[0]
    block = rows // (x_all * z_all)
    half = z_all * block
    e = lax.axis_index("expert")
    s = lax.axis_index("shard")
    z, x = e // x_all, lax.rem(e, x_all)
    y, core = s // 2, lax.rem(s, 2)

    def y_peer(d):
        return {"shard": lax.rem(y + d, y_all) * 2 + core}

    partner = {"shard": y * 2 + (1 - core)}

    def x_peer(d):
        return {"expert": z * x_all + lax.rem(x + d, x_all)}

    def z_peer(d):
        return {"expert": lax.rem(z + d, z_all) * x_all + x}

    def copy(src, dst, send, recv, peer):
        return pltpu.make_async_remote_copy(
            src_ref=src, dst_ref=dst, send_sem=send, recv_sem=recv, device_id=peer,
            device_id_type=pl.DeviceIdType.MESH,
        )

    def cols(c):
        return pl.ds(pl.multiple_of(c * width, width), width)

    def y_copy(d, c):
        return copy(grads_ref.at[:, cols(c)], gall.at[2 * d - 1, c], y_s.at[d - 1], y_r.at[d - 1, c], y_peer(d))

    def core_copy(c):
        return copy(grads_ref.at[:, cols(c)], gall.at[0, c], core_s.at[0], core_r.at[c], partner)

    def fwd_copy(d, c):
        return copy(gall.at[2 * d - 1, c], gall.at[2 * d, c], fwd_s.at[d - 1], fwd_r.at[d - 1, c], partner)

    def x_copy(d, c):
        return copy(xsend.at[d - 1, c], xrecv.at[d - 1, c], x_s.at[d - 1], x_r.at[d - 1, c], x_peer(d))

    def z_copy(d, c):
        return copy(zsend.at[d - 1, c], zrecv.at[d - 1, c], z_s.at[d - 1], z_r.at[d - 1, c], z_peer(d))

    def zb_copy(d, c):
        here = fin.at[c, pl.ds(pl.multiple_of((x * z_all + z) * block, block), block)]
        return copy(here, here, zb_s.at[d - 1], zb_r.at[d - 1, c], z_peer(d))

    def xb_copy(d, c):
        here = fin.at[c, pl.ds(pl.multiple_of(x * half, half), half)]
        return copy(here, here, xb_s.at[d - 1], xb_r.at[d - 1, c], x_peer(d))

    barrier = pltpu.get_barrier_semaphore()
    peers = (
        [y_peer(d) for d in range(1, y_all)]
        + [partner]
        + [x_peer(d) for d in range(1, x_all)]
        + [z_peer(d) for d in range(1, z_all)]
    )
    for peer in peers:
        pl.semaphore_signal(barrier, inc=1, device_id=peer, device_id_type=pl.DeviceIdType.MESH)
    pl.semaphore_wait(barrier, len(peers))

    def first(c, carry):
        for d in range(1, y_all):
            y_copy(d, c).start()
        core_copy(c).start()
        return carry

    lax.fori_loop(0, steps, first, 0)
    slots = acc.shape[0]

    def step(t, carry):
        def stage(k, body):
            c = t - k * lag
            pl.when((c >= 0) & (c < steps))(lambda: body(c))

        @functools.partial(stage, 5)
        def _(c):
            for d in range(1, x_all):
                xb_copy(d, c).wait_recv()
            out_ref[:, cols(c)] = fin[c]

        @functools.partial(stage, 4)
        def _(c):
            for d in range(1, z_all):
                zb_copy(d, c).wait_recv()
            for d in range(1, x_all):
                xb_copy(d, c).start()

        @functools.partial(stage, 3)
        def _(c):
            slot = lax.rem(c, slots)
            total = acc[slot, pl.ds(pl.multiple_of(z * block, block), block), :]
            for d in range(1, z_all):
                z_copy(d, c).wait_recv()
                total = total + zrecv[d - 1, c].astype(f32)
            fin[c, pl.ds(pl.multiple_of((x * z_all + z) * block, block), block), :] = total.astype(bf16)
            for d in range(1, z_all):
                zb_copy(d, c).start()

        @functools.partial(stage, 2)
        def _(c):
            slot = lax.rem(c, slots)
            total = acc[slot]
            for d in range(1, x_all):
                x_copy(d, c).wait_recv()
                total = total + xrecv[d - 1, c].astype(f32)
            acc[slot] = total
            for d in range(1, z_all):
                there = lax.rem(z + d, z_all)
                zsend[d - 1, c] = acc[slot, pl.ds(pl.multiple_of(there * block, block), block), :].astype(bf16)
                z_copy(d, c).start()

        @functools.partial(stage, 1)
        def _(c):
            core_copy(c).wait_recv()
            for d in range(1, y_all):
                fwd_copy(d, c).wait_recv()
            others = gall[:, c].reshape((2 * y_all - 1) * length, width)
            mine = grads_ref[:, cols(c)]

            def product(there):
                at = pl.ds(pl.multiple_of(there * half, half), half)
                return jnp.dot(columns_ref[at, :length], mine, preferred_element_type=f32) + jnp.dot(
                    columns_ref[at, length:], others, preferred_element_type=f32
                )

            for d in range(1, x_all):
                xsend[d - 1, c] = product(lax.rem(x + d, x_all)).astype(bf16)
                x_copy(d, c).start()
            acc[lax.rem(c, slots)] = product(x)

        @functools.partial(stage, 0)
        def _(c):
            for d in range(1, y_all):
                y_copy(d, c).wait_recv()
                fwd_copy(d, c).start()

        return carry

    lax.fori_loop(0, steps + 5 * lag, step, 0)

    for d in range(1, y_all):
        copy(grads_ref, grads_ref, y_s.at[d - 1], y_r.at[d - 1, 0], y_peer(d)).wait_send()
        whole = gall.at[2 * d - 1]
        copy(whole, whole, fwd_s.at[d - 1], fwd_r.at[d - 1, 0], partner).wait_send()
    copy(grads_ref, grads_ref, core_s.at[0], core_r.at[0], partner).wait_send()
    for d in range(1, x_all):
        whole = xsend.at[d - 1]
        copy(whole, whole, x_s.at[d - 1], x_r.at[d - 1, 0], x_peer(d)).wait_send()
        copy(whole, whole, xb_s.at[d - 1], xb_r.at[d - 1, 0], x_peer(d)).wait_send()
    for d in range(1, z_all):
        whole = zsend.at[d - 1]
        copy(whole, whole, z_s.at[d - 1], z_r.at[d - 1, 0], z_peer(d)).wait_send()
        copy(whole, whole, zb_s.at[d - 1], zb_r.at[d - 1, 0], z_peer(d)).wait_send()


def summed_rows(columns, grads, expert_group, shard_group, z_all, width, lag, name_id):
    x_all, y_all = expert_group // z_all, shard_group // 2
    length, total = grads.shape
    rows = columns.shape[0]
    steps = total // width
    block = rows // expert_group
    half = z_all * block
    bf16 = jnp.bfloat16
    dma = pltpu.SemaphoreType.DMA
    n1 = max(y_all - 1, 1)
    x1 = max(x_all - 1, 1)
    z1 = max(z_all - 1, 1)
    slots = min(steps, 2 * lag + 1)
    return pl.pallas_call(
        functools.partial(tail_kernel, (steps, width, x_all, z_all, y_all, lag)),
        out_shape=jax.ShapeDtypeStruct((rows, total), bf16),
        in_specs=[pl.BlockSpec(memory_space=pltpu.VMEM)] * 2,
        out_specs=pl.BlockSpec(memory_space=pltpu.VMEM),
        scratch_shapes=[
            pltpu.VMEM((shard_group - 1, steps, length, width), bf16),
            pltpu.VMEM((x1, steps, half, width), bf16),
            pltpu.VMEM((x1, steps, half, width), bf16),
            pltpu.VMEM((z1, steps, block, width), bf16),
            pltpu.VMEM((z1, steps, block, width), bf16),
            pltpu.VMEM((slots, half, width), jnp.float32),
            pltpu.VMEM((steps, rows, width), bf16),
            dma((n1,)), dma((n1, steps)),
            dma((1,)), dma((steps,)),
            dma((n1,)), dma((n1, steps)),
            dma((x1,)), dma((x1, steps)),
            dma((z1,)), dma((z1, steps)),
            dma((z1,)), dma((z1, steps)),
            dma((x1,)), dma((x1, steps)),
        ],
        compiler_params=pltpu.CompilerParams(
            collective_id=name_id, has_side_effects=True, vmem_limit_bytes=60 * 1024 * 1024
        ),
        cost_estimate=pl.CostEstimate(
            flops=2 * rows * length * shard_group * total, bytes_accessed=16 * 1024 * 1024, transcendentals=0
        ),
    )(grads, columns)


def body(
    tokens,
    cotangent,
    segments,
    routes,
    tile_counts,
    norm_one,
    norm_query,
    norm_key,
    norm_two,
    qkv_weight,
    out_weight,
    router_weight,
    gate_up_weight,
    down_weight,
):
    f32, bf16 = jnp.float32, jnp.bfloat16
    length, model_width = tokens.shape
    experts_all = tile_counts.shape[0]
    local_experts = gate_up_weight.shape[0]
    expert_group = lax.axis_size("expert")
    shard_group = lax.axis_size("shard")
    capacity = length * TOP // (experts_all * TILE) * TILE
    score_scale = HEAD_DIM ** (-0.5)
    own_expert = lax.axis_index("expert")
    own_shard = lax.axis_index("shard")
    sources = relative_sources(expert_group)

    def gather(values, axis):
        return lax.all_gather(values, axis, axis=0, tiled=True)

    qkv_full = gather(qkv_weight, "shard")
    out_full = gather(out_weight, "shard")
    router_full = gather(router_weight, "shard")
    gains = lax.all_gather(
        jnp.stack([norm_one, norm_query, norm_key, norm_two]), "shard", axis=1, tiled=True
    ).astype(f32)
    gain_one, gain_query, gain_key, gain_two = gains[0], gains[1], gains[2], gains[3]

    expert_ids = jnp.arange(experts_all, dtype=jnp.int32)
    chosen = jnp.any(routes[:, :, None] == expert_ids[None, None, :], axis=1)
    position = jnp.arange(length, dtype=jnp.int32)
    earlier = (position[:, None] > position[None, :]).astype(bf16)
    rank = jnp.dot(earlier, chosen.astype(bf16), preferred_element_type=f32)
    kept = chosen & (rank < (tile_counts * TILE).astype(f32)[None, :])
    place = jnp.where(kept, rank, -1.0)
    place_all = lax.all_gather(place, "expert", axis=0, tiled=False)[sources]
    place_own = lax.dynamic_slice_in_dim(
        place_all, own_expert * local_experts, local_experts, axis=2
    )
    place_own = place_own.transpose(0, 2, 1)
    slots = jnp.arange(capacity, dtype=jnp.int32).astype(f32)
    one_hot = place_own[:, :, None, :] == slots[None, None, :, None]
    one_hot_low = one_hot.astype(bf16)
    upstream_all = jnp.stack(gather_expert(cotangent, expert_group))

    inputs = tokens.astype(f32)
    scaled_one, first_pull = jax.vjp(rms_scale, inputs, gain_one)
    hidden_one = scaled_one.astype(bf16)
    hidden_one_columns = own_columns(hidden_one, shard_group).T
    projected = jnp.dot(hidden_one, qkv_full, preferred_element_type=f32)
    cosine, sine_table = rotary_tables(length)

    def query_key_local(raw_query, raw_key, query_gain, key_gain):
        return query_key(raw_query, raw_key, query_gain, key_gain, cosine, sine_table)

    rotated, rotary_pull = jax.vjp(
        query_key_local,
        projected[:, :model_width],
        projected[:, model_width : 2 * model_width],
        gain_query,
        gain_key,
    )
    query_low = rotated[0].astype(bf16)
    key_low = rotated[1].astype(bf16)
    value_low = projected[:, 2 * model_width :].astype(bf16).reshape(length, HEADS, HEAD_DIM)
    allowed = (position[:, None] >= position[None, :]) & (
        segments[0][:, None] == segments[0][None, :]
    )
    masked = jnp.where(
        allowed[None],
        jnp.einsum("qhd,khd->hqk", query_low, key_low, preferred_element_type=f32) * score_scale,
        -1e30,
    )
    probs = softmax_rows(masked)
    probs_low = probs.astype(bf16)
    attended_low = (
        jnp.einsum("hqk,khd->qhd", probs_low, value_low, preferred_element_type=f32)
        .reshape(length, model_width)
        .astype(bf16)
    )
    attended_columns = own_columns(attended_low, shard_group)
    middle = inputs + jnp.dot(attended_low, out_full, preferred_element_type=f32)
    scaled_two, second_pull = jax.vjp(rms_scale, middle, gain_two)
    hidden_two = scaled_two.astype(bf16)
    hidden_all = jnp.stack(gather_expert(hidden_two, expert_group))
    router = softmax_rows(jnp.dot(hidden_two, router_full, preferred_element_type=f32))
    router_all = softmax_rows(jnp.dot(hidden_all, router_full, preferred_element_type=f32))
    prob_own = lax.dynamic_slice_in_dim(
        router_all, own_expert * local_experts, local_experts, axis=2
    ).transpose(0, 2, 1)

    expert_rows = jnp.einsum(
        "sect,std->escd", one_hot_low, hidden_all, preferred_element_type=f32
    ).astype(bf16)
    row_count = expert_group * capacity
    expert_rows = expert_rows.reshape(local_experts, row_count, model_width)
    gate_up = jnp.einsum("erd,edf->erf", expert_rows, gate_up_weight, preferred_element_type=f32)
    activated_full, swiglu_pull = jax.vjp(swiglu, gate_up)
    activated = activated_full.astype(bf16)
    expert_out = jnp.einsum(
        "erf,efd->erd", activated, down_weight, preferred_element_type=f32
    ).astype(bf16)
    weighted = jnp.where(one_hot, prob_own[:, :, None, :], 0.0)
    weighted_high = weighted.astype(bf16)
    weighted_low = (weighted - weighted_high.astype(f32)).astype(bf16)
    out_rows = expert_out.reshape(local_experts, expert_group, capacity, model_width)
    mixture_parts = (
        jnp.einsum("sect,escd->std", weighted_high, out_rows, preferred_element_type=f32)
        + jnp.einsum("sect,escd->std", weighted_low, out_rows, preferred_element_type=f32)
    ).astype(bf16)
    mixture = reduce_expert([mixture_parts[i] for i in range(expert_group)], expert_group)
    block_out = (middle + mixture).astype(bf16)

    prob_rows = jnp.sum(weighted, axis=3).transpose(1, 0, 2).reshape(local_experts, row_count)
    upstream_rows = jnp.einsum(
        "sect,std->escd", one_hot_low, upstream_all, preferred_element_type=f32
    ).reshape(local_experts, row_count, model_width)
    grad_expert = (prob_rows[:, :, None] * upstream_rows).astype(bf16)
    grad_prob_rows = jnp.sum(upstream_rows * expert_out.astype(f32), axis=-1).reshape(
        local_experts, expert_group, capacity
    )
    grad_router_parts = jnp.sum(
        jnp.where(one_hot, grad_prob_rows.transpose(1, 0, 2)[:, :, :, None], 0.0), axis=2
    )
    z_all = z_size(expert_group)
    x_all = expert_group // z_all
    back = jnp.stack(
        [
            part if i == 0 else shift(part, expert_group, -(i // x_all), -(i % x_all))
            for i, part in enumerate(grad_router_parts)
        ]
    )
    owners = jnp.arange(expert_group, dtype=jnp.int32)
    entry = ((owners // x_all - own_expert // x_all) % z_all) * x_all + (
        owners % x_all - own_expert % x_all
    ) % x_all
    grad_router = back[entry].reshape(experts_all, length).T
    grad_activated = jnp.einsum("erd,efd->erf", grad_expert, down_weight, preferred_element_type=f32)
    grad_gate_up_low = swiglu_pull(grad_activated)[0].astype(bf16)
    grad_row = jnp.einsum(
        "erf,edf->erd", grad_gate_up_low, gate_up_weight, preferred_element_type=f32
    ).astype(bf16)
    grad_hidden_parts = jnp.einsum(
        "sect,escd->std",
        one_hot_low,
        grad_row.reshape(local_experts, expert_group, capacity, model_width),
        preferred_element_type=f32,
    ).astype(bf16)
    grad_rows_sum = reduce_expert([grad_hidden_parts[i] for i in range(expert_group)], expert_group)
    grad_down_full = jnp.einsum("erf,erd->efd", activated, grad_expert, preferred_element_type=f32)
    grad_gate_up_full = jnp.einsum(
        "erd,erf->edf", expert_rows, grad_gate_up_low, preferred_element_type=f32
    )
    grad_gate_up_weight = lax.psum_scatter(
        grad_gate_up_full.astype(bf16), "shard", scatter_dimension=1, tiled=True
    ).astype(f32)
    grad_down_weight = lax.psum_scatter(
        grad_down_full.astype(bf16), "shard", scatter_dimension=2, tiled=True
    ).astype(f32)

    upstream = cotangent.astype(f32)
    grad_logits = (
        router * (grad_router - jnp.sum(router * grad_router, axis=-1, keepdims=True))
    ).astype(bf16)
    grad_hidden_two = grad_rows_sum + jnp.einsum(
        "te,de->td", grad_logits, router_full, preferred_element_type=f32
    )
    grad_middle_norm, grad_gain_two = second_pull(grad_hidden_two)
    grad_middle = upstream + grad_middle_norm
    grad_branch_low = grad_middle.astype(bf16)
    grad_attended_low = (
        jnp.einsum("te,de->td", grad_branch_low, out_full, preferred_element_type=f32)
        .astype(bf16)
        .reshape(length, HEADS, HEAD_DIM)
    )
    grad_probs = jnp.einsum(
        "qhd,khd->hqk", grad_attended_low, value_low, preferred_element_type=f32
    )
    grad_scores_low = (
        probs * (grad_probs - jnp.sum(probs * grad_probs, axis=-1, keepdims=True))
    ).astype(bf16)
    grad_queries = (
        jnp.einsum("hqk,khd->qhd", grad_scores_low, key_low, preferred_element_type=f32)
        * score_scale
    )
    grad_keys = (
        jnp.einsum("hqk,qhd->khd", grad_scores_low, query_low, preferred_element_type=f32)
        * score_scale
    )
    grad_values = jnp.einsum(
        "hqk,qhd->khd", probs_low, grad_attended_low, preferred_element_type=f32
    )
    grad_raw_query, grad_raw_key, grad_gain_query, grad_gain_key = rotary_pull(
        (grad_queries, grad_keys)
    )
    grad_projected_low = jnp.concatenate(
        [grad_raw_query, grad_raw_key, grad_values.reshape(length, model_width)], axis=-1
    ).astype(bf16)
    grad_hidden_one = jnp.einsum(
        "te,de->td", grad_projected_low, qkv_full, preferred_element_type=f32
    )
    grad_inputs_norm, grad_gain_one = first_pull(grad_hidden_one)
    grad_tokens = grad_middle + grad_inputs_norm

    branch_all = jnp.concatenate(gather_shard(grad_branch_low, shard_group), axis=0)
    grad_out_part = jnp.einsum(
        "td,te->de", attended_columns, branch_all, preferred_element_type=f32
    )
    grad_out_weight = lax.psum(grad_out_part.astype(bf16), "expert").astype(f32)
    grad_qkv_weight = summed_rows(
        hidden_one_columns, grad_projected_low, expert_group, shard_group, z_all, 256, 2, 1
    ).astype(f32)
    grad_router_part = jnp.einsum(
        "td,te->ed", hidden_two, grad_logits, preferred_element_type=f32
    )
    small = jnp.concatenate(
        [
            grad_router_part,
            jnp.stack([grad_gain_one, grad_gain_query, grad_gain_key, grad_gain_two]),
        ],
        axis=0,
    )
    small = lax.psum(small, ("expert", "shard"))
    width = norm_one.shape[0]
    small = lax.dynamic_slice_in_dim(small, own_shard * width, width, axis=1)
    return (
        block_out,
        grad_tokens,
        small[experts_all],
        small[experts_all + 1],
        small[experts_all + 2],
        small[experts_all + 3],
        grad_qkv_weight,
        grad_out_weight,
        small[:experts_all].T,
        grad_gate_up_weight,
        grad_down_weight,
    )


def solution(mesh):
    return jax.shard_map(
        body,
        mesh=mesh,
        in_specs=(
            P(("expert", "shard"), None),
            P(("expert", "shard"), None),
            P(("expert", "shard"), None),
            P(("expert", "shard"), None),
            P(),
            P("shard"),
            P("shard"),
            P("shard"),
            P("shard"),
            P("shard", None),
            P("shard", None),
            P("shard", None),
            P("expert", None, None),
            P("expert", None, None),
        ),
        out_specs=(
            P(("expert", "shard"), None),
            P(("expert", "shard"), None),
            P("shard"),
            P("shard"),
            P("shard"),
            P("shard"),
            P("shard", None),
            P("shard", None),
            P("shard", None),
            P("expert", "shard", None),
            P("expert", None, "shard"),
        ),
        check_vma=False,
    )
```

```python
import functools

import jax
import jax.numpy as jnp
from jax import lax
from jax.experimental import pallas as pl
from jax.experimental.pallas import tpu as pltpu
from jax.sharding import PartitionSpec as P

HEADS = 16
HEAD_DIM = 128
TOP = 8
TILE = 8


epsilon = 1e-05
rope_base = 10000.0


def rms_scale(values, scale_gain):
    return (
        values * lax.rsqrt(jnp.mean(values * values, axis=-1, keepdims=True) + epsilon) * scale_gain
    )


def rotary_tables(length):
    half_dim = HEAD_DIM // 2
    position = jnp.arange(length, dtype=jnp.float32)[:, None]
    frequency = rope_base ** (-jnp.arange(half_dim, dtype=jnp.float32) * 2.0 / HEAD_DIM)
    angles = position * frequency[None, :]
    angles = jnp.concatenate([angles, angles], axis=-1)
    return (jnp.cos(angles)[:, None, :], jnp.sin(angles)[:, None, :])


def rotate(vectors, cosine, sine_table):
    half_dim = vectors.shape[-1] // 2
    turned = jnp.concatenate([-vectors[..., half_dim:], vectors[..., :half_dim]], axis=-1)
    return vectors * cosine + turned * sine_table


def query_key(raw_query, raw_key, query_gain, key_gain, cosine, sine_table):
    length = raw_query.shape[0]
    queries = rms_scale(raw_query, query_gain).reshape(length, HEADS, HEAD_DIM)
    keys_rot = rms_scale(raw_key, key_gain).reshape(length, HEADS, HEAD_DIM)
    return (rotate(queries, cosine, sine_table), rotate(keys_rot, cosine, sine_table))


def swiglu(gate_up):
    half_dim = gate_up.shape[-1] // 2
    gate_part = gate_up[..., :half_dim]
    return gate_part / (1.0 + jnp.exp(-gate_part)) * gate_up[..., half_dim:]


def softmax_rows(logits):
    largest = jnp.max(logits, axis=-1, keepdims=True)
    raised = jnp.exp(logits - largest)
    return raised / jnp.sum(raised, axis=-1, keepdims=True)


def z_size(expert_group):
    return 4 if expert_group % 4 == 0 else 1


def shift(values, expert_group, dz, dx):
    z_all = z_size(expert_group)
    x_all = expert_group // z_all
    pairs = [
        (i, ((i // x_all + dz) % z_all) * x_all + (i % x_all + dx) % x_all)
        for i in range(expert_group)
    ]
    return lax.ppermute(values, "expert", pairs)


def gather_expert(block, expert_group):
    z_all = z_size(expert_group)
    x_all = expert_group // z_all
    rows = [block] + [shift(block, expert_group, dz, 0) for dz in range(1, z_all)]
    return [
        rows[dz] if dx == 0 else shift(rows[dz], expert_group, 0, dx)
        for dz in range(z_all)
        for dx in range(x_all)
    ]


def reduce_expert(parts, expert_group):
    z_all = z_size(expert_group)
    rows = parts[0].astype(jnp.float32)
    for dx in range(1, len(parts)):
        rows = rows + shift(parts[dx], expert_group, 0, -dx).astype(jnp.float32)
    total = rows[0]
    for dz in range(1, z_all):
        total = total + shift(
            rows[dz].astype(jnp.bfloat16), expert_group, -dz, 0
        ).astype(jnp.float32)
    return total


def relative_sources(expert_group):
    z_all = z_size(expert_group)
    x_all = expert_group // z_all
    me = lax.axis_index("expert")
    order = jnp.arange(expert_group, dtype=jnp.int32)
    return ((me // x_all - order // x_all) % z_all) * x_all + (me % x_all - order % x_all) % x_all


def shard_shift(values, shard_group, dy, flip):
    y_all = shard_group // 2
    pairs = [(i, ((i // 2 + dy) % y_all) * 2 + (i % 2 + flip) % 2) for i in range(shard_group)]
    return lax.ppermute(values, "shard", pairs)


def gather_shard(block, shard_group):
    found = []
    for dy in range(shard_group // 2):
        straight = block if dy == 0 else shard_shift(block, shard_group, dy, 0)
        found += [straight, shard_shift(straight, shard_group, 0, 1)]
    return found


def own_columns(values, shard_group):
    me = lax.axis_index("shard")
    y_all = shard_group // 2
    width = values.shape[1] // shard_group
    found = []
    for dy in range(y_all):
        for flip in range(2):
            there = ((me // 2 + dy) % y_all) * 2 + (me % 2 + flip) % 2
            piece = lax.dynamic_slice_in_dim(values, there * width, width, axis=1)
            found.append(piece if dy + flip == 0 else shard_shift(piece, shard_group, dy, flip))
    return jnp.concatenate(found, axis=0)


def tail_kernel(dims, grads_ref, columns_ref, out_ref, gall, xsend, xrecv, zsend, zrecv, acc, fin, *sems):
    steps, width, x_all, z_all, y_all, lag = dims
    (y_s, y_r, core_s, core_r, fwd_s, fwd_r, x_s, x_r, z_s, z_r, zb_s, zb_r, xb_s, xb_r) = sems
    f32, bf16 = jnp.float32, jnp.bfloat16
    length = grads_ref.shape[0]
    rows = columns_ref.shape[0]
    block = rows // (x_all * z_all)
    half = z_all * block
    e = lax.axis_index("expert")
    s = lax.axis_index("shard")
    z, x = e // x_all, lax.rem(e, x_all)
    y, core = s // 2, lax.rem(s, 2)

    def y_peer(d):
        return {"shard": lax.rem(y + d, y_all) * 2 + core}

    partner = {"shard": y * 2 + (1 - core)}

    def x_peer(d):
        return {"expert": z * x_all + lax.rem(x + d, x_all)}

    def z_peer(d):
        return {"expert": lax.rem(z + d, z_all) * x_all + x}

    def copy(src, dst, send, recv, peer):
        return pltpu.make_async_remote_copy(
            src_ref=src, dst_ref=dst, send_sem=send, recv_sem=recv, device_id=peer,
            device_id_type=pl.DeviceIdType.MESH,
        )

    def cols(c):
        return pl.ds(pl.multiple_of(c * width, width), width)

    def y_copy(d, c):
        return copy(grads_ref.at[:, cols(c)], gall.at[2 * d - 1, c], y_s.at[d - 1], y_r.at[d - 1, c], y_peer(d))

    def core_copy(c):
        return copy(grads_ref.at[:, cols(c)], gall.at[0, c], core_s.at[0], core_r.at[c], partner)

    def fwd_copy(d, c):
        return copy(gall.at[2 * d - 1, c], gall.at[2 * d, c], fwd_s.at[d - 1], fwd_r.at[d - 1, c], partner)

    def x_copy(d, c):
        return copy(xsend.at[d - 1, c], xrecv.at[d - 1, c], x_s.at[d - 1], x_r.at[d - 1, c], x_peer(d))

    def z_copy(d, c):
        return copy(zsend.at[d - 1, c], zrecv.at[d - 1, c], z_s.at[d - 1], z_r.at[d - 1, c], z_peer(d))

    def zb_copy(d, c):
        here = fin.at[c, pl.ds(pl.multiple_of((x * z_all + z) * block, block), block)]
        return copy(here, here, zb_s.at[d - 1], zb_r.at[d - 1, c], z_peer(d))

    def xb_copy(d, c):
        here = fin.at[c, pl.ds(pl.multiple_of(x * half, half), half)]
        return copy(here, here, xb_s.at[d - 1], xb_r.at[d - 1, c], x_peer(d))

    barrier = pltpu.get_barrier_semaphore()
    peers = (
        [y_peer(d) for d in range(1, y_all)]
        + [partner]
        + [x_peer(d) for d in range(1, x_all)]
        + [z_peer(d) for d in range(1, z_all)]
    )
    for peer in peers:
        pl.semaphore_signal(barrier, inc=1, device_id=peer, device_id_type=pl.DeviceIdType.MESH)
    pl.semaphore_wait(barrier, len(peers))

    def first(c, carry):
        for d in range(1, y_all):
            y_copy(d, c).start()
        core_copy(c).start()
        return carry

    lax.fori_loop(0, steps, first, 0)
    slots = acc.shape[0]

    def step(t, carry):
        def stage(k, body):
            c = t - k * lag
            pl.when((c >= 0) & (c < steps))(lambda: body(c))

        @functools.partial(stage, 5)
        def _(c):
            for d in range(1, x_all):
                xb_copy(d, c).wait_recv()
            out_ref[:, cols(c)] = fin[c]

        @functools.partial(stage, 4)
        def _(c):
            for d in range(1, z_all):
                zb_copy(d, c).wait_recv()
            for d in range(1, x_all):
                xb_copy(d, c).start()

        @functools.partial(stage, 3)
        def _(c):
            slot = lax.rem(c, slots)
            total = acc[slot, pl.ds(pl.multiple_of(z * block, block), block), :]
            for d in range(1, z_all):
                z_copy(d, c).wait_recv()
                total = total + zrecv[d - 1, c].astype(f32)
            fin[c, pl.ds(pl.multiple_of((x * z_all + z) * block, block), block), :] = total.astype(bf16)
            for d in range(1, z_all):
                zb_copy(d, c).start()

        @functools.partial(stage, 2)
        def _(c):
            slot = lax.rem(c, slots)
            total = acc[slot]
            for d in range(1, x_all):
                x_copy(d, c).wait_recv()
                total = total + xrecv[d - 1, c].astype(f32)
            acc[slot] = total
            for d in range(1, z_all):
                there = lax.rem(z + d, z_all)
                zsend[d - 1, c] = acc[slot, pl.ds(pl.multiple_of(there * block, block), block), :].astype(bf16)
                z_copy(d, c).start()

        @functools.partial(stage, 1)
        def _(c):
            core_copy(c).wait_recv()
            for d in range(1, y_all):
                fwd_copy(d, c).wait_recv()
            others = gall[:, c].reshape((2 * y_all - 1) * length, width)
            mine = grads_ref[:, cols(c)]

            def product(there):
                at = pl.ds(pl.multiple_of(there * half, half), half)
                return jnp.dot(columns_ref[at, :length], mine, preferred_element_type=f32) + jnp.dot(
                    columns_ref[at, length:], others, preferred_element_type=f32
                )

            for d in range(1, x_all):
                xsend[d - 1, c] = product(lax.rem(x + d, x_all)).astype(bf16)
                x_copy(d, c).start()
            acc[lax.rem(c, slots)] = product(x)

        @functools.partial(stage, 0)
        def _(c):
            for d in range(1, y_all):
                y_copy(d, c).wait_recv()
                fwd_copy(d, c).start()

        return carry

    lax.fori_loop(0, steps + 5 * lag, step, 0)

    for d in range(1, y_all):
        copy(grads_ref, grads_ref, y_s.at[d - 1], y_r.at[d - 1, 0], y_peer(d)).wait_send()
        whole = gall.at[2 * d - 1]
        copy(whole, whole, fwd_s.at[d - 1], fwd_r.at[d - 1, 0], partner).wait_send()
    copy(grads_ref, grads_ref, core_s.at[0], core_r.at[0], partner).wait_send()
    for d in range(1, x_all):
        whole = xsend.at[d - 1]
        copy(whole, whole, x_s.at[d - 1], x_r.at[d - 1, 0], x_peer(d)).wait_send()
        copy(whole, whole, xb_s.at[d - 1], xb_r.at[d - 1, 0], x_peer(d)).wait_send()
    for d in range(1, z_all):
        whole = zsend.at[d - 1]
        copy(whole, whole, z_s.at[d - 1], z_r.at[d - 1, 0], z_peer(d)).wait_send()
        copy(whole, whole, zb_s.at[d - 1], zb_r.at[d - 1, 0], z_peer(d)).wait_send()


def summed_rows(columns, grads, expert_group, shard_group, z_all, width, lag, name_id):
    x_all, y_all = expert_group // z_all, shard_group // 2
    length, total = grads.shape
    rows = columns.shape[0]
    steps = total // width
    block = rows // expert_group
    half = z_all * block
    bf16 = jnp.bfloat16
    dma = pltpu.SemaphoreType.DMA
    n1 = max(y_all - 1, 1)
    x1 = max(x_all - 1, 1)
    z1 = max(z_all - 1, 1)
    slots = min(steps, 2 * lag + 1)
    return pl.pallas_call(
        functools.partial(tail_kernel, (steps, width, x_all, z_all, y_all, lag)),
        out_shape=jax.ShapeDtypeStruct((rows, total), bf16),
        in_specs=[pl.BlockSpec(memory_space=pltpu.VMEM)] * 2,
        out_specs=pl.BlockSpec(memory_space=pltpu.VMEM),
        scratch_shapes=[
            pltpu.VMEM((shard_group - 1, steps, length, width), bf16),
            pltpu.VMEM((x1, steps, half, width), bf16),
            pltpu.VMEM((x1, steps, half, width), bf16),
            pltpu.VMEM((z1, steps, block, width), bf16),
            pltpu.VMEM((z1, steps, block, width), bf16),
            pltpu.VMEM((slots, half, width), jnp.float32),
            pltpu.VMEM((steps, rows, width), bf16),
            dma((n1,)), dma((n1, steps)),
            dma((1,)), dma((steps,)),
            dma((n1,)), dma((n1, steps)),
            dma((x1,)), dma((x1, steps)),
            dma((z1,)), dma((z1, steps)),
            dma((z1,)), dma((z1, steps)),
            dma((x1,)), dma((x1, steps)),
        ],
        compiler_params=pltpu.CompilerParams(
            collective_id=name_id, has_side_effects=True, vmem_limit_bytes=60 * 1024 * 1024
        ),
        cost_estimate=pl.CostEstimate(
            flops=2 * rows * length * shard_group * total, bytes_accessed=16 * 1024 * 1024, transcendentals=0
        ),
    )(grads, columns)


MOE_CHUNKS = 4


def moe_kernel(
    dims, hidden_hbm, upstream_hbm, place_ref, place_t_ref, router_ref, router_t_ref, gate_up_hbm, down_hbm,
    rows_hbm, activated_hbm, grad_out_hbm, grad_gate_up_hbm, grad_ref, grad_router_ref, found_hbm, summed_hbm,
    *rest,
):
    x_all, capacity = dims
    mixture_hbm = rest[:x_all]
    (
    gate_up_w, down_w, hid, ups, prob, prob_t, rows, gate_up, activated, out_rows, grad_expert, grad_gate_up, grad_rows,
    mix_stage, part_stage, own_part, z_landed, router_stage,
    w_sem, own_sem, load_sem, store_sem, zs, zr, xs, xr, fs, fr, ps, pr, qs, qr, rs, rr, lsem, mix_sem,
    ) = rest[x_all:]
    z_all = 4
    f32, bf16 = jnp.float32, jnp.bfloat16
    length, width = hidden_hbm.shape
    local_experts, _, twice = gate_up_w.shape
    half = twice // 2
    tile = min(512, half)
    narrow = min(256, half)
    chunk = length // MOE_CHUNKS
    e = lax.axis_index("expert")
    z, x = e // x_all, lax.rem(e, x_all)

    def peer(dz, dx):
        return {"expert": lax.rem(z + dz + 4 * z_all, z_all) * x_all + lax.rem(x + dx + 4 * x_all, x_all)}

    def copy(src, dst, send, recv, to):
        return pltpu.make_async_remote_copy(
            src_ref=src, dst_ref=dst, send_sem=send, recv_sem=recv, device_id=to,
            device_id_type=pl.DeviceIdType.MESH,
        )

    def at(c):
        return pl.ds(pl.multiple_of(c * chunk, chunk), chunk)

    def z_copy(d, c):
        return copy(hidden_hbm.at[at(c)], found_hbm.at[d, 0, at(c)], zs.at[d - 1, c], zr.at[d - 1, c], peer(d, 0))

    def x_copy(d, c):
        return copy(hidden_hbm.at[at(c)], found_hbm.at[0, d, at(c)], xs.at[d - 1, c], xr.at[d - 1, c], peer(0, d))

    def f_copy(dz, dx, c):
        return copy(
            found_hbm.at[dz, 0, at(c)], found_hbm.at[dz, dx, at(c)],
            fs.at[dz - 1, dx - 1, c], fr.at[dz - 1, dx - 1, c], peer(0, dx),
        )

    def p_copy(dz, dx):
        return copy(part_stage.at[dx - 1], summed_hbm.at[dz, dx - 1], ps.at[dx - 1], pr.at[dz, dx - 1], peer(0, -dx))

    def q_copy(dz):
        return copy(own_part.at[dz], z_landed.at[dz - 1], qs.at[dz - 1], qr.at[dz - 1], peer(-dz, 0))

    def r_copy(dz, dx):
        return copy(
            router_stage.at[dz, dx], grad_router_ref.at[e], rs.at[dz, dx], rr.at[dz, dx], peer(-dz, -dx)
        )

    def cols(n, w):
        return pl.ds(pl.multiple_of(n * w, w), w)

    barrier = pltpu.get_barrier_semaphore()
    others = [(dz, dx) for dz in range(z_all) for dx in range(x_all) if dz + dx > 0]
    for dz, dx in others:
        pl.semaphore_signal(barrier, inc=1, device_id=peer(dz, dx), device_id_type=pl.DeviceIdType.MESH)
    pl.semaphore_wait(barrier, len(others))

    own = pltpu.make_async_copy(hidden_hbm, found_hbm.at[0, 0], own_sem)
    own.start()
    weights = [
        pltpu.make_async_copy(gate_up_hbm, gate_up_w, w_sem.at[0]),
        pltpu.make_async_copy(down_hbm, down_w, w_sem.at[1]),
    ]
    for w in weights:
        w.start()

    def send_own(c, carry):
        for d in range(1, x_all):
            x_copy(d, c).start()
        return carry

    lax.fori_loop(0, MOE_CHUNKS, send_own, 0)
    for d in (2, 1, 3):

        def send_z(c, carry):
            z_copy(d, c).start()
            return carry

        lax.fori_loop(0, MOE_CHUNKS, send_z, 0)

    def events(first):
        def one(k, carry):
            @pl.when(k < 3 * MOE_CHUNKS)
            def _():
                j = k // MOE_CHUNKS
                c = lax.rem(k, MOE_CHUNKS)
                d = 2 - j + 3 * (j // 2)
                z_copy(d, c).wait_recv()
                for dx in range(1, x_all):
                    f_copy(d, dx, c).start()

            return carry

        lax.fori_loop(first, first + 2, one, 0)

    def finish(g):
        dz = g // 2 + 2 * lax.rem(g, 2)
        for dx in range(1, x_all):
            p_copy(dz, dx).wait_recv()
            load = pltpu.make_async_copy(summed_hbm.at[dz, dx - 1], hid.at[0], lsem)
            load.start()
            load.wait()

            def add(n, carry):
                c = cols(n, tile)
                own_part[dz, :, c] = (own_part[dz, :, c].astype(f32) + hid[0, :, c].astype(f32)).astype(bf16)
                return carry

            lax.fori_loop(0, width // tile, add, 0)

        @pl.when(dz > 0)
        def _():
            q_copy(dz).start()

    mix_slots = mix_stage.shape[0]

    def mix_copy(dz, dx):
        slot = dx % mix_slots
        return pltpu.make_async_copy(mix_stage.at[slot], mixture_hbm[dx].at[dz], mix_sem.at[slot])

    slot_row = lax.broadcasted_iota(jnp.int32, (capacity, length), 0).astype(f32)
    slot_col = lax.broadcasted_iota(jnp.int32, (length, capacity), 1).astype(f32)
    own.wait()
    events(0)

    def group(g, carry):
        dz = g // 2 + 2 * lax.rem(g, 2)

        def arrive(c, inner):
            for dx in range(1, x_all):

                @pl.when(dz == 0)
                def _():
                    x_copy(dx, c).wait_recv()

                @pl.when(dz > 0)
                def _():
                    f_copy(dz, dx, c).wait_recv()

            return inner

        lax.fori_loop(0, MOE_CHUNKS, arrive, 0)
        loads = []
        for dx in range(x_all):
            loads.append(pltpu.make_async_copy(found_hbm.at[dz, dx], hid.at[dx], load_sem.at[0, dx]))
            loads.append(pltpu.make_async_copy(upstream_hbm.at[dz, dx], ups.at[dx], load_sem.at[1, dx]))
        for load in loads:
            load.start()
        for load in loads:
            load.wait()
        pl.when(g == 0)(lambda: [w.wait() for w in weights] and None)

        for dx in range(x_all):
            logits = jnp.dot(hid[dx], router_ref[...], preferred_element_type=f32)
            raised = jnp.exp(logits - jnp.max(logits, axis=1, keepdims=True))
            prob[dx] = raised / jnp.sum(raised, axis=1, keepdims=True)
            logits = lax.dot_general(
                router_t_ref[...], hid[dx], (((1,), (1,)), ((), ())), preferred_element_type=f32
            )
            raised = jnp.exp(logits - jnp.max(logits, axis=0, keepdims=True))
            prob_t[dx] = raised / jnp.sum(raised, axis=0, keepdims=True)
            router_stage[dz, dx] = jnp.zeros(router_stage.shape[2:], f32)

        def store(kind, buffer, hbm, le):
            return pltpu.make_async_copy(buffer, hbm.at[le, dz], store_sem.at[kind])

        def expert(le, inner):
            @pl.when(g + le > 0)
            def _():
                store(0, rows, rows_hbm, le).wait()
                store(1, activated, activated_hbm, le).wait()
                store(2, grad_expert, grad_out_hbm, le).wait()
                store(3, grad_gate_up, grad_gate_up_hbm, le).wait()

            chosen = [place_ref[dz, dx, pl.ds(le, 1), :] == slot_row for dx in range(x_all)]
            chosen_low = [c.astype(f32).astype(bf16) for c in chosen]

            def dispatch(n, c0):
                c = cols(n, tile)
                for dx in range(x_all):
                    rows[dx * capacity : (dx + 1) * capacity, c] = jnp.dot(
                        chosen_low[dx], hid[dx, :, c], preferred_element_type=f32
                    ).astype(bf16)
                return c0

            lax.fori_loop(0, width // tile, dispatch, 0)
            store(0, rows, rows_hbm, le).start()

            def up_step(n, c0):
                c = cols(n, tile)
                gate_up[:, c] = jnp.dot(rows[...], gate_up_w[le, :, c], preferred_element_type=f32)
                return c0

            lax.fori_loop(0, twice // tile, up_step, 0)

            def act_step(n, c0):
                gate = gate_up[:, cols(n, narrow)]
                up = gate_up[:, pl.ds(pl.multiple_of(half + n * narrow, narrow), narrow)]
                activated[:, cols(n, narrow)] = (gate / (1.0 + jnp.exp(-gate)) * up).astype(bf16)
                return c0

            lax.fori_loop(0, half // narrow, act_step, 0)
            store(1, activated, activated_hbm, le).start()

            def down_step(n, c0):
                c = cols(n, tile)
                out_rows[le, :, c] = jnp.dot(
                    activated[...], down_w[le, :, c], preferred_element_type=f32
                ).astype(bf16)
                return c0

            lax.fori_loop(0, width // tile, down_step, 0)

            mine = e * local_experts + le
            weight_rows = [
                jnp.sum(jnp.where(chosen[dx], prob_t[dx, pl.ds(mine, 1), :], 0.0), axis=1, keepdims=True)
                for dx in range(x_all)
            ]

            def grad_step(n, totals):
                c = cols(n, tile)
                new = []
                for dx in range(x_all):
                    r = slice(dx * capacity, (dx + 1) * capacity)
                    up_rows = jnp.dot(chosen_low[dx], ups[dx, :, c], preferred_element_type=f32)
                    grad_expert[r, c] = (weight_rows[dx] * up_rows).astype(bf16)
                    new.append(
                        totals[dx]
                        + jnp.sum(up_rows * out_rows[le, r, c].astype(f32), axis=1, keepdims=True)
                    )
                return tuple(new)

            totals = lax.fori_loop(
                0, width // tile, grad_step, tuple(jnp.zeros((capacity, 1), f32) for _ in range(x_all))
            )
            store(2, grad_expert, grad_out_hbm, le).start()
            for dx in range(x_all):
                router_stage[dz, dx, pl.ds(le, 1), :] = jnp.sum(
                    jnp.where(chosen[dx], totals[dx], 0.0), axis=0, keepdims=True
                )

            def back_step(n, c0):
                ga = lax.dot_general(
                    grad_expert[...], down_w[le, cols(n, narrow), :], (((1,), (1,)), ((), ())),
                    preferred_element_type=f32,
                )
                gate = gate_up[:, cols(n, narrow)]
                c_up = pl.ds(pl.multiple_of(half + n * narrow, narrow), narrow)
                up = gate_up[:, c_up]
                sg = 1.0 / (1.0 + jnp.exp(-gate))
                grad_gate_up[:, cols(n, narrow)] = (ga * up * sg * (1.0 + gate * (1.0 - sg))).astype(bf16)
                grad_gate_up[:, c_up] = (ga * (gate * sg)).astype(bf16)
                return c0

            lax.fori_loop(0, half // narrow, back_step, 0)
            store(3, grad_gate_up, grad_gate_up_hbm, le).start()

            def row_step(n, c0):
                grad_rows[le, :, cols(n, narrow)] = lax.dot_general(
                    grad_gate_up[...], gate_up_w[le, cols(n, narrow), :], (((1,), (1,)), ((), ())),
                    preferred_element_type=f32,
                ).astype(bf16)
                return c0

            lax.fori_loop(0, width // narrow, row_step, 0)
            events(4 * g + 2 + 2 * le)
            return inner

        assert local_experts == 2
        lax.fori_loop(0, local_experts, expert, 0)

        def stages():
            for dx in range(1, x_all):
                p_copy(dz, dx).wait_send()

        pl.when(g > 0)(stages)
        for dx in range(x_all):
            r = slice(dx * capacity, (dx + 1) * capacity)
            low, high, remainder = [], [], []
            for le in range(local_experts):
                mask = place_t_ref[dz, dx, :, le : le + 1] == slot_col
                lane = lax.broadcasted_iota(jnp.int32, prob.shape[1:], 1)
                p = jnp.sum(jnp.where(lane == e * local_experts + le, prob[dx], 0.0), axis=1, keepdims=True)
                weight = jnp.where(mask, p, 0.0)
                top = weight.astype(bf16)
                low.append(mask.astype(f32).astype(bf16))
                high.append(top)
                remainder.append((weight - top.astype(f32)).astype(bf16))

            if dx < mix_slots:
                pl.when(g > 0)(mix_copy(0, dx).wait)
            else:
                mix_copy(0, dx).wait()

            def combine(n, c0):
                c = cols(n, tile)
                mix = jnp.zeros((length, tile), f32)
                grad = jnp.zeros((length, tile), f32)
                for le in range(local_experts):
                    mix = mix + jnp.dot(high[le], out_rows[le, r, c], preferred_element_type=f32)
                    mix = mix + jnp.dot(remainder[le], out_rows[le, r, c], preferred_element_type=f32)
                    grad = grad + jnp.dot(low[le], grad_rows[le, r, c], preferred_element_type=f32)
                mix_stage[dx % mix_slots, :, c] = mix.astype(bf16)
                if dx == 0:
                    own_part[dz, :, c] = grad.astype(bf16)
                else:
                    part_stage[dx - 1, :, c] = grad.astype(bf16)
                return c0

            lax.fori_loop(0, width // tile, combine, 0)
            mix_copy(dz, dx).start()
            if dx > 0:
                p_copy(dz, dx).start()
                r_copy(dz, dx).start()
            else:

                @pl.when(dz > 0)
                def _():
                    r_copy(dz, 0).start()

                @pl.when(dz == 0)
                def _():
                    grad_router_ref[e] = router_stage[0, 0]

        pl.when(g > 0)(lambda: finish(g - 1))
        return carry

    lax.fori_loop(0, z_all, group, 0)
    finish(jnp.int32(z_all - 1))

    def total(n, carry):
        c = cols(n, tile)
        grad_ref[:, c] = own_part[0, :, c].astype(f32)
        return carry

    lax.fori_loop(0, width // tile, total, 0)
    for d in (2, 1, 3):
        q_copy(d).wait_recv()

        def more(n, carry):
            c = cols(n, tile)
            grad_ref[:, c] = grad_ref[:, c] + z_landed[d - 1, :, c].astype(f32)
            return carry

        lax.fori_loop(0, width // tile, more, 0)

    for kind, buffer, hbm in (
        (0, rows, rows_hbm), (1, activated, activated_hbm), (2, grad_expert, grad_out_hbm),
        (3, grad_gate_up, grad_gate_up_hbm),
    ):
        pltpu.make_async_copy(buffer, hbm.at[0, 0], store_sem.at[kind]).wait()
    for dx in range(mix_slots):
        mix_copy(0, dx).wait()
    for dx in range(1, x_all):
        p_copy(0, dx).wait_send()
    for d in range(1, z_all):
        q_copy(d).wait_send()
    for dz, dx in others:
        r_copy(dz, dx).wait_send()
        r_copy(dz, dx).wait_recv()

    def sent(c, carry):
        for d in range(1, z_all):
            z_copy(d, c).wait_send()
            for dx in range(1, x_all):
                f_copy(d, dx, c).wait_send()
        for d in range(1, x_all):
            x_copy(d, c).wait_send()
        return carry

    lax.fori_loop(0, MOE_CHUNKS, sent, 0)


def moe_layer(hidden, upstream_all, place, router_weight, gate_up_weight, down_weight, expert_group, capacity, name_id):
    f32, bf16 = jnp.float32, jnp.bfloat16
    length, width = hidden.shape
    local_experts, _, twice = gate_up_weight.shape
    half = twice // 2
    experts_all = router_weight.shape[1]
    x_all = expert_group // 4
    count = x_all * capacity
    dma = pltpu.SemaphoreType.DMA
    x1 = max(x_all - 1, 1)
    place_t = place.transpose(0, 1, 3, 2)
    spare = (-local_experts) % 8
    place = jnp.pad(place, ((0, 0), (0, 0), (0, spare), (0, 0)), constant_values=-1.0)
    any_spec = pl.BlockSpec(memory_space=pl.ANY)
    vmem_spec = pl.BlockSpec(memory_space=pltpu.VMEM)
    out = pl.pallas_call(
        functools.partial(moe_kernel, (x_all, capacity)),
        out_shape=[
            jax.ShapeDtypeStruct((local_experts, 4, count, width), bf16),
            jax.ShapeDtypeStruct((local_experts, 4, count, half), bf16),
            jax.ShapeDtypeStruct((local_experts, 4, count, width), bf16),
            jax.ShapeDtypeStruct((local_experts, 4, count, twice), bf16),
            jax.ShapeDtypeStruct((length, width), f32),
            jax.ShapeDtypeStruct((expert_group, 8, length), f32),
            jax.ShapeDtypeStruct((4, x_all, length, width), bf16),
            jax.ShapeDtypeStruct((4, x1, length, width), bf16),
        ]
        + [jax.ShapeDtypeStruct((4, length, width), bf16)] * x_all,
        in_specs=[any_spec, any_spec, vmem_spec, vmem_spec, vmem_spec, vmem_spec, any_spec, any_spec],
        out_specs=[any_spec] * 4 + [vmem_spec, vmem_spec] + [any_spec] * (2 + x_all),
        scratch_shapes=[
            pltpu.VMEM(gate_up_weight.shape, bf16),
            pltpu.VMEM(down_weight.shape, bf16),
            pltpu.VMEM((x_all, length, width), bf16),
            pltpu.VMEM((x_all, length, width), bf16),
            pltpu.VMEM((x_all, length, experts_all), f32),
            pltpu.VMEM((x_all, experts_all, length), f32),
            pltpu.VMEM((count, width), bf16),
            pltpu.VMEM((count, twice), f32),
            pltpu.VMEM((count, half), bf16),
            pltpu.VMEM((local_experts, count, width), bf16),
            pltpu.VMEM((count, width), bf16),
            pltpu.VMEM((count, twice), bf16),
            pltpu.VMEM((local_experts, count, width), bf16),
            pltpu.VMEM((min(2, x_all), length, width), bf16),
            pltpu.VMEM((x1, length, width), bf16),
            pltpu.VMEM((4, length, width), bf16),
            pltpu.VMEM((3, length, width), bf16),
            pltpu.VMEM((4, x_all, 8, length), f32),
            dma((2,)), dma, dma((2, x_all)), dma((4,)),
            dma((3, MOE_CHUNKS)), dma((3, MOE_CHUNKS)),
            dma((x1, MOE_CHUNKS)), dma((x1, MOE_CHUNKS)),
            dma((3, x1, MOE_CHUNKS)), dma((3, x1, MOE_CHUNKS)),
            dma((x1,)), dma((4, x1)),
            dma((3,)), dma((3,)),
            dma((4, x_all)), dma((4, x_all)),
            dma, dma((min(2, x_all),)),
        ],
        compiler_params=pltpu.CompilerParams(
            collective_id=name_id, has_side_effects=True, vmem_limit_bytes=62 * 1024 * 1024
        ),
        cost_estimate=pl.CostEstimate(
            flops=12 * 4 * local_experts * count * width * twice, bytes_accessed=64 * 1024 * 1024,
            transcendentals=0,
        ),
    )(
        hidden, upstream_all, place, place_t, router_weight, router_weight.T, gate_up_weight, down_weight
    )
    return out[:6], out[8:]


def body(
    tokens,
    cotangent,
    segments,
    routes,
    tile_counts,
    norm_one,
    norm_query,
    norm_key,
    norm_two,
    qkv_weight,
    out_weight,
    router_weight,
    gate_up_weight,
    down_weight,
):
    f32, bf16 = jnp.float32, jnp.bfloat16
    length, model_width = tokens.shape
    experts_all = tile_counts.shape[0]
    local_experts = gate_up_weight.shape[0]
    expert_group = lax.axis_size("expert")
    shard_group = lax.axis_size("shard")
    capacity = length * TOP // (experts_all * TILE) * TILE
    score_scale = HEAD_DIM ** (-0.5)
    own_expert = lax.axis_index("expert")
    own_shard = lax.axis_index("shard")
    sources = relative_sources(expert_group)

    def gather(values, axis):
        return lax.all_gather(values, axis, axis=0, tiled=True)

    qkv_full = gather(qkv_weight, "shard")
    out_full = gather(out_weight, "shard")
    router_full = gather(router_weight, "shard")
    gains = lax.all_gather(
        jnp.stack([norm_one, norm_query, norm_key, norm_two]), "shard", axis=1, tiled=True
    ).astype(f32)
    gain_one, gain_query, gain_key, gain_two = gains[0], gains[1], gains[2], gains[3]

    expert_ids = jnp.arange(experts_all, dtype=jnp.int32)
    chosen = jnp.any(routes[:, :, None] == expert_ids[None, None, :], axis=1)
    position = jnp.arange(length, dtype=jnp.int32)
    earlier = (position[:, None] > position[None, :]).astype(bf16)
    rank = jnp.dot(earlier, chosen.astype(bf16), preferred_element_type=f32)
    kept = chosen & (rank < (tile_counts * TILE).astype(f32)[None, :])
    place = jnp.where(kept, rank, -1.0)
    place_all = lax.all_gather(place, "expert", axis=0, tiled=False)[sources]
    place_own = lax.dynamic_slice_in_dim(
        place_all, own_expert * local_experts, local_experts, axis=2
    )
    z_all = z_size(expert_group)
    x_all = expert_group // z_all
    place_own = place_own.transpose(0, 2, 1).reshape(z_all, x_all, local_experts, length)
    upstream_all = jnp.stack(gather_expert(cotangent, expert_group))
    upstream_all = upstream_all.reshape(z_all, x_all, length, model_width)

    inputs = tokens.astype(f32)
    scaled_one, first_pull = jax.vjp(rms_scale, inputs, gain_one)
    hidden_one = scaled_one.astype(bf16)
    hidden_one_columns = own_columns(hidden_one, shard_group).T
    projected = jnp.dot(hidden_one, qkv_full, preferred_element_type=f32)
    cosine, sine_table = rotary_tables(length)

    def query_key_local(raw_query, raw_key, query_gain, key_gain):
        return query_key(raw_query, raw_key, query_gain, key_gain, cosine, sine_table)

    rotated, rotary_pull = jax.vjp(
        query_key_local,
        projected[:, :model_width],
        projected[:, model_width : 2 * model_width],
        gain_query,
        gain_key,
    )
    query_low = rotated[0].astype(bf16)
    key_low = rotated[1].astype(bf16)
    value_low = projected[:, 2 * model_width :].astype(bf16).reshape(length, HEADS, HEAD_DIM)
    allowed = (position[:, None] >= position[None, :]) & (
        segments[0][:, None] == segments[0][None, :]
    )
    masked = jnp.where(
        allowed[None],
        jnp.einsum("qhd,khd->hqk", query_low, key_low, preferred_element_type=f32) * score_scale,
        -1e30,
    )
    probs = softmax_rows(masked)
    probs_low = probs.astype(bf16)
    attended_low = (
        jnp.einsum("hqk,khd->qhd", probs_low, value_low, preferred_element_type=f32)
        .reshape(length, model_width)
        .astype(bf16)
    )
    attended_columns = own_columns(attended_low, shard_group)
    middle = inputs + jnp.dot(attended_low, out_full, preferred_element_type=f32)
    scaled_two, second_pull = jax.vjp(rms_scale, middle, gain_two)
    hidden_two = scaled_two.astype(bf16)
    router = softmax_rows(jnp.dot(hidden_two, router_full, preferred_element_type=f32))
    row_count = expert_group * capacity
    done, mixture_parts = moe_layer(
        hidden_two,
        upstream_all,
        place_own,
        router_full,
        gate_up_weight,
        down_weight,
        expert_group,
        capacity,
        2,
    )
    expert_rows, activated, grad_expert, grad_gate_up_low = (
        a.reshape(local_experts, row_count, a.shape[-1]) for a in done[:4]
    )
    grad_rows_sum = done[4]
    grad_router = done[5][:, :local_experts].reshape(experts_all, length).T
    mixture = reduce_expert(mixture_parts, expert_group)
    block_out = (middle + mixture).astype(bf16)
    grad_down_full = jnp.einsum("erf,erd->efd", activated, grad_expert, preferred_element_type=f32)
    grad_gate_up_full = jnp.einsum(
        "erd,erf->edf", expert_rows, grad_gate_up_low, preferred_element_type=f32
    )
    grad_gate_up_weight = lax.psum_scatter(
        grad_gate_up_full.astype(bf16), "shard", scatter_dimension=1, tiled=True
    ).astype(f32)
    grad_down_weight = lax.psum_scatter(
        grad_down_full.astype(bf16), "shard", scatter_dimension=2, tiled=True
    ).astype(f32)

    upstream = cotangent.astype(f32)
    grad_logits = (
        router * (grad_router - jnp.sum(router * grad_router, axis=-1, keepdims=True))
    ).astype(bf16)
    grad_hidden_two = grad_rows_sum + jnp.einsum(
        "te,de->td", grad_logits, router_full, preferred_element_type=f32
    )
    grad_middle_norm, grad_gain_two = second_pull(grad_hidden_two)
    grad_middle = upstream + grad_middle_norm
    grad_branch_low = grad_middle.astype(bf16)
    grad_attended_low = (
        jnp.einsum("te,de->td", grad_branch_low, out_full, preferred_element_type=f32)
        .astype(bf16)
        .reshape(length, HEADS, HEAD_DIM)
    )
    grad_probs = jnp.einsum(
        "qhd,khd->hqk", grad_attended_low, value_low, preferred_element_type=f32
    )
    grad_scores_low = (
        probs * (grad_probs - jnp.sum(probs * grad_probs, axis=-1, keepdims=True))
    ).astype(bf16)
    grad_queries = (
        jnp.einsum("hqk,khd->qhd", grad_scores_low, key_low, preferred_element_type=f32)
        * score_scale
    )
    grad_keys = (
        jnp.einsum("hqk,qhd->khd", grad_scores_low, query_low, preferred_element_type=f32)
        * score_scale
    )
    grad_values = jnp.einsum(
        "hqk,qhd->khd", probs_low, grad_attended_low, preferred_element_type=f32
    )
    grad_raw_query, grad_raw_key, grad_gain_query, grad_gain_key = rotary_pull(
        (grad_queries, grad_keys)
    )
    grad_projected_low = jnp.concatenate(
        [grad_raw_query, grad_raw_key, grad_values.reshape(length, model_width)], axis=-1
    ).astype(bf16)
    grad_hidden_one = jnp.einsum(
        "te,de->td", grad_projected_low, qkv_full, preferred_element_type=f32
    )
    grad_inputs_norm, grad_gain_one = first_pull(grad_hidden_one)
    grad_tokens = grad_middle + grad_inputs_norm

    branch_all = jnp.concatenate(gather_shard(grad_branch_low, shard_group), axis=0)
    grad_out_part = jnp.einsum(
        "td,te->de", attended_columns, branch_all, preferred_element_type=f32
    )
    grad_out_weight = lax.psum(grad_out_part.astype(bf16), "expert").astype(f32)
    grad_qkv_weight = summed_rows(
        hidden_one_columns, grad_projected_low, expert_group, shard_group, z_all, 256, 2, 1
    ).astype(f32)
    grad_router_part = jnp.einsum(
        "td,te->ed", hidden_two, grad_logits, preferred_element_type=f32
    )
    small = jnp.concatenate(
        [
            grad_router_part,
            jnp.stack([grad_gain_one, grad_gain_query, grad_gain_key, grad_gain_two]),
        ],
        axis=0,
    )
    small = lax.psum(small, ("expert", "shard"))
    width = norm_one.shape[0]
    small = lax.dynamic_slice_in_dim(small, own_shard * width, width, axis=1)
    return (
        block_out,
        grad_tokens,
        small[experts_all],
        small[experts_all + 1],
        small[experts_all + 2],
        small[experts_all + 3],
        grad_qkv_weight,
        grad_out_weight,
        small[:experts_all].T,
        grad_gate_up_weight,
        grad_down_weight,
    )


def solution(mesh):
    return jax.shard_map(
        body,
        mesh=mesh,
        in_specs=(
            P(("expert", "shard"), None),
            P(("expert", "shard"), None),
            P(("expert", "shard"), None),
            P(("expert", "shard"), None),
            P(),
            P("shard"),
            P("shard"),
            P("shard"),
            P("shard"),
            P("shard", None),
            P("shard", None),
            P("shard", None),
            P("expert", None, None),
            P("expert", None, None),
        ),
        out_specs=(
            P(("expert", "shard"), None),
            P(("expert", "shard"), None),
            P("shard"),
            P("shard"),
            P("shard"),
            P("shard"),
            P("shard", None),
            P("shard", None),
            P("shard", None),
            P("expert", "shard", None),
            P("expert", None, "shard"),
        ),
        check_vma=False,
    )
```

```python
import functools

import jax
import jax.numpy as jnp
from jax import lax
from jax.experimental import pallas as pl
from jax.experimental.pallas import tpu as pltpu
from jax.sharding import PartitionSpec as P

HEADS = 16
HEAD_DIM = 128
TOP = 8
TILE = 8


epsilon = 1e-05
rope_base = 10000.0


def rms_scale(values, scale_gain):
    return (
        values * lax.rsqrt(jnp.mean(values * values, axis=-1, keepdims=True) + epsilon) * scale_gain
    )


def rotary_tables(length):
    half_dim = HEAD_DIM // 2
    position = jnp.arange(length, dtype=jnp.float32)[:, None]
    frequency = rope_base ** (-jnp.arange(half_dim, dtype=jnp.float32) * 2.0 / HEAD_DIM)
    angles = position * frequency[None, :]
    angles = jnp.concatenate([angles, angles], axis=-1)
    return (jnp.cos(angles)[:, None, :], jnp.sin(angles)[:, None, :])


def rotate(vectors, cosine, sine_table):
    half_dim = vectors.shape[-1] // 2
    turned = jnp.concatenate([-vectors[..., half_dim:], vectors[..., :half_dim]], axis=-1)
    return vectors * cosine + turned * sine_table


def query_key(raw_query, raw_key, query_gain, key_gain, cosine, sine_table):
    length = raw_query.shape[0]
    queries = rms_scale(raw_query, query_gain).reshape(length, HEADS, HEAD_DIM)
    keys_rot = rms_scale(raw_key, key_gain).reshape(length, HEADS, HEAD_DIM)
    return (rotate(queries, cosine, sine_table), rotate(keys_rot, cosine, sine_table))


def swiglu(gate_up):
    half_dim = gate_up.shape[-1] // 2
    gate_part = gate_up[..., :half_dim]
    return gate_part / (1.0 + jnp.exp(-gate_part)) * gate_up[..., half_dim:]


def softmax_rows(logits):
    largest = jnp.max(logits, axis=-1, keepdims=True)
    raised = jnp.exp(logits - largest)
    return raised / jnp.sum(raised, axis=-1, keepdims=True)


def z_size(expert_group):
    return 4 if expert_group % 4 == 0 else 1


def shift(values, expert_group, dz, dx):
    z_all = z_size(expert_group)
    x_all = expert_group // z_all
    pairs = [
        (i, ((i // x_all + dz) % z_all) * x_all + (i % x_all + dx) % x_all)
        for i in range(expert_group)
    ]
    return lax.ppermute(values, "expert", pairs)


def gather_expert(block, expert_group):
    z_all = z_size(expert_group)
    x_all = expert_group // z_all
    rows = [block] + [shift(block, expert_group, dz, 0) for dz in range(1, z_all)]
    return [
        rows[dz] if dx == 0 else shift(rows[dz], expert_group, 0, dx)
        for dz in range(z_all)
        for dx in range(x_all)
    ]


def reduce_expert(parts, expert_group):
    z_all = z_size(expert_group)
    x_all = expert_group // z_all
    rows = {}
    for dz in sorted(range(z_all), key=lambda d: -min(d, z_all - d)):
        rows[dz] = parts[dz * x_all].astype(jnp.float32)
        for dx in range(1, x_all):
            rows[dz] = rows[dz] + shift(parts[dz * x_all + dx], expert_group, 0, -dx).astype(
                jnp.float32
            )
        if dz:
            rows[dz] = shift(rows[dz].astype(jnp.bfloat16), expert_group, -dz, 0).astype(jnp.float32)
    return sum(rows[dz] for dz in range(z_all))


def relative_sources(expert_group):
    z_all = z_size(expert_group)
    x_all = expert_group // z_all
    me = lax.axis_index("expert")
    order = jnp.arange(expert_group, dtype=jnp.int32)
    return ((me // x_all - order // x_all) % z_all) * x_all + (me % x_all - order % x_all) % x_all


def shard_shift(values, shard_group, dy, flip):
    y_all = shard_group // 2
    pairs = [(i, ((i // 2 + dy) % y_all) * 2 + (i % 2 + flip) % 2) for i in range(shard_group)]
    return lax.ppermute(values, "shard", pairs)


def own_columns(values, shard_group):
    me = lax.axis_index("shard")
    y_all = shard_group // 2
    width = values.shape[1] // shard_group
    found = []
    for dy in range(y_all):
        for flip in range(2):
            there = ((me // 2 + dy) % y_all) * 2 + (me % 2 + flip) % 2
            piece = lax.dynamic_slice_in_dim(values, there * width, width, axis=1)
            found.append(piece if dy + flip == 0 else shard_shift(piece, shard_group, dy, flip))
    return jnp.concatenate(found, axis=0)


def tail_kernel(
    dims, grads_ref, columns_ref, small_ref, out_ref, small_out_ref,
    gall, xsend, xrecv, zsend, zrecv, acc, fin, group_small, own_small, all_small, *sems
):
    steps, width, x_all, z_all, y_all, lag, first_steps = dims
    (gs_s, gs_r, es_s, es_r) = sems[14:]
    (y_s, y_r, core_s, core_r, fwd_s, fwd_r, x_s, x_r, z_s, z_r, zb_s, zb_r, xb_s, xb_r) = sems[:14]
    f32, bf16 = jnp.float32, jnp.bfloat16
    length = grads_ref.shape[0]
    rows = columns_ref.shape[1]
    block = rows // (x_all * z_all)
    half = z_all * block
    e = lax.axis_index("expert")
    s = lax.axis_index("shard")
    z, x = e // x_all, lax.rem(e, x_all)
    y, core = s // 2, lax.rem(s, 2)

    def y_peer(d):
        return {"shard": lax.rem(y + d, y_all) * 2 + core}

    partner = {"shard": y * 2 + (1 - core)}

    def x_peer(d):
        return {"expert": z * x_all + lax.rem(x + d, x_all)}

    def z_peer(d):
        return {"expert": lax.rem(z + d, z_all) * x_all + x}

    def copy(src, dst, send, recv, peer):
        return pltpu.make_async_remote_copy(
            src_ref=src, dst_ref=dst, send_sem=send, recv_sem=recv, device_id=peer,
            device_id_type=pl.DeviceIdType.MESH,
        )

    def cols(c):
        return pl.ds(pl.multiple_of(c * width, width), width)

    def y_copy(d, c):
        return copy(grads_ref.at[:, cols(c)], gall.at[2 * d - 1, c], y_s.at[d - 1], y_r.at[d - 1, c], y_peer(d))

    def core_copy(c):
        return copy(grads_ref.at[:, cols(c)], gall.at[0, c], core_s.at[0], core_r.at[c], partner)

    def fwd_copy(d, c):
        return copy(gall.at[2 * d - 1, c], gall.at[2 * d, c], fwd_s.at[d - 1], fwd_r.at[d - 1, c], partner)

    def x_copy(d, c):
        return copy(xsend.at[d - 1, c], xrecv.at[d - 1, c], x_s.at[d - 1], x_r.at[d - 1, c], x_peer(d))

    def z_copy(d, c):
        return copy(zsend.at[d - 1, c], zrecv.at[d - 1, c], z_s.at[d - 1], z_r.at[d - 1, c], z_peer(d))

    def zb_copy(d, c):
        here = fin.at[c, pl.ds(pl.multiple_of((x * z_all + z) * block, block), block)]
        return copy(here, here, zb_s.at[d - 1], zb_r.at[d - 1, c], z_peer(d))

    def xb_copy(d, c):
        here = fin.at[c, pl.ds(pl.multiple_of(x * half, half), half)]
        return copy(here, here, xb_s.at[d - 1], xb_r.at[d - 1, c], x_peer(d))

    near = [(d, flip) for d in range(y_all) for flip in range(2) if d + flip > 0]
    far = [(dz, dx) for dz in range(z_all) for dx in range(x_all) if dz + dx > 0]

    def near_peer(d, flip):
        return {"shard": lax.rem(y + d, y_all) * 2 + lax.rem(core + flip, 2)}

    def far_peer(dz, dx):
        return {"expert": lax.rem(z + dz, z_all) * x_all + lax.rem(x + dx, x_all)}

    def near_small(d, flip):
        j = 2 * d + flip
        return copy(small_ref.at[j], group_small.at[j - 1], gs_s.at[j - 1], gs_r.at[j - 1], near_peer(d, flip))

    def far_small(dz, dx):
        i = dz * x_all + dx
        return copy(own_small, all_small.at[i - 1], es_s.at[i - 1], es_r.at[i - 1], far_peer(dz, dx))

    barrier = pltpu.get_barrier_semaphore()
    peers = [near_peer(*p) for p in near] + [far_peer(*p) for p in far]
    for peer in peers:
        pl.semaphore_signal(barrier, inc=1, device_id=peer, device_id_type=pl.DeviceIdType.MESH)
    pl.semaphore_wait(barrier, len(peers))

    for p in near:
        near_small(*p).start()

    def first(c, carry):
        for d in range(1, y_all):
            y_copy(d, c).start()
        core_copy(c).start()
        return carry

    lax.fori_loop(0, steps, first, 0)
    slots = acc.shape[0]

    def step(t, carry):
        def stage(k, body):
            c = t - k * lag
            pl.when((c >= 0) & (c < steps))(lambda: body(c))

        @functools.partial(stage, 5)
        def _(c):
            for d in range(1, x_all):
                xb_copy(d, c).wait_recv()
            out_ref[:, cols(c)] = fin[c]

        @functools.partial(stage, 4)
        def _(c):
            for d in range(1, z_all):
                zb_copy(d, c).wait_recv()
            for d in range(1, x_all):
                xb_copy(d, c).start()

        @functools.partial(stage, 3)
        def _(c):
            slot = lax.rem(c, slots)
            total = acc[slot, pl.ds(pl.multiple_of(z * block, block), block), :]
            for d in range(1, z_all):
                z_copy(d, c).wait_recv()
                total = total + zrecv[d - 1, c].astype(f32)
            fin[c, pl.ds(pl.multiple_of((x * z_all + z) * block, block), block), :] = total.astype(bf16)
            for d in range(1, z_all):
                zb_copy(d, c).start()

        @functools.partial(stage, 2)
        def _(c):
            slot = lax.rem(c, slots)
            total = acc[slot]
            for d in range(1, x_all):
                x_copy(d, c).wait_recv()
                total = total + xrecv[d - 1, c].astype(f32)
            acc[slot] = total
            for d in range(1, z_all):
                there = lax.rem(z + d, z_all)
                zsend[d - 1, c] = acc[slot, pl.ds(pl.multiple_of(there * block, block), block), :].astype(bf16)
                z_copy(d, c).start()

        @functools.partial(stage, 1)
        def _(c):
            core_copy(c).wait_recv()
            for d in range(1, y_all):
                fwd_copy(d, c).wait_recv()
            kind = (c >= first_steps).astype(jnp.int32)
            others = gall[:, c].reshape((2 * y_all - 1) * length, width)
            mine = grads_ref[:, cols(c)]

            def product(there):
                at = pl.ds(pl.multiple_of(there * half, half), half)
                return jnp.dot(columns_ref[kind, at, :length], mine, preferred_element_type=f32) + jnp.dot(
                    columns_ref[kind, at, length:], others, preferred_element_type=f32
                )

            for d in range(1, x_all):
                xsend[d - 1, c] = product(lax.rem(x + d, x_all)).astype(bf16)
                x_copy(d, c).start()
            acc[lax.rem(c, slots)] = product(x)

        @functools.partial(stage, 0)
        def _(c):
            for d in range(1, y_all):
                y_copy(d, c).wait_recv()
                fwd_copy(d, c).start()

        @pl.when(t == 2)
        def _():
            total = small_ref[0]
            for j, p in enumerate(near):
                near_small(*p).wait_recv()
                total = total + group_small[j]
            own_small[...] = total
            for p in far:
                far_small(*p).start()

        return carry

    lax.fori_loop(0, steps + 5 * lag, step, 0)
    total = own_small[...]
    for i, p in enumerate(far):
        far_small(*p).wait_recv()
        total = total + all_small[i]
    small_out_ref[...] = total
    for p in near:
        near_small(*p).wait_send()
    for p in far:
        far_small(*p).wait_send()

    for d in range(1, y_all):
        copy(grads_ref, grads_ref, y_s.at[d - 1], y_r.at[d - 1, 0], y_peer(d)).wait_send()
        whole = gall.at[2 * d - 1]
        copy(whole, whole, fwd_s.at[d - 1], fwd_r.at[d - 1, 0], partner).wait_send()
    copy(grads_ref, grads_ref, core_s.at[0], core_r.at[0], partner).wait_send()
    for d in range(1, x_all):
        whole = xsend.at[d - 1]
        copy(whole, whole, x_s.at[d - 1], x_r.at[d - 1, 0], x_peer(d)).wait_send()
        copy(whole, whole, xb_s.at[d - 1], xb_r.at[d - 1, 0], x_peer(d)).wait_send()
    for d in range(1, z_all):
        whole = zsend.at[d - 1]
        copy(whole, whole, z_s.at[d - 1], z_r.at[d - 1, 0], z_peer(d)).wait_send()
        copy(whole, whole, zb_s.at[d - 1], zb_r.at[d - 1, 0], z_peer(d)).wait_send()


def summed_rows(columns, grads, first_total, small, expert_group, shard_group, z_all, width, lag, name_id):
    x_all, y_all = expert_group // z_all, shard_group // 2
    length, total = grads.shape
    rows = columns.shape[1]
    steps = total // width
    block = rows // expert_group
    half = z_all * block
    bf16 = jnp.bfloat16
    dma = pltpu.SemaphoreType.DMA
    n1 = max(y_all - 1, 1)
    x1 = max(x_all - 1, 1)
    z1 = max(z_all - 1, 1)
    slots = min(steps, 2 * lag + 1)
    return pl.pallas_call(
        functools.partial(tail_kernel, (steps, width, x_all, z_all, y_all, lag, first_total // width)),
        out_shape=[
            jax.ShapeDtypeStruct((rows, total), bf16),
            jax.ShapeDtypeStruct(small.shape[1:], jnp.float32),
        ],
        in_specs=[pl.BlockSpec(memory_space=pltpu.VMEM)] * 3,
        out_specs=[pl.BlockSpec(memory_space=pltpu.VMEM)] * 2,
        scratch_shapes=[
            pltpu.VMEM((shard_group - 1, steps, length, width), bf16),
            pltpu.VMEM((x1, steps, half, width), bf16),
            pltpu.VMEM((x1, steps, half, width), bf16),
            pltpu.VMEM((z1, steps, block, width), bf16),
            pltpu.VMEM((z1, steps, block, width), bf16),
            pltpu.VMEM((slots, half, width), jnp.float32),
            pltpu.VMEM((steps, rows, width), bf16),
            pltpu.VMEM((shard_group - 1, *small.shape[1:]), jnp.float32),
            pltpu.VMEM(small.shape[1:], jnp.float32),
            pltpu.VMEM((expert_group - 1, *small.shape[1:]), jnp.float32),
            dma((n1,)), dma((n1, steps)),
            dma((1,)), dma((steps,)),
            dma((n1,)), dma((n1, steps)),
            dma((x1,)), dma((x1, steps)),
            dma((z1,)), dma((z1, steps)),
            dma((z1,)), dma((z1, steps)),
            dma((x1,)), dma((x1, steps)),
            dma((shard_group - 1,)), dma((shard_group - 1,)),
            dma((expert_group - 1,)), dma((expert_group - 1,)),
        ],
        compiler_params=pltpu.CompilerParams(
            collective_id=name_id, has_side_effects=True, vmem_limit_bytes=60 * 1024 * 1024
        ),
        cost_estimate=pl.CostEstimate(
            flops=2 * rows * length * shard_group * total, bytes_accessed=16 * 1024 * 1024, transcendentals=0
        ),
    )(grads, columns, small)


MOE_CHUNKS = 4


def moe_kernel(
    dims, hidden_hbm, upstream_hbm, place_ref, place_t_ref, router_ref, router_t_ref, gate_up_hbm, down_hbm,
    rows_hbm, activated_hbm, grad_out_hbm, grad_gate_up_hbm, grad_ref, grad_router_ref, found_hbm, summed_hbm,
    *rest,
):
    x_all, capacity = dims
    mixture_hbm = rest[: 4 * x_all]
    (
    gate_up_w, down_w, hid, ups, prob, prob_t, rows, gate_up, activated, out_rows, grad_expert, grad_gate_up, grad_rows,
    mix_stage, part_stage, own_part, z_landed, router_stage,
    w_sem, own_sem, load_sem, store_sem, zs, zr, xs, xr, fs, fr, ps, pr, qs, qr, rs, rr, lsem, mix_sem,
    ) = rest[4 * x_all :]
    z_all = 4
    f32, bf16 = jnp.float32, jnp.bfloat16
    length, width = hidden_hbm.shape
    local_experts, _, twice = gate_up_w.shape
    half = twice // 2
    tile = min(512, half)
    narrow = min(256, half)
    chunk = length // MOE_CHUNKS
    e = lax.axis_index("expert")
    z, x = e // x_all, lax.rem(e, x_all)

    def peer(dz, dx):
        return {"expert": lax.rem(z + dz + 4 * z_all, z_all) * x_all + lax.rem(x + dx + 4 * x_all, x_all)}

    def copy(src, dst, send, recv, to):
        return pltpu.make_async_remote_copy(
            src_ref=src, dst_ref=dst, send_sem=send, recv_sem=recv, device_id=to,
            device_id_type=pl.DeviceIdType.MESH,
        )

    def at(c):
        return pl.ds(pl.multiple_of(c * chunk, chunk), chunk)

    def z_copy(d, c):
        return copy(hidden_hbm.at[at(c)], found_hbm.at[d, 0, at(c)], zs.at[d - 1, c], zr.at[d - 1, c], peer(d, 0))

    def x_copy(d, c):
        return copy(hidden_hbm.at[at(c)], found_hbm.at[0, d, at(c)], xs.at[d - 1, c], xr.at[d - 1, c], peer(0, d))

    def f_copy(dz, dx, c):
        return copy(
            found_hbm.at[dz, 0, at(c)], found_hbm.at[dz, dx, at(c)],
            fs.at[dz - 1, dx - 1, c], fr.at[dz - 1, dx - 1, c], peer(0, dx),
        )

    def p_copy(dz, dx):
        return copy(part_stage.at[dx - 1], summed_hbm.at[dz, dx - 1], ps.at[dx - 1], pr.at[dz, dx - 1], peer(0, -dx))

    def q_copy(dz):
        return copy(own_part.at[dz], z_landed.at[dz - 1], qs.at[dz - 1], qr.at[dz - 1], peer(-dz, 0))

    def r_copy(dz, dx):
        return copy(
            router_stage.at[dz, dx], grad_router_ref.at[e], rs.at[dz, dx], rr.at[dz, dx], peer(-dz, -dx)
        )

    def cols(n, w):
        return pl.ds(pl.multiple_of(n * w, w), w)

    barrier = pltpu.get_barrier_semaphore()
    others = [(dz, dx) for dz in range(z_all) for dx in range(x_all) if dz + dx > 0]
    for dz, dx in others:
        pl.semaphore_signal(barrier, inc=1, device_id=peer(dz, dx), device_id_type=pl.DeviceIdType.MESH)
    pl.semaphore_wait(barrier, len(others))

    own = pltpu.make_async_copy(hidden_hbm, found_hbm.at[0, 0], own_sem)
    own.start()
    weights = [
        pltpu.make_async_copy(gate_up_hbm, gate_up_w, w_sem.at[0]),
        pltpu.make_async_copy(down_hbm, down_w, w_sem.at[1]),
    ]
    for w in weights:
        w.start()

    def send_own(c, carry):
        for d in range(1, x_all):
            x_copy(d, c).start()
        return carry

    lax.fori_loop(0, MOE_CHUNKS, send_own, 0)
    for d in (2, 1, 3):

        def send_z(c, carry):
            z_copy(d, c).start()
            return carry

        lax.fori_loop(0, MOE_CHUNKS, send_z, 0)

    def events(first):
        def one(k, carry):
            @pl.when(k < 3 * MOE_CHUNKS)
            def _():
                j = k // MOE_CHUNKS
                c = lax.rem(k, MOE_CHUNKS)
                d = 2 - j + 3 * (j // 2)
                z_copy(d, c).wait_recv()
                for dx in range(1, x_all):
                    f_copy(d, dx, c).start()

            return carry

        lax.fori_loop(first, first + 2, one, 0)

    def own_slots(le):
        return pl.ds(pl.multiple_of(le * capacity, capacity), capacity)

    def finish(g):
        dz = g // 2 + 2 * lax.rem(g, 2)
        for dx in range(1, x_all):
            p_copy(dz, dx).wait_recv()
            load = pltpu.make_async_copy(summed_hbm.at[dz, dx - 1], hid.at[0], lsem)
            load.start()
            load.wait()

            def add(n, carry):
                c = cols(n, tile)
                own_part[dz, :, c] = (own_part[dz, :, c].astype(f32) + hid[0, :, c].astype(f32)).astype(bf16)
                return carry

            lax.fori_loop(0, width // tile, add, 0)

        @pl.when(dz > 0)
        def _():
            q_copy(dz).start()

    mix_slots = mix_stage.shape[0]

    def mix_copy(dz, dx):
        slot = dx % mix_slots
        return pltpu.make_async_copy(mix_stage.at[slot], mixture_hbm[dz * x_all + dx], mix_sem.at[slot])

    slot_row = lax.broadcasted_iota(jnp.int32, (capacity, length), 0).astype(f32)
    slot_col = lax.broadcasted_iota(jnp.int32, (length, local_experts * capacity), 1).astype(f32)
    own.wait()
    events(0)

    def group(g, carry):
        dz = g // 2 + 2 * lax.rem(g, 2)

        def arrive(c, inner):
            for dx in range(1, x_all):

                @pl.when(dz == 0)
                def _():
                    x_copy(dx, c).wait_recv()

                @pl.when(dz > 0)
                def _():
                    f_copy(dz, dx, c).wait_recv()

            return inner

        lax.fori_loop(0, MOE_CHUNKS, arrive, 0)
        loads = []
        for dx in range(x_all):
            loads.append(pltpu.make_async_copy(found_hbm.at[dz, dx], hid.at[dx], load_sem.at[0, dx]))
            loads.append(pltpu.make_async_copy(upstream_hbm.at[dz, dx], ups.at[dx], load_sem.at[1, dx]))
        for load in loads:
            load.start()
        for load in loads:
            load.wait()
        pl.when(g == 0)(lambda: [w.wait() for w in weights] and None)

        for dx in range(x_all):
            logits = jnp.dot(hid[dx], router_ref[...], preferred_element_type=f32)
            raised = jnp.exp(logits - jnp.max(logits, axis=1, keepdims=True))
            prob[dx] = raised / jnp.sum(raised, axis=1, keepdims=True)
            logits = lax.dot_general(
                router_t_ref[...], hid[dx], (((1,), (1,)), ((), ())), preferred_element_type=f32
            )
            raised = jnp.exp(logits - jnp.max(logits, axis=0, keepdims=True))
            prob_t[dx] = raised / jnp.sum(raised, axis=0, keepdims=True)
            router_stage[dz, dx] = jnp.zeros(router_stage.shape[2:], f32)

        def store(kind, buffer, hbm, le):
            return pltpu.make_async_copy(buffer, hbm.at[le, dz], store_sem.at[kind])

        def expert(le, inner):
            @pl.when(g + le > 0)
            def _():
                store(0, rows, rows_hbm, le).wait()
                store(1, activated, activated_hbm, le).wait()
                store(2, grad_expert, grad_out_hbm, le).wait()
                store(3, grad_gate_up, grad_gate_up_hbm, le).wait()

            chosen = [place_ref[dz, dx, pl.ds(le, 1), :] == slot_row for dx in range(x_all)]
            chosen_low = [c.astype(f32).astype(bf16) for c in chosen]

            def dispatch(n, c0):
                c = cols(n, tile)
                for dx in range(x_all):
                    rows[dx * capacity : (dx + 1) * capacity, c] = jnp.dot(
                        chosen_low[dx], hid[dx, :, c], preferred_element_type=f32
                    ).astype(bf16)
                return c0

            lax.fori_loop(0, width // tile, dispatch, 0)
            store(0, rows, rows_hbm, le).start()

            def up_step(n, c0):
                c = cols(n, tile)
                gate_up[:, c] = jnp.dot(rows[...], gate_up_w[le, :, c], preferred_element_type=f32)
                return c0

            lax.fori_loop(0, twice // tile, up_step, 0)

            def act_step(n, c0):
                gate = gate_up[:, cols(n, narrow)]
                up = gate_up[:, pl.ds(pl.multiple_of(half + n * narrow, narrow), narrow)]
                activated[:, cols(n, narrow)] = (gate / (1.0 + jnp.exp(-gate)) * up).astype(bf16)
                return c0

            lax.fori_loop(0, half // narrow, act_step, 0)
            store(1, activated, activated_hbm, le).start()

            def down_step(n, c0):
                c = cols(n, tile)
                result = jnp.dot(activated[...], down_w[le, :, c], preferred_element_type=f32)
                for dx in range(x_all):
                    r = slice(dx * capacity, (dx + 1) * capacity)
                    out_rows[dx, own_slots(le), c] = result[r].astype(bf16)
                return c0

            lax.fori_loop(0, width // tile, down_step, 0)

            mine = e * local_experts + le
            weight_rows = [
                jnp.sum(jnp.where(chosen[dx], prob_t[dx, pl.ds(mine, 1), :], 0.0), axis=1, keepdims=True)
                for dx in range(x_all)
            ]

            def grad_step(n, totals):
                c = cols(n, tile)
                new = []
                for dx in range(x_all):
                    r = slice(dx * capacity, (dx + 1) * capacity)
                    up_rows = jnp.dot(chosen_low[dx], ups[dx, :, c], preferred_element_type=f32)
                    grad_expert[r, c] = (weight_rows[dx] * up_rows).astype(bf16)
                    new.append(
                        totals[dx]
                        + jnp.sum(up_rows * out_rows[dx, own_slots(le), c].astype(f32), axis=1, keepdims=True)
                    )
                return tuple(new)

            totals = lax.fori_loop(
                0, width // tile, grad_step, tuple(jnp.zeros((capacity, 1), f32) for _ in range(x_all))
            )
            store(2, grad_expert, grad_out_hbm, le).start()
            for dx in range(x_all):
                router_stage[dz, dx, pl.ds(le, 1), :] = jnp.sum(
                    jnp.where(chosen[dx], totals[dx], 0.0), axis=0, keepdims=True
                )

            def back_step(n, c0):
                ga = lax.dot_general(
                    grad_expert[...], down_w[le, cols(n, narrow), :], (((1,), (1,)), ((), ())),
                    preferred_element_type=f32,
                )
                gate = gate_up[:, cols(n, narrow)]
                c_up = pl.ds(pl.multiple_of(half + n * narrow, narrow), narrow)
                up = gate_up[:, c_up]
                sg = 1.0 / (1.0 + jnp.exp(-gate))
                grad_gate_up[:, cols(n, narrow)] = (ga * up * sg * (1.0 + gate * (1.0 - sg))).astype(bf16)
                grad_gate_up[:, c_up] = (ga * (gate * sg)).astype(bf16)
                return c0

            lax.fori_loop(0, half // narrow, back_step, 0)
            store(3, grad_gate_up, grad_gate_up_hbm, le).start()

            def row_step(n, c0):
                result = lax.dot_general(
                    grad_gate_up[...], gate_up_w[le, cols(n, narrow), :], (((1,), (1,)), ((), ())),
                    preferred_element_type=f32,
                )
                for dx in range(x_all):
                    r = slice(dx * capacity, (dx + 1) * capacity)
                    grad_rows[dx, own_slots(le), cols(n, narrow)] = result[r].astype(bf16)
                return c0

            lax.fori_loop(0, width // narrow, row_step, 0)
            events(4 * g + 2 + 2 * le)
            return inner

        assert local_experts == 2
        lax.fori_loop(0, local_experts, expert, 0)

        def stages():
            for dx in range(1, x_all):
                p_copy(dz, dx).wait_send()

        pl.when(g > 0)(stages)
        for dx in range(x_all):
            weight = jnp.zeros(slot_col.shape, f32)
            mask = jnp.zeros(slot_col.shape, f32)
            lane = lax.broadcasted_iota(jnp.int32, prob.shape[1:], 1)
            for le in range(local_experts):
                spot = place_t_ref[dz, dx, :, le : le + 1]
                here = jnp.where(spot < 0.0, -1.0, spot + le * capacity) == slot_col
                p = jnp.sum(jnp.where(lane == e * local_experts + le, prob[dx], 0.0), axis=1, keepdims=True)
                weight = jnp.where(here, p, weight)
                mask = jnp.where(here, 1.0, mask)
            low = mask.astype(bf16)
            high = weight.astype(bf16)
            remainder = (weight - high.astype(f32)).astype(bf16)

            if dx < mix_slots:
                pl.when(g > 0)(mix_copy(0, dx).wait)
            else:
                mix_copy(0, dx).wait()

            def combine(n, c0):
                c = cols(n, tile)
                mix = jnp.dot(high, out_rows[dx, :, c], preferred_element_type=f32) + jnp.dot(
                    remainder, out_rows[dx, :, c], preferred_element_type=f32
                )
                grad = jnp.dot(low, grad_rows[dx, :, c], preferred_element_type=f32)
                mix_stage[dx % mix_slots, :, c] = mix.astype(bf16)
                if dx == 0:
                    own_part[dz, :, c] = grad.astype(bf16)
                else:
                    part_stage[dx - 1, :, c] = grad.astype(bf16)
                return c0

            lax.fori_loop(0, width // tile, combine, 0)
            for k in range(z_all):
                pl.when(dz == k)(mix_copy(k, dx).start)
            if dx > 0:
                p_copy(dz, dx).start()
                r_copy(dz, dx).start()
            else:

                @pl.when(dz > 0)
                def _():
                    r_copy(dz, 0).start()

                @pl.when(dz == 0)
                def _():
                    grad_router_ref[e] = router_stage[0, 0]

        pl.when(g > 0)(lambda: finish(g - 1))
        return carry

    lax.fori_loop(0, z_all, group, 0)
    finish(jnp.int32(z_all - 1))

    def total(n, carry):
        c = cols(n, tile)
        grad_ref[:, c] = own_part[0, :, c].astype(f32)
        return carry

    lax.fori_loop(0, width // tile, total, 0)
    for d in (2, 1, 3):
        q_copy(d).wait_recv()

        def more(n, carry):
            c = cols(n, tile)
            grad_ref[:, c] = grad_ref[:, c] + z_landed[d - 1, :, c].astype(f32)
            return carry

        lax.fori_loop(0, width // tile, more, 0)

    for kind, buffer, hbm in (
        (0, rows, rows_hbm), (1, activated, activated_hbm), (2, grad_expert, grad_out_hbm),
        (3, grad_gate_up, grad_gate_up_hbm),
    ):
        pltpu.make_async_copy(buffer, hbm.at[0, 0], store_sem.at[kind]).wait()
    for dx in range(mix_slots):
        mix_copy(0, dx).wait()
    for dx in range(1, x_all):
        p_copy(0, dx).wait_send()
    for d in range(1, z_all):
        q_copy(d).wait_send()
    for dz, dx in others:
        r_copy(dz, dx).wait_send()
        r_copy(dz, dx).wait_recv()

    def sent(c, carry):
        for d in range(1, z_all):
            z_copy(d, c).wait_send()
            for dx in range(1, x_all):
                f_copy(d, dx, c).wait_send()
        for d in range(1, x_all):
            x_copy(d, c).wait_send()
        return carry

    lax.fori_loop(0, MOE_CHUNKS, sent, 0)


def moe_layer(hidden, upstream_all, place, router_weight, gate_up_weight, down_weight, expert_group, capacity, name_id):
    f32, bf16 = jnp.float32, jnp.bfloat16
    length, width = hidden.shape
    local_experts, _, twice = gate_up_weight.shape
    half = twice // 2
    experts_all = router_weight.shape[1]
    x_all = expert_group // 4
    count = x_all * capacity
    dma = pltpu.SemaphoreType.DMA
    x1 = max(x_all - 1, 1)
    place_t = place.transpose(0, 1, 3, 2)
    spare = (-local_experts) % 8
    place = jnp.pad(place, ((0, 0), (0, 0), (0, spare), (0, 0)), constant_values=-1.0)
    any_spec = pl.BlockSpec(memory_space=pl.ANY)
    vmem_spec = pl.BlockSpec(memory_space=pltpu.VMEM)
    out = pl.pallas_call(
        functools.partial(moe_kernel, (x_all, capacity)),
        out_shape=[
            jax.ShapeDtypeStruct((local_experts, 4, count, width), bf16),
            jax.ShapeDtypeStruct((local_experts, 4, count, half), bf16),
            jax.ShapeDtypeStruct((local_experts, 4, count, width), bf16),
            jax.ShapeDtypeStruct((local_experts, 4, count, twice), bf16),
            jax.ShapeDtypeStruct((length, width), f32),
            jax.ShapeDtypeStruct((expert_group, 8, length), f32),
            jax.ShapeDtypeStruct((4, x_all, length, width), bf16),
            jax.ShapeDtypeStruct((4, x1, length, width), bf16),
        ]
        + [jax.ShapeDtypeStruct((length, width), bf16)] * (4 * x_all),
        in_specs=[any_spec, any_spec, vmem_spec, vmem_spec, vmem_spec, vmem_spec, any_spec, any_spec],
        out_specs=[any_spec] * 4 + [vmem_spec, vmem_spec] + [any_spec] * (2 + 4 * x_all),
        scratch_shapes=[
            pltpu.VMEM(gate_up_weight.shape, bf16),
            pltpu.VMEM(down_weight.shape, bf16),
            pltpu.VMEM((x_all, length, width), bf16),
            pltpu.VMEM((x_all, length, width), bf16),
            pltpu.VMEM((x_all, length, experts_all), f32),
            pltpu.VMEM((x_all, experts_all, length), f32),
            pltpu.VMEM((count, width), bf16),
            pltpu.VMEM((count, twice), f32),
            pltpu.VMEM((count, half), bf16),
            pltpu.VMEM((x_all, local_experts * capacity, width), bf16),
            pltpu.VMEM((count, width), bf16),
            pltpu.VMEM((count, twice), bf16),
            pltpu.VMEM((x_all, local_experts * capacity, width), bf16),
            pltpu.VMEM((min(2, x_all), length, width), bf16),
            pltpu.VMEM((x1, length, width), bf16),
            pltpu.VMEM((4, length, width), bf16),
            pltpu.VMEM((3, length, width), bf16),
            pltpu.VMEM((4, x_all, 8, length), f32),
            dma((2,)), dma, dma((2, x_all)), dma((4,)),
            dma((3, MOE_CHUNKS)), dma((3, MOE_CHUNKS)),
            dma((x1, MOE_CHUNKS)), dma((x1, MOE_CHUNKS)),
            dma((3, x1, MOE_CHUNKS)), dma((3, x1, MOE_CHUNKS)),
            dma((x1,)), dma((4, x1)),
            dma((3,)), dma((3,)),
            dma((4, x_all)), dma((4, x_all)),
            dma, dma((min(2, x_all),)),
        ],
        compiler_params=pltpu.CompilerParams(
            collective_id=name_id, has_side_effects=True, vmem_limit_bytes=62 * 1024 * 1024
        ),
        cost_estimate=pl.CostEstimate(
            flops=12 * 4 * local_experts * count * width * twice, bytes_accessed=64 * 1024 * 1024,
            transcendentals=0,
        ),
    )(
        hidden, upstream_all, place, place_t, router_weight, router_weight.T, gate_up_weight, down_weight
    )
    return out[:6], out[8:]


def body(
    tokens,
    cotangent,
    segments,
    routes,
    tile_counts,
    norm_one,
    norm_query,
    norm_key,
    norm_two,
    qkv_weight,
    out_weight,
    router_weight,
    gate_up_weight,
    down_weight,
):
    f32, bf16 = jnp.float32, jnp.bfloat16
    length, model_width = tokens.shape
    experts_all = tile_counts.shape[0]
    local_experts = gate_up_weight.shape[0]
    expert_group = lax.axis_size("expert")
    shard_group = lax.axis_size("shard")
    capacity = length * TOP // (experts_all * TILE) * TILE
    score_scale = HEAD_DIM ** (-0.5)
    own_expert = lax.axis_index("expert")
    own_shard = lax.axis_index("shard")
    sources = relative_sources(expert_group)

    def gather(values, axis):
        return lax.all_gather(values, axis, axis=0, tiled=True)

    qkv_full = gather(qkv_weight, "shard")
    out_full = gather(out_weight, "shard")
    router_full = gather(router_weight, "shard")
    gains = lax.all_gather(
        jnp.stack([norm_one, norm_query, norm_key, norm_two]), "shard", axis=1, tiled=True
    ).astype(f32)
    gain_one, gain_query, gain_key, gain_two = gains[0], gains[1], gains[2], gains[3]

    expert_ids = jnp.arange(experts_all, dtype=jnp.int32)
    chosen = jnp.any(routes[:, :, None] == expert_ids[None, None, :], axis=1)
    position = jnp.arange(length, dtype=jnp.int32)
    earlier = (position[:, None] > position[None, :]).astype(bf16)
    rank = jnp.dot(earlier, chosen.astype(bf16), preferred_element_type=f32)
    kept = chosen & (rank < (tile_counts * TILE).astype(f32)[None, :])
    place = jnp.where(kept, rank, -1.0)
    place_all = lax.all_gather(place, "expert", axis=0, tiled=False)[sources]
    place_own = lax.dynamic_slice_in_dim(
        place_all, own_expert * local_experts, local_experts, axis=2
    )
    z_all = z_size(expert_group)
    x_all = expert_group // z_all
    place_own = place_own.transpose(0, 2, 1).reshape(z_all, x_all, local_experts, length)
    upstream_all = jnp.stack(gather_expert(cotangent, expert_group))
    upstream_all = upstream_all.reshape(z_all, x_all, length, model_width)

    inputs = tokens.astype(f32)
    scaled_one, first_pull = jax.vjp(rms_scale, inputs, gain_one)
    hidden_one = scaled_one.astype(bf16)
    hidden_one_columns = own_columns(hidden_one, shard_group)
    projected = jnp.dot(hidden_one, qkv_full, preferred_element_type=f32)
    cosine, sine_table = rotary_tables(length)

    def query_key_local(raw_query, raw_key, query_gain, key_gain):
        return query_key(raw_query, raw_key, query_gain, key_gain, cosine, sine_table)

    rotated, rotary_pull = jax.vjp(
        query_key_local,
        projected[:, :model_width],
        projected[:, model_width : 2 * model_width],
        gain_query,
        gain_key,
    )
    query_low = rotated[0].astype(bf16)
    key_low = rotated[1].astype(bf16)
    value_low = projected[:, 2 * model_width :].astype(bf16).reshape(length, HEADS, HEAD_DIM)
    allowed = (position[:, None] >= position[None, :]) & (
        segments[0][:, None] == segments[0][None, :]
    )
    masked = jnp.where(
        allowed[None],
        jnp.einsum("qhd,khd->hqk", query_low, key_low, preferred_element_type=f32) * score_scale,
        -1e30,
    )
    probs = softmax_rows(masked)
    probs_low = probs.astype(bf16)
    attended_low = (
        jnp.einsum("hqk,khd->qhd", probs_low, value_low, preferred_element_type=f32)
        .reshape(length, model_width)
        .astype(bf16)
    )
    attended_columns = own_columns(attended_low, shard_group)
    middle = inputs + jnp.dot(attended_low, out_full, preferred_element_type=f32)
    scaled_two, second_pull = jax.vjp(rms_scale, middle, gain_two)
    hidden_two = scaled_two.astype(bf16)
    router = softmax_rows(jnp.dot(hidden_two, router_full, preferred_element_type=f32))
    row_count = expert_group * capacity
    done, mixture_parts = moe_layer(
        hidden_two,
        upstream_all,
        place_own,
        router_full,
        gate_up_weight,
        down_weight,
        expert_group,
        capacity,
        2,
    )
    expert_rows, activated, grad_expert, grad_gate_up_low = (
        a.reshape(local_experts, row_count, a.shape[-1]) for a in done[:4]
    )
    grad_rows_sum = done[4]
    grad_router = done[5][:, :local_experts].reshape(experts_all, length).T
    mixture = reduce_expert(mixture_parts, expert_group)
    upstream = cotangent.astype(f32)
    grad_logits = (
        router * (grad_router - jnp.sum(router * grad_router, axis=-1, keepdims=True))
    ).astype(bf16)
    grad_hidden_two = grad_rows_sum + jnp.einsum(
        "te,de->td", grad_logits, router_full, preferred_element_type=f32
    )
    grad_middle_norm, grad_gain_two = second_pull(grad_hidden_two)
    grad_middle = upstream + grad_middle_norm
    grad_branch_low = grad_middle.astype(bf16)
    grad_attended_low = (
        jnp.einsum("te,de->td", grad_branch_low, out_full, preferred_element_type=f32)
        .astype(bf16)
        .reshape(length, HEADS, HEAD_DIM)
    )
    grad_attended_low, expert_rows, activated, grad_expert, grad_gate_up_low = (
        lax.optimization_barrier(
            (grad_attended_low, expert_rows, activated, grad_expert, grad_gate_up_low)
        )
    )
    grad_down_full = jnp.einsum("erf,erd->efd", activated, grad_expert, preferred_element_type=f32)
    grad_gate_up_full = jnp.einsum(
        "erd,erf->edf", expert_rows, grad_gate_up_low, preferred_element_type=f32
    )
    grad_gate_up_full, grad_down_full, grad_attended_low = lax.optimization_barrier(
        (grad_gate_up_full.astype(bf16), grad_down_full.astype(bf16), grad_attended_low)
    )
    grad_gate_up_weight = lax.psum_scatter(
        grad_gate_up_full, "shard", scatter_dimension=1, tiled=True
    ).astype(f32)
    grad_down_weight = lax.psum_scatter(
        grad_down_full, "shard", scatter_dimension=2, tiled=True
    ).astype(f32)

    grad_probs = jnp.einsum(
        "qhd,khd->hqk", grad_attended_low, value_low, preferred_element_type=f32
    )
    grad_scores_low = (
        probs * (grad_probs - jnp.sum(probs * grad_probs, axis=-1, keepdims=True))
    ).astype(bf16)
    grad_queries = (
        jnp.einsum("hqk,khd->qhd", grad_scores_low, key_low, preferred_element_type=f32)
        * score_scale
    )
    grad_keys = (
        jnp.einsum("hqk,qhd->khd", grad_scores_low, query_low, preferred_element_type=f32)
        * score_scale
    )
    grad_values = jnp.einsum(
        "hqk,qhd->khd", probs_low, grad_attended_low, preferred_element_type=f32
    )
    grad_raw_query, grad_raw_key, grad_gain_query, grad_gain_key = rotary_pull(
        (grad_queries, grad_keys)
    )
    grad_projected_low = jnp.concatenate(
        [grad_raw_query, grad_raw_key, grad_values.reshape(length, model_width)], axis=-1
    ).astype(bf16)
    grad_hidden_one = jnp.einsum(
        "te,de->td", grad_projected_low, qkv_full, preferred_element_type=f32
    )
    grad_inputs_norm, grad_gain_one = first_pull(grad_hidden_one)
    grad_tokens = grad_middle + grad_inputs_norm

    grad_router_part = jnp.einsum("td,te->ed", hidden_two, grad_logits, preferred_element_type=f32)
    small = jnp.concatenate(
        [
            grad_router_part,
            jnp.stack([grad_gain_one, grad_gain_query, grad_gain_key, grad_gain_two]),
            jnp.zeros((-(experts_all + 4) % 8, model_width), f32),
        ],
        axis=0,
    )
    keep = norm_one.shape[0]
    small = jnp.stack(
        [
            lax.dynamic_slice_in_dim(
                small,
                (((own_shard // 2 + dy) % (shard_group // 2)) * 2 + (own_shard % 2 + flip) % 2) * keep,
                keep,
                axis=1,
            )
            for dy in range(shard_group // 2)
            for flip in range(2)
        ]
    )

    grads_low = jnp.concatenate([grad_branch_low, grad_projected_low], axis=1)
    grads_low, mixture = lax.optimization_barrier((grads_low, mixture))
    block_out = (middle + mixture).astype(bf16)
    columns = jnp.stack([attended_columns.T, hidden_one_columns.T])
    grad_rows_kept, small = summed_rows(
        columns, grads_low, model_width, small, expert_group, shard_group, z_all, 256, 2, 1
    )
    grad_out_weight = grad_rows_kept[:, :model_width].astype(f32)
    grad_qkv_weight = grad_rows_kept[:, model_width:].astype(f32)
    return (
        block_out,
        grad_tokens,
        small[experts_all],
        small[experts_all + 1],
        small[experts_all + 2],
        small[experts_all + 3],
        grad_qkv_weight,
        grad_out_weight,
        small[:experts_all].T,
        grad_gate_up_weight,
        grad_down_weight,
    )


def solution(mesh):
    return jax.shard_map(
        body,
        mesh=mesh,
        in_specs=(
            P(("expert", "shard"), None),
            P(("expert", "shard"), None),
            P(("expert", "shard"), None),
            P(("expert", "shard"), None),
            P(),
            P("shard"),
            P("shard"),
            P("shard"),
            P("shard"),
            P("shard", None),
            P("shard", None),
            P("shard", None),
            P("expert", None, None),
            P("expert", None, None),
        ),
        out_specs=(
            P(("expert", "shard"), None),
            P(("expert", "shard"), None),
            P("shard"),
            P("shard"),
            P("shard"),
            P("shard"),
            P("shard", None),
            P("shard", None),
            P("shard", None),
            P("expert", "shard", None),
            P("expert", None, "shard"),
        ),
        check_vma=False,
    )
```

```python
import functools

import jax
import jax.numpy as jnp
from jax import lax
from jax.experimental import pallas as pl
from jax.experimental.pallas import tpu as pltpu
from jax.sharding import PartitionSpec as P

HEADS = 16
HEAD_DIM = 128
TOP = 8
TILE = 8


epsilon = 1e-05
rope_base = 10000.0


def rms_scale(values, scale_gain):
    return (
        values * lax.rsqrt(jnp.mean(values * values, axis=-1, keepdims=True) + epsilon) * scale_gain
    )


def rotary_tables(length):
    half_dim = HEAD_DIM // 2
    position = jnp.arange(length, dtype=jnp.float32)[:, None]
    frequency = rope_base ** (-jnp.arange(half_dim, dtype=jnp.float32) * 2.0 / HEAD_DIM)
    angles = position * frequency[None, :]
    angles = jnp.concatenate([angles, angles], axis=-1)
    return (jnp.cos(angles)[:, None, :], jnp.sin(angles)[:, None, :])


def rotate(vectors, cosine, sine_table):
    half_dim = vectors.shape[-1] // 2
    turned = jnp.concatenate([-vectors[..., half_dim:], vectors[..., :half_dim]], axis=-1)
    return vectors * cosine + turned * sine_table


def query_key(raw_query, raw_key, query_gain, key_gain, cosine, sine_table):
    length = raw_query.shape[0]
    queries = rms_scale(raw_query, query_gain).reshape(length, HEADS, HEAD_DIM)
    keys_rot = rms_scale(raw_key, key_gain).reshape(length, HEADS, HEAD_DIM)
    return (rotate(queries, cosine, sine_table), rotate(keys_rot, cosine, sine_table))


def swiglu(gate_up):
    half_dim = gate_up.shape[-1] // 2
    gate_part = gate_up[..., :half_dim]
    return gate_part / (1.0 + jnp.exp(-gate_part)) * gate_up[..., half_dim:]


def softmax_rows(logits):
    largest = jnp.max(logits, axis=-1, keepdims=True)
    raised = jnp.exp(logits - largest)
    return raised / jnp.sum(raised, axis=-1, keepdims=True)


def z_size(expert_group):
    return 4 if expert_group % 4 == 0 else 1


def shift(values, expert_group, dz, dx):
    z_all = z_size(expert_group)
    x_all = expert_group // z_all
    pairs = [
        (i, ((i // x_all + dz) % z_all) * x_all + (i % x_all + dx) % x_all)
        for i in range(expert_group)
    ]
    return lax.ppermute(values, "expert", pairs)


def gather_expert(block, expert_group):
    z_all = z_size(expert_group)
    x_all = expert_group // z_all
    rows = [block] + [shift(block, expert_group, dz, 0) for dz in range(1, z_all)]
    return [
        rows[dz] if dx == 0 else shift(rows[dz], expert_group, 0, dx)
        for dz in range(z_all)
        for dx in range(x_all)
    ]


def sum_over_x(parts, dz, expert_group):
    x_all = expert_group // z_size(expert_group)
    total = parts[dz * x_all].astype(jnp.float32)
    for dx in range(1, x_all):
        total = total + shift(parts[dz * x_all + dx], expert_group, 0, -dx).astype(jnp.float32)
    return total


def back_along_z(total, dz, expert_group):
    if dz == 0:
        return total
    return shift(total.astype(jnp.bfloat16), expert_group, -dz, 0).astype(jnp.float32)


def shard_shift(values, shard_group, dy, flip):
    y_all = shard_group // 2
    pairs = [(i, ((i // 2 + dy) % y_all) * 2 + (i % 2 + flip) % 2) for i in range(shard_group)]
    return lax.ppermute(values, "shard", pairs)


def own_columns(values, shard_group):
    me = lax.axis_index("shard")
    y_all = shard_group // 2
    width = values.shape[1] // shard_group
    found = []
    for dy in range(y_all):
        for flip in range(2):
            there = ((me // 2 + dy) % y_all) * 2 + (me % 2 + flip) % 2
            piece = lax.dynamic_slice_in_dim(values, there * width, width, axis=1)
            found.append(piece if dy + flip == 0 else shard_shift(piece, shard_group, dy, flip))
    return jnp.concatenate(found, axis=0)


def tail_kernel(
    dims, grads_ref, columns_ref, small_ref, out_ref, small_out_ref,
    gall, xsend, xrecv, zsend, zrecv, acc, fin, group_small, own_small, all_small, *sems
):
    steps, width, x_all, z_all, y_all, lag, first_steps = dims
    (gs_s, gs_r, es_s, es_r) = sems[14:]
    (y_s, y_r, core_s, core_r, fwd_s, fwd_r, x_s, x_r, z_s, z_r, zb_s, zb_r, xb_s, xb_r) = sems[:14]
    f32, bf16 = jnp.float32, jnp.bfloat16
    length = grads_ref.shape[0]
    rows = columns_ref.shape[1]
    block = rows // (x_all * z_all)
    half = z_all * block
    e = lax.axis_index("expert")
    s = lax.axis_index("shard")
    z, x = e // x_all, lax.rem(e, x_all)
    y, core = s // 2, lax.rem(s, 2)

    def y_peer(d):
        return {"shard": lax.rem(y + d, y_all) * 2 + core}

    partner = {"shard": y * 2 + (1 - core)}

    def x_peer(d):
        return {"expert": z * x_all + lax.rem(x + d, x_all)}

    def z_peer(d):
        return {"expert": lax.rem(z + d, z_all) * x_all + x}

    def copy(src, dst, send, recv, peer):
        return pltpu.make_async_remote_copy(
            src_ref=src, dst_ref=dst, send_sem=send, recv_sem=recv, device_id=peer,
            device_id_type=pl.DeviceIdType.MESH,
        )

    def cols(c):
        return pl.ds(pl.multiple_of(c * width, width), width)

    def y_copy(d, c):
        return copy(grads_ref.at[:, cols(c)], gall.at[2 * d - 1, c], y_s.at[d - 1], y_r.at[d - 1, c], y_peer(d))

    def core_copy(c):
        return copy(grads_ref.at[:, cols(c)], gall.at[0, c], core_s.at[0], core_r.at[c], partner)

    def fwd_copy(d, c):
        return copy(gall.at[2 * d - 1, c], gall.at[2 * d, c], fwd_s.at[d - 1], fwd_r.at[d - 1, c], partner)

    def x_copy(d, c):
        return copy(xsend.at[d - 1, c], xrecv.at[d - 1, c], x_s.at[d - 1], x_r.at[d - 1, c], x_peer(d))

    def z_copy(d, c):
        return copy(zsend.at[d - 1, c], zrecv.at[d - 1, c], z_s.at[d - 1], z_r.at[d - 1, c], z_peer(d))

    def zb_copy(d, c):
        here = fin.at[c, pl.ds(pl.multiple_of((x * z_all + z) * block, block), block)]
        return copy(here, here, zb_s.at[d - 1], zb_r.at[d - 1, c], z_peer(d))

    def xb_copy(d, c):
        here = fin.at[c, pl.ds(pl.multiple_of(x * half, half), half)]
        return copy(here, here, xb_s.at[d - 1], xb_r.at[d - 1, c], x_peer(d))

    near = [(d, flip) for d in range(y_all) for flip in range(2) if d + flip > 0]
    far = [(dz, dx) for dz in range(z_all) for dx in range(x_all) if dz + dx > 0]

    def near_peer(d, flip):
        return {"shard": lax.rem(y + d, y_all) * 2 + lax.rem(core + flip, 2)}

    def far_peer(dz, dx):
        return {"expert": lax.rem(z + dz, z_all) * x_all + lax.rem(x + dx, x_all)}

    def near_small(d, flip):
        j = 2 * d + flip
        return copy(small_ref.at[j], group_small.at[j - 1], gs_s.at[j - 1], gs_r.at[j - 1], near_peer(d, flip))

    def far_small(dz, dx):
        i = dz * x_all + dx
        return copy(own_small, all_small.at[i - 1], es_s.at[i - 1], es_r.at[i - 1], far_peer(dz, dx))

    barrier = pltpu.get_barrier_semaphore()
    peers = [near_peer(*p) for p in near] + [far_peer(*p) for p in far]
    for peer in peers:
        pl.semaphore_signal(barrier, inc=1, device_id=peer, device_id_type=pl.DeviceIdType.MESH)
    pl.semaphore_wait(barrier, len(peers))

    for p in near:
        near_small(*p).start()

    def first(c, carry):
        for d in range(1, y_all):
            y_copy(d, c).start()
        core_copy(c).start()
        return carry

    lax.fori_loop(0, steps, first, 0)
    slots = acc.shape[0]

    def step(t, carry):
        def stage(k, body):
            c = t - k * lag
            pl.when((c >= 0) & (c < steps))(lambda: body(c))

        @functools.partial(stage, 5)
        def _(c):
            for d in range(1, x_all):
                xb_copy(d, c).wait_recv()
            out_ref[:, cols(c)] = fin[c]

        @functools.partial(stage, 4)
        def _(c):
            for d in range(1, z_all):
                zb_copy(d, c).wait_recv()
            for d in range(1, x_all):
                xb_copy(d, c).start()

        @functools.partial(stage, 3)
        def _(c):
            slot = lax.rem(c, slots)
            total = acc[slot, pl.ds(pl.multiple_of(z * block, block), block), :]
            for d in range(1, z_all):
                z_copy(d, c).wait_recv()
                total = total + zrecv[d - 1, c].astype(f32)
            fin[c, pl.ds(pl.multiple_of((x * z_all + z) * block, block), block), :] = total.astype(bf16)
            for d in range(1, z_all):
                zb_copy(d, c).start()

        @functools.partial(stage, 2)
        def _(c):
            slot = lax.rem(c, slots)
            total = acc[slot]
            for d in range(1, x_all):
                x_copy(d, c).wait_recv()
                total = total + xrecv[d - 1, c].astype(f32)
            acc[slot] = total
            for d in range(1, z_all):
                there = lax.rem(z + d, z_all)
                zsend[d - 1, c] = acc[slot, pl.ds(pl.multiple_of(there * block, block), block), :].astype(bf16)
                z_copy(d, c).start()

        @functools.partial(stage, 1)
        def _(c):
            core_copy(c).wait_recv()
            for d in range(1, y_all):
                fwd_copy(d, c).wait_recv()
            kind = (c >= first_steps).astype(jnp.int32)
            others = gall[:, c].reshape((2 * y_all - 1) * length, width)
            mine = grads_ref[:, cols(c)]

            def product(there):
                at = pl.ds(pl.multiple_of(there * half, half), half)
                return jnp.dot(columns_ref[kind, at, :length], mine, preferred_element_type=f32) + jnp.dot(
                    columns_ref[kind, at, length:], others, preferred_element_type=f32
                )

            for d in range(1, x_all):
                xsend[d - 1, c] = product(lax.rem(x + d, x_all)).astype(bf16)
                x_copy(d, c).start()
            acc[lax.rem(c, slots)] = product(x)

        @functools.partial(stage, 0)
        def _(c):
            for d in range(1, y_all):
                y_copy(d, c).wait_recv()
                fwd_copy(d, c).start()

        @pl.when(t == 2)
        def _():
            total = small_ref[0]
            for j, p in enumerate(near):
                near_small(*p).wait_recv()
                total = total + group_small[j]
            own_small[...] = total
            for p in far:
                far_small(*p).start()

        return carry

    lax.fori_loop(0, steps + 5 * lag, step, 0)
    total = own_small[...]
    for i, p in enumerate(far):
        far_small(*p).wait_recv()
        total = total + all_small[i]
    small_out_ref[...] = total
    for p in near:
        near_small(*p).wait_send()
    for p in far:
        far_small(*p).wait_send()

    for d in range(1, y_all):
        copy(grads_ref, grads_ref, y_s.at[d - 1], y_r.at[d - 1, 0], y_peer(d)).wait_send()
        whole = gall.at[2 * d - 1]
        copy(whole, whole, fwd_s.at[d - 1], fwd_r.at[d - 1, 0], partner).wait_send()
    copy(grads_ref, grads_ref, core_s.at[0], core_r.at[0], partner).wait_send()
    for d in range(1, x_all):
        whole = xsend.at[d - 1]
        copy(whole, whole, x_s.at[d - 1], x_r.at[d - 1, 0], x_peer(d)).wait_send()
        copy(whole, whole, xb_s.at[d - 1], xb_r.at[d - 1, 0], x_peer(d)).wait_send()
    for d in range(1, z_all):
        whole = zsend.at[d - 1]
        copy(whole, whole, z_s.at[d - 1], z_r.at[d - 1, 0], z_peer(d)).wait_send()
        copy(whole, whole, zb_s.at[d - 1], zb_r.at[d - 1, 0], z_peer(d)).wait_send()


def summed_rows(columns, grads, first_total, small, expert_group, shard_group, z_all, width, lag, name_id):
    x_all, y_all = expert_group // z_all, shard_group // 2
    length, total = grads.shape
    rows = columns.shape[1]
    steps = total // width
    block = rows // expert_group
    half = z_all * block
    bf16 = jnp.bfloat16
    dma = pltpu.SemaphoreType.DMA
    n1 = max(y_all - 1, 1)
    x1 = max(x_all - 1, 1)
    z1 = max(z_all - 1, 1)
    slots = min(steps, 2 * lag + 1)
    return pl.pallas_call(
        functools.partial(tail_kernel, (steps, width, x_all, z_all, y_all, lag, first_total // width)),
        out_shape=[
            jax.ShapeDtypeStruct((rows, total), bf16),
            jax.ShapeDtypeStruct(small.shape[1:], jnp.float32),
        ],
        in_specs=[pl.BlockSpec(memory_space=pltpu.VMEM)] * 3,
        out_specs=[pl.BlockSpec(memory_space=pltpu.VMEM)] * 2,
        scratch_shapes=[
            pltpu.VMEM((shard_group - 1, steps, length, width), bf16),
            pltpu.VMEM((x1, steps, half, width), bf16),
            pltpu.VMEM((x1, steps, half, width), bf16),
            pltpu.VMEM((z1, steps, block, width), bf16),
            pltpu.VMEM((z1, steps, block, width), bf16),
            pltpu.VMEM((slots, half, width), jnp.float32),
            pltpu.VMEM((steps, rows, width), bf16),
            pltpu.VMEM((shard_group - 1, *small.shape[1:]), jnp.float32),
            pltpu.VMEM(small.shape[1:], jnp.float32),
            pltpu.VMEM((expert_group - 1, *small.shape[1:]), jnp.float32),
            dma((n1,)), dma((n1, steps)),
            dma((1,)), dma((steps,)),
            dma((n1,)), dma((n1, steps)),
            dma((x1,)), dma((x1, steps)),
            dma((z1,)), dma((z1, steps)),
            dma((z1,)), dma((z1, steps)),
            dma((x1,)), dma((x1, steps)),
            dma((shard_group - 1,)), dma((shard_group - 1,)),
            dma((expert_group - 1,)), dma((expert_group - 1,)),
        ],
        compiler_params=pltpu.CompilerParams(
            collective_id=name_id, has_side_effects=True, vmem_limit_bytes=60 * 1024 * 1024
        ),
        cost_estimate=pl.CostEstimate(
            flops=2 * rows * length * shard_group * total, bytes_accessed=16 * 1024 * 1024, transcendentals=0
        ),
    )(grads, columns, small)


MOE_CHUNKS = 4


def moe_kernel(
    dims, hidden_hbm, upstream_hbm, place_ref, place_t_ref, router_ref, router_t_ref, gate_up_hbm, down_hbm,
    rows_hbm, activated_hbm, grad_out_hbm, grad_gate_up_hbm, grad_ref, grad_router_ref, found_hbm, summed_hbm,
    *rest,
):
    x_all, capacity = dims
    mixture_hbm = rest[: 4 * x_all]
    (
    gate_up_w, down_w, hid, ups, prob, prob_t, rows, gate_up, activated, out_rows, grad_expert, grad_gate_up, grad_rows,
    mix_stage, part_stage, own_part, z_landed, router_stage,
    w_sem, own_sem, load_sem, store_sem, zs, zr, xs, xr, fs, fr, ps, pr, qs, qr, rs, rr, lsem, mix_sem,
    ) = rest[4 * x_all :]
    z_all = 4
    f32, bf16 = jnp.float32, jnp.bfloat16
    length, width = hidden_hbm.shape
    local_experts, _, twice = gate_up_w.shape
    half = twice // 2
    tile = min(512, half)
    narrow = min(256, half)
    chunk = length // MOE_CHUNKS
    e = lax.axis_index("expert")
    z, x = e // x_all, lax.rem(e, x_all)

    def peer(dz, dx):
        return {"expert": lax.rem(z + dz + 4 * z_all, z_all) * x_all + lax.rem(x + dx + 4 * x_all, x_all)}

    def copy(src, dst, send, recv, to):
        return pltpu.make_async_remote_copy(
            src_ref=src, dst_ref=dst, send_sem=send, recv_sem=recv, device_id=to,
            device_id_type=pl.DeviceIdType.MESH,
        )

    def at(c):
        return pl.ds(pl.multiple_of(c * chunk, chunk), chunk)

    def z_copy(d, c):
        return copy(hidden_hbm.at[at(c)], found_hbm.at[d, 0, at(c)], zs.at[d - 1, c], zr.at[d - 1, c], peer(d, 0))

    def x_copy(d, c):
        return copy(hidden_hbm.at[at(c)], found_hbm.at[0, d, at(c)], xs.at[d - 1, c], xr.at[d - 1, c], peer(0, d))

    def f_copy(dz, dx, c):
        return copy(
            found_hbm.at[dz, 0, at(c)], found_hbm.at[dz, dx, at(c)],
            fs.at[dz - 1, dx - 1, c], fr.at[dz - 1, dx - 1, c], peer(0, dx),
        )

    def p_copy(dz, dx, c):
        return copy(
            part_stage.at[dx - 1, at(c)], summed_hbm.at[dz, dx - 1, at(c)],
            ps.at[dx - 1], pr.at[dz, dx - 1, c], peer(0, -dx),
        )

    def p_sent(dx):
        whole = part_stage.at[dx - 1]
        copy(whole, whole, ps.at[dx - 1], pr.at[0, dx - 1, 0], peer(0, -dx)).wait_send()

    def q_copy(dz, c):
        return copy(
            own_part.at[dz, at(c)], z_landed.at[dz - 1, at(c)], qs.at[dz - 1], qr.at[dz - 1, c], peer(-dz, 0)
        )

    def r_copy(dz, dx):
        return copy(
            router_stage.at[dz, dx], grad_router_ref.at[e], rs.at[dz, dx], rr.at[dz, dx], peer(-dz, -dx)
        )

    def cols(n, w):
        return pl.ds(pl.multiple_of(n * w, w), w)

    barrier = pltpu.get_barrier_semaphore()
    others = [(dz, dx) for dz in range(z_all) for dx in range(x_all) if dz + dx > 0]
    for dz, dx in others:
        pl.semaphore_signal(barrier, inc=1, device_id=peer(dz, dx), device_id_type=pl.DeviceIdType.MESH)
    pl.semaphore_wait(barrier, len(others))

    own = pltpu.make_async_copy(hidden_hbm, found_hbm.at[0, 0], own_sem)
    own.start()
    weights = [
        pltpu.make_async_copy(gate_up_hbm, gate_up_w, w_sem.at[0]),
        pltpu.make_async_copy(down_hbm, down_w, w_sem.at[1]),
    ]
    for w in weights:
        w.start()

    def send_own(c, carry):
        for d in range(1, x_all):
            x_copy(d, c).start()
        return carry

    lax.fori_loop(0, MOE_CHUNKS, send_own, 0)
    for d in (1, 3, 2):

        def send_z(c, carry):
            z_copy(d, c).start()
            return carry

        lax.fori_loop(0, MOE_CHUNKS, send_z, 0)

    def events(first, last):
        def one(k, carry):
            @pl.when(k < last)
            def _():
                j = k // MOE_CHUNKS
                c = lax.rem(k, MOE_CHUNKS)
                d = 1 + 2 * j - 3 * (j // 2)
                z_copy(d, c).wait_recv()
                for dx in range(1, x_all):
                    f_copy(d, dx, c).start()

            return carry

        lax.fori_loop(first, first + MOE_CHUNKS, one, 0)

    def own_slots(le):
        return pl.ds(pl.multiple_of(le * capacity, capacity), capacity)

    def finish(dz, last):
        def load(c):
            return pltpu.make_async_copy(summed_hbm.at[dz, dx - 1, at(c)], hid.at[0, at(c)], lsem.at[c])

        def add(c):
            load(c).wait()
            own_part[dz, at(c), :] = (
                own_part[dz, at(c), :].astype(f32) + hid[0, at(c), :].astype(f32)
            ).astype(bf16)
            if dx == x_all - 1:
                pl.when(dz > 0)(lambda: q_copy(dz, c).start())

        def arrive(c, carry):
            p_copy(dz, dx, c).wait_recv()
            load(c).start()
            if last:
                add(c)
            return carry

        def rest(c, carry):
            add(c)
            return carry

        for dx in range(1, x_all):
            lax.fori_loop(0, MOE_CHUNKS, arrive, 0)
            if not last:
                lax.fori_loop(0, MOE_CHUNKS, rest, 0)

    mix_slots = mix_stage.shape[0]

    def mix_copy(dz, dx):
        slot = dx % mix_slots
        return pltpu.make_async_copy(mix_stage.at[slot], mixture_hbm[dz * x_all + dx], mix_sem.at[slot])

    slot_row = lax.broadcasted_iota(jnp.int32, (capacity, length), 0).astype(f32)
    slot_col = lax.broadcasted_iota(jnp.int32, (length, local_experts * capacity), 1).astype(f32)
    own.wait()
    events(0, 4)

    def load_upstream(dz):
        return [pltpu.make_async_copy(upstream_hbm.at[dz, dx], ups.at[dx], load_sem.at[1, dx]) for dx in range(x_all)]

    for load in load_upstream(0):
        load.start()

    def group(dz, carry):
        g = dz

        def arrive(c, inner):
            for dx in range(1, x_all):

                @pl.when(dz == 0)
                def _():
                    x_copy(dx, c).wait_recv()

                @pl.when(dz > 0)
                def _():
                    f_copy(dz, dx, c).wait_recv()

            return inner

        lax.fori_loop(0, MOE_CHUNKS, arrive, 0)
        loads = []
        for dx in range(x_all):
            loads.append(pltpu.make_async_copy(found_hbm.at[dz, dx], hid.at[dx], load_sem.at[0, dx]))
        for load in loads:
            load.start()
        for load in loads + load_upstream(dz):
            load.wait()
        pl.when(g == 0)(lambda: [w.wait() for w in weights] and None)

        for dx in range(x_all):
            logits = jnp.dot(hid[dx], router_ref[...], preferred_element_type=f32)
            raised = jnp.exp(logits - jnp.max(logits, axis=1, keepdims=True))
            prob[dx] = raised / jnp.sum(raised, axis=1, keepdims=True)
            logits = lax.dot_general(
                router_t_ref[...], hid[dx], (((1,), (1,)), ((), ())), preferred_element_type=f32
            )
            raised = jnp.exp(logits - jnp.max(logits, axis=0, keepdims=True))
            prob_t[dx] = raised / jnp.sum(raised, axis=0, keepdims=True)
            router_stage[dz, dx] = jnp.zeros(router_stage.shape[2:], f32)

        def store(kind, buffer, hbm, le):
            return pltpu.make_async_copy(buffer, hbm.at[le, dz], store_sem.at[kind])

        def expert(le, inner):
            @pl.when(g + le > 0)
            def _():
                store(0, rows, rows_hbm, le).wait()
                store(1, activated, activated_hbm, le).wait()
                store(2, grad_expert, grad_out_hbm, le).wait()
                store(3, grad_gate_up, grad_gate_up_hbm, le).wait()

            chosen = [place_ref[dz, dx, pl.ds(le, 1), :] == slot_row for dx in range(x_all)]
            chosen_low = [c.astype(f32).astype(bf16) for c in chosen]

            def dispatch(n, c0):
                c = cols(n, tile)
                for dx in range(x_all):
                    rows[dx * capacity : (dx + 1) * capacity, c] = jnp.dot(
                        chosen_low[dx], hid[dx, :, c], preferred_element_type=f32
                    ).astype(bf16)
                return c0

            lax.fori_loop(0, width // tile, dispatch, 0, unroll=True)
            store(0, rows, rows_hbm, le).start()

            def up_step(n, c0):
                c = cols(n, tile)
                gate_up[:, c] = jnp.dot(rows[...], gate_up_w[le, :, c], preferred_element_type=f32)
                return c0

            lax.fori_loop(0, twice // tile, up_step, 0, unroll=True)

            def act_step(n, c0):
                gate = gate_up[:, cols(n, narrow)]
                up = gate_up[:, pl.ds(pl.multiple_of(half + n * narrow, narrow), narrow)]
                activated[:, cols(n, narrow)] = (gate / (1.0 + jnp.exp(-gate)) * up).astype(bf16)
                return c0

            lax.fori_loop(0, half // narrow, act_step, 0, unroll=True)
            store(1, activated, activated_hbm, le).start()

            def down_step(n, c0):
                c = cols(n, tile)
                result = jnp.dot(activated[...], down_w[le, :, c], preferred_element_type=f32)
                for dx in range(x_all):
                    r = slice(dx * capacity, (dx + 1) * capacity)
                    out_rows[dx, own_slots(le), c] = result[r].astype(bf16)
                return c0

            lax.fori_loop(0, width // tile, down_step, 0, unroll=True)

            mine = e * local_experts + le
            weight_rows = [
                jnp.sum(jnp.where(chosen[dx], prob_t[dx, pl.ds(mine, 1), :], 0.0), axis=1, keepdims=True)
                for dx in range(x_all)
            ]

            def grad_step(n, totals):
                c = cols(n, tile)
                new = []
                for dx in range(x_all):
                    r = slice(dx * capacity, (dx + 1) * capacity)
                    up_rows = jnp.dot(chosen_low[dx], ups[dx, :, c], preferred_element_type=f32)
                    grad_expert[r, c] = (weight_rows[dx] * up_rows).astype(bf16)
                    new.append(
                        totals[dx]
                        + jnp.sum(up_rows * out_rows[dx, own_slots(le), c].astype(f32), axis=1, keepdims=True)
                    )
                return tuple(new)

            totals = lax.fori_loop(
                0, width // tile, grad_step, tuple(jnp.zeros((capacity, 1), f32) for _ in range(x_all)),
                unroll=True,
            )
            store(2, grad_expert, grad_out_hbm, le).start()
            for dx in range(x_all):
                router_stage[dz, dx, pl.ds(le, 1), :] = jnp.sum(
                    jnp.where(chosen[dx], totals[dx], 0.0), axis=0, keepdims=True
                )

            def back_step(n, c0):
                ga = lax.dot_general(
                    grad_expert[...], down_w[le, cols(n, narrow), :], (((1,), (1,)), ((), ())),
                    preferred_element_type=f32,
                )
                gate = gate_up[:, cols(n, narrow)]
                c_up = pl.ds(pl.multiple_of(half + n * narrow, narrow), narrow)
                up = gate_up[:, c_up]
                sg = 1.0 / (1.0 + jnp.exp(-gate))
                grad_gate_up[:, cols(n, narrow)] = (ga * up * sg * (1.0 + gate * (1.0 - sg))).astype(bf16)
                grad_gate_up[:, c_up] = (ga * (gate * sg)).astype(bf16)
                return c0

            lax.fori_loop(0, half // narrow, back_step, 0, unroll=True)
            store(3, grad_gate_up, grad_gate_up_hbm, le).start()

            def row_step(n, c0):
                result = lax.dot_general(
                    grad_gate_up[...], gate_up_w[le, cols(n, narrow), :], (((1,), (1,)), ((), ())),
                    preferred_element_type=f32,
                )
                for dx in range(x_all):
                    r = slice(dx * capacity, (dx + 1) * capacity)
                    grad_rows[dx, own_slots(le), cols(n, narrow)] = result[r].astype(bf16)
                return c0

            lax.fori_loop(0, width // narrow, row_step, 0, unroll=True)
            k = 2 * g + le
            events(
                jnp.where(k == 0, 4, jnp.where(k == 1, 7, jnp.where(k == 2, 9, 11))),
                jnp.where(k == 0, 7, jnp.where(k == 1, 9, jnp.where(k == 2, 11, jnp.where(k == 3, 12, 0)))),
            )
            return inner

        assert local_experts == 2
        lax.fori_loop(0, local_experts, expert, 0)

        @pl.when(g < z_all - 1)
        def _():
            for load in load_upstream(dz + 1):
                load.start()

        def stages():
            for dx in range(1, x_all):
                p_sent(dx)

        pl.when(g > 0)(stages)
        for dx in range(x_all):
            weight = jnp.zeros(slot_col.shape, f32)
            mask = jnp.zeros(slot_col.shape, f32)
            lane = lax.broadcasted_iota(jnp.int32, prob.shape[1:], 1)
            for le in range(local_experts):
                spot = place_t_ref[dz, dx, :, le : le + 1]
                here = jnp.where(spot < 0.0, -1.0, spot + le * capacity) == slot_col
                p = jnp.sum(jnp.where(lane == e * local_experts + le, prob[dx], 0.0), axis=1, keepdims=True)
                weight = jnp.where(here, p, weight)
                mask = jnp.where(here, 1.0, mask)
            low = mask.astype(bf16)
            high = weight.astype(bf16)
            remainder = (weight - high.astype(f32)).astype(bf16)

            if dx < mix_slots:
                pl.when(g > 0)(mix_copy(0, dx).wait)
            else:
                mix_copy(0, dx).wait()

            def combine(n, c0):
                c = cols(n, tile)
                mix = jnp.dot(high, out_rows[dx, :, c], preferred_element_type=f32) + jnp.dot(
                    remainder, out_rows[dx, :, c], preferred_element_type=f32
                )
                grad = jnp.dot(low, grad_rows[dx, :, c], preferred_element_type=f32)
                mix_stage[dx % mix_slots, :, c] = mix.astype(bf16)
                if dx == 0:
                    own_part[dz, :, c] = grad.astype(bf16)
                else:
                    part_stage[dx - 1, :, c] = grad.astype(bf16)
                return c0

            lax.fori_loop(0, width // tile, combine, 0, unroll=True)
            for k in range(z_all):
                pl.when(dz == k)(mix_copy(k, dx).start)
            if dx > 0:
                for c in range(MOE_CHUNKS):
                    p_copy(dz, dx, c).start()
                r_copy(dz, dx).start()
            else:

                @pl.when(dz > 0)
                def _():
                    r_copy(dz, 0).start()

                @pl.when(dz == 0)
                def _():
                    grad_router_ref[e] = router_stage[0, 0]

        pl.when(g > 0)(lambda: finish(dz - 1, False))
        return carry

    lax.fori_loop(0, z_all, group, 0)
    finish(z_all - 1, True)

    def total(c, carry):
        grad_ref[at(c), :] = own_part[0, at(c), :].astype(f32)
        for d in (1, 2, 3):
            q_copy(d, c).wait_recv()
            grad_ref[at(c), :] = grad_ref[at(c), :] + z_landed[d - 1, at(c), :].astype(f32)
        return carry

    lax.fori_loop(0, MOE_CHUNKS, total, 0)

    for kind, buffer, hbm in (
        (0, rows, rows_hbm), (1, activated, activated_hbm), (2, grad_expert, grad_out_hbm),
        (3, grad_gate_up, grad_gate_up_hbm),
    ):
        pltpu.make_async_copy(buffer, hbm.at[0, 0], store_sem.at[kind]).wait()
    for dx in range(mix_slots):
        mix_copy(0, dx).wait()
    for dx in range(1, x_all):
        p_sent(dx)
    for d in range(1, z_all):
        whole = own_part.at[d]
        copy(whole, whole, qs.at[d - 1], qr.at[d - 1, 0], peer(-d, 0)).wait_send()
    for dz, dx in others:
        r_copy(dz, dx).wait_send()
        r_copy(dz, dx).wait_recv()

    def sent(c, carry):
        for d in range(1, z_all):
            z_copy(d, c).wait_send()
            for dx in range(1, x_all):
                f_copy(d, dx, c).wait_send()
        for d in range(1, x_all):
            x_copy(d, c).wait_send()
        return carry

    lax.fori_loop(0, MOE_CHUNKS, sent, 0)


def moe_layer(hidden, upstream_all, place, router_weight, gate_up_weight, down_weight, expert_group, capacity, name_id):
    f32, bf16 = jnp.float32, jnp.bfloat16
    length, width = hidden.shape
    local_experts, _, twice = gate_up_weight.shape
    half = twice // 2
    experts_all = router_weight.shape[1]
    x_all = expert_group // 4
    count = x_all * capacity
    dma = pltpu.SemaphoreType.DMA
    x1 = max(x_all - 1, 1)
    place_t = place.transpose(0, 1, 3, 2)
    spare = (-local_experts) % 8
    place = jnp.pad(place, ((0, 0), (0, 0), (0, spare), (0, 0)), constant_values=-1.0)
    any_spec = pl.BlockSpec(memory_space=pl.ANY)
    vmem_spec = pl.BlockSpec(memory_space=pltpu.VMEM)
    out = pl.pallas_call(
        functools.partial(moe_kernel, (x_all, capacity)),
        out_shape=[
            jax.ShapeDtypeStruct((local_experts, 4, count, width), bf16),
            jax.ShapeDtypeStruct((local_experts, 4, count, half), bf16),
            jax.ShapeDtypeStruct((local_experts, 4, count, width), bf16),
            jax.ShapeDtypeStruct((local_experts, 4, count, twice), bf16),
            jax.ShapeDtypeStruct((length, width), f32),
            jax.ShapeDtypeStruct((expert_group, 8, length), f32),
            jax.ShapeDtypeStruct((4, x_all, length, width), bf16),
            jax.ShapeDtypeStruct((4, x1, length, width), bf16),
        ]
        + [jax.ShapeDtypeStruct((length, width), bf16)] * (4 * x_all),
        in_specs=[any_spec, any_spec, vmem_spec, vmem_spec, vmem_spec, vmem_spec, any_spec, any_spec],
        out_specs=[any_spec] * 4 + [vmem_spec, vmem_spec] + [any_spec] * (2 + 4 * x_all),
        scratch_shapes=[
            pltpu.VMEM(gate_up_weight.shape, bf16),
            pltpu.VMEM(down_weight.shape, bf16),
            pltpu.VMEM((x_all, length, width), bf16),
            pltpu.VMEM((x_all, length, width), bf16),
            pltpu.VMEM((x_all, length, experts_all), f32),
            pltpu.VMEM((x_all, experts_all, length), f32),
            pltpu.VMEM((count, width), bf16),
            pltpu.VMEM((count, twice), f32),
            pltpu.VMEM((count, half), bf16),
            pltpu.VMEM((x_all, local_experts * capacity, width), bf16),
            pltpu.VMEM((count, width), bf16),
            pltpu.VMEM((count, twice), bf16),
            pltpu.VMEM((x_all, local_experts * capacity, width), bf16),
            pltpu.VMEM((min(2, x_all), length, width), bf16),
            pltpu.VMEM((x1, length, width), bf16),
            pltpu.VMEM((4, length, width), bf16),
            pltpu.VMEM((3, length, width), bf16),
            pltpu.VMEM((4, x_all, 8, length), f32),
            dma((2,)), dma, dma((2, x_all)), dma((4,)),
            dma((3, MOE_CHUNKS)), dma((3, MOE_CHUNKS)),
            dma((x1, MOE_CHUNKS)), dma((x1, MOE_CHUNKS)),
            dma((3, x1, MOE_CHUNKS)), dma((3, x1, MOE_CHUNKS)),
            dma((x1,)), dma((4, x1, MOE_CHUNKS)),
            dma((3,)), dma((3, MOE_CHUNKS)),
            dma((4, x_all)), dma((4, x_all)),
            dma((MOE_CHUNKS,)), dma((min(2, x_all),)),
        ],
        compiler_params=pltpu.CompilerParams(
            collective_id=name_id, has_side_effects=True, vmem_limit_bytes=62 * 1024 * 1024
        ),
        cost_estimate=pl.CostEstimate(
            flops=12 * 4 * local_experts * count * width * twice, bytes_accessed=64 * 1024 * 1024,
            transcendentals=0,
        ),
    )(
        hidden, upstream_all, place, place_t, router_weight, router_weight.T, gate_up_weight, down_weight
    )
    return out[:6], out[8:]


def start_kernel(
    dims, weight_hbm, upstream_hbm, router_hbm, gains_ref, tokens_ref, routes_ref, tiles_ref,
    full_hbm, ups_hbm, router_full_hbm, gains_full_ref, place_all_ref, hidden_ref, *sems,
):
    x_all, y_all = dims
    z_all, parts = 4, 4
    (own_sem, ys, yr, rs, rr, cs, cr, fs, fr, gs, gr, zs, zr, xs, xr, us, ur, ns, nr, ps, pr, ms, mr) = sems
    f32, bf16 = jnp.float32, jnp.bfloat16
    rows = weight_hbm.shape[0]
    length = tokens_ref.shape[0]
    piece = rows // 8
    chunk = length // parts
    e = lax.axis_index("expert")
    s = lax.axis_index("shard")
    z, x = e // x_all, lax.rem(e, x_all)
    y, core = s // 2, lax.rem(s, 2)
    parity = lax.rem(z, 2)

    def expert_peer(dz, dx):
        return {"expert": lax.rem(z + dz, z_all) * x_all + lax.rem(x + dx, x_all)}

    def shard_peer(dy, flip):
        return {"shard": lax.rem(y + dy, y_all) * 2 + lax.rem(core + flip, 2)}

    beside = {"expert": (z + 1 - 2 * parity) * x_all + x}
    partner = shard_peer(0, 1)
    far = [(dz, dx) for dz in range(z_all) for dx in range(x_all) if dz + dx > 0]
    near = [(dy, flip) for dy in range(y_all) for flip in range(2) if dy + flip > 0]

    def copy(src, dst, send, recv, to):
        return pltpu.make_async_remote_copy(
            src_ref=src, dst_ref=dst, send_sem=send, recv_sem=recv, device_id=to,
            device_id_type=pl.DeviceIdType.MESH,
        )

    def piece_of(i, who):
        return jnp.where(i < 2, 4 + 2 * who + i, i - 2)

    def span(owner, k):
        return pl.ds(pl.multiple_of(owner * rows + k * piece, piece), piece)

    def y_copy(dy, i):
        k = piece_of(i, parity)
        src = weight_hbm.at[pl.ds(pl.multiple_of(k * piece, piece), piece)]
        return copy(src, full_hbm.at[span(s, k)], ys.at[dy - 1, i], yr.at[dy - 1, i], shard_peer(dy, 0))

    def owner(dy):
        return lax.rem(y - dy + y_all, y_all) * 2 + core

    def relay(dy, i):
        here = full_hbm.at[span(owner(dy), 4 + 2 * parity + i)]
        return copy(here, here, rs.at[dy - 1, i], rr.at[dy - 1, i], beside)

    def core_y(dy, i):
        here = full_hbm.at[span(owner(dy), piece_of(i, parity))]
        return copy(here, here, cs.at[dy - 1, i], cr.at[dy - 1, i], partner)

    def core_r(dy, i):
        here = full_hbm.at[span(owner(dy), 4 + 2 * (1 - parity) + i)]
        return copy(here, here, fs.at[dy - 1, i], fr.at[dy - 1, i], partner)

    whole = pl.ds(pl.multiple_of(s * rows, rows), rows)
    core_own = copy(weight_hbm, full_hbm.at[whole], gs, gr, partner)

    def at(c):
        return pl.ds(pl.multiple_of(c * chunk, chunk), chunk)

    def z_copy(d, c):
        return copy(upstream_hbm.at[at(c)], ups_hbm.at[d, 0, at(c)], zs.at[d - 1, c], zr.at[d - 1, c], expert_peer(d, 0))

    def x_copy(d):
        return copy(upstream_hbm, ups_hbm.at[0, d], xs.at[d - 1], xr.at[d - 1], expert_peer(0, d))

    def u_copy(dz, dx, c):
        return copy(
            ups_hbm.at[dz, 0, at(c)], ups_hbm.at[dz, dx, at(c)],
            us.at[dz - 1, dx - 1, c], ur.at[dz - 1, dx - 1, c], expert_peer(0, dx),
        )

    def router_copy(n, p):
        return copy(router_hbm, router_full_hbm.at[whole], ns.at[n], nr.at[n], shard_peer(*p))

    def gains_copy(n, p):
        return copy(gains_ref, gains_full_ref.at[s], ms.at[n], mr.at[n], shard_peer(*p))

    def place_copy(n, p):
        return copy(place_all_ref.at[0, 0], place_all_ref.at[p[0], p[1]], ps.at[n], pr.at[n], expert_peer(*p))

    barrier = pltpu.get_barrier_semaphore()
    peers = [expert_peer(*p) for p in far] + [shard_peer(*p) for p in near]
    for peer in peers:
        pl.semaphore_signal(barrier, inc=1, device_id=peer, device_id_type=pl.DeviceIdType.MESH)
    pl.semaphore_wait(barrier, len(peers))

    own = [
        pltpu.make_async_copy(weight_hbm, full_hbm.at[whole], own_sem.at[0]),
        pltpu.make_async_copy(upstream_hbm, ups_hbm.at[0, 0], own_sem.at[1]),
        pltpu.make_async_copy(router_hbm, router_full_hbm.at[whole], own_sem.at[2]),
    ]
    for n, p in enumerate(near):
        gains_copy(n, p).start()
        router_copy(n, p).start()
    for i in range(2):
        for dy in range(1, y_all):
            y_copy(dy, i).start()
    for d in range(1, x_all):
        x_copy(d).start()
    for d in (1, 3, 2):
        for c in range(parts):
            z_copy(d, c).start()
    core_own.start()
    for o in own:
        o.start()

    count = place_all_ref.shape[2]
    ids = lax.broadcasted_iota(jnp.int32, (count, length), 0)
    chosen = jnp.zeros((count, length), f32)
    for k in range(TOP):
        chosen = jnp.where(routes_ref[k : k + 1, :] == ids, 1.0, chosen)
    before = lax.broadcasted_iota(jnp.int32, (length, length), 0)
    after = lax.broadcasted_iota(jnp.int32, (length, length), 1)
    earlier = jnp.where(before < after, 1.0, 0.0).astype(bf16)
    rank = jnp.dot(chosen.astype(bf16), earlier, preferred_element_type=f32)
    limit = (tiles_ref[...] * TILE).astype(f32)
    place_all_ref[0, 0] = jnp.where((chosen > 0.5) & (rank < limit), rank, -1.0)
    for n, p in enumerate(far):
        place_copy(n, p).start()

    gains_full_ref[s] = gains_ref[...]
    for n, p in enumerate(near):
        gains_copy(n, p).wait_recv()
    keep = gains_ref.shape[1]
    tall = 64

    def norm(t, carry):
        r = pl.ds(pl.multiple_of(t * tall, tall), tall)
        values = tokens_ref[r, :].astype(f32)
        scale = lax.rsqrt(jnp.mean(values * values, axis=1, keepdims=True) + epsilon)
        for j in range(2 * y_all):
            c = slice(j * keep, (j + 1) * keep)
            gain = gains_full_ref[j, 0:1, :].astype(f32)
            hidden_ref[r, c] = (values[:, c] * scale * gain).astype(bf16)
        return carry

    lax.fori_loop(0, length // tall, norm, 0)

    def forward(events):
        for d, c in events:
            z_copy(d, c).wait_recv()
            for dx in range(1, x_all):
                u_copy(d, dx, c).start()

    order = {
        0: [(1, 0)], 1: [(1, 1), (1, 2)], 2: [(1, 3), (3, 0), (3, 1)], 3: [(3, 2), (3, 3), (2, 0)],
        4: [(2, 1), (2, 2), (2, 3)], 5: [],
    }
    for i in range(6):
        for dy in range(1, y_all):
            y_copy(dy, i).wait_recv()
            if i < 2:
                relay(dy, i).start()
            core_y(dy, i).start()
            if i < 4:
                y_copy(dy, i + 2).start()
        forward(order[i])
        if i in (3, 4):
            for dy in range(1, y_all):
                here = full_hbm.at[span(owner(dy), 4 + 2 * (1 - parity) + i - 3)]
                copy(here, here, rs.at[dy - 1, i - 3], rr.at[dy - 1, i - 3], beside).wait_recv()
                core_r(dy, i - 3).start()

    for o in own:
        o.wait()
    core_own.wait()
    for n, p in enumerate(near):
        gains_copy(n, p).wait_send()
        router_copy(n, p).wait()
    for n, p in enumerate(far):
        place_copy(n, p).wait()
    for d in range(1, x_all):
        x_copy(d).wait()
    for dy in range(1, y_all):
        for i in range(6):
            y_copy(dy, i).wait_send()
            core_y(dy, i).wait()
        for i in range(2):
            relay(dy, i).wait_send()
            core_r(dy, i).wait()
    for d in range(1, z_all):
        for c in range(parts):
            z_copy(d, c).wait_send()
            for dx in range(1, x_all):
                u_copy(d, dx, c).wait()


def start_layer(weight, upstream, router, gains, tokens, routes, tile_counts, expert_group, shard_group, name_id):
    f32, bf16 = jnp.float32, jnp.bfloat16
    length, width = tokens.shape
    x_all, y_all = expert_group // 4, shard_group // 2
    experts_all = tile_counts.shape[0]
    dma = pltpu.SemaphoreType.DMA
    y1, x1 = max(y_all - 1, 1), max(x_all - 1, 1)
    any_spec = pl.BlockSpec(memory_space=pl.ANY)
    vmem_spec = pl.BlockSpec(memory_space=pltpu.VMEM)
    return pl.pallas_call(
        functools.partial(start_kernel, (x_all, y_all)),
        out_shape=[
            jax.ShapeDtypeStruct((weight.shape[0] * shard_group, weight.shape[1]), bf16),
            jax.ShapeDtypeStruct((4, x_all, length, width), bf16),
            jax.ShapeDtypeStruct((router.shape[0] * shard_group, router.shape[1]), bf16),
            jax.ShapeDtypeStruct((shard_group, *gains.shape), bf16),
            jax.ShapeDtypeStruct((4, x_all, experts_all, length), f32),
            jax.ShapeDtypeStruct((length, width), bf16),
        ],
        in_specs=[any_spec] * 3 + [vmem_spec] * 4,
        out_specs=[any_spec] * 3 + [vmem_spec] * 3,
        scratch_shapes=[
            dma((3,)),
            dma((y1, 6)), dma((y1, 6)),
            dma((y1, 2)), dma((y1, 2)),
            dma((y1, 6)), dma((y1, 6)),
            dma((y1, 2)), dma((y1, 2)),
            dma, dma,
            dma((3, 4)), dma((3, 4)),
            dma((x1,)), dma((x1,)),
            dma((3, x1, 4)), dma((3, x1, 4)),
            dma((shard_group - 1,)), dma((shard_group - 1,)),
            dma((expert_group - 1,)), dma((expert_group - 1,)),
            dma((shard_group - 1,)), dma((shard_group - 1,)),
        ],
        compiler_params=pltpu.CompilerParams(
            collective_id=name_id, has_side_effects=True, vmem_limit_bytes=32 * 1024 * 1024
        ),
        cost_estimate=pl.CostEstimate(
            flops=16 * length * width, bytes_accessed=64 * 1024 * 1024, transcendentals=0
        ),
    )(weight, upstream, router, gains, tokens, routes.T, tile_counts[:, None])


def body(
    tokens,
    cotangent,
    segments,
    routes,
    tile_counts,
    norm_one,
    norm_query,
    norm_key,
    norm_two,
    qkv_weight,
    out_weight,
    router_weight,
    gate_up_weight,
    down_weight,
):
    f32, bf16 = jnp.float32, jnp.bfloat16
    length, model_width = tokens.shape
    experts_all = tile_counts.shape[0]
    local_experts = gate_up_weight.shape[0]
    expert_group = lax.axis_size("expert")
    shard_group = lax.axis_size("shard")
    capacity = length * TOP // (experts_all * TILE) * TILE
    score_scale = HEAD_DIM ** (-0.5)
    own_expert = lax.axis_index("expert")
    own_shard = lax.axis_index("shard")
    z_all = z_size(expert_group)
    x_all = expert_group // z_all

    gain_rows = jnp.stack([norm_one, norm_query, norm_key, norm_two])
    gain_rows = jnp.pad(gain_rows, ((0, 12), (0, 0)))
    qkv_full, upstream_all, router_full, gains, place_all, hidden_one = start_layer(
        qkv_weight,
        cotangent,
        router_weight,
        gain_rows,
        tokens,
        routes,
        tile_counts,
        expert_group,
        shard_group,
        3,
    )
    out_own, gains = lax.optimization_barrier((out_weight, gains))
    out_full = lax.all_gather(out_own, "shard", axis=0, tiled=True)
    gains = gains.transpose(1, 0, 2).reshape(gains.shape[1], model_width).astype(f32)
    gain_one, gain_query, gain_key, gain_two = gains[0], gains[1], gains[2], gains[3]
    place_own = lax.dynamic_slice_in_dim(
        place_all, own_expert * local_experts, local_experts, axis=2
    )
    position = jnp.arange(length, dtype=jnp.int32)

    inputs = tokens.astype(f32)
    _, first_pull = jax.vjp(rms_scale, inputs, gain_one)
    hidden_one_columns = own_columns(hidden_one, shard_group)
    projected = jnp.dot(hidden_one, qkv_full, preferred_element_type=f32)
    cosine, sine_table = rotary_tables(length)

    def query_key_local(raw_query, raw_key, query_gain, key_gain):
        return query_key(raw_query, raw_key, query_gain, key_gain, cosine, sine_table)

    rotated, rotary_pull = jax.vjp(
        query_key_local,
        projected[:, :model_width],
        projected[:, model_width : 2 * model_width],
        gain_query,
        gain_key,
    )
    query_low = rotated[0].astype(bf16)
    key_low = rotated[1].astype(bf16)
    value_low = projected[:, 2 * model_width :].astype(bf16).reshape(length, HEADS, HEAD_DIM)
    allowed = (position[:, None] >= position[None, :]) & (
        segments[0][:, None] == segments[0][None, :]
    )
    masked = jnp.where(
        allowed[None],
        jnp.einsum("qhd,khd->hqk", query_low, key_low, preferred_element_type=f32) * score_scale,
        -1e30,
    )
    probs = softmax_rows(masked)
    probs_low = probs.astype(bf16)
    attended_low = (
        jnp.einsum("hqk,khd->qhd", probs_low, value_low, preferred_element_type=f32)
        .reshape(length, model_width)
        .astype(bf16)
    )
    attended_columns = own_columns(attended_low, shard_group)
    middle = inputs + jnp.dot(attended_low, out_full, preferred_element_type=f32)
    scaled_two, second_pull = jax.vjp(rms_scale, middle, gain_two)
    hidden_two = scaled_two.astype(bf16)
    router = softmax_rows(jnp.dot(hidden_two, router_full, preferred_element_type=f32))
    row_count = expert_group * capacity
    done, mixture_parts = moe_layer(
        hidden_two,
        upstream_all,
        place_own,
        router_full,
        gate_up_weight,
        down_weight,
        expert_group,
        capacity,
        2,
    )
    expert_rows, activated, grad_expert, grad_gate_up_low = (
        a.reshape(local_experts, row_count, a.shape[-1]) for a in done[:4]
    )
    grad_rows_sum = done[4]
    grad_router = done[5][:, :local_experts].reshape(experts_all, length).T
    upstream = cotangent.astype(f32)
    grad_logits = (
        router * (grad_router - jnp.sum(router * grad_router, axis=-1, keepdims=True))
    ).astype(bf16)
    grad_hidden_two = grad_rows_sum + jnp.einsum(
        "te,de->td", grad_logits, router_full, preferred_element_type=f32
    )
    grad_middle_norm, grad_gain_two = second_pull(grad_hidden_two)
    grad_middle = upstream + grad_middle_norm
    grad_branch_low = grad_middle.astype(bf16)
    grad_attended_low = (
        jnp.einsum("te,de->td", grad_branch_low, out_full, preferred_element_type=f32)
        .astype(bf16)
        .reshape(length, HEADS, HEAD_DIM)
    )
    mixture_two = sum_over_x(mixture_parts, 2, expert_group)
    grad_attended_low, expert_rows, activated, grad_expert, grad_gate_up_low, mixture_two = (
        lax.optimization_barrier(
            (
                grad_attended_low,
                expert_rows,
                activated,
                grad_expert,
                grad_gate_up_low,
                mixture_two,
            )
        )
    )
    mixture_two = back_along_z(mixture_two, 2, expert_group)
    mixture_one = sum_over_x(mixture_parts, 1, expert_group)
    mixture_three = sum_over_x(mixture_parts, 3, expert_group)
    grad_down_full = jnp.einsum("erf,erd->efd", activated, grad_expert, preferred_element_type=f32)
    grad_gate_up_full = jnp.einsum(
        "erd,erf->edf", expert_rows, grad_gate_up_low, preferred_element_type=f32
    )
    (
        grad_gate_up_full,
        grad_down_full,
        grad_attended_low,
        mixture_one,
        mixture_two,
        mixture_three,
    ) = lax.optimization_barrier(
        (
            grad_gate_up_full.astype(bf16),
            grad_down_full.astype(bf16),
            grad_attended_low,
            mixture_one,
            mixture_two,
            mixture_three,
        )
    )
    mixture_one = back_along_z(mixture_one, 1, expert_group)
    mixture_three = back_along_z(mixture_three, 3, expert_group)
    mixture_own = sum_over_x(mixture_parts, 0, expert_group)
    grad_gate_up_weight = lax.psum_scatter(
        grad_gate_up_full, "shard", scatter_dimension=1, tiled=True
    ).astype(f32)
    grad_down_weight = lax.psum_scatter(
        grad_down_full, "shard", scatter_dimension=2, tiled=True
    ).astype(f32)

    grad_probs = jnp.einsum(
        "qhd,khd->hqk", grad_attended_low, value_low, preferred_element_type=f32
    )
    grad_scores_low = (
        probs * (grad_probs - jnp.sum(probs * grad_probs, axis=-1, keepdims=True))
    ).astype(bf16)
    grad_scores_low, mixture_own, mixture_one = lax.optimization_barrier(
        (grad_scores_low, mixture_own, mixture_one)
    )
    grad_queries = (
        jnp.einsum("hqk,khd->qhd", grad_scores_low, key_low, preferred_element_type=f32)
        * score_scale
    )
    grad_keys = (
        jnp.einsum("hqk,qhd->khd", grad_scores_low, query_low, preferred_element_type=f32)
        * score_scale
    )
    grad_values = jnp.einsum(
        "hqk,qhd->khd", probs_low, grad_attended_low, preferred_element_type=f32
    )
    grad_raw_query, grad_raw_key, grad_gain_query, grad_gain_key = rotary_pull(
        (grad_queries, grad_keys)
    )
    grad_projected_low = jnp.concatenate(
        [grad_raw_query, grad_raw_key, grad_values.reshape(length, model_width)], axis=-1
    ).astype(bf16)
    grad_hidden_one = jnp.einsum(
        "te,de->td", grad_projected_low, qkv_full, preferred_element_type=f32
    )
    grad_inputs_norm, grad_gain_one = first_pull(grad_hidden_one)
    grad_tokens = grad_middle + grad_inputs_norm

    grad_router_part = jnp.einsum("td,te->ed", hidden_two, grad_logits, preferred_element_type=f32)
    small = jnp.concatenate(
        [
            grad_router_part,
            jnp.stack([grad_gain_one, grad_gain_query, grad_gain_key, grad_gain_two]),
            jnp.zeros((-(experts_all + 4) % 8, model_width), f32),
        ],
        axis=0,
    )
    keep = norm_one.shape[0]
    small = jnp.stack(
        [
            lax.dynamic_slice_in_dim(
                small,
                (((own_shard // 2 + dy) % (shard_group // 2)) * 2 + (own_shard % 2 + flip) % 2) * keep,
                keep,
                axis=1,
            )
            for dy in range(shard_group // 2)
            for flip in range(2)
        ]
    )

    grads_low = jnp.concatenate([grad_branch_low, grad_projected_low], axis=1)
    grads_low, mixture_three = lax.optimization_barrier((grads_low, mixture_three))
    mixture = mixture_own + mixture_one + mixture_two + mixture_three
    block_out = (middle + mixture).astype(bf16)
    columns = jnp.stack([attended_columns.T, hidden_one_columns.T])
    grad_rows_kept, small = summed_rows(
        columns, grads_low, model_width, small, expert_group, shard_group, z_all, 256, 2, 1
    )
    grad_out_weight = grad_rows_kept[:, :model_width].astype(f32)
    grad_qkv_weight = grad_rows_kept[:, model_width:].astype(f32)
    return (
        block_out,
        grad_tokens,
        small[experts_all],
        small[experts_all + 1],
        small[experts_all + 2],
        small[experts_all + 3],
        grad_qkv_weight,
        grad_out_weight,
        small[:experts_all].T,
        grad_gate_up_weight,
        grad_down_weight,
    )


def solution(mesh):
    return jax.shard_map(
        body,
        mesh=mesh,
        in_specs=(
            P(("expert", "shard"), None),
            P(("expert", "shard"), None),
            P(("expert", "shard"), None),
            P(("expert", "shard"), None),
            P(),
            P("shard"),
            P("shard"),
            P("shard"),
            P("shard"),
            P("shard", None),
            P("shard", None),
            P("shard", None),
            P("expert", None, None),
            P("expert", None, None),
        ),
        out_specs=(
            P(("expert", "shard"), None),
            P(("expert", "shard"), None),
            P("shard"),
            P("shard"),
            P("shard"),
            P("shard"),
            P("shard", None),
            P("shard", None),
            P("shard", None),
            P("expert", "shard", None),
            P("expert", None, "shard"),
        ),
        check_vma=False,
    )
```

```python
import functools

import jax
import jax.numpy as jnp
from jax import lax
from jax.experimental import pallas as pl
from jax.experimental.pallas import tpu as pltpu
from jax.sharding import PartitionSpec as P

HEADS = 16
HEAD_DIM = 128
TOP = 8
TILE = 8


epsilon = 1e-05
rope_base = 10000.0


def rms_scale(values, scale_gain):
    return (
        values * lax.rsqrt(jnp.mean(values * values, axis=-1, keepdims=True) + epsilon) * scale_gain
    )


def rotary_tables(length):
    half_dim = HEAD_DIM // 2
    position = jnp.arange(length, dtype=jnp.float32)[:, None]
    frequency = rope_base ** (-jnp.arange(half_dim, dtype=jnp.float32) * 2.0 / HEAD_DIM)
    angles = position * frequency[None, :]
    angles = jnp.concatenate([angles, angles], axis=-1)
    return (jnp.cos(angles)[:, None, :], jnp.sin(angles)[:, None, :])


def rotate(vectors, cosine, sine_table):
    half_dim = vectors.shape[-1] // 2
    turned = jnp.concatenate([-vectors[..., half_dim:], vectors[..., :half_dim]], axis=-1)
    return vectors * cosine + turned * sine_table


def query_key(raw_query, raw_key, query_gain, key_gain, cosine, sine_table):
    length = raw_query.shape[0]
    queries = rms_scale(raw_query, query_gain).reshape(length, HEADS, HEAD_DIM)
    keys_rot = rms_scale(raw_key, key_gain).reshape(length, HEADS, HEAD_DIM)
    return (rotate(queries, cosine, sine_table), rotate(keys_rot, cosine, sine_table))


def swiglu(gate_up):
    half_dim = gate_up.shape[-1] // 2
    gate_part = gate_up[..., :half_dim]
    return gate_part / (1.0 + jnp.exp(-gate_part)) * gate_up[..., half_dim:]


def softmax_rows(logits):
    largest = jnp.max(logits, axis=-1, keepdims=True)
    raised = jnp.exp(logits - largest)
    return raised / jnp.sum(raised, axis=-1, keepdims=True)


def z_size(expert_group):
    return 4 if expert_group % 4 == 0 else 1


def shift(values, expert_group, dz, dx):
    z_all = z_size(expert_group)
    x_all = expert_group // z_all
    pairs = [
        (i, ((i // x_all + dz) % z_all) * x_all + (i % x_all + dx) % x_all)
        for i in range(expert_group)
    ]
    return lax.ppermute(values, "expert", pairs)


def gather_expert(block, expert_group):
    z_all = z_size(expert_group)
    x_all = expert_group // z_all
    rows = [block] + [shift(block, expert_group, dz, 0) for dz in range(1, z_all)]
    return [
        rows[dz] if dx == 0 else shift(rows[dz], expert_group, 0, dx)
        for dz in range(z_all)
        for dx in range(x_all)
    ]


def sum_over_x(parts, dz, expert_group):
    x_all = expert_group // z_size(expert_group)
    total = parts[dz * x_all].astype(jnp.float32)
    for dx in range(1, x_all):
        total = total + shift(parts[dz * x_all + dx], expert_group, 0, -dx).astype(jnp.float32)
    return total


def back_along_z(total, dz, expert_group):
    if dz == 0:
        return total
    return shift(total.astype(jnp.bfloat16), expert_group, -dz, 0).astype(jnp.float32)


def tail_kernel(
    dims, grads_ref, columns_ref, small_ref, out_ref, small_out_ref,
    gall, xsend, xrecv, zsend, zrecv, acc, fin, group_small, own_small, all_small, *sems
):
    steps, width, x_all, z_all, y_all, lag, first_steps = dims
    (gs_s, gs_r, es_s, es_r) = sems[14:]
    (y_s, y_r, core_s, core_r, fwd_s, fwd_r, x_s, x_r, z_s, z_r, zb_s, zb_r, xb_s, xb_r) = sems[:14]
    f32, bf16 = jnp.float32, jnp.bfloat16
    length = grads_ref.shape[0]
    rows = columns_ref.shape[1]
    block = rows // (x_all * z_all)
    half = z_all * block
    e = lax.axis_index("expert")
    s = lax.axis_index("shard")
    z, x = e // x_all, lax.rem(e, x_all)
    y, core = s // 2, lax.rem(s, 2)

    def y_peer(d):
        return {"shard": lax.rem(y + d, y_all) * 2 + core}

    partner = {"shard": y * 2 + (1 - core)}

    def x_peer(d):
        return {"expert": z * x_all + lax.rem(x + d, x_all)}

    def z_peer(d):
        return {"expert": lax.rem(z + d, z_all) * x_all + x}

    def copy(src, dst, send, recv, peer):
        return pltpu.make_async_remote_copy(
            src_ref=src, dst_ref=dst, send_sem=send, recv_sem=recv, device_id=peer,
            device_id_type=pl.DeviceIdType.MESH,
        )

    def cols(c):
        return pl.ds(pl.multiple_of(c * width, width), width)

    def y_copy(d, c):
        return copy(grads_ref.at[:, cols(c)], gall.at[2 * d - 1, c], y_s.at[d - 1], y_r.at[d - 1, c], y_peer(d))

    def core_copy(c):
        return copy(grads_ref.at[:, cols(c)], gall.at[0, c], core_s.at[0], core_r.at[c], partner)

    def fwd_copy(d, c):
        return copy(gall.at[2 * d - 1, c], gall.at[2 * d, c], fwd_s.at[d - 1], fwd_r.at[d - 1, c], partner)

    def x_copy(d, c):
        return copy(xsend.at[d - 1, c], xrecv.at[d - 1, c], x_s.at[d - 1], x_r.at[d - 1, c], x_peer(d))

    def z_copy(d, c):
        return copy(zsend.at[d - 1, c], zrecv.at[d - 1, c], z_s.at[d - 1], z_r.at[d - 1, c], z_peer(d))

    def zb_copy(d, c):
        here = fin.at[c, pl.ds(pl.multiple_of((x * z_all + z) * block, block), block)]
        return copy(here, here, zb_s.at[d - 1], zb_r.at[d - 1, c], z_peer(d))

    def xb_copy(d, c):
        here = fin.at[c, pl.ds(pl.multiple_of(x * half, half), half)]
        return copy(here, here, xb_s.at[d - 1], xb_r.at[d - 1, c], x_peer(d))

    near = [(d, flip) for d in range(y_all) for flip in range(2) if d + flip > 0]
    far = [(dz, dx) for dz in range(z_all) for dx in range(x_all) if dz + dx > 0]

    def near_peer(d, flip):
        return {"shard": lax.rem(y + d, y_all) * 2 + lax.rem(core + flip, 2)}

    def far_peer(dz, dx):
        return {"expert": lax.rem(z + dz, z_all) * x_all + lax.rem(x + dx, x_all)}

    def near_small(d, flip):
        j = 2 * d + flip
        return copy(small_ref.at[j], group_small.at[j - 1], gs_s.at[j - 1], gs_r.at[j - 1], near_peer(d, flip))

    def far_small(dz, dx):
        i = dz * x_all + dx
        return copy(own_small, all_small.at[i - 1], es_s.at[i - 1], es_r.at[i - 1], far_peer(dz, dx))

    barrier = pltpu.get_barrier_semaphore()
    peers = [near_peer(*p) for p in near] + [far_peer(*p) for p in far]
    for peer in peers:
        pl.semaphore_signal(barrier, inc=1, device_id=peer, device_id_type=pl.DeviceIdType.MESH)
    pl.semaphore_wait(barrier, len(peers))

    for p in near:
        near_small(*p).start()

    def first(c, carry):
        for d in range(1, y_all):
            y_copy(d, c).start()
        core_copy(c).start()
        return carry

    lax.fori_loop(0, steps, first, 0)
    slots = acc.shape[0]

    def step(t, carry):
        def stage(k, body):
            c = t - k * lag
            pl.when((c >= 0) & (c < steps))(lambda: body(c))

        @functools.partial(stage, 5)
        def _(c):
            for d in range(1, x_all):
                xb_copy(d, c).wait_recv()
            out_ref[:, cols(c)] = fin[c]

        @functools.partial(stage, 4)
        def _(c):
            for d in range(1, z_all):
                zb_copy(d, c).wait_recv()
            for d in range(1, x_all):
                xb_copy(d, c).start()

        @functools.partial(stage, 3)
        def _(c):
            slot = lax.rem(c, slots)
            total = acc[slot, pl.ds(pl.multiple_of(z * block, block), block), :]
            for d in range(1, z_all):
                z_copy(d, c).wait_recv()
                total = total + zrecv[d - 1, c].astype(f32)
            fin[c, pl.ds(pl.multiple_of((x * z_all + z) * block, block), block), :] = total.astype(bf16)
            for d in range(1, z_all):
                zb_copy(d, c).start()

        @functools.partial(stage, 2)
        def _(c):
            slot = lax.rem(c, slots)
            total = acc[slot]
            for d in range(1, x_all):
                x_copy(d, c).wait_recv()
                total = total + xrecv[d - 1, c].astype(f32)
            acc[slot] = total
            for d in range(1, z_all):
                there = lax.rem(z + d, z_all)
                zsend[d - 1, c] = acc[slot, pl.ds(pl.multiple_of(there * block, block), block), :].astype(bf16)
                z_copy(d, c).start()

        @functools.partial(stage, 1)
        def _(c):
            core_copy(c).wait_recv()
            for d in range(1, y_all):
                fwd_copy(d, c).wait_recv()
            kind = (c >= first_steps).astype(jnp.int32)
            others = gall[:, c].reshape((2 * y_all - 1) * length, width)
            mine = grads_ref[:, cols(c)]

            def product(there):
                at = pl.ds(pl.multiple_of(there * half, half), half)
                return jnp.dot(columns_ref[kind, at, :length], mine, preferred_element_type=f32) + jnp.dot(
                    columns_ref[kind, at, length:], others, preferred_element_type=f32
                )

            for d in range(1, x_all):
                xsend[d - 1, c] = product(lax.rem(x + d, x_all)).astype(bf16)
                x_copy(d, c).start()
            acc[lax.rem(c, slots)] = product(x)

        @functools.partial(stage, 0)
        def _(c):
            for d in range(1, y_all):
                y_copy(d, c).wait_recv()
                fwd_copy(d, c).start()

        @pl.when(t == 2)
        def _():
            total = small_ref[0]
            for j, p in enumerate(near):
                near_small(*p).wait_recv()
                total = total + group_small[j]
            own_small[...] = total
            for p in far:
                far_small(*p).start()

        return carry

    lax.fori_loop(0, steps + 5 * lag, step, 0)
    total = own_small[...]
    for i, p in enumerate(far):
        far_small(*p).wait_recv()
        total = total + all_small[i]
    small_out_ref[...] = total
    for p in near:
        near_small(*p).wait_send()
    for p in far:
        far_small(*p).wait_send()

    for d in range(1, y_all):
        copy(grads_ref, grads_ref, y_s.at[d - 1], y_r.at[d - 1, 0], y_peer(d)).wait_send()
        whole = gall.at[2 * d - 1]
        copy(whole, whole, fwd_s.at[d - 1], fwd_r.at[d - 1, 0], partner).wait_send()
    copy(grads_ref, grads_ref, core_s.at[0], core_r.at[0], partner).wait_send()
    for d in range(1, x_all):
        whole = xsend.at[d - 1]
        copy(whole, whole, x_s.at[d - 1], x_r.at[d - 1, 0], x_peer(d)).wait_send()
        copy(whole, whole, xb_s.at[d - 1], xb_r.at[d - 1, 0], x_peer(d)).wait_send()
    for d in range(1, z_all):
        whole = zsend.at[d - 1]
        copy(whole, whole, z_s.at[d - 1], z_r.at[d - 1, 0], z_peer(d)).wait_send()
        copy(whole, whole, zb_s.at[d - 1], zb_r.at[d - 1, 0], z_peer(d)).wait_send()


def summed_rows(columns, grads, first_total, small, expert_group, shard_group, z_all, width, lag, name_id):
    x_all, y_all = expert_group // z_all, shard_group // 2
    length, total = grads.shape
    rows = columns.shape[1]
    steps = total // width
    block = rows // expert_group
    half = z_all * block
    bf16 = jnp.bfloat16
    dma = pltpu.SemaphoreType.DMA
    n1 = max(y_all - 1, 1)
    x1 = max(x_all - 1, 1)
    z1 = max(z_all - 1, 1)
    slots = min(steps, 2 * lag + 1)
    return pl.pallas_call(
        functools.partial(tail_kernel, (steps, width, x_all, z_all, y_all, lag, first_total // width)),
        out_shape=[
            jax.ShapeDtypeStruct((rows, total), bf16),
            jax.ShapeDtypeStruct(small.shape[1:], jnp.float32),
        ],
        in_specs=[pl.BlockSpec(memory_space=pltpu.VMEM)] * 3,
        out_specs=[pl.BlockSpec(memory_space=pltpu.VMEM)] * 2,
        scratch_shapes=[
            pltpu.VMEM((shard_group - 1, steps, length, width), bf16),
            pltpu.VMEM((x1, steps, half, width), bf16),
            pltpu.VMEM((x1, steps, half, width), bf16),
            pltpu.VMEM((z1, steps, block, width), bf16),
            pltpu.VMEM((z1, steps, block, width), bf16),
            pltpu.VMEM((slots, half, width), jnp.float32),
            pltpu.VMEM((steps, rows, width), bf16),
            pltpu.VMEM((shard_group - 1, *small.shape[1:]), jnp.float32),
            pltpu.VMEM(small.shape[1:], jnp.float32),
            pltpu.VMEM((expert_group - 1, *small.shape[1:]), jnp.float32),
            dma((n1,)), dma((n1, steps)),
            dma((1,)), dma((steps,)),
            dma((n1,)), dma((n1, steps)),
            dma((x1,)), dma((x1, steps)),
            dma((z1,)), dma((z1, steps)),
            dma((z1,)), dma((z1, steps)),
            dma((x1,)), dma((x1, steps)),
            dma((shard_group - 1,)), dma((shard_group - 1,)),
            dma((expert_group - 1,)), dma((expert_group - 1,)),
        ],
        compiler_params=pltpu.CompilerParams(
            collective_id=name_id, has_side_effects=True, vmem_limit_bytes=60 * 1024 * 1024
        ),
        cost_estimate=pl.CostEstimate(
            flops=2 * rows * length * shard_group * total, bytes_accessed=16 * 1024 * 1024, transcendentals=0
        ),
    )(grads, columns, small)


MOE_CHUNKS = 4


def moe_kernel(
    dims, hidden_hbm, upstream_hbm, place_ref, place_t_ref, router_ref, router_t_ref, gate_up_hbm, down_hbm,
    first_hbm, second_hbm, rows_hbm, activated_hbm, grad_out_hbm, grad_gate_up_hbm, grad_ref, grad_router_ref, columns_hbm, found_hbm, summed_hbm,
    *rest,
):
    x_all, capacity, y_all = dims
    mixture_hbm = rest[: 4 * x_all]
    (
    gate_up_w, down_w, hid, ups, prob, prob_t, rows, gate_up, activated, out_rows, grad_expert, grad_gate_up, grad_rows,
    mix_stage, part_stage, own_part, z_landed, router_stage,
    w_sem, own_sem, load_sem, store_sem, zs, zr, xs, xr, fs, fr, ps, pr, qs, qr, rs, rr, lsem, mix_sem, cs, cr, own_c,
    ) = rest[4 * x_all :]
    z_all = 4
    f32, bf16 = jnp.float32, jnp.bfloat16
    length, width = hidden_hbm.shape
    local_experts, _, twice = gate_up_w.shape
    half = twice // 2
    tile = min(512, half)
    narrow = min(256, half)
    chunk = length // MOE_CHUNKS
    e = lax.axis_index("expert")
    z, x = e // x_all, lax.rem(e, x_all)

    def peer(dz, dx):
        return {"expert": lax.rem(z + dz + 4 * z_all, z_all) * x_all + lax.rem(x + dx + 4 * x_all, x_all)}

    def copy(src, dst, send, recv, to):
        return pltpu.make_async_remote_copy(
            src_ref=src, dst_ref=dst, send_sem=send, recv_sem=recv, device_id=to,
            device_id_type=pl.DeviceIdType.MESH,
        )

    def at(c):
        return pl.ds(pl.multiple_of(c * chunk, chunk), chunk)

    def z_copy(d, c):
        return copy(hidden_hbm.at[at(c)], found_hbm.at[d, 0, at(c)], zs.at[d - 1, c], zr.at[d - 1, c], peer(d, 0))

    def x_copy(d, c):
        return copy(hidden_hbm.at[at(c)], found_hbm.at[0, d, at(c)], xs.at[d - 1, c], xr.at[d - 1, c], peer(0, d))

    def f_copy(dz, dx, c):
        return copy(
            found_hbm.at[dz, 0, at(c)], found_hbm.at[dz, dx, at(c)],
            fs.at[dz - 1, dx - 1, c], fr.at[dz - 1, dx - 1, c], peer(0, dx),
        )

    def p_copy(dz, dx, c):
        return copy(
            part_stage.at[dx - 1, at(c)], summed_hbm.at[dz, dx - 1, at(c)],
            ps.at[dx - 1], pr.at[dz, dx - 1, c], peer(0, -dx),
        )

    def p_sent(dx):
        whole = part_stage.at[dx - 1]
        copy(whole, whole, ps.at[dx - 1], pr.at[0, dx - 1, 0], peer(0, -dx)).wait_send()

    def q_copy(dz, c):
        return copy(
            own_part.at[dz, at(c)], z_landed.at[dz - 1, at(c)], qs.at[dz - 1], qr.at[dz - 1, c], peer(-dz, 0)
        )

    def r_copy(dz, dx):
        return copy(
            router_stage.at[dz, dx], grad_router_ref.at[e], rs.at[dz, dx], rr.at[dz, dx], peer(-dz, -dx)
        )

    def cols(n, w):
        return pl.ds(pl.multiple_of(n * w, w), w)

    barrier = pltpu.get_barrier_semaphore()
    others = [(dz, dx) for dz in range(z_all) for dx in range(x_all) if dz + dx > 0]
    near = [(dy, flip) for dy in range(y_all) for flip in range(2) if dy + flip > 0]
    shard = lax.axis_index("shard")

    def near_at(dy, flip):
        return lax.rem(shard // 2 + dy, y_all) * 2 + lax.rem(lax.rem(shard, 2) + flip, 2)

    for dz, dx in others:
        pl.semaphore_signal(barrier, inc=1, device_id=peer(dz, dx), device_id_type=pl.DeviceIdType.MESH)
    for dy, flip in near:
        pl.semaphore_signal(
            barrier, inc=1, device_id={"shard": near_at(dy, flip)}, device_id_type=pl.DeviceIdType.MESH
        )
    pl.semaphore_wait(barrier, len(others) + len(near))

    keep = columns_hbm.shape[3]

    def column_copy(kind, source, dy, flip):
        j = 2 * dy + flip
        there = near_at(dy, flip)
        src = source.at[:, pl.ds(pl.multiple_of(there * keep, keep), keep)]
        if j == 0:
            return pltpu.make_async_copy(src, columns_hbm.at[kind, 0], own_c.at[kind])
        return copy(src, columns_hbm.at[kind, j], cs.at[kind, j - 1], cr.at[kind, j - 1], {"shard": there})

    column_copies = [
        column_copy(kind, source, dy, flip)
        for kind, source in enumerate((first_hbm, second_hbm))
        for dy, flip in [(0, 0)] + near
    ]
    for c in column_copies:
        c.start()

    own = pltpu.make_async_copy(hidden_hbm, found_hbm.at[0, 0], own_sem)
    own.start()
    weights = [
        pltpu.make_async_copy(gate_up_hbm, gate_up_w, w_sem.at[0]),
        pltpu.make_async_copy(down_hbm, down_w, w_sem.at[1]),
    ]
    for w in weights:
        w.start()

    def send_own(c, carry):
        for d in range(1, x_all):
            x_copy(d, c).start()
        return carry

    lax.fori_loop(0, MOE_CHUNKS, send_own, 0)
    for d in (1, 3, 2):

        def send_z(c, carry):
            z_copy(d, c).start()
            return carry

        lax.fori_loop(0, MOE_CHUNKS, send_z, 0)

    def events(first, last):
        def one(k, carry):
            @pl.when(k < last)
            def _():
                j = k // MOE_CHUNKS
                c = lax.rem(k, MOE_CHUNKS)
                d = 1 + 2 * j - 3 * (j // 2)
                z_copy(d, c).wait_recv()
                for dx in range(1, x_all):
                    f_copy(d, dx, c).start()

            return carry

        lax.fori_loop(first, first + MOE_CHUNKS, one, 0)

    def own_slots(le):
        return pl.ds(pl.multiple_of(le * capacity, capacity), capacity)

    def finish(dz, last):
        def load(c):
            return pltpu.make_async_copy(summed_hbm.at[dz, dx - 1, at(c)], hid.at[0, at(c)], lsem.at[c])

        def add(c):
            load(c).wait()
            own_part[dz, at(c), :] = (
                own_part[dz, at(c), :].astype(f32) + hid[0, at(c), :].astype(f32)
            ).astype(bf16)
            if dx == x_all - 1:
                pl.when(dz > 0)(lambda: q_copy(dz, c).start())

        def arrive(c, carry):
            p_copy(dz, dx, c).wait_recv()
            load(c).start()
            if last:
                add(c)
            return carry

        def rest(c, carry):
            add(c)
            return carry

        for dx in range(1, x_all):
            lax.fori_loop(0, MOE_CHUNKS, arrive, 0)
            if not last:
                lax.fori_loop(0, MOE_CHUNKS, rest, 0)

    mix_slots = mix_stage.shape[0]

    def mix_copy(dz, dx):
        slot = dx % mix_slots
        return pltpu.make_async_copy(mix_stage.at[slot], mixture_hbm[dz * x_all + dx], mix_sem.at[slot])

    slot_row = lax.broadcasted_iota(jnp.int32, (capacity, length), 0).astype(f32)
    slot_col = lax.broadcasted_iota(jnp.int32, (length, local_experts * capacity), 1).astype(f32)
    own.wait()
    events(0, 4)

    def load_upstream(dz):
        return [pltpu.make_async_copy(upstream_hbm.at[dz, dx], ups.at[dx], load_sem.at[1, dx]) for dx in range(x_all)]

    for load in load_upstream(0):
        load.start()

    def group(dz, carry):
        g = dz

        def arrive(c, inner):
            for dx in range(1, x_all):

                @pl.when(dz == 0)
                def _():
                    x_copy(dx, c).wait_recv()

                @pl.when(dz > 0)
                def _():
                    f_copy(dz, dx, c).wait_recv()

            return inner

        lax.fori_loop(0, MOE_CHUNKS, arrive, 0)
        loads = []
        for dx in range(x_all):
            loads.append(pltpu.make_async_copy(found_hbm.at[dz, dx], hid.at[dx], load_sem.at[0, dx]))
        for load in loads:
            load.start()
        for load in loads + load_upstream(dz):
            load.wait()
        pl.when(g == 0)(lambda: [w.wait() for w in weights] and None)

        for dx in range(x_all):
            logits = jnp.dot(hid[dx], router_ref[...], preferred_element_type=f32)
            raised = jnp.exp(logits - jnp.max(logits, axis=1, keepdims=True))
            prob[dx] = raised / jnp.sum(raised, axis=1, keepdims=True)
            logits = lax.dot_general(
                router_t_ref[...], hid[dx], (((1,), (1,)), ((), ())), preferred_element_type=f32
            )
            raised = jnp.exp(logits - jnp.max(logits, axis=0, keepdims=True))
            prob_t[dx] = raised / jnp.sum(raised, axis=0, keepdims=True)
            router_stage[dz, dx] = jnp.zeros(router_stage.shape[2:], f32)

        def store(kind, buffer, hbm, le):
            return pltpu.make_async_copy(buffer, hbm.at[le, dz], store_sem.at[kind])

        def expert(le, inner):
            @pl.when(g + le > 0)
            def _():
                store(0, rows, rows_hbm, le).wait()
                store(1, activated, activated_hbm, le).wait()
                store(2, grad_expert, grad_out_hbm, le).wait()
                store(3, grad_gate_up, grad_gate_up_hbm, le).wait()

            chosen = [place_ref[dz, dx, pl.ds(le, 1), :] == slot_row for dx in range(x_all)]
            chosen_low = [c.astype(f32).astype(bf16) for c in chosen]

            def dispatch(n, c0):
                c = cols(n, tile)
                for dx in range(x_all):
                    rows[dx * capacity : (dx + 1) * capacity, c] = jnp.dot(
                        chosen_low[dx], hid[dx, :, c], preferred_element_type=f32
                    ).astype(bf16)
                return c0

            lax.fori_loop(0, width // tile, dispatch, 0, unroll=True)
            store(0, rows, rows_hbm, le).start()

            def up_step(n, c0):
                c = cols(n, tile)
                gate_up[:, c] = jnp.dot(rows[...], gate_up_w[le, :, c], preferred_element_type=f32)
                return c0

            lax.fori_loop(0, twice // tile, up_step, 0, unroll=True)

            def act_step(n, c0):
                gate = gate_up[:, cols(n, narrow)]
                up = gate_up[:, pl.ds(pl.multiple_of(half + n * narrow, narrow), narrow)]
                activated[:, cols(n, narrow)] = (gate / (1.0 + jnp.exp(-gate)) * up).astype(bf16)
                return c0

            lax.fori_loop(0, half // narrow, act_step, 0, unroll=True)
            store(1, activated, activated_hbm, le).start()

            def down_step(n, c0):
                c = cols(n, tile)
                result = jnp.dot(activated[...], down_w[le, :, c], preferred_element_type=f32)
                for dx in range(x_all):
                    r = slice(dx * capacity, (dx + 1) * capacity)
                    out_rows[dx, own_slots(le), c] = result[r].astype(bf16)
                return c0

            lax.fori_loop(0, width // tile, down_step, 0, unroll=True)

            mine = e * local_experts + le
            weight_rows = [
                jnp.sum(jnp.where(chosen[dx], prob_t[dx, pl.ds(mine, 1), :], 0.0), axis=1, keepdims=True)
                for dx in range(x_all)
            ]

            def grad_step(n, totals):
                c = cols(n, tile)
                new = []
                for dx in range(x_all):
                    r = slice(dx * capacity, (dx + 1) * capacity)
                    up_rows = jnp.dot(chosen_low[dx], ups[dx, :, c], preferred_element_type=f32)
                    grad_expert[r, c] = (weight_rows[dx] * up_rows).astype(bf16)
                    new.append(
                        totals[dx]
                        + jnp.sum(up_rows * out_rows[dx, own_slots(le), c].astype(f32), axis=1, keepdims=True)
                    )
                return tuple(new)

            totals = lax.fori_loop(
                0, width // tile, grad_step, tuple(jnp.zeros((capacity, 1), f32) for _ in range(x_all)),
                unroll=True,
            )
            store(2, grad_expert, grad_out_hbm, le).start()
            for dx in range(x_all):
                router_stage[dz, dx, pl.ds(le, 1), :] = jnp.sum(
                    jnp.where(chosen[dx], totals[dx], 0.0), axis=0, keepdims=True
                )

            def back_step(n, c0):
                ga = lax.dot_general(
                    grad_expert[...], down_w[le, cols(n, narrow), :], (((1,), (1,)), ((), ())),
                    preferred_element_type=f32,
                )
                gate = gate_up[:, cols(n, narrow)]
                c_up = pl.ds(pl.multiple_of(half + n * narrow, narrow), narrow)
                up = gate_up[:, c_up]
                sg = 1.0 / (1.0 + jnp.exp(-gate))
                grad_gate_up[:, cols(n, narrow)] = (ga * up * sg * (1.0 + gate * (1.0 - sg))).astype(bf16)
                grad_gate_up[:, c_up] = (ga * (gate * sg)).astype(bf16)
                return c0

            lax.fori_loop(0, half // narrow, back_step, 0, unroll=True)
            store(3, grad_gate_up, grad_gate_up_hbm, le).start()

            def row_step(n, c0):
                result = lax.dot_general(
                    grad_gate_up[...], gate_up_w[le, cols(n, narrow), :], (((1,), (1,)), ((), ())),
                    preferred_element_type=f32,
                )
                for dx in range(x_all):
                    r = slice(dx * capacity, (dx + 1) * capacity)
                    grad_rows[dx, own_slots(le), cols(n, narrow)] = result[r].astype(bf16)
                return c0

            lax.fori_loop(0, width // narrow, row_step, 0, unroll=True)
            k = 2 * g + le
            events(
                jnp.where(k == 0, 4, jnp.where(k == 1, 7, jnp.where(k == 2, 9, 11))),
                jnp.where(k == 0, 7, jnp.where(k == 1, 9, jnp.where(k == 2, 11, jnp.where(k == 3, 12, 0)))),
            )
            return inner

        assert local_experts == 2
        lax.fori_loop(0, local_experts, expert, 0)

        @pl.when(g < z_all - 1)
        def _():
            for load in load_upstream(dz + 1):
                load.start()

        def stages():
            for dx in range(1, x_all):
                p_sent(dx)

        pl.when(g > 0)(stages)
        for dx in range(x_all):
            weight = jnp.zeros(slot_col.shape, f32)
            mask = jnp.zeros(slot_col.shape, f32)
            lane = lax.broadcasted_iota(jnp.int32, prob.shape[1:], 1)
            for le in range(local_experts):
                spot = place_t_ref[dz, dx, :, le : le + 1]
                here = jnp.where(spot < 0.0, -1.0, spot + le * capacity) == slot_col
                p = jnp.sum(jnp.where(lane == e * local_experts + le, prob[dx], 0.0), axis=1, keepdims=True)
                weight = jnp.where(here, p, weight)
                mask = jnp.where(here, 1.0, mask)
            low = mask.astype(bf16)
            high = weight.astype(bf16)
            remainder = (weight - high.astype(f32)).astype(bf16)

            if dx < mix_slots:
                pl.when(g > 0)(mix_copy(0, dx).wait)
            else:
                mix_copy(0, dx).wait()

            def combine(n, c0):
                c = cols(n, tile)
                mix = jnp.dot(high, out_rows[dx, :, c], preferred_element_type=f32) + jnp.dot(
                    remainder, out_rows[dx, :, c], preferred_element_type=f32
                )
                grad = jnp.dot(low, grad_rows[dx, :, c], preferred_element_type=f32)
                mix_stage[dx % mix_slots, :, c] = mix.astype(bf16)
                if dx == 0:
                    own_part[dz, :, c] = grad.astype(bf16)
                else:
                    part_stage[dx - 1, :, c] = grad.astype(bf16)
                return c0

            lax.fori_loop(0, width // tile, combine, 0, unroll=True)
            for k in range(z_all):
                pl.when(dz == k)(mix_copy(k, dx).start)
            if dx > 0:
                for c in range(MOE_CHUNKS):
                    p_copy(dz, dx, c).start()
                r_copy(dz, dx).start()
            else:

                @pl.when(dz > 0)
                def _():
                    r_copy(dz, 0).start()

                @pl.when(dz == 0)
                def _():
                    grad_router_ref[e] = router_stage[0, 0]

        pl.when(g > 0)(lambda: finish(dz - 1, False))
        return carry

    lax.fori_loop(0, z_all, group, 0)
    finish(z_all - 1, True)

    def total(c, carry):
        grad_ref[at(c), :] = own_part[0, at(c), :].astype(f32)
        for d in (1, 2, 3):
            q_copy(d, c).wait_recv()
            grad_ref[at(c), :] = grad_ref[at(c), :] + z_landed[d - 1, at(c), :].astype(f32)
        return carry

    lax.fori_loop(0, MOE_CHUNKS, total, 0)

    for c in column_copies:
        c.wait()
    for kind, buffer, hbm in (
        (0, rows, rows_hbm), (1, activated, activated_hbm), (2, grad_expert, grad_out_hbm),
        (3, grad_gate_up, grad_gate_up_hbm),
    ):
        pltpu.make_async_copy(buffer, hbm.at[0, 0], store_sem.at[kind]).wait()
    for dx in range(mix_slots):
        mix_copy(0, dx).wait()
    for dx in range(1, x_all):
        p_sent(dx)
    for d in range(1, z_all):
        whole = own_part.at[d]
        copy(whole, whole, qs.at[d - 1], qr.at[d - 1, 0], peer(-d, 0)).wait_send()
    for dz, dx in others:
        r_copy(dz, dx).wait_send()
        r_copy(dz, dx).wait_recv()

    def sent(c, carry):
        for d in range(1, z_all):
            z_copy(d, c).wait_send()
            for dx in range(1, x_all):
                f_copy(d, dx, c).wait_send()
        for d in range(1, x_all):
            x_copy(d, c).wait_send()
        return carry

    lax.fori_loop(0, MOE_CHUNKS, sent, 0)


def moe_layer(
    hidden, upstream_all, place, router_weight, gate_up_weight, down_weight, first, second, expert_group, shard_group,
    capacity, name_id,
):
    f32, bf16 = jnp.float32, jnp.bfloat16
    length, width = hidden.shape
    local_experts, _, twice = gate_up_weight.shape
    half = twice // 2
    experts_all = router_weight.shape[1]
    x_all = expert_group // 4
    count = x_all * capacity
    dma = pltpu.SemaphoreType.DMA
    x1 = max(x_all - 1, 1)
    place_t = place.transpose(0, 1, 3, 2)
    spare = (-local_experts) % 8
    place = jnp.pad(place, ((0, 0), (0, 0), (0, spare), (0, 0)), constant_values=-1.0)
    any_spec = pl.BlockSpec(memory_space=pl.ANY)
    vmem_spec = pl.BlockSpec(memory_space=pltpu.VMEM)
    out = pl.pallas_call(
        functools.partial(moe_kernel, (x_all, capacity, shard_group // 2)),
        out_shape=[
            jax.ShapeDtypeStruct((local_experts, 4, count, width), bf16),
            jax.ShapeDtypeStruct((local_experts, 4, count, half), bf16),
            jax.ShapeDtypeStruct((local_experts, 4, count, width), bf16),
            jax.ShapeDtypeStruct((local_experts, 4, count, twice), bf16),
            jax.ShapeDtypeStruct((length, width), f32),
            jax.ShapeDtypeStruct((expert_group, 8, length), f32),
            jax.ShapeDtypeStruct((2, shard_group, length, width // shard_group), bf16),
            jax.ShapeDtypeStruct((4, x_all, length, width), bf16),
            jax.ShapeDtypeStruct((4, x1, length, width), bf16),
        ]
        + [jax.ShapeDtypeStruct((length, width), bf16)] * (4 * x_all),
        in_specs=[any_spec, any_spec, vmem_spec, vmem_spec, vmem_spec, vmem_spec, any_spec, any_spec, any_spec, any_spec],
        out_specs=[any_spec] * 4 + [vmem_spec, vmem_spec] + [any_spec] * (3 + 4 * x_all),
        scratch_shapes=[
            pltpu.VMEM(gate_up_weight.shape, bf16),
            pltpu.VMEM(down_weight.shape, bf16),
            pltpu.VMEM((x_all, length, width), bf16),
            pltpu.VMEM((x_all, length, width), bf16),
            pltpu.VMEM((x_all, length, experts_all), f32),
            pltpu.VMEM((x_all, experts_all, length), f32),
            pltpu.VMEM((count, width), bf16),
            pltpu.VMEM((count, twice), f32),
            pltpu.VMEM((count, half), bf16),
            pltpu.VMEM((x_all, local_experts * capacity, width), bf16),
            pltpu.VMEM((count, width), bf16),
            pltpu.VMEM((count, twice), bf16),
            pltpu.VMEM((x_all, local_experts * capacity, width), bf16),
            pltpu.VMEM((min(2, x_all), length, width), bf16),
            pltpu.VMEM((x1, length, width), bf16),
            pltpu.VMEM((4, length, width), bf16),
            pltpu.VMEM((3, length, width), bf16),
            pltpu.VMEM((4, x_all, 8, length), f32),
            dma((2,)), dma, dma((2, x_all)), dma((4,)),
            dma((3, MOE_CHUNKS)), dma((3, MOE_CHUNKS)),
            dma((x1, MOE_CHUNKS)), dma((x1, MOE_CHUNKS)),
            dma((3, x1, MOE_CHUNKS)), dma((3, x1, MOE_CHUNKS)),
            dma((x1,)), dma((4, x1, MOE_CHUNKS)),
            dma((3,)), dma((3, MOE_CHUNKS)),
            dma((4, x_all)), dma((4, x_all)),
            dma((MOE_CHUNKS,)), dma((min(2, x_all),)),
            dma((2, shard_group - 1)), dma((2, shard_group - 1)), dma((2,)),
        ],
        compiler_params=pltpu.CompilerParams(
            collective_id=name_id, has_side_effects=True, vmem_limit_bytes=62 * 1024 * 1024
        ),
        cost_estimate=pl.CostEstimate(
            flops=12 * 4 * local_experts * count * width * twice, bytes_accessed=64 * 1024 * 1024,
            transcendentals=0,
        ),
    )(
        hidden, upstream_all, place, place_t, router_weight, router_weight.T, gate_up_weight, down_weight,
        first, second,
    )
    return out[:7], out[9:]


def start_kernel(
    dims, weight_hbm, upstream_hbm, router_hbm, gains_ref, tokens_ref, routes_ref, tiles_ref,
    full_hbm, ups_hbm, router_full_hbm, gains_full_ref, place_all_ref, hidden_ref, *sems,
):
    x_all, y_all = dims
    z_all, parts = 4, 4
    (own_sem, ys, yr, rs, rr, cs, cr, fs, fr, gs, gr, zs, zr, xs, xr, us, ur, ns, nr, ps, pr, ms, mr) = sems
    f32, bf16 = jnp.float32, jnp.bfloat16
    rows = weight_hbm.shape[0]
    length = tokens_ref.shape[0]
    piece = rows // 8
    chunk = length // parts
    e = lax.axis_index("expert")
    s = lax.axis_index("shard")
    z, x = e // x_all, lax.rem(e, x_all)
    y, core = s // 2, lax.rem(s, 2)
    parity = lax.rem(z, 2)

    def expert_peer(dz, dx):
        return {"expert": lax.rem(z + dz, z_all) * x_all + lax.rem(x + dx, x_all)}

    def shard_peer(dy, flip):
        return {"shard": lax.rem(y + dy, y_all) * 2 + lax.rem(core + flip, 2)}

    beside = {"expert": (z + 1 - 2 * parity) * x_all + x}
    partner = shard_peer(0, 1)
    far = [(dz, dx) for dz in range(z_all) for dx in range(x_all) if dz + dx > 0]
    near = [(dy, flip) for dy in range(y_all) for flip in range(2) if dy + flip > 0]

    def copy(src, dst, send, recv, to):
        return pltpu.make_async_remote_copy(
            src_ref=src, dst_ref=dst, send_sem=send, recv_sem=recv, device_id=to,
            device_id_type=pl.DeviceIdType.MESH,
        )

    def piece_of(i, who):
        return jnp.where(i < 2, 4 + 2 * who + i, i - 2)

    def span(owner, k):
        return pl.ds(pl.multiple_of(owner * rows + k * piece, piece), piece)

    def y_copy(dy, i):
        k = piece_of(i, parity)
        src = weight_hbm.at[pl.ds(pl.multiple_of(k * piece, piece), piece)]
        return copy(src, full_hbm.at[span(s, k)], ys.at[dy - 1, i], yr.at[dy - 1, i], shard_peer(dy, 0))

    def owner(dy):
        return lax.rem(y - dy + y_all, y_all) * 2 + core

    def relay(dy, i):
        here = full_hbm.at[span(owner(dy), 4 + 2 * parity + i)]
        return copy(here, here, rs.at[dy - 1, i], rr.at[dy - 1, i], beside)

    def core_y(dy, i):
        here = full_hbm.at[span(owner(dy), piece_of(i, parity))]
        return copy(here, here, cs.at[dy - 1, i], cr.at[dy - 1, i], partner)

    def core_r(dy, i):
        here = full_hbm.at[span(owner(dy), 4 + 2 * (1 - parity) + i)]
        return copy(here, here, fs.at[dy - 1, i], fr.at[dy - 1, i], partner)

    whole = pl.ds(pl.multiple_of(s * rows, rows), rows)
    core_own = copy(weight_hbm, full_hbm.at[whole], gs, gr, partner)

    def at(c):
        return pl.ds(pl.multiple_of(c * chunk, chunk), chunk)

    def z_copy(d, c):
        return copy(upstream_hbm.at[at(c)], ups_hbm.at[d, 0, at(c)], zs.at[d - 1, c], zr.at[d - 1, c], expert_peer(d, 0))

    def x_copy(d):
        return copy(upstream_hbm, ups_hbm.at[0, d], xs.at[d - 1], xr.at[d - 1], expert_peer(0, d))

    def u_copy(dz, dx, c):
        return copy(
            ups_hbm.at[dz, 0, at(c)], ups_hbm.at[dz, dx, at(c)],
            us.at[dz - 1, dx - 1, c], ur.at[dz - 1, dx - 1, c], expert_peer(0, dx),
        )

    def router_copy(n, p):
        return copy(router_hbm, router_full_hbm.at[whole], ns.at[n], nr.at[n], shard_peer(*p))

    def gains_copy(n, p):
        return copy(gains_ref, gains_full_ref.at[s], ms.at[n], mr.at[n], shard_peer(*p))

    def place_copy(n, p):
        return copy(place_all_ref.at[0, 0], place_all_ref.at[p[0], p[1]], ps.at[n], pr.at[n], expert_peer(*p))

    barrier = pltpu.get_barrier_semaphore()
    peers = [expert_peer(*p) for p in far] + [shard_peer(*p) for p in near]
    for peer in peers:
        pl.semaphore_signal(barrier, inc=1, device_id=peer, device_id_type=pl.DeviceIdType.MESH)
    pl.semaphore_wait(barrier, len(peers))

    own = [
        pltpu.make_async_copy(weight_hbm, full_hbm.at[whole], own_sem.at[0]),
        pltpu.make_async_copy(upstream_hbm, ups_hbm.at[0, 0], own_sem.at[1]),
        pltpu.make_async_copy(router_hbm, router_full_hbm.at[whole], own_sem.at[2]),
    ]
    for n, p in enumerate(near):
        gains_copy(n, p).start()
        router_copy(n, p).start()
    for i in range(2):
        for dy in range(1, y_all):
            y_copy(dy, i).start()
    for d in range(1, x_all):
        x_copy(d).start()
    for d in (1, 3, 2):
        for c in range(parts):
            z_copy(d, c).start()
    core_own.start()
    for o in own:
        o.start()

    count = place_all_ref.shape[2]
    ids = lax.broadcasted_iota(jnp.int32, (count, length), 0)
    chosen = jnp.zeros((count, length), f32)
    for k in range(TOP):
        chosen = jnp.where(routes_ref[k : k + 1, :] == ids, 1.0, chosen)
    before = lax.broadcasted_iota(jnp.int32, (length, length), 0)
    after = lax.broadcasted_iota(jnp.int32, (length, length), 1)
    earlier = jnp.where(before < after, 1.0, 0.0).astype(bf16)
    rank = jnp.dot(chosen.astype(bf16), earlier, preferred_element_type=f32)
    limit = (tiles_ref[...] * TILE).astype(f32)
    place_all_ref[0, 0] = jnp.where((chosen > 0.5) & (rank < limit), rank, -1.0)
    for n, p in enumerate(far):
        place_copy(n, p).start()

    gains_full_ref[s] = gains_ref[...]
    for n, p in enumerate(near):
        gains_copy(n, p).wait_recv()
    keep = gains_ref.shape[1]
    tall = 64

    def norm(t, carry):
        r = pl.ds(pl.multiple_of(t * tall, tall), tall)
        values = tokens_ref[r, :].astype(f32)
        scale = lax.rsqrt(jnp.mean(values * values, axis=1, keepdims=True) + epsilon)
        for j in range(2 * y_all):
            c = slice(j * keep, (j + 1) * keep)
            gain = gains_full_ref[j, 0:1, :].astype(f32)
            hidden_ref[r, c] = (values[:, c] * scale * gain).astype(bf16)
        return carry

    lax.fori_loop(0, length // tall, norm, 0)

    def forward(events):
        for d, c in events:
            z_copy(d, c).wait_recv()
            for dx in range(1, x_all):
                u_copy(d, dx, c).start()

    order = {
        0: [(1, 0)], 1: [(1, 1), (1, 2)], 2: [(1, 3), (3, 0), (3, 1)], 3: [(3, 2), (3, 3), (2, 0)],
        4: [(2, 1), (2, 2), (2, 3)], 5: [],
    }
    for i in range(6):
        for dy in range(1, y_all):
            y_copy(dy, i).wait_recv()
            if i < 2:
                relay(dy, i).start()
            core_y(dy, i).start()
            if i < 4:
                y_copy(dy, i + 2).start()
        forward(order[i])
        if i in (3, 4):
            for dy in range(1, y_all):
                here = full_hbm.at[span(owner(dy), 4 + 2 * (1 - parity) + i - 3)]
                copy(here, here, rs.at[dy - 1, i - 3], rr.at[dy - 1, i - 3], beside).wait_recv()
                core_r(dy, i - 3).start()

    for o in own:
        o.wait()
    core_own.wait()
    for n, p in enumerate(near):
        gains_copy(n, p).wait_send()
        router_copy(n, p).wait()
    for n, p in enumerate(far):
        place_copy(n, p).wait()
    for d in range(1, x_all):
        x_copy(d).wait()
    for dy in range(1, y_all):
        for i in range(6):
            y_copy(dy, i).wait_send()
            core_y(dy, i).wait()
        for i in range(2):
            relay(dy, i).wait_send()
            core_r(dy, i).wait()
    for d in range(1, z_all):
        for c in range(parts):
            z_copy(d, c).wait_send()
            for dx in range(1, x_all):
                u_copy(d, dx, c).wait()


def start_layer(weight, upstream, router, gains, tokens, routes, tile_counts, expert_group, shard_group, name_id):
    f32, bf16 = jnp.float32, jnp.bfloat16
    length, width = tokens.shape
    x_all, y_all = expert_group // 4, shard_group // 2
    experts_all = tile_counts.shape[0]
    dma = pltpu.SemaphoreType.DMA
    y1, x1 = max(y_all - 1, 1), max(x_all - 1, 1)
    any_spec = pl.BlockSpec(memory_space=pl.ANY)
    vmem_spec = pl.BlockSpec(memory_space=pltpu.VMEM)
    return pl.pallas_call(
        functools.partial(start_kernel, (x_all, y_all)),
        out_shape=[
            jax.ShapeDtypeStruct((weight.shape[0] * shard_group, weight.shape[1]), bf16),
            jax.ShapeDtypeStruct((4, x_all, length, width), bf16),
            jax.ShapeDtypeStruct((router.shape[0] * shard_group, router.shape[1]), bf16),
            jax.ShapeDtypeStruct((shard_group, *gains.shape), bf16),
            jax.ShapeDtypeStruct((4, x_all, experts_all, length), f32),
            jax.ShapeDtypeStruct((length, width), bf16),
        ],
        in_specs=[any_spec] * 3 + [vmem_spec] * 4,
        out_specs=[any_spec] * 3 + [vmem_spec] * 3,
        scratch_shapes=[
            dma((3,)),
            dma((y1, 6)), dma((y1, 6)),
            dma((y1, 2)), dma((y1, 2)),
            dma((y1, 6)), dma((y1, 6)),
            dma((y1, 2)), dma((y1, 2)),
            dma, dma,
            dma((3, 4)), dma((3, 4)),
            dma((x1,)), dma((x1,)),
            dma((3, x1, 4)), dma((3, x1, 4)),
            dma((shard_group - 1,)), dma((shard_group - 1,)),
            dma((expert_group - 1,)), dma((expert_group - 1,)),
            dma((shard_group - 1,)), dma((shard_group - 1,)),
        ],
        compiler_params=pltpu.CompilerParams(
            collective_id=name_id, has_side_effects=True, vmem_limit_bytes=32 * 1024 * 1024
        ),
        cost_estimate=pl.CostEstimate(
            flops=16 * length * width, bytes_accessed=64 * 1024 * 1024, transcendentals=0
        ),
    )(weight, upstream, router, gains, tokens, routes.T, tile_counts[:, None])


def body(
    tokens,
    cotangent,
    segments,
    routes,
    tile_counts,
    norm_one,
    norm_query,
    norm_key,
    norm_two,
    qkv_weight,
    out_weight,
    router_weight,
    gate_up_weight,
    down_weight,
):
    f32, bf16 = jnp.float32, jnp.bfloat16
    length, model_width = tokens.shape
    experts_all = tile_counts.shape[0]
    local_experts = gate_up_weight.shape[0]
    expert_group = lax.axis_size("expert")
    shard_group = lax.axis_size("shard")
    capacity = length * TOP // (experts_all * TILE) * TILE
    score_scale = HEAD_DIM ** (-0.5)
    own_expert = lax.axis_index("expert")
    own_shard = lax.axis_index("shard")
    z_all = z_size(expert_group)
    x_all = expert_group // z_all

    gain_rows = jnp.stack([norm_one, norm_query, norm_key, norm_two])
    gain_rows = jnp.pad(gain_rows, ((0, 12), (0, 0)))
    qkv_full, upstream_all, router_full, gains, place_all, hidden_one = start_layer(
        qkv_weight,
        cotangent,
        router_weight,
        gain_rows,
        tokens,
        routes,
        tile_counts,
        expert_group,
        shard_group,
        3,
    )
    out_own, gains = lax.optimization_barrier((out_weight, gains))
    out_full = lax.all_gather(out_own, "shard", axis=0, tiled=True)
    gains = gains.transpose(1, 0, 2).reshape(gains.shape[1], model_width).astype(f32)
    gain_one, gain_query, gain_key, gain_two = gains[0], gains[1], gains[2], gains[3]
    place_own = lax.dynamic_slice_in_dim(
        place_all, own_expert * local_experts, local_experts, axis=2
    )
    position = jnp.arange(length, dtype=jnp.int32)

    inputs = tokens.astype(f32)
    _, first_pull = jax.vjp(rms_scale, inputs, gain_one)
    projected = jnp.dot(hidden_one, qkv_full, preferred_element_type=f32)
    cosine, sine_table = rotary_tables(length)

    def query_key_local(raw_query, raw_key, query_gain, key_gain):
        return query_key(raw_query, raw_key, query_gain, key_gain, cosine, sine_table)

    rotated, rotary_pull = jax.vjp(
        query_key_local,
        projected[:, :model_width],
        projected[:, model_width : 2 * model_width],
        gain_query,
        gain_key,
    )
    query_low = rotated[0].astype(bf16)
    key_low = rotated[1].astype(bf16)
    value_low = projected[:, 2 * model_width :].astype(bf16).reshape(length, HEADS, HEAD_DIM)
    allowed = (position[:, None] >= position[None, :]) & (
        segments[0][:, None] == segments[0][None, :]
    )
    masked = jnp.where(
        allowed[None],
        jnp.einsum("qhd,khd->hqk", query_low, key_low, preferred_element_type=f32) * score_scale,
        -1e30,
    )
    probs = softmax_rows(masked)
    probs_low = probs.astype(bf16)
    attended_low = (
        jnp.einsum("hqk,khd->qhd", probs_low, value_low, preferred_element_type=f32)
        .reshape(length, model_width)
        .astype(bf16)
    )
    middle = inputs + jnp.dot(attended_low, out_full, preferred_element_type=f32)
    scaled_two, second_pull = jax.vjp(rms_scale, middle, gain_two)
    hidden_two = scaled_two.astype(bf16)
    router = softmax_rows(jnp.dot(hidden_two, router_full, preferred_element_type=f32))
    row_count = expert_group * capacity
    done, mixture_parts = moe_layer(
        hidden_two,
        upstream_all,
        place_own,
        router_full,
        gate_up_weight,
        down_weight,
        attended_low,
        hidden_one,
        expert_group,
        shard_group,
        capacity,
        2,
    )
    columns = done[6].reshape(2, shard_group * length, -1).swapaxes(1, 2)
    expert_rows, activated, grad_expert, grad_gate_up_low = (
        a.reshape(local_experts, row_count, a.shape[-1]) for a in done[:4]
    )
    grad_rows_sum = done[4]
    grad_router = done[5][:, :local_experts].reshape(experts_all, length).T
    parts = dict(enumerate(mixture_parts))

    def hold(values, *names):
        held = lax.optimization_barrier((values, [parts[n] for n in names]))
        parts.update(zip(names, held[1], strict=True))
        return held[0]

    def group(dz):
        return [dz * x_all + dx for dx in range(x_all)]

    two = sum_over_x(parts, 2, expert_group)
    grad_gate_up_full = jnp.einsum(
        "erd,erf->edf", expert_rows, grad_gate_up_low, preferred_element_type=f32
    ).astype(bf16)
    grad_gate_up_full, activated, two = hold(
        (grad_gate_up_full, activated, two), *group(1)
    )
    two = back_along_z(two, 2, expert_group)
    one = sum_over_x(parts, 1, expert_group)
    grad_down_full = jnp.einsum(
        "erf,erd->efd", activated, grad_expert, preferred_element_type=f32
    ).astype(bf16)
    grad_down_full, grad_rows_sum, one = hold(
        (grad_down_full, grad_rows_sum, one), *group(3), *group(0)
    )
    one = back_along_z(one, 1, expert_group)
    grad_gate_up_weight = lax.psum_scatter(
        grad_gate_up_full, "shard", scatter_dimension=1, tiled=True
    ).astype(f32)
    grad_down_weight = lax.psum_scatter(
        grad_down_full, "shard", scatter_dimension=2, tiled=True
    ).astype(f32)

    upstream = cotangent.astype(f32)
    grad_logits = (
        router * (grad_router - jnp.sum(router * grad_router, axis=-1, keepdims=True))
    ).astype(bf16)
    grad_hidden_two = grad_rows_sum + jnp.einsum(
        "te,de->td", grad_logits, router_full, preferred_element_type=f32
    )
    grad_middle_norm, grad_gain_two = second_pull(grad_hidden_two)
    grad_middle = upstream + grad_middle_norm
    grad_branch_low = grad_middle.astype(bf16)
    grad_attended_low = (
        jnp.einsum("te,de->td", grad_branch_low, out_full, preferred_element_type=f32)
        .astype(bf16)
        .reshape(length, HEADS, HEAD_DIM)
    )
    grad_probs = jnp.einsum(
        "qhd,khd->hqk", grad_attended_low, value_low, preferred_element_type=f32
    )
    grad_scores_low = (
        probs * (grad_probs - jnp.sum(probs * grad_probs, axis=-1, keepdims=True))
    ).astype(bf16)
    three = sum_over_x(parts, 3, expert_group)
    here = sum_over_x(parts, 0, expert_group)
    grad_scores_low, two, three, here = lax.optimization_barrier(
        (grad_scores_low, two, three, here)
    )
    three = back_along_z(three, 3, expert_group)
    grad_queries = (
        jnp.einsum("hqk,khd->qhd", grad_scores_low, key_low, preferred_element_type=f32)
        * score_scale
    )
    grad_keys = (
        jnp.einsum("hqk,qhd->khd", grad_scores_low, query_low, preferred_element_type=f32)
        * score_scale
    )
    grad_values = jnp.einsum(
        "hqk,qhd->khd", probs_low, grad_attended_low, preferred_element_type=f32
    )
    grad_raw_query, grad_raw_key, grad_gain_query, grad_gain_key = rotary_pull(
        (grad_queries, grad_keys)
    )
    grad_projected_low = jnp.concatenate(
        [grad_raw_query, grad_raw_key, grad_values.reshape(length, model_width)], axis=-1
    ).astype(bf16)
    grad_hidden_one = jnp.einsum(
        "te,de->td", grad_projected_low, qkv_full, preferred_element_type=f32
    )
    grad_inputs_norm, grad_gain_one = first_pull(grad_hidden_one)
    grad_tokens = grad_middle + grad_inputs_norm

    grad_router_part = jnp.einsum("td,te->ed", hidden_two, grad_logits, preferred_element_type=f32)
    small = jnp.concatenate(
        [
            grad_router_part,
            jnp.stack([grad_gain_one, grad_gain_query, grad_gain_key, grad_gain_two]),
            jnp.zeros((-(experts_all + 4) % 8, model_width), f32),
        ],
        axis=0,
    )
    keep = norm_one.shape[0]
    small = jnp.stack(
        [
            lax.dynamic_slice_in_dim(
                small,
                (((own_shard // 2 + dy) % (shard_group // 2)) * 2 + (own_shard % 2 + flip) % 2) * keep,
                keep,
                axis=1,
            )
            for dy in range(shard_group // 2)
            for flip in range(2)
        ]
    )

    grads_low = jnp.concatenate([grad_branch_low, grad_projected_low], axis=1)
    grads_low, one, three = lax.optimization_barrier((grads_low, one, three))
    mixture = here + one + two + three
    block_out = (middle + mixture).astype(bf16)
    grad_rows_kept, small = summed_rows(
        columns, grads_low, model_width, small, expert_group, shard_group, z_all, 256, 2, 1
    )
    grad_out_weight = grad_rows_kept[:, :model_width].astype(f32)
    grad_qkv_weight = grad_rows_kept[:, model_width:].astype(f32)
    return (
        block_out,
        grad_tokens,
        small[experts_all],
        small[experts_all + 1],
        small[experts_all + 2],
        small[experts_all + 3],
        grad_qkv_weight,
        grad_out_weight,
        small[:experts_all].T,
        grad_gate_up_weight,
        grad_down_weight,
    )


def solution(mesh):
    return jax.shard_map(
        body,
        mesh=mesh,
        in_specs=(
            P(("expert", "shard"), None),
            P(("expert", "shard"), None),
            P(("expert", "shard"), None),
            P(("expert", "shard"), None),
            P(),
            P("shard"),
            P("shard"),
            P("shard"),
            P("shard"),
            P("shard", None),
            P("shard", None),
            P("shard", None),
            P("expert", None, None),
            P("expert", None, None),
        ),
        out_specs=(
            P(("expert", "shard"), None),
            P(("expert", "shard"), None),
            P("shard"),
            P("shard"),
            P("shard"),
            P("shard"),
            P("shard", None),
            P("shard", None),
            P("shard", None),
            P("expert", "shard", None),
            P("expert", None, "shard"),
        ),
        check_vma=False,
    )
```

```python
import functools

import jax
import jax.numpy as jnp
from jax import lax
from jax.experimental import pallas as pl
from jax.experimental.pallas import tpu as pltpu
from jax.sharding import PartitionSpec as P

HEADS = 16
HEAD_DIM = 128
TOP = 8
TILE = 8


epsilon = 1e-05
rope_base = 10000.0


def rms_scale(values, scale_gain):
    return (
        values * lax.rsqrt(jnp.mean(values * values, axis=-1, keepdims=True) + epsilon) * scale_gain
    )


def rotary_tables(length):
    half_dim = HEAD_DIM // 2
    position = jnp.arange(length, dtype=jnp.float32)[:, None]
    frequency = rope_base ** (-jnp.arange(half_dim, dtype=jnp.float32) * 2.0 / HEAD_DIM)
    angles = position * frequency[None, :]
    angles = jnp.concatenate([angles, angles], axis=-1)
    return (jnp.cos(angles)[:, None, :], jnp.sin(angles)[:, None, :])


def rotate(vectors, cosine, sine_table):
    half_dim = vectors.shape[-1] // 2
    turned = jnp.concatenate([-vectors[..., half_dim:], vectors[..., :half_dim]], axis=-1)
    return vectors * cosine + turned * sine_table


def query_key(raw_query, raw_key, query_gain, key_gain, cosine, sine_table):
    length = raw_query.shape[0]
    queries = rms_scale(raw_query, query_gain).reshape(length, HEADS, HEAD_DIM)
    keys_rot = rms_scale(raw_key, key_gain).reshape(length, HEADS, HEAD_DIM)
    return (rotate(queries, cosine, sine_table), rotate(keys_rot, cosine, sine_table))


def swiglu(gate_up):
    half_dim = gate_up.shape[-1] // 2
    gate_part = gate_up[..., :half_dim]
    return gate_part / (1.0 + jnp.exp(-gate_part)) * gate_up[..., half_dim:]


def softmax_rows(logits):
    largest = jnp.max(logits, axis=-1, keepdims=True)
    raised = jnp.exp(logits - largest)
    return raised / jnp.sum(raised, axis=-1, keepdims=True)


def z_size(expert_group):
    return 4 if expert_group % 4 == 0 else 1


def shift(values, expert_group, dz, dx):
    z_all = z_size(expert_group)
    x_all = expert_group // z_all
    pairs = [
        (i, ((i // x_all + dz) % z_all) * x_all + (i % x_all + dx) % x_all)
        for i in range(expert_group)
    ]
    return lax.ppermute(values, "expert", pairs)


def gather_expert(block, expert_group):
    z_all = z_size(expert_group)
    x_all = expert_group // z_all
    rows = [block] + [shift(block, expert_group, dz, 0) for dz in range(1, z_all)]
    return [
        rows[dz] if dx == 0 else shift(rows[dz], expert_group, 0, dx)
        for dz in range(z_all)
        for dx in range(x_all)
    ]


def sum_over_x(parts, dz, expert_group):
    x_all = expert_group // z_size(expert_group)
    total = parts[dz * x_all].astype(jnp.float32)
    for dx in range(1, x_all):
        total = total + shift(parts[dz * x_all + dx], expert_group, 0, -dx).astype(jnp.float32)
    return total


def back_along_z(total, dz, expert_group):
    return shift(total, expert_group, -dz, 0)


def tail_kernel(
    dims, grads_ref, columns_ref, small_ref, out_ref, small_out_ref,
    gall, xsend, xrecv, zsend, zrecv, acc, fin, group_small, own_small, all_small, *sems
):
    steps, width, x_all, z_all, y_all, lag, first_steps = dims
    (gs_s, gs_r, es_s, es_r) = sems[14:]
    (y_s, y_r, core_s, core_r, fwd_s, fwd_r, x_s, x_r, z_s, z_r, zb_s, zb_r, xb_s, xb_r) = sems[:14]
    f32, bf16 = jnp.float32, jnp.bfloat16
    length = grads_ref.shape[0]
    rows = columns_ref.shape[1]
    block = rows // (x_all * z_all)
    half = z_all * block
    e = lax.axis_index("expert")
    s = lax.axis_index("shard")
    z, x = e // x_all, lax.rem(e, x_all)
    y, core = s // 2, lax.rem(s, 2)

    def y_peer(d):
        return {"shard": lax.rem(y + d, y_all) * 2 + core}

    partner = {"shard": y * 2 + (1 - core)}

    def x_peer(d):
        return {"expert": z * x_all + lax.rem(x + d, x_all)}

    def z_peer(d):
        return {"expert": lax.rem(z + d, z_all) * x_all + x}

    def copy(src, dst, send, recv, peer):
        return pltpu.make_async_remote_copy(
            src_ref=src, dst_ref=dst, send_sem=send, recv_sem=recv, device_id=peer,
            device_id_type=pl.DeviceIdType.MESH,
        )

    def cols(c):
        return pl.ds(pl.multiple_of(c * width, width), width)

    def y_copy(d, c):
        return copy(grads_ref.at[:, cols(c)], gall.at[2 * d - 1, c], y_s.at[d - 1], y_r.at[d - 1, c], y_peer(d))

    def core_copy(c):
        return copy(grads_ref.at[:, cols(c)], gall.at[0, c], core_s.at[0], core_r.at[c], partner)

    def fwd_copy(d, c):
        return copy(gall.at[2 * d - 1, c], gall.at[2 * d, c], fwd_s.at[d - 1], fwd_r.at[d - 1, c], partner)

    def x_copy(d, c):
        return copy(xsend.at[d - 1, c], xrecv.at[d - 1, c], x_s.at[d - 1], x_r.at[d - 1, c], x_peer(d))

    def z_copy(d, c):
        return copy(zsend.at[d - 1, c], zrecv.at[d - 1, c], z_s.at[d - 1], z_r.at[d - 1, c], z_peer(d))

    def zb_copy(d, c):
        here = fin.at[c, pl.ds(pl.multiple_of((x * z_all + z) * block, block), block)]
        return copy(here, here, zb_s.at[d - 1], zb_r.at[d - 1, c], z_peer(d))

    def xb_copy(d, c):
        here = fin.at[c, pl.ds(pl.multiple_of(x * half, half), half)]
        return copy(here, here, xb_s.at[d - 1], xb_r.at[d - 1, c], x_peer(d))

    near = [(d, flip) for d in range(y_all) for flip in range(2) if d + flip > 0]
    far = [(dz, dx) for dz in range(z_all) for dx in range(x_all) if dz + dx > 0]

    def near_peer(d, flip):
        return {"shard": lax.rem(y + d, y_all) * 2 + lax.rem(core + flip, 2)}

    def far_peer(dz, dx):
        return {"expert": lax.rem(z + dz, z_all) * x_all + lax.rem(x + dx, x_all)}

    def near_small(d, flip):
        j = 2 * d + flip
        return copy(small_ref.at[j], group_small.at[j - 1], gs_s.at[j - 1], gs_r.at[j - 1], near_peer(d, flip))

    def far_small(dz, dx):
        i = dz * x_all + dx
        return copy(own_small, all_small.at[i - 1], es_s.at[i - 1], es_r.at[i - 1], far_peer(dz, dx))

    barrier = pltpu.get_barrier_semaphore()
    peers = [near_peer(*p) for p in near] + [far_peer(*p) for p in far]
    for peer in peers:
        pl.semaphore_signal(barrier, inc=1, device_id=peer, device_id_type=pl.DeviceIdType.MESH)
    pl.semaphore_wait(barrier, len(peers))

    for p in near:
        near_small(*p).start()

    def first(c, carry):
        for d in range(1, y_all):
            y_copy(d, c).start()
        core_copy(c).start()
        return carry

    lax.fori_loop(0, steps, first, 0)
    slots = acc.shape[0]

    def step(t, carry):
        def stage(k, body):
            c = t - k * lag
            pl.when((c >= 0) & (c < steps))(lambda: body(c))

        @functools.partial(stage, 5)
        def _(c):
            for d in range(1, x_all):
                xb_copy(d, c).wait_recv()
            out_ref[:, cols(c)] = fin[c]

        @functools.partial(stage, 4)
        def _(c):
            for d in range(1, z_all):
                zb_copy(d, c).wait_recv()
            for d in range(1, x_all):
                xb_copy(d, c).start()

        @functools.partial(stage, 3)
        def _(c):
            slot = lax.rem(c, slots)
            total = acc[slot, pl.ds(pl.multiple_of(z * block, block), block), :]
            for d in range(1, z_all):
                z_copy(d, c).wait_recv()
                total = total + zrecv[d - 1, c].astype(f32)
            fin[c, pl.ds(pl.multiple_of((x * z_all + z) * block, block), block), :] = total.astype(bf16)
            for d in range(1, z_all):
                zb_copy(d, c).start()

        @functools.partial(stage, 2)
        def _(c):
            slot = lax.rem(c, slots)
            total = acc[slot]
            for d in range(1, x_all):
                x_copy(d, c).wait_recv()
                total = total + xrecv[d - 1, c].astype(f32)
            acc[slot] = total
            for d in range(1, z_all):
                there = lax.rem(z + d, z_all)
                zsend[d - 1, c] = acc[slot, pl.ds(pl.multiple_of(there * block, block), block), :].astype(bf16)
                z_copy(d, c).start()

        @functools.partial(stage, 1)
        def _(c):
            core_copy(c).wait_recv()
            for d in range(1, y_all):
                fwd_copy(d, c).wait_recv()
            kind = (c >= first_steps).astype(jnp.int32)
            others = gall[:, c].reshape((2 * y_all - 1) * length, width)
            mine = grads_ref[:, cols(c)]

            def product(there):
                at = pl.ds(pl.multiple_of(there * half, half), half)
                return jnp.dot(columns_ref[kind, at, :length], mine, preferred_element_type=f32) + jnp.dot(
                    columns_ref[kind, at, length:], others, preferred_element_type=f32
                )

            for d in range(1, x_all):
                xsend[d - 1, c] = product(lax.rem(x + d, x_all)).astype(bf16)
                x_copy(d, c).start()
            acc[lax.rem(c, slots)] = product(x)

        @functools.partial(stage, 0)
        def _(c):
            for d in range(1, y_all):
                y_copy(d, c).wait_recv()
                fwd_copy(d, c).start()

        @pl.when(t == 2)
        def _():
            total = small_ref[0]
            for j, p in enumerate(near):
                near_small(*p).wait_recv()
                total = total + group_small[j]
            own_small[...] = total
            for p in far:
                far_small(*p).start()

        return carry

    lax.fori_loop(0, steps + 5 * lag, step, 0)
    total = own_small[...]
    for i, p in enumerate(far):
        far_small(*p).wait_recv()
        total = total + all_small[i]
    small_out_ref[...] = total
    for p in near:
        near_small(*p).wait_send()
    for p in far:
        far_small(*p).wait_send()

    for d in range(1, y_all):
        copy(grads_ref, grads_ref, y_s.at[d - 1], y_r.at[d - 1, 0], y_peer(d)).wait_send()
        whole = gall.at[2 * d - 1]
        copy(whole, whole, fwd_s.at[d - 1], fwd_r.at[d - 1, 0], partner).wait_send()
    copy(grads_ref, grads_ref, core_s.at[0], core_r.at[0], partner).wait_send()
    for d in range(1, x_all):
        whole = xsend.at[d - 1]
        copy(whole, whole, x_s.at[d - 1], x_r.at[d - 1, 0], x_peer(d)).wait_send()
        copy(whole, whole, xb_s.at[d - 1], xb_r.at[d - 1, 0], x_peer(d)).wait_send()
    for d in range(1, z_all):
        whole = zsend.at[d - 1]
        copy(whole, whole, z_s.at[d - 1], z_r.at[d - 1, 0], z_peer(d)).wait_send()
        copy(whole, whole, zb_s.at[d - 1], zb_r.at[d - 1, 0], z_peer(d)).wait_send()


def summed_rows(columns, grads, first_total, small, expert_group, shard_group, z_all, width, lag, name_id):
    x_all, y_all = expert_group // z_all, shard_group // 2
    length, total = grads.shape
    rows = columns.shape[1]
    steps = total // width
    block = rows // expert_group
    half = z_all * block
    bf16 = jnp.bfloat16
    dma = pltpu.SemaphoreType.DMA
    n1 = max(y_all - 1, 1)
    x1 = max(x_all - 1, 1)
    z1 = max(z_all - 1, 1)
    slots = min(steps, 2 * lag + 1)
    return pl.pallas_call(
        functools.partial(tail_kernel, (steps, width, x_all, z_all, y_all, lag, first_total // width)),
        out_shape=[
            jax.ShapeDtypeStruct((rows, total), bf16),
            jax.ShapeDtypeStruct(small.shape[1:], jnp.float32),
        ],
        in_specs=[pl.BlockSpec(memory_space=pltpu.VMEM)] * 3,
        out_specs=[pl.BlockSpec(memory_space=pltpu.VMEM)] * 2,
        scratch_shapes=[
            pltpu.VMEM((shard_group - 1, steps, length, width), bf16),
            pltpu.VMEM((x1, steps, half, width), bf16),
            pltpu.VMEM((x1, steps, half, width), bf16),
            pltpu.VMEM((z1, steps, block, width), bf16),
            pltpu.VMEM((z1, steps, block, width), bf16),
            pltpu.VMEM((slots, half, width), jnp.float32),
            pltpu.VMEM((steps, rows, width), bf16),
            pltpu.VMEM((shard_group - 1, *small.shape[1:]), jnp.float32),
            pltpu.VMEM(small.shape[1:], jnp.float32),
            pltpu.VMEM((expert_group - 1, *small.shape[1:]), jnp.float32),
            dma((n1,)), dma((n1, steps)),
            dma((1,)), dma((steps,)),
            dma((n1,)), dma((n1, steps)),
            dma((x1,)), dma((x1, steps)),
            dma((z1,)), dma((z1, steps)),
            dma((z1,)), dma((z1, steps)),
            dma((x1,)), dma((x1, steps)),
            dma((shard_group - 1,)), dma((shard_group - 1,)),
            dma((expert_group - 1,)), dma((expert_group - 1,)),
        ],
        compiler_params=pltpu.CompilerParams(
            collective_id=name_id, has_side_effects=True, vmem_limit_bytes=60 * 1024 * 1024
        ),
        cost_estimate=pl.CostEstimate(
            flops=2 * rows * length * shard_group * total, bytes_accessed=16 * 1024 * 1024, transcendentals=0
        ),
    )(grads, columns, small)


MOE_CHUNKS = 4


def moe_kernel(
    dims, hidden_hbm, upstream_hbm, place_ref, place_t_ref, router_ref, router_t_ref, gate_up_hbm, down_hbm,
    first_hbm, second_hbm, rows_hbm, activated_hbm, grad_out_hbm, grad_gate_up_hbm, grad_ref, grad_router_ref, columns_hbm, found_hbm, summed_hbm,
    *rest,
):
    x_all, capacity, y_all = dims
    mixture_hbm = rest[: 4 * x_all]
    (
    gate_up_w, down_w, hid, ups, prob, prob_t, rows, gate_up, activated, out_rows, grad_expert, grad_gate_up, grad_rows,
    mix_stage, part_stage, own_part, z_landed, router_stage,
    w_sem, own_sem, load_sem, store_sem, zs, zr, xs, xr, fs, fr, ps, pr, qs, qr, rs, rr, lsem, mix_sem, cs, cr, own_c,
    ) = rest[4 * x_all :]
    z_all = 4
    f32, bf16 = jnp.float32, jnp.bfloat16
    length, width = hidden_hbm.shape
    local_experts, _, twice = gate_up_w.shape
    half = twice // 2
    tile = min(512, half)
    narrow = min(256, half)
    chunk = length // MOE_CHUNKS
    e = lax.axis_index("expert")
    z, x = e // x_all, lax.rem(e, x_all)

    def peer(dz, dx):
        return {"expert": lax.rem(z + dz + 4 * z_all, z_all) * x_all + lax.rem(x + dx + 4 * x_all, x_all)}

    def copy(src, dst, send, recv, to):
        return pltpu.make_async_remote_copy(
            src_ref=src, dst_ref=dst, send_sem=send, recv_sem=recv, device_id=to,
            device_id_type=pl.DeviceIdType.MESH,
        )

    def at(c):
        return pl.ds(pl.multiple_of(c * chunk, chunk), chunk)

    def z_copy(d, c):
        return copy(hidden_hbm.at[at(c)], found_hbm.at[d, 0, at(c)], zs.at[d - 1, c], zr.at[d - 1, c], peer(d, 0))

    def x_copy(d, c):
        return copy(hidden_hbm.at[at(c)], found_hbm.at[0, d, at(c)], xs.at[d - 1, c], xr.at[d - 1, c], peer(0, d))

    def f_copy(dz, dx, c):
        return copy(
            found_hbm.at[dz, 0, at(c)], found_hbm.at[dz, dx, at(c)],
            fs.at[dz - 1, dx - 1, c], fr.at[dz - 1, dx - 1, c], peer(0, dx),
        )

    def p_copy(dz, dx, c):
        return copy(
            part_stage.at[dx - 1, at(c)], summed_hbm.at[dz, dx - 1, at(c)],
            ps.at[dx - 1], pr.at[dz, dx - 1, c], peer(0, -dx),
        )

    def p_sent(dx):
        whole = part_stage.at[dx - 1]
        copy(whole, whole, ps.at[dx - 1], pr.at[0, dx - 1, 0], peer(0, -dx)).wait_send()

    def q_copy(dz, c):
        return copy(
            own_part.at[dz, at(c)], z_landed.at[dz - 1, at(c)], qs.at[dz - 1], qr.at[dz - 1, c], peer(-dz, 0)
        )

    def r_copy(dz, dx):
        return copy(
            router_stage.at[dz, dx], grad_router_ref.at[e], rs.at[dz, dx], rr.at[dz, dx], peer(-dz, -dx)
        )

    def cols(n, w):
        return pl.ds(pl.multiple_of(n * w, w), w)

    barrier = pltpu.get_barrier_semaphore()
    others = [(dz, dx) for dz in range(z_all) for dx in range(x_all) if dz + dx > 0]
    near = [(dy, flip) for dy in range(y_all) for flip in range(2) if dy + flip > 0]
    shard = lax.axis_index("shard")

    def near_at(dy, flip):
        return lax.rem(shard // 2 + dy, y_all) * 2 + lax.rem(lax.rem(shard, 2) + flip, 2)

    for dz, dx in others:
        pl.semaphore_signal(barrier, inc=1, device_id=peer(dz, dx), device_id_type=pl.DeviceIdType.MESH)
    for dy, flip in near:
        pl.semaphore_signal(
            barrier, inc=1, device_id={"shard": near_at(dy, flip)}, device_id_type=pl.DeviceIdType.MESH
        )
    pl.semaphore_wait(barrier, len(others) + len(near))

    keep = columns_hbm.shape[3]

    def column_copy(kind, source, dy, flip):
        j = 2 * dy + flip
        there = near_at(dy, flip)
        src = source.at[:, pl.ds(pl.multiple_of(there * keep, keep), keep)]
        if j == 0:
            return pltpu.make_async_copy(src, columns_hbm.at[kind, 0], own_c.at[kind])
        return copy(src, columns_hbm.at[kind, j], cs.at[kind, j - 1], cr.at[kind, j - 1], {"shard": there})

    column_copies = [
        column_copy(kind, source, dy, flip)
        for kind, source in enumerate((first_hbm, second_hbm))
        for dy, flip in [(0, 0)] + near
    ]
    own = pltpu.make_async_copy(hidden_hbm, found_hbm.at[0, 0], own_sem)
    own.start()
    weights = [
        pltpu.make_async_copy(gate_up_hbm, gate_up_w, w_sem.at[0]),
        pltpu.make_async_copy(down_hbm, down_w, w_sem.at[1]),
    ]
    for w in weights:
        w.start()

    def send_own(c, carry):
        for d in range(1, x_all):
            x_copy(d, c).start()
        return carry

    for d in (1, 2, 3):

        def send_z(c, carry):
            z_copy(d, c).start()
            return carry

        lax.fori_loop(0, MOE_CHUNKS, send_z, 0)

    for c in column_copies:
        c.start()

    def events(first, last):
        def one(k, carry):
            @pl.when(k < last)
            def _():
                j = k // MOE_CHUNKS
                c = lax.rem(k, MOE_CHUNKS)
                d = 1 + j
                z_copy(d, c).wait_recv()
                for dx in range(1, x_all):
                    f_copy(d, dx, c).start()

            return carry

        lax.fori_loop(first, first + MOE_CHUNKS, one, 0)

    def own_slots(le):
        return pl.ds(pl.multiple_of(le * capacity, capacity), capacity)

    def finish(dz, last):
        def load(c):
            return pltpu.make_async_copy(summed_hbm.at[dz, dx - 1, at(c)], mix_stage.at[0, at(c)], lsem.at[c])

        def add(c):
            load(c).wait()
            own_part[dz, at(c), :] = (
                own_part[dz, at(c), :].astype(f32) + mix_stage[0, at(c), :].astype(f32)
            ).astype(bf16)
            if dx == x_all - 1:
                if not last:
                    q_copy(dz, c).start()

        def arrive(c, carry):
            p_copy(dz, dx, c).wait_recv()
            load(c).start()
            if last:
                add(c)
            return carry

        def rest(c, carry):
            add(c)
            return carry

        for dx in range(1, x_all):
            lax.fori_loop(0, MOE_CHUNKS, arrive, 0)
            if not last:
                lax.fori_loop(0, MOE_CHUNKS, rest, 0)

    mix_slots = mix_stage.shape[0]

    def mix_copy(dz, dx):
        slot = dx % mix_slots
        return pltpu.make_async_copy(mix_stage.at[slot], mixture_hbm[dz * x_all + dx], mix_sem.at[slot])

    def pieces(p):
        return 4 + sum(n * (p >= k).astype(jnp.int32) for k, n in enumerate((1, 1, 1, 1, 1, 2, 1, 0)))

    def group_at(g):
        return lax.rem(g + 1, z_all)

    slot_row = lax.broadcasted_iota(jnp.int32, (capacity, length), 0).astype(f32)
    slot_col = lax.broadcasted_iota(jnp.int32, (length, local_experts * capacity), 1).astype(f32)
    own.wait()
    events(0, 4)
    lax.fori_loop(0, MOE_CHUNKS, send_own, 0)

    def load_upstream(dz):
        return [pltpu.make_async_copy(upstream_hbm.at[dz, dx], ups.at[dx], load_sem.at[1, dx]) for dx in range(x_all)]

    for load in load_upstream(1):
        load.start()

    def group(g, carry):
        dz = group_at(g)

        def arrive(c, inner):
            for dx in range(1, x_all):

                @pl.when(dz == 0)
                def _():
                    x_copy(dx, c).wait_recv()

                @pl.when(dz > 0)
                def _():
                    f_copy(dz, dx, c).wait_recv()

            return inner

        lax.fori_loop(0, MOE_CHUNKS, arrive, 0)
        loads = []
        for dx in range(x_all):
            loads.append(pltpu.make_async_copy(found_hbm.at[dz, dx], hid.at[dx], load_sem.at[0, dx]))
        for load in loads:
            load.start()
        for load in loads + load_upstream(dz):
            load.wait()
        pl.when(g == 0)(lambda: [w.wait() for w in weights] and None)

        for dx in range(x_all):
            logits = jnp.dot(hid[dx], router_ref[...], preferred_element_type=f32)
            raised = jnp.exp(logits - jnp.max(logits, axis=1, keepdims=True))
            prob[dx] = raised / jnp.sum(raised, axis=1, keepdims=True)
            logits = lax.dot_general(
                router_t_ref[...], hid[dx], (((1,), (1,)), ((), ())), preferred_element_type=f32
            )
            raised = jnp.exp(logits - jnp.max(logits, axis=0, keepdims=True))
            prob_t[dx] = raised / jnp.sum(raised, axis=0, keepdims=True)
            router_stage[dz, dx] = jnp.zeros(router_stage.shape[2:], f32)

        def store(kind, buffer, hbm, le):
            return pltpu.make_async_copy(buffer, hbm.at[le, dz], store_sem.at[kind])

        def expert(le, inner):
            @pl.when(g + le > 0)
            def _():
                store(0, rows, rows_hbm, le).wait()
                store(1, activated, activated_hbm, le).wait()
                store(2, grad_expert, grad_out_hbm, le).wait()
                store(3, grad_gate_up, grad_gate_up_hbm, le).wait()

            chosen = [place_ref[dz, dx, pl.ds(le, 1), :] == slot_row for dx in range(x_all)]
            chosen_low = [c.astype(f32).astype(bf16) for c in chosen]

            def dispatch(n, c0):
                c = cols(n, tile)
                for dx in range(x_all):
                    rows[dx * capacity : (dx + 1) * capacity, c] = jnp.dot(
                        chosen_low[dx], hid[dx, :, c], preferred_element_type=f32
                    ).astype(bf16)
                return c0

            lax.fori_loop(0, width // tile, dispatch, 0, unroll=True)
            store(0, rows, rows_hbm, le).start()

            def up_step(n, c0):
                c = cols(n, tile)
                gate_up[:, c] = jnp.dot(rows[...], gate_up_w[le, :, c], preferred_element_type=f32)
                return c0

            lax.fori_loop(0, twice // tile, up_step, 0, unroll=True)

            def act_step(n, c0):
                gate = gate_up[:, cols(n, narrow)]
                up = gate_up[:, pl.ds(pl.multiple_of(half + n * narrow, narrow), narrow)]
                activated[:, cols(n, narrow)] = (gate / (1.0 + jnp.exp(-gate)) * up).astype(bf16)
                return c0

            lax.fori_loop(0, half // narrow, act_step, 0, unroll=True)
            store(1, activated, activated_hbm, le).start()

            def down_step(n, c0):
                c = cols(n, tile)
                result = jnp.dot(activated[...], down_w[le, :, c], preferred_element_type=f32)
                for dx in range(x_all):
                    r = slice(dx * capacity, (dx + 1) * capacity)
                    out_rows[dx, own_slots(le), c] = result[r].astype(bf16)
                return c0

            lax.fori_loop(0, width // tile, down_step, 0, unroll=True)

            events(pieces(4 * g + 2 * le - 1), pieces(4 * g + 2 * le))

            mine = e * local_experts + le
            weight_rows = [
                jnp.sum(jnp.where(chosen[dx], prob_t[dx, pl.ds(mine, 1), :], 0.0), axis=1, keepdims=True)
                for dx in range(x_all)
            ]

            def grad_step(n, totals):
                c = cols(n, tile)
                new = []
                for dx in range(x_all):
                    r = slice(dx * capacity, (dx + 1) * capacity)
                    up_rows = jnp.dot(chosen_low[dx], ups[dx, :, c], preferred_element_type=f32)
                    grad_expert[r, c] = (weight_rows[dx] * up_rows).astype(bf16)
                    new.append(
                        totals[dx]
                        + jnp.sum(up_rows * out_rows[dx, own_slots(le), c].astype(f32), axis=1, keepdims=True)
                    )
                return tuple(new)

            totals = lax.fori_loop(
                0, width // tile, grad_step, tuple(jnp.zeros((capacity, 1), f32) for _ in range(x_all)),
                unroll=True,
            )
            store(2, grad_expert, grad_out_hbm, le).start()
            for dx in range(x_all):
                router_stage[dz, dx, pl.ds(le, 1), :] = jnp.sum(
                    jnp.where(chosen[dx], totals[dx], 0.0), axis=0, keepdims=True
                )

            def back_step(n, c0):
                ga = lax.dot_general(
                    grad_expert[...], down_w[le, cols(n, narrow), :], (((1,), (1,)), ((), ())),
                    preferred_element_type=f32,
                )
                gate = gate_up[:, cols(n, narrow)]
                c_up = pl.ds(pl.multiple_of(half + n * narrow, narrow), narrow)
                up = gate_up[:, c_up]
                sg = 1.0 / (1.0 + jnp.exp(-gate))
                grad_gate_up[:, cols(n, narrow)] = (ga * up * sg * (1.0 + gate * (1.0 - sg))).astype(bf16)
                grad_gate_up[:, c_up] = (ga * (gate * sg)).astype(bf16)
                return c0

            lax.fori_loop(0, half // narrow, back_step, 0, unroll=True)
            store(3, grad_gate_up, grad_gate_up_hbm, le).start()

            def row_step(n, c0):
                result = lax.dot_general(
                    grad_gate_up[...], gate_up_w[le, cols(n, narrow), :], (((1,), (1,)), ((), ())),
                    preferred_element_type=f32,
                )
                for dx in range(x_all):
                    r = slice(dx * capacity, (dx + 1) * capacity)
                    grad_rows[dx, own_slots(le), cols(n, narrow)] = result[r].astype(bf16)
                return c0

            lax.fori_loop(0, width // narrow, row_step, 0, unroll=True)
            events(pieces(4 * g + 2 * le), pieces(4 * g + 2 * le + 1))

            @pl.when((le == 0) & (g > 0))
            def _():
                for dx in range(mix_slots):
                    mix_copy(0, dx).wait()
                finish(group_at(g - 1), False)

            return inner

        assert local_experts == 2
        lax.fori_loop(0, local_experts, expert, 0)

        @pl.when(g < z_all - 1)
        def _():
            for load in load_upstream(group_at(g + 1)):
                load.start()

        def stages():
            for dx in range(1, x_all):
                p_sent(dx)

        pl.when(g > 0)(stages)
        for dx in range(x_all):
            weight = jnp.zeros(slot_col.shape, f32)
            mask = jnp.zeros(slot_col.shape, f32)
            lane = lax.broadcasted_iota(jnp.int32, prob.shape[1:], 1)
            for le in range(local_experts):
                spot = place_t_ref[dz, dx, :, le : le + 1]
                here = jnp.where(spot < 0.0, -1.0, spot + le * capacity) == slot_col
                p = jnp.sum(jnp.where(lane == e * local_experts + le, prob[dx], 0.0), axis=1, keepdims=True)
                weight = jnp.where(here, p, weight)
                mask = jnp.where(here, 1.0, mask)
            low = mask.astype(bf16)
            high = weight.astype(bf16)
            remainder = (weight - high.astype(f32)).astype(bf16)

            if dx >= mix_slots:
                mix_copy(0, dx).wait()

            def combine(n, c0):
                c = cols(n, tile)
                mix = jnp.dot(high, out_rows[dx, :, c], preferred_element_type=f32) + jnp.dot(
                    remainder, out_rows[dx, :, c], preferred_element_type=f32
                )
                grad = jnp.dot(low, grad_rows[dx, :, c], preferred_element_type=f32)
                mix_stage[dx % mix_slots, :, c] = mix.astype(bf16)
                if dx == 0:
                    own_part[dz, :, c] = grad.astype(bf16)
                else:
                    part_stage[dx - 1, :, c] = grad.astype(bf16)
                return c0

            lax.fori_loop(0, width // tile, combine, 0, unroll=True)
            for k in range(z_all):
                pl.when(dz == k)(mix_copy(k, dx).start)
            if dx > 0:
                for c in range(MOE_CHUNKS):
                    p_copy(dz, dx, c).start()
                r_copy(dz, dx).start()
            else:

                @pl.when(dz > 0)
                def _():
                    r_copy(dz, 0).start()

                @pl.when(dz == 0)
                def _():
                    grad_router_ref[e] = router_stage[0, 0]

        return carry

    lax.fori_loop(0, z_all, group, 0)
    for dx in range(mix_slots):
        mix_copy(0, dx).wait()
    finish(0, True)

    def total(c, carry):
        grad_ref[at(c), :] = own_part[0, at(c), :].astype(f32)
        for d in (1, 2, 3):
            q_copy(d, c).wait_recv()
            grad_ref[at(c), :] = grad_ref[at(c), :] + z_landed[d - 1, at(c), :].astype(f32)
        return carry

    lax.fori_loop(0, MOE_CHUNKS, total, 0)

    for c in column_copies:
        c.wait()
    for kind, buffer, hbm in (
        (0, rows, rows_hbm), (1, activated, activated_hbm), (2, grad_expert, grad_out_hbm),
        (3, grad_gate_up, grad_gate_up_hbm),
    ):
        pltpu.make_async_copy(buffer, hbm.at[0, 0], store_sem.at[kind]).wait()
    for dx in range(1, x_all):
        p_sent(dx)
    for d in range(1, z_all):
        whole = own_part.at[d]
        copy(whole, whole, qs.at[d - 1], qr.at[d - 1, 0], peer(-d, 0)).wait_send()
    for dz, dx in others:
        r_copy(dz, dx).wait_send()
        r_copy(dz, dx).wait_recv()

    def sent(c, carry):
        for d in range(1, z_all):
            z_copy(d, c).wait_send()
            for dx in range(1, x_all):
                f_copy(d, dx, c).wait_send()
        for d in range(1, x_all):
            x_copy(d, c).wait_send()
        return carry

    lax.fori_loop(0, MOE_CHUNKS, sent, 0)


def moe_layer(
    hidden, upstream_all, place, router_weight, gate_up_weight, down_weight, first, second, expert_group, shard_group,
    capacity, name_id,
):
    f32, bf16 = jnp.float32, jnp.bfloat16
    length, width = hidden.shape
    local_experts, _, twice = gate_up_weight.shape
    half = twice // 2
    experts_all = router_weight.shape[1]
    x_all = expert_group // 4
    count = x_all * capacity
    dma = pltpu.SemaphoreType.DMA
    x1 = max(x_all - 1, 1)
    place_t = place.transpose(0, 1, 3, 2)
    spare = (-local_experts) % 8
    place = jnp.pad(place, ((0, 0), (0, 0), (0, spare), (0, 0)), constant_values=-1.0)
    any_spec = pl.BlockSpec(memory_space=pl.ANY)
    vmem_spec = pl.BlockSpec(memory_space=pltpu.VMEM)
    out = pl.pallas_call(
        functools.partial(moe_kernel, (x_all, capacity, shard_group // 2)),
        out_shape=[
            jax.ShapeDtypeStruct((local_experts, 4, count, width), bf16),
            jax.ShapeDtypeStruct((local_experts, 4, count, half), bf16),
            jax.ShapeDtypeStruct((local_experts, 4, count, width), bf16),
            jax.ShapeDtypeStruct((local_experts, 4, count, twice), bf16),
            jax.ShapeDtypeStruct((length, width), f32),
            jax.ShapeDtypeStruct((expert_group, 8, length), f32),
            jax.ShapeDtypeStruct((2, shard_group, length, width // shard_group), bf16),
            jax.ShapeDtypeStruct((4, x_all, length, width), bf16),
            jax.ShapeDtypeStruct((4, x1, length, width), bf16),
        ]
        + [jax.ShapeDtypeStruct((length, width), bf16)] * (4 * x_all),
        in_specs=[any_spec, any_spec, vmem_spec, vmem_spec, vmem_spec, vmem_spec, any_spec, any_spec, any_spec, any_spec],
        out_specs=[any_spec] * 4 + [vmem_spec, vmem_spec] + [any_spec] * (3 + 4 * x_all),
        scratch_shapes=[
            pltpu.VMEM(gate_up_weight.shape, bf16),
            pltpu.VMEM(down_weight.shape, bf16),
            pltpu.VMEM((x_all, length, width), bf16),
            pltpu.VMEM((x_all, length, width), bf16),
            pltpu.VMEM((x_all, length, experts_all), f32),
            pltpu.VMEM((x_all, experts_all, length), f32),
            pltpu.VMEM((count, width), bf16),
            pltpu.VMEM((count, twice), f32),
            pltpu.VMEM((count, half), bf16),
            pltpu.VMEM((x_all, local_experts * capacity, width), bf16),
            pltpu.VMEM((count, width), bf16),
            pltpu.VMEM((count, twice), bf16),
            pltpu.VMEM((x_all, local_experts * capacity, width), bf16),
            pltpu.VMEM((min(2, x_all), length, width), bf16),
            pltpu.VMEM((x1, length, width), bf16),
            pltpu.VMEM((4, length, width), bf16),
            pltpu.VMEM((3, length, width), bf16),
            pltpu.VMEM((4, x_all, 8, length), f32),
            dma((2,)), dma, dma((2, x_all)), dma((4,)),
            dma((3, MOE_CHUNKS)), dma((3, MOE_CHUNKS)),
            dma((x1, MOE_CHUNKS)), dma((x1, MOE_CHUNKS)),
            dma((3, x1, MOE_CHUNKS)), dma((3, x1, MOE_CHUNKS)),
            dma((x1,)), dma((4, x1, MOE_CHUNKS)),
            dma((3,)), dma((3, MOE_CHUNKS)),
            dma((4, x_all)), dma((4, x_all)),
            dma((MOE_CHUNKS,)), dma((min(2, x_all),)),
            dma((2, shard_group - 1)), dma((2, shard_group - 1)), dma((2,)),
        ],
        compiler_params=pltpu.CompilerParams(
            collective_id=name_id, has_side_effects=True, vmem_limit_bytes=62 * 1024 * 1024
        ),
        cost_estimate=pl.CostEstimate(
            flops=12 * 4 * local_experts * count * width * twice, bytes_accessed=64 * 1024 * 1024,
            transcendentals=0,
        ),
    )(
        hidden, upstream_all, place, place_t, router_weight, router_weight.T, gate_up_weight, down_weight,
        first, second,
    )
    return out[:7], out[9:]


def start_kernel(
    dims, weight_hbm, upstream_hbm, router_hbm, gains_ref, tokens_ref, routes_ref, tiles_ref,
    full_hbm, ups_hbm, router_full_hbm, gains_full_ref, place_all_ref, hidden_ref, *sems,
):
    x_all, y_all = dims
    z_all, parts = 4, 4
    (own_sem, ys, yr, rs, rr, cs, cr, fs, fr, gs, gr, zs, zr, xs, xr, us, ur, ns, nr, ps, pr, ms, mr) = sems
    f32, bf16 = jnp.float32, jnp.bfloat16
    rows = weight_hbm.shape[0]
    length = tokens_ref.shape[0]
    piece = rows // 8
    chunk = length // parts
    e = lax.axis_index("expert")
    s = lax.axis_index("shard")
    z, x = e // x_all, lax.rem(e, x_all)
    y, core = s // 2, lax.rem(s, 2)
    parity = lax.rem(z, 2)

    def expert_peer(dz, dx):
        return {"expert": lax.rem(z + dz, z_all) * x_all + lax.rem(x + dx, x_all)}

    def shard_peer(dy, flip):
        return {"shard": lax.rem(y + dy, y_all) * 2 + lax.rem(core + flip, 2)}

    beside = {"expert": (z + 1 - 2 * parity) * x_all + x}
    partner = shard_peer(0, 1)
    far = [(dz, dx) for dz in range(z_all) for dx in range(x_all) if dz + dx > 0]
    near = [(dy, flip) for dy in range(y_all) for flip in range(2) if dy + flip > 0]

    def copy(src, dst, send, recv, to):
        return pltpu.make_async_remote_copy(
            src_ref=src, dst_ref=dst, send_sem=send, recv_sem=recv, device_id=to,
            device_id_type=pl.DeviceIdType.MESH,
        )

    def piece_of(i, who):
        return jnp.where(i < 2, 4 + 2 * who + i, i - 2)

    def span(owner, k):
        return pl.ds(pl.multiple_of(owner * rows + k * piece, piece), piece)

    def y_copy(dy, i):
        k = piece_of(i, parity)
        src = weight_hbm.at[pl.ds(pl.multiple_of(k * piece, piece), piece)]
        return copy(src, full_hbm.at[span(s, k)], ys.at[dy - 1, i], yr.at[dy - 1, i], shard_peer(dy, 0))

    def owner(dy):
        return lax.rem(y - dy + y_all, y_all) * 2 + core

    def relay(dy, i):
        here = full_hbm.at[span(owner(dy), 4 + 2 * parity + i)]
        return copy(here, here, rs.at[dy - 1, i], rr.at[dy - 1, i], beside)

    def core_y(dy, i):
        here = full_hbm.at[span(owner(dy), piece_of(i, parity))]
        return copy(here, here, cs.at[dy - 1, i], cr.at[dy - 1, i], partner)

    def core_r(dy, i):
        here = full_hbm.at[span(owner(dy), 4 + 2 * (1 - parity) + i)]
        return copy(here, here, fs.at[dy - 1, i], fr.at[dy - 1, i], partner)

    whole = pl.ds(pl.multiple_of(s * rows, rows), rows)
    core_own = copy(weight_hbm, full_hbm.at[whole], gs, gr, partner)

    def at(c):
        return pl.ds(pl.multiple_of(c * chunk, chunk), chunk)

    def z_copy(d, c):
        return copy(upstream_hbm.at[at(c)], ups_hbm.at[d, 0, at(c)], zs.at[d - 1, c], zr.at[d - 1, c], expert_peer(d, 0))

    def x_copy(d):
        return copy(upstream_hbm, ups_hbm.at[0, d], xs.at[d - 1], xr.at[d - 1], expert_peer(0, d))

    def u_copy(dz, dx, c):
        return copy(
            ups_hbm.at[dz, 0, at(c)], ups_hbm.at[dz, dx, at(c)],
            us.at[dz - 1, dx - 1, c], ur.at[dz - 1, dx - 1, c], expert_peer(0, dx),
        )

    def router_copy(n, p):
        return copy(router_hbm, router_full_hbm.at[whole], ns.at[n], nr.at[n], shard_peer(*p))

    def gains_copy(n, p):
        return copy(gains_ref, gains_full_ref.at[s], ms.at[n], mr.at[n], shard_peer(*p))

    def place_copy(n, p):
        return copy(place_all_ref.at[0, 0], place_all_ref.at[p[0], p[1]], ps.at[n], pr.at[n], expert_peer(*p))

    barrier = pltpu.get_barrier_semaphore()
    peers = [expert_peer(*p) for p in far] + [shard_peer(*p) for p in near]
    for peer in peers:
        pl.semaphore_signal(barrier, inc=1, device_id=peer, device_id_type=pl.DeviceIdType.MESH)
    pl.semaphore_wait(barrier, len(peers))

    own = [
        pltpu.make_async_copy(weight_hbm, full_hbm.at[whole], own_sem.at[0]),
        pltpu.make_async_copy(upstream_hbm, ups_hbm.at[0, 0], own_sem.at[1]),
        pltpu.make_async_copy(router_hbm, router_full_hbm.at[whole], own_sem.at[2]),
    ]
    for n, p in enumerate(near):
        gains_copy(n, p).start()
        router_copy(n, p).start()
    for i in range(2):
        for dy in range(1, y_all):
            y_copy(dy, i).start()
    for d in range(1, x_all):
        x_copy(d).start()
    for d in (1, 3, 2):
        for c in range(parts):
            z_copy(d, c).start()
    core_own.start()
    for o in own:
        o.start()

    count = place_all_ref.shape[2]
    ids = lax.broadcasted_iota(jnp.int32, (count, length), 0)
    chosen = jnp.zeros((count, length), f32)
    for k in range(TOP):
        chosen = jnp.where(routes_ref[k : k + 1, :] == ids, 1.0, chosen)
    before = lax.broadcasted_iota(jnp.int32, (length, length), 0)
    after = lax.broadcasted_iota(jnp.int32, (length, length), 1)
    earlier = jnp.where(before < after, 1.0, 0.0).astype(bf16)
    rank = jnp.dot(chosen.astype(bf16), earlier, preferred_element_type=f32)
    limit = (tiles_ref[...] * TILE).astype(f32)
    place_all_ref[0, 0] = jnp.where((chosen > 0.5) & (rank < limit), rank, -1.0)
    for n, p in enumerate(far):
        place_copy(n, p).start()

    gains_full_ref[s] = gains_ref[...]
    for n, p in enumerate(near):
        gains_copy(n, p).wait_recv()
    keep = gains_ref.shape[1]
    tall = 64

    def norm(t, carry):
        r = pl.ds(pl.multiple_of(t * tall, tall), tall)
        values = tokens_ref[r, :].astype(f32)
        scale = lax.rsqrt(jnp.mean(values * values, axis=1, keepdims=True) + epsilon)
        for j in range(2 * y_all):
            c = slice(j * keep, (j + 1) * keep)
            gain = gains_full_ref[j, 0:1, :].astype(f32)
            hidden_ref[r, c] = (values[:, c] * scale * gain).astype(bf16)
        return carry

    lax.fori_loop(0, length // tall, norm, 0)

    def forward(events):
        for d, c in events:
            z_copy(d, c).wait_recv()
            for dx in range(1, x_all):
                u_copy(d, dx, c).start()

    order = {
        0: [(1, 0)], 1: [(1, 1), (1, 2)], 2: [(1, 3), (3, 0), (3, 1)], 3: [(3, 2), (3, 3), (2, 0)],
        4: [(2, 1), (2, 2), (2, 3)], 5: [],
    }
    for i in range(6):
        for dy in range(1, y_all):
            y_copy(dy, i).wait_recv()
            if i < 2:
                relay(dy, i).start()
            core_y(dy, i).start()
            if i < 4:
                y_copy(dy, i + 2).start()
        forward(order[i])
        if i in (3, 4):
            for dy in range(1, y_all):
                here = full_hbm.at[span(owner(dy), 4 + 2 * (1 - parity) + i - 3)]
                copy(here, here, rs.at[dy - 1, i - 3], rr.at[dy - 1, i - 3], beside).wait_recv()
                core_r(dy, i - 3).start()

    for o in own:
        o.wait()
    core_own.wait()
    for n, p in enumerate(near):
        gains_copy(n, p).wait_send()
        router_copy(n, p).wait()
    for n, p in enumerate(far):
        place_copy(n, p).wait()
    for d in range(1, x_all):
        x_copy(d).wait()
    for dy in range(1, y_all):
        for i in range(6):
            y_copy(dy, i).wait_send()
            core_y(dy, i).wait()
        for i in range(2):
            relay(dy, i).wait_send()
            core_r(dy, i).wait()
    for d in range(1, z_all):
        for c in range(parts):
            z_copy(d, c).wait_send()
            for dx in range(1, x_all):
                u_copy(d, dx, c).wait()


def start_layer(weight, upstream, router, gains, tokens, routes, tile_counts, expert_group, shard_group, name_id):
    f32, bf16 = jnp.float32, jnp.bfloat16
    length, width = tokens.shape
    x_all, y_all = expert_group // 4, shard_group // 2
    experts_all = tile_counts.shape[0]
    dma = pltpu.SemaphoreType.DMA
    y1, x1 = max(y_all - 1, 1), max(x_all - 1, 1)
    any_spec = pl.BlockSpec(memory_space=pl.ANY)
    vmem_spec = pl.BlockSpec(memory_space=pltpu.VMEM)
    return pl.pallas_call(
        functools.partial(start_kernel, (x_all, y_all)),
        out_shape=[
            jax.ShapeDtypeStruct((weight.shape[0] * shard_group, weight.shape[1]), bf16),
            jax.ShapeDtypeStruct((4, x_all, length, width), bf16),
            jax.ShapeDtypeStruct((router.shape[0] * shard_group, router.shape[1]), bf16),
            jax.ShapeDtypeStruct((shard_group, *gains.shape), bf16),
            jax.ShapeDtypeStruct((4, x_all, experts_all, length), f32),
            jax.ShapeDtypeStruct((length, width), bf16),
        ],
        in_specs=[any_spec] * 3 + [vmem_spec] * 4,
        out_specs=[any_spec] * 3 + [vmem_spec] * 3,
        scratch_shapes=[
            dma((3,)),
            dma((y1, 6)), dma((y1, 6)),
            dma((y1, 2)), dma((y1, 2)),
            dma((y1, 6)), dma((y1, 6)),
            dma((y1, 2)), dma((y1, 2)),
            dma, dma,
            dma((3, 4)), dma((3, 4)),
            dma((x1,)), dma((x1,)),
            dma((3, x1, 4)), dma((3, x1, 4)),
            dma((shard_group - 1,)), dma((shard_group - 1,)),
            dma((expert_group - 1,)), dma((expert_group - 1,)),
            dma((shard_group - 1,)), dma((shard_group - 1,)),
        ],
        compiler_params=pltpu.CompilerParams(
            collective_id=name_id, has_side_effects=True, vmem_limit_bytes=32 * 1024 * 1024
        ),
        cost_estimate=pl.CostEstimate(
            flops=16 * length * width, bytes_accessed=64 * 1024 * 1024, transcendentals=0
        ),
    )(weight, upstream, router, gains, tokens, routes.T, tile_counts[:, None])


def body(
    tokens,
    cotangent,
    segments,
    routes,
    tile_counts,
    norm_one,
    norm_query,
    norm_key,
    norm_two,
    qkv_weight,
    out_weight,
    router_weight,
    gate_up_weight,
    down_weight,
):
    f32, bf16 = jnp.float32, jnp.bfloat16
    length, model_width = tokens.shape
    experts_all = tile_counts.shape[0]
    local_experts = gate_up_weight.shape[0]
    expert_group = lax.axis_size("expert")
    shard_group = lax.axis_size("shard")
    capacity = length * TOP // (experts_all * TILE) * TILE
    score_scale = HEAD_DIM ** (-0.5)
    own_expert = lax.axis_index("expert")
    own_shard = lax.axis_index("shard")
    z_all = z_size(expert_group)
    x_all = expert_group // z_all

    gain_rows = jnp.stack([norm_one, norm_query, norm_key, norm_two])
    gain_rows = jnp.pad(gain_rows, ((0, 12), (0, 0)))
    qkv_full, upstream_all, router_full, gains, place_all, hidden_one = start_layer(
        qkv_weight,
        cotangent,
        router_weight,
        gain_rows,
        tokens,
        routes,
        tile_counts,
        expert_group,
        shard_group,
        3,
    )
    out_own, gains = lax.optimization_barrier((out_weight, gains))
    out_full = lax.all_gather(out_own, "shard", axis=0, tiled=True)
    gains = gains.transpose(1, 0, 2).reshape(gains.shape[1], model_width).astype(f32)
    gain_one, gain_query, gain_key, gain_two = gains[0], gains[1], gains[2], gains[3]
    place_own = lax.dynamic_slice_in_dim(
        place_all, own_expert * local_experts, local_experts, axis=2
    )
    position = jnp.arange(length, dtype=jnp.int32)

    inputs = tokens.astype(f32)
    _, first_pull = jax.vjp(rms_scale, inputs, gain_one)
    projected = jnp.dot(hidden_one, qkv_full, preferred_element_type=f32)
    cosine, sine_table = rotary_tables(length)

    def query_key_local(raw_query, raw_key, query_gain, key_gain):
        return query_key(raw_query, raw_key, query_gain, key_gain, cosine, sine_table)

    rotated, rotary_pull = jax.vjp(
        query_key_local,
        projected[:, :model_width],
        projected[:, model_width : 2 * model_width],
        gain_query,
        gain_key,
    )
    query_low = rotated[0].astype(bf16)
    key_low = rotated[1].astype(bf16)
    value_low = projected[:, 2 * model_width :].astype(bf16).reshape(length, HEADS, HEAD_DIM)
    allowed = (position[:, None] >= position[None, :]) & (
        segments[0][:, None] == segments[0][None, :]
    )
    masked = jnp.where(
        allowed[None],
        jnp.einsum("qhd,khd->hqk", query_low, key_low, preferred_element_type=f32) * score_scale,
        -1e30,
    )
    probs = softmax_rows(masked)
    probs_low = probs.astype(bf16)
    attended_low = (
        jnp.einsum("hqk,khd->qhd", probs_low, value_low, preferred_element_type=f32)
        .reshape(length, model_width)
        .astype(bf16)
    )
    middle = inputs + jnp.dot(attended_low, out_full, preferred_element_type=f32)
    scaled_two, second_pull = jax.vjp(rms_scale, middle, gain_two)
    hidden_two = scaled_two.astype(bf16)
    router = softmax_rows(jnp.dot(hidden_two, router_full, preferred_element_type=f32))
    row_count = expert_group * capacity
    done, mixture_parts = moe_layer(
        hidden_two,
        upstream_all,
        place_own,
        router_full,
        gate_up_weight,
        down_weight,
        attended_low,
        hidden_one,
        expert_group,
        shard_group,
        capacity,
        2,
    )
    columns = done[6].reshape(2, shard_group * length, -1).swapaxes(1, 2)
    expert_rows, activated, grad_expert, grad_gate_up_low = (
        a.reshape(local_experts, row_count, a.shape[-1]) for a in done[:4]
    )
    grad_rows_sum = done[4]
    grad_router = done[5][:, :local_experts].reshape(experts_all, length).T
    parts = dict(enumerate(mixture_parts))

    def slot(values, *names):
        held = lax.optimization_barrier((values, [parts[n] for n in names]))
        parts.update(zip(names, held[1], strict=True))
        return held[0]

    def group(dz):
        return [dz * x_all + dx for dx in range(x_all)]

    upstream = cotangent.astype(f32)
    grad_logits = (
        router * (grad_router - jnp.sum(router * grad_router, axis=-1, keepdims=True))
    ).astype(bf16)
    grad_hidden_two = grad_rows_sum + jnp.einsum(
        "te,de->td", grad_logits, router_full, preferred_element_type=f32
    )
    grad_middle_norm, grad_gain_two = second_pull(grad_hidden_two)
    grad_middle = upstream + grad_middle_norm
    two = sum_over_x(parts, 2, expert_group).astype(bf16)
    grad_middle, expert_rows, two = slot((grad_middle, expert_rows, two), *group(1))
    halves = [two[: length // 2], two[length // 2 :]]
    halves[0] = back_along_z(halves[0], 2, expert_group)
    one = sum_over_x(parts, 1, expert_group).astype(bf16)
    grad_gate_up_full = jnp.einsum(
        "erd,erf->edf", expert_rows, grad_gate_up_low, preferred_element_type=f32
    ).astype(bf16)
    grad_middle, grad_gate_up_full, activated, halves, one = slot(
        (grad_middle, grad_gate_up_full, activated, halves, one), *group(3)
    )
    grad_gate_up_weight = lax.psum_scatter(
        grad_gate_up_full, "shard", scatter_dimension=1, tiled=True
    ).astype(f32)
    halves[1] = back_along_z(halves[1], 2, expert_group)
    three = sum_over_x(parts, 3, expert_group).astype(bf16)
    grad_down_full = jnp.einsum(
        "erf,erd->efd", activated, grad_expert, preferred_element_type=f32
    ).astype(bf16)
    grad_middle, grad_down_full, halves, one, three = slot(
        (grad_middle, grad_down_full, halves, one, three), *group(0)
    )
    grad_down_weight = lax.psum_scatter(
        grad_down_full, "shard", scatter_dimension=2, tiled=True
    ).astype(f32)
    one = back_along_z(one, 1, expert_group)
    here = sum_over_x(parts, 0, expert_group)
    grad_branch_low = grad_middle.astype(bf16)
    grad_attended_low = (
        jnp.einsum("te,de->td", grad_branch_low, out_full, preferred_element_type=f32)
        .astype(bf16)
        .reshape(length, HEADS, HEAD_DIM)
    )
    grad_probs = jnp.einsum(
        "qhd,khd->hqk", grad_attended_low, value_low, preferred_element_type=f32
    )
    grad_scores_low = (
        probs * (grad_probs - jnp.sum(probs * grad_probs, axis=-1, keepdims=True))
    ).astype(bf16)
    grad_scores_low, one, here, three = slot((grad_scores_low, one, here, three))
    three = back_along_z(three, 3, expert_group)
    grad_queries = (
        jnp.einsum("hqk,khd->qhd", grad_scores_low, key_low, preferred_element_type=f32)
        * score_scale
    )
    grad_keys = (
        jnp.einsum("hqk,qhd->khd", grad_scores_low, query_low, preferred_element_type=f32)
        * score_scale
    )
    grad_values = jnp.einsum(
        "hqk,qhd->khd", probs_low, grad_attended_low, preferred_element_type=f32
    )
    grad_raw_query, grad_raw_key, grad_gain_query, grad_gain_key = rotary_pull(
        (grad_queries, grad_keys)
    )
    grad_projected_low = jnp.concatenate(
        [grad_raw_query, grad_raw_key, grad_values.reshape(length, model_width)], axis=-1
    ).astype(bf16)
    grad_hidden_one = jnp.einsum(
        "te,de->td", grad_projected_low, qkv_full, preferred_element_type=f32
    )
    grad_inputs_norm, grad_gain_one = first_pull(grad_hidden_one)
    grad_tokens = grad_middle + grad_inputs_norm

    grad_router_part = jnp.einsum("td,te->ed", hidden_two, grad_logits, preferred_element_type=f32)
    small = jnp.concatenate(
        [
            grad_router_part,
            jnp.stack([grad_gain_one, grad_gain_query, grad_gain_key, grad_gain_two]),
            jnp.zeros((-(experts_all + 4) % 8, model_width), f32),
        ],
        axis=0,
    )
    keep = norm_one.shape[0]
    small = jnp.stack(
        [
            lax.dynamic_slice_in_dim(
                small,
                (((own_shard // 2 + dy) % (shard_group // 2)) * 2 + (own_shard % 2 + flip) % 2) * keep,
                keep,
                axis=1,
            )
            for dy in range(shard_group // 2)
            for flip in range(2)
        ]
    )

    grads_low = jnp.concatenate([grad_branch_low, grad_projected_low], axis=1)
    grads_low, three = slot((grads_low, three))
    mixture = sum((a.astype(f32) for a in (one, jnp.concatenate(halves), three)), here)
    block_out = (middle + mixture).astype(bf16)
    grad_rows_kept, small = summed_rows(
        columns, grads_low, model_width, small, expert_group, shard_group, z_all, 256, 2, 1
    )
    grad_out_weight = grad_rows_kept[:, :model_width].astype(f32)
    grad_qkv_weight = grad_rows_kept[:, model_width:].astype(f32)
    return (
        block_out,
        grad_tokens,
        small[experts_all],
        small[experts_all + 1],
        small[experts_all + 2],
        small[experts_all + 3],
        grad_qkv_weight,
        grad_out_weight,
        small[:experts_all].T,
        grad_gate_up_weight,
        grad_down_weight,
    )


def solution(mesh):
    return jax.shard_map(
        body,
        mesh=mesh,
        in_specs=(
            P(("expert", "shard"), None),
            P(("expert", "shard"), None),
            P(("expert", "shard"), None),
            P(("expert", "shard"), None),
            P(),
            P("shard"),
            P("shard"),
            P("shard"),
            P("shard"),
            P("shard", None),
            P("shard", None),
            P("shard", None),
            P("expert", None, None),
            P("expert", None, None),
        ),
        out_specs=(
            P(("expert", "shard"), None),
            P(("expert", "shard"), None),
            P("shard"),
            P("shard"),
            P("shard"),
            P("shard"),
            P("shard", None),
            P("shard", None),
            P("shard", None),
            P("expert", "shard", None),
            P("expert", None, "shard"),
        ),
        check_vma=False,
    )
```

```python
import functools

import jax
import jax.numpy as jnp
from jax import lax
from jax.experimental import pallas as pl
from jax.experimental.pallas import tpu as pltpu
from jax.sharding import PartitionSpec as P

HEADS = 16
HEAD_DIM = 128
TOP = 8
TILE = 8


epsilon = 1e-05
rope_base = 10000.0


def rms_scale(values, scale_gain):
    return (
        values * lax.rsqrt(jnp.mean(values * values, axis=-1, keepdims=True) + epsilon) * scale_gain
    )


def rotary_tables(length):
    half_dim = HEAD_DIM // 2
    position = jnp.arange(length, dtype=jnp.float32)[:, None]
    frequency = rope_base ** (-jnp.arange(half_dim, dtype=jnp.float32) * 2.0 / HEAD_DIM)
    angles = position * frequency[None, :]
    angles = jnp.concatenate([angles, angles], axis=-1)
    return (jnp.cos(angles)[:, None, :], jnp.sin(angles)[:, None, :])


def rotate(vectors, cosine, sine_table):
    half_dim = vectors.shape[-1] // 2
    turned = jnp.concatenate([-vectors[..., half_dim:], vectors[..., :half_dim]], axis=-1)
    return vectors * cosine + turned * sine_table


def query_key(raw_query, raw_key, query_gain, key_gain, cosine, sine_table):
    length = raw_query.shape[0]
    queries = rms_scale(raw_query, query_gain).reshape(length, HEADS, HEAD_DIM)
    keys_rot = rms_scale(raw_key, key_gain).reshape(length, HEADS, HEAD_DIM)
    return (rotate(queries, cosine, sine_table), rotate(keys_rot, cosine, sine_table))


def swiglu(gate_up):
    half_dim = gate_up.shape[-1] // 2
    gate_part = gate_up[..., :half_dim]
    return gate_part / (1.0 + jnp.exp(-gate_part)) * gate_up[..., half_dim:]


def softmax_rows(logits):
    largest = jnp.max(logits, axis=-1, keepdims=True)
    raised = jnp.exp(logits - largest)
    return raised / jnp.sum(raised, axis=-1, keepdims=True)


def z_size(expert_group):
    return 4 if expert_group % 4 == 0 else 1


def shift(values, expert_group, dz, dx):
    z_all = z_size(expert_group)
    x_all = expert_group // z_all
    pairs = [
        (i, ((i // x_all + dz) % z_all) * x_all + (i % x_all + dx) % x_all)
        for i in range(expert_group)
    ]
    return lax.ppermute(values, "expert", pairs)


def gather_expert(block, expert_group):
    z_all = z_size(expert_group)
    x_all = expert_group // z_all
    rows = [block] + [shift(block, expert_group, dz, 0) for dz in range(1, z_all)]
    return [
        rows[dz] if dx == 0 else shift(rows[dz], expert_group, 0, dx)
        for dz in range(z_all)
        for dx in range(x_all)
    ]


def sum_over_x(parts, dz, expert_group):
    x_all = expert_group // z_size(expert_group)
    total = parts[dz * x_all].astype(jnp.float32)
    for dx in range(1, x_all):
        total = total + shift(parts[dz * x_all + dx], expert_group, 0, -dx).astype(jnp.float32)
    return total


def back_along_z(total, dz, expert_group):
    return shift(total, expert_group, -dz, 0)


def tail_kernel(
    dims, grads_ref, columns_ref, small_ref, out_ref, small_out_ref,
    gall, xsend, xrecv, zsend, zrecv, acc, fin, group_small, own_small, all_small, *sems
):
    steps, width, x_all, z_all, y_all, lag, first_steps = dims
    (gs_s, gs_r, es_s, es_r) = sems[14:]
    (y_s, y_r, core_s, core_r, fwd_s, fwd_r, x_s, x_r, z_s, z_r, zb_s, zb_r, xb_s, xb_r) = sems[:14]
    f32, bf16 = jnp.float32, jnp.bfloat16
    length = grads_ref.shape[0]
    rows = columns_ref.shape[1]
    block = rows // (x_all * z_all)
    half = z_all * block
    e = lax.axis_index("expert")
    s = lax.axis_index("shard")
    z, x = e // x_all, lax.rem(e, x_all)
    y, core = s // 2, lax.rem(s, 2)

    def y_peer(d):
        return {"shard": lax.rem(y + d, y_all) * 2 + core}

    partner = {"shard": y * 2 + (1 - core)}

    def x_peer(d):
        return {"expert": z * x_all + lax.rem(x + d, x_all)}

    def z_peer(d):
        return {"expert": lax.rem(z + d, z_all) * x_all + x}

    def copy(src, dst, send, recv, peer):
        return pltpu.make_async_remote_copy(
            src_ref=src, dst_ref=dst, send_sem=send, recv_sem=recv, device_id=peer,
            device_id_type=pl.DeviceIdType.MESH,
        )

    def cols(c):
        return pl.ds(pl.multiple_of(c * width, width), width)

    def y_copy(d, c):
        return copy(grads_ref.at[:, cols(c)], gall.at[2 * d - 1, c], y_s.at[d - 1], y_r.at[d - 1, c], y_peer(d))

    def core_copy(c):
        return copy(grads_ref.at[:, cols(c)], gall.at[0, c], core_s.at[0], core_r.at[c], partner)

    def fwd_copy(d, c):
        return copy(gall.at[2 * d - 1, c], gall.at[2 * d, c], fwd_s.at[d - 1], fwd_r.at[d - 1, c], partner)

    def x_copy(d, c):
        return copy(xsend.at[d - 1, c], xrecv.at[d - 1, c], x_s.at[d - 1], x_r.at[d - 1, c], x_peer(d))

    def z_copy(d, c):
        return copy(zsend.at[d - 1, c], zrecv.at[d - 1, c], z_s.at[d - 1], z_r.at[d - 1, c], z_peer(d))

    def zb_copy(d, c):
        here = fin.at[c, pl.ds(pl.multiple_of((x * z_all + z) * block, block), block)]
        return copy(here, here, zb_s.at[d - 1], zb_r.at[d - 1, c], z_peer(d))

    def xb_copy(d, c):
        here = fin.at[c, pl.ds(pl.multiple_of(x * half, half), half)]
        return copy(here, here, xb_s.at[d - 1], xb_r.at[d - 1, c], x_peer(d))

    near = [(d, flip) for d in range(y_all) for flip in range(2) if d + flip > 0]
    far = [(dz, dx) for dz in range(z_all) for dx in range(x_all) if dz + dx > 0]

    def near_peer(d, flip):
        return {"shard": lax.rem(y + d, y_all) * 2 + lax.rem(core + flip, 2)}

    def far_peer(dz, dx):
        return {"expert": lax.rem(z + dz, z_all) * x_all + lax.rem(x + dx, x_all)}

    def near_small(d, flip):
        j = 2 * d + flip
        return copy(small_ref.at[j], group_small.at[j - 1], gs_s.at[j - 1], gs_r.at[j - 1], near_peer(d, flip))

    def far_small(dz, dx):
        i = dz * x_all + dx
        return copy(own_small, all_small.at[i - 1], es_s.at[i - 1], es_r.at[i - 1], far_peer(dz, dx))

    barrier = pltpu.get_barrier_semaphore()
    peers = [near_peer(*p) for p in near] + [far_peer(*p) for p in far]
    for peer in peers:
        pl.semaphore_signal(barrier, inc=1, device_id=peer, device_id_type=pl.DeviceIdType.MESH)
    pl.semaphore_wait(barrier, len(peers))

    for p in near:
        near_small(*p).start()

    def first(c, carry):
        for d in range(1, y_all):
            y_copy(d, c).start()
        core_copy(c).start()
        return carry

    lax.fori_loop(0, steps, first, 0)
    slots = acc.shape[0]

    def step(t, carry):
        def stage(k, body):
            c = t - k * lag
            pl.when((c >= 0) & (c < steps))(lambda: body(c))

        @functools.partial(stage, 5)
        def _(c):
            for d in range(1, x_all):
                xb_copy(d, c).wait_recv()
            out_ref[:, cols(c)] = fin[c]

        @functools.partial(stage, 4)
        def _(c):
            for d in range(1, z_all):
                zb_copy(d, c).wait_recv()
            for d in range(1, x_all):
                xb_copy(d, c).start()

        @functools.partial(stage, 3)
        def _(c):
            slot = lax.rem(c, slots)
            total = acc[slot, pl.ds(pl.multiple_of(z * block, block), block), :]
            for d in range(1, z_all):
                z_copy(d, c).wait_recv()
                total = total + zrecv[d - 1, c].astype(f32)
            fin[c, pl.ds(pl.multiple_of((x * z_all + z) * block, block), block), :] = total.astype(bf16)
            for d in range(1, z_all):
                zb_copy(d, c).start()

        @functools.partial(stage, 2)
        def _(c):
            slot = lax.rem(c, slots)
            total = acc[slot]
            for d in range(1, x_all):
                x_copy(d, c).wait_recv()
                total = total + xrecv[d - 1, c].astype(f32)
            acc[slot] = total
            for d in range(1, z_all):
                there = lax.rem(z + d, z_all)
                zsend[d - 1, c] = acc[slot, pl.ds(pl.multiple_of(there * block, block), block), :].astype(bf16)
                z_copy(d, c).start()

        @functools.partial(stage, 1)
        def _(c):
            core_copy(c).wait_recv()
            for d in range(1, y_all):
                fwd_copy(d, c).wait_recv()
            kind = (c >= first_steps).astype(jnp.int32)
            others = gall[:, c].reshape((2 * y_all - 1) * length, width)
            mine = grads_ref[:, cols(c)]

            def product(there):
                at = pl.ds(pl.multiple_of(there * half, half), half)
                return jnp.dot(columns_ref[kind, at, :length], mine, preferred_element_type=f32) + jnp.dot(
                    columns_ref[kind, at, length:], others, preferred_element_type=f32
                )

            for d in range(1, x_all):
                xsend[d - 1, c] = product(lax.rem(x + d, x_all)).astype(bf16)
                x_copy(d, c).start()
            acc[lax.rem(c, slots)] = product(x)

        @functools.partial(stage, 0)
        def _(c):
            for d in range(1, y_all):
                y_copy(d, c).wait_recv()
                fwd_copy(d, c).start()

        @pl.when(t == 2)
        def _():
            total = small_ref[0]
            for j, p in enumerate(near):
                near_small(*p).wait_recv()
                total = total + group_small[j]
            own_small[...] = total
            for p in far:
                far_small(*p).start()

        return carry

    lax.fori_loop(0, steps + 5 * lag, step, 0)
    total = own_small[...]
    for i, p in enumerate(far):
        far_small(*p).wait_recv()
        total = total + all_small[i]
    small_out_ref[...] = total
    for p in near:
        near_small(*p).wait_send()
    for p in far:
        far_small(*p).wait_send()

    for d in range(1, y_all):
        copy(grads_ref, grads_ref, y_s.at[d - 1], y_r.at[d - 1, 0], y_peer(d)).wait_send()
        whole = gall.at[2 * d - 1]
        copy(whole, whole, fwd_s.at[d - 1], fwd_r.at[d - 1, 0], partner).wait_send()
    copy(grads_ref, grads_ref, core_s.at[0], core_r.at[0], partner).wait_send()
    for d in range(1, x_all):
        whole = xsend.at[d - 1]
        copy(whole, whole, x_s.at[d - 1], x_r.at[d - 1, 0], x_peer(d)).wait_send()
        copy(whole, whole, xb_s.at[d - 1], xb_r.at[d - 1, 0], x_peer(d)).wait_send()
    for d in range(1, z_all):
        whole = zsend.at[d - 1]
        copy(whole, whole, z_s.at[d - 1], z_r.at[d - 1, 0], z_peer(d)).wait_send()
        copy(whole, whole, zb_s.at[d - 1], zb_r.at[d - 1, 0], z_peer(d)).wait_send()


def summed_rows(columns, grads, first_total, small, expert_group, shard_group, z_all, width, lag, name_id):
    x_all, y_all = expert_group // z_all, shard_group // 2
    length, total = grads.shape
    rows = columns.shape[1]
    steps = total // width
    block = rows // expert_group
    half = z_all * block
    bf16 = jnp.bfloat16
    dma = pltpu.SemaphoreType.DMA
    n1 = max(y_all - 1, 1)
    x1 = max(x_all - 1, 1)
    z1 = max(z_all - 1, 1)
    slots = min(steps, 2 * lag + 1)
    return pl.pallas_call(
        functools.partial(tail_kernel, (steps, width, x_all, z_all, y_all, lag, first_total // width)),
        out_shape=[
            jax.ShapeDtypeStruct((rows, total), bf16),
            jax.ShapeDtypeStruct(small.shape[1:], jnp.float32),
        ],
        in_specs=[pl.BlockSpec(memory_space=pltpu.VMEM)] * 3,
        out_specs=[pl.BlockSpec(memory_space=pltpu.VMEM)] * 2,
        scratch_shapes=[
            pltpu.VMEM((shard_group - 1, steps, length, width), bf16),
            pltpu.VMEM((x1, steps, half, width), bf16),
            pltpu.VMEM((x1, steps, half, width), bf16),
            pltpu.VMEM((z1, steps, block, width), bf16),
            pltpu.VMEM((z1, steps, block, width), bf16),
            pltpu.VMEM((slots, half, width), jnp.float32),
            pltpu.VMEM((steps, rows, width), bf16),
            pltpu.VMEM((shard_group - 1, *small.shape[1:]), jnp.float32),
            pltpu.VMEM(small.shape[1:], jnp.float32),
            pltpu.VMEM((expert_group - 1, *small.shape[1:]), jnp.float32),
            dma((n1,)), dma((n1, steps)),
            dma((1,)), dma((steps,)),
            dma((n1,)), dma((n1, steps)),
            dma((x1,)), dma((x1, steps)),
            dma((z1,)), dma((z1, steps)),
            dma((z1,)), dma((z1, steps)),
            dma((x1,)), dma((x1, steps)),
            dma((shard_group - 1,)), dma((shard_group - 1,)),
            dma((expert_group - 1,)), dma((expert_group - 1,)),
        ],
        compiler_params=pltpu.CompilerParams(
            collective_id=name_id, has_side_effects=True, vmem_limit_bytes=60 * 1024 * 1024
        ),
        cost_estimate=pl.CostEstimate(
            flops=2 * rows * length * shard_group * total, bytes_accessed=16 * 1024 * 1024, transcendentals=0
        ),
    )(grads, columns, small)


MOE_CHUNKS = 4


def moe_kernel(
    dims, hidden_hbm, upstream_hbm, place_ref, place_t_ref, router_ref, router_t_ref, gate_up_hbm, down_hbm,
    first_hbm, second_hbm, rows_hbm, activated_hbm, grad_out_hbm, grad_gate_up_hbm, grad_ref, grad_router_ref, columns_hbm, grad_up_w_hbm, grad_down_w_hbm,
    came_hbm, found_hbm, summed_hbm,
    *rest,
):
    x_all, capacity, y_all = dims
    mixture_hbm = rest[: 4 * x_all]
    (
    gate_up_w, down_w, hid, ups, prob, prob_t, rows, gate_up, activated, out_rows, grad_expert, grad_gate_up, grad_rows,
    mix_stage, part_stage, own_part, z_landed, router_stage,
    w_sem, own_sem, load_sem, store_sem, zs, zr, xs, xr, fs, fr, ps, pr, qs, qr, rs, rr, lsem, mix_sem, cs, cr, own_c, back_sem, out_sem, ms, mr,
    ) = rest[4 * x_all :]
    z_all = 4
    f32, bf16 = jnp.float32, jnp.bfloat16
    length, width = hidden_hbm.shape
    local_experts, _, twice = gate_up_w.shape
    half = twice // 2
    tile = min(512, half)
    narrow = min(256, half)
    chunk = length // MOE_CHUNKS
    count = x_all * capacity
    e = lax.axis_index("expert")
    z, x = e // x_all, lax.rem(e, x_all)

    def peer(dz, dx):
        return {"expert": lax.rem(z + dz + 4 * z_all, z_all) * x_all + lax.rem(x + dx + 4 * x_all, x_all)}

    def copy(src, dst, send, recv, to):
        return pltpu.make_async_remote_copy(
            src_ref=src, dst_ref=dst, send_sem=send, recv_sem=recv, device_id=to,
            device_id_type=pl.DeviceIdType.MESH,
        )

    def at(c):
        return pl.ds(pl.multiple_of(c * chunk, chunk), chunk)

    def z_copy(d, c):
        return copy(hidden_hbm.at[at(c)], found_hbm.at[d, 0, at(c)], zs.at[d - 1, c], zr.at[d - 1, c], peer(d, 0))

    def x_copy(d, c):
        return copy(hidden_hbm.at[at(c)], found_hbm.at[0, d, at(c)], xs.at[d - 1, c], xr.at[d - 1, c], peer(0, d))

    def f_copy(dz, dx, c):
        return copy(
            found_hbm.at[dz, 0, at(c)], found_hbm.at[dz, dx, at(c)],
            fs.at[dz - 1, dx - 1, c], fr.at[dz - 1, dx - 1, c], peer(0, dx),
        )

    def p_copy(dz, dx, c):
        return copy(
            part_stage.at[dx - 1, at(c)], summed_hbm.at[dz, dx - 1, at(c)],
            ps.at[dx - 1], pr.at[dz, dx - 1, c], peer(0, -dx),
        )

    def p_sent(dx):
        whole = part_stage.at[dx - 1]
        copy(whole, whole, ps.at[dx - 1], pr.at[0, dx - 1, 0], peer(0, -dx)).wait_send()

    def m_copy(dz, dx):
        return copy(
            mixture_hbm[dz * x_all + dx], came_hbm.at[dz - 1, dx - 1],
            ms.at[dz - 1, dx - 1], mr.at[dz - 1, dx - 1], peer(0, -dx),
        )

    def q_copy(dz, c):
        return copy(
            own_part.at[dz, at(c)], z_landed.at[dz - 1, at(c)], qs.at[dz - 1], qr.at[dz - 1, c], peer(-dz, 0)
        )

    def r_copy(dz, dx):
        return copy(
            router_stage.at[dz, dx], grad_router_ref.at[e], rs.at[dz, dx], rr.at[dz, dx], peer(-dz, -dx)
        )

    def cols(n, w):
        return pl.ds(pl.multiple_of(n * w, w), w)

    barrier = pltpu.get_barrier_semaphore()
    others = [(dz, dx) for dz in range(z_all) for dx in range(x_all) if dz + dx > 0]
    near = [(dy, flip) for dy in range(y_all) for flip in range(2) if dy + flip > 0]
    shard = lax.axis_index("shard")

    def near_at(dy, flip):
        return lax.rem(shard // 2 + dy, y_all) * 2 + lax.rem(lax.rem(shard, 2) + flip, 2)

    for dz, dx in others:
        pl.semaphore_signal(barrier, inc=1, device_id=peer(dz, dx), device_id_type=pl.DeviceIdType.MESH)
    for dy, flip in near:
        pl.semaphore_signal(
            barrier, inc=1, device_id={"shard": near_at(dy, flip)}, device_id_type=pl.DeviceIdType.MESH
        )
    pl.semaphore_wait(barrier, len(others) + len(near))

    keep = columns_hbm.shape[3]

    def column_copy(kind, source, dy, flip):
        j = 2 * dy + flip
        there = near_at(dy, flip)
        src = source.at[:, pl.ds(pl.multiple_of(there * keep, keep), keep)]
        if j == 0:
            return pltpu.make_async_copy(src, columns_hbm.at[kind, 0], own_c.at[kind])
        return copy(src, columns_hbm.at[kind, j], cs.at[kind, j - 1], cr.at[kind, j - 1], {"shard": there})

    column_copies = [
        column_copy(kind, source, dy, flip)
        for kind, source in enumerate((first_hbm, second_hbm))
        for dy, flip in [(0, 0)] + near
    ]
    own = pltpu.make_async_copy(hidden_hbm, found_hbm.at[0, 0], own_sem)
    own.start()
    weights = [
        pltpu.make_async_copy(gate_up_hbm, gate_up_w, w_sem.at[0]),
        pltpu.make_async_copy(down_hbm, down_w, w_sem.at[1]),
    ]
    for w in weights:
        w.start()

    def send_own(c, carry):
        for d in range(1, x_all):
            x_copy(d, c).start()
        return carry

    for d in (1, 2, 3):

        def send_z(c, carry):
            z_copy(d, c).start()
            return carry

        lax.fori_loop(0, MOE_CHUNKS, send_z, 0)

    for c in column_copies:
        c.start()

    def events(first, last):
        def one(k, carry):
            @pl.when(k < last)
            def _():
                j = k // MOE_CHUNKS
                c = lax.rem(k, MOE_CHUNKS)
                d = 1 + j
                z_copy(d, c).wait_recv()
                for dx in range(1, x_all):
                    f_copy(d, dx, c).start()

            return carry

        lax.fori_loop(first, first + MOE_CHUNKS, one, 0)

    def own_slots(le):
        return pl.ds(pl.multiple_of(le * capacity, capacity), capacity)

    def finish(dz, last):
        def load(c):
            return pltpu.make_async_copy(summed_hbm.at[dz, dx - 1, at(c)], mix_stage.at[0, at(c)], lsem.at[c])

        def add(c):
            load(c).wait()
            own_part[dz, at(c), :] = (
                own_part[dz, at(c), :].astype(f32) + mix_stage[0, at(c), :].astype(f32)
            ).astype(bf16)
            if dx == x_all - 1:
                if not last:
                    q_copy(dz, c).start()

        def arrive(c, carry):
            p_copy(dz, dx, c).wait_recv()
            load(c).start()
            return carry

        def rest(c, carry):
            add(c)
            return carry

        for dx in range(1, x_all):
            lax.fori_loop(0, MOE_CHUNKS, arrive, 0)
            lax.fori_loop(0, MOE_CHUNKS, rest, 0)

    mix_slots = mix_stage.shape[0]

    def mix_copy(dz, dx):
        slot = dx % mix_slots
        return pltpu.make_async_copy(mix_stage.at[slot], mixture_hbm[dz * x_all + dx], mix_sem.at[slot])

    def pieces(p):
        return 4 + sum(n * (p >= k).astype(jnp.int32) for k, n in enumerate((1, 1, 1, 1, 1, 2, 1, 0)))

    def group_at(g):
        return lax.rem(g + 1, z_all)

    slot_row = lax.broadcasted_iota(jnp.int32, (capacity, length), 0).astype(f32)
    slot_col = lax.broadcasted_iota(jnp.int32, (length, local_experts * capacity), 1).astype(f32)
    own.wait()
    events(0, 4)
    lax.fori_loop(0, MOE_CHUNKS, send_own, 0)

    def load_upstream(dz):
        return [pltpu.make_async_copy(upstream_hbm.at[dz, dx], ups.at[dx], load_sem.at[1, dx]) for dx in range(x_all)]

    for load in load_upstream(1):
        load.start()

    def group(g, carry):
        dz = group_at(g)

        def arrive(c, inner):
            for dx in range(1, x_all):

                @pl.when(dz == 0)
                def _():
                    x_copy(dx, c).wait_recv()

                @pl.when(dz > 0)
                def _():
                    f_copy(dz, dx, c).wait_recv()

            return inner

        lax.fori_loop(0, MOE_CHUNKS, arrive, 0)
        loads = []
        for dx in range(x_all):
            loads.append(pltpu.make_async_copy(found_hbm.at[dz, dx], hid.at[dx], load_sem.at[0, dx]))
        for load in loads:
            load.start()
        for load in loads + load_upstream(dz):
            load.wait()
        pl.when(g == 0)(lambda: [w.wait() for w in weights] and None)

        for dx in range(x_all):
            logits = jnp.dot(hid[dx], router_ref[...], preferred_element_type=f32)
            raised = jnp.exp(logits - jnp.max(logits, axis=1, keepdims=True))
            prob[dx] = raised / jnp.sum(raised, axis=1, keepdims=True)
            logits = lax.dot_general(
                router_t_ref[...], hid[dx], (((1,), (1,)), ((), ())), preferred_element_type=f32
            )
            raised = jnp.exp(logits - jnp.max(logits, axis=0, keepdims=True))
            prob_t[dx] = raised / jnp.sum(raised, axis=0, keepdims=True)
            router_stage[dz, dx] = jnp.zeros(router_stage.shape[2:], f32)

        def store(kind, buffer, hbm, le):
            return pltpu.make_async_copy(buffer, hbm.at[le, dz], store_sem.at[kind])

        def expert(le, inner):
            @pl.when(g + le > 0)
            def _():
                store(0, rows, rows_hbm, le).wait()
                store(1, activated, activated_hbm, le).wait()
                store(2, grad_expert, grad_out_hbm, le).wait()
                store(3, grad_gate_up, grad_gate_up_hbm, le).wait()

            chosen = [place_ref[dz, dx, pl.ds(le, 1), :] == slot_row for dx in range(x_all)]
            chosen_low = [c.astype(f32).astype(bf16) for c in chosen]

            def dispatch(n, c0):
                c = cols(n, tile)
                for dx in range(x_all):
                    rows[dx * capacity : (dx + 1) * capacity, c] = jnp.dot(
                        chosen_low[dx], hid[dx, :, c], preferred_element_type=f32
                    ).astype(bf16)
                return c0

            lax.fori_loop(0, width // tile, dispatch, 0, unroll=True)
            store(0, rows, rows_hbm, le).start()

            def up_step(n, c0):
                c = cols(n, tile)
                gate_up[:, c] = jnp.dot(rows[...], gate_up_w[le, :, c], preferred_element_type=f32)
                return c0

            lax.fori_loop(0, twice // tile, up_step, 0, unroll=True)

            def act_step(n, c0):
                gate = gate_up[:, cols(n, narrow)]
                up = gate_up[:, pl.ds(pl.multiple_of(half + n * narrow, narrow), narrow)]
                activated[:, cols(n, narrow)] = (gate / (1.0 + jnp.exp(-gate)) * up).astype(bf16)
                return c0

            lax.fori_loop(0, half // narrow, act_step, 0, unroll=True)
            store(1, activated, activated_hbm, le).start()

            def down_step(n, c0):
                c = cols(n, tile)
                result = jnp.dot(activated[...], down_w[le, :, c], preferred_element_type=f32)
                for dx in range(x_all):
                    r = slice(dx * capacity, (dx + 1) * capacity)
                    out_rows[dx, own_slots(le), c] = result[r].astype(bf16)
                return c0

            lax.fori_loop(0, width // tile, down_step, 0, unroll=True)

            events(pieces(4 * g + 2 * le - 1), pieces(4 * g + 2 * le))

            mine = e * local_experts + le
            weight_rows = [
                jnp.sum(jnp.where(chosen[dx], prob_t[dx, pl.ds(mine, 1), :], 0.0), axis=1, keepdims=True)
                for dx in range(x_all)
            ]

            def grad_step(n, totals):
                c = cols(n, tile)
                new = []
                for dx in range(x_all):
                    r = slice(dx * capacity, (dx + 1) * capacity)
                    up_rows = jnp.dot(chosen_low[dx], ups[dx, :, c], preferred_element_type=f32)
                    grad_expert[r, c] = (weight_rows[dx] * up_rows).astype(bf16)
                    new.append(
                        totals[dx]
                        + jnp.sum(up_rows * out_rows[dx, own_slots(le), c].astype(f32), axis=1, keepdims=True)
                    )
                return tuple(new)

            totals = lax.fori_loop(
                0, width // tile, grad_step, tuple(jnp.zeros((capacity, 1), f32) for _ in range(x_all)),
                unroll=True,
            )
            store(2, grad_expert, grad_out_hbm, le).start()
            for dx in range(x_all):
                router_stage[dz, dx, pl.ds(le, 1), :] = jnp.sum(
                    jnp.where(chosen[dx], totals[dx], 0.0), axis=0, keepdims=True
                )

            def back_step(n, c0):
                ga = lax.dot_general(
                    grad_expert[...], down_w[le, cols(n, narrow), :], (((1,), (1,)), ((), ())),
                    preferred_element_type=f32,
                )
                gate = gate_up[:, cols(n, narrow)]
                c_up = pl.ds(pl.multiple_of(half + n * narrow, narrow), narrow)
                up = gate_up[:, c_up]
                sg = 1.0 / (1.0 + jnp.exp(-gate))
                grad_gate_up[:, cols(n, narrow)] = (ga * up * sg * (1.0 + gate * (1.0 - sg))).astype(bf16)
                grad_gate_up[:, c_up] = (ga * (gate * sg)).astype(bf16)
                return c0

            lax.fori_loop(0, half // narrow, back_step, 0, unroll=True)
            store(3, grad_gate_up, grad_gate_up_hbm, le).start()

            def row_step(n, c0):
                result = lax.dot_general(
                    grad_gate_up[...], gate_up_w[le, cols(n, narrow), :], (((1,), (1,)), ((), ())),
                    preferred_element_type=f32,
                )
                for dx in range(x_all):
                    r = slice(dx * capacity, (dx + 1) * capacity)
                    grad_rows[dx, own_slots(le), cols(n, narrow)] = result[r].astype(bf16)
                return c0

            lax.fori_loop(0, width // narrow, row_step, 0, unroll=True)
            events(pieces(4 * g + 2 * le), pieces(4 * g + 2 * le + 1))

            @pl.when((le == 0) & (g > 0))
            def _():
                for dx in range(mix_slots):
                    mix_copy(0, dx).wait()
                finish(group_at(g - 1), False)

                @pl.when(g == z_all - 1)
                def _():
                    for k in (2, 1):
                        for dx in range(1, x_all):
                            m_copy(k, dx).start()

            return inner

        assert local_experts == 2
        lax.fori_loop(0, local_experts, expert, 0)

        @pl.when(g < z_all - 1)
        def _():
            for load in load_upstream(group_at(g + 1)):
                load.start()

        def stages():
            for dx in range(1, x_all):
                p_sent(dx)

        pl.when(g > 0)(stages)
        for dx in range(x_all):
            weight = jnp.zeros(slot_col.shape, f32)
            mask = jnp.zeros(slot_col.shape, f32)
            lane = lax.broadcasted_iota(jnp.int32, prob.shape[1:], 1)
            for le in range(local_experts):
                spot = place_t_ref[dz, dx, :, le : le + 1]
                here = jnp.where(spot < 0.0, -1.0, spot + le * capacity) == slot_col
                p = jnp.sum(jnp.where(lane == e * local_experts + le, prob[dx], 0.0), axis=1, keepdims=True)
                weight = jnp.where(here, p, weight)
                mask = jnp.where(here, 1.0, mask)
            low = mask.astype(bf16)
            high = weight.astype(bf16)
            remainder = (weight - high.astype(f32)).astype(bf16)

            if dx >= mix_slots:
                mix_copy(0, dx).wait()

            def combine(n, c0):
                c = cols(n, tile)
                mix = jnp.dot(high, out_rows[dx, :, c], preferred_element_type=f32) + jnp.dot(
                    remainder, out_rows[dx, :, c], preferred_element_type=f32
                )
                grad = jnp.dot(low, grad_rows[dx, :, c], preferred_element_type=f32)
                mix_stage[dx % mix_slots, :, c] = mix.astype(bf16)
                if dx == 0:
                    own_part[dz, :, c] = grad.astype(bf16)
                else:
                    part_stage[dx - 1, :, c] = grad.astype(bf16)
                return c0

            lax.fori_loop(0, width // tile, combine, 0, unroll=True)
            for k in range(z_all):
                pl.when(dz == k)(mix_copy(k, dx).start)
            if dx > 0:
                for c in range(MOE_CHUNKS):
                    p_copy(dz, dx, c).start()
                r_copy(dz, dx).start()
            else:

                @pl.when(dz > 0)
                def _():
                    r_copy(dz, 0).start()

                @pl.when(dz == 0)
                def _():
                    grad_router_ref[e] = router_stage[0, 0]

        return carry

    lax.fori_loop(0, z_all, group, 0)
    for kind, buffer, hbm in (
        (0, rows, rows_hbm), (1, activated, activated_hbm), (2, grad_expert, grad_out_hbm),
        (3, grad_gate_up, grad_gate_up_hbm),
    ):
        pltpu.make_async_copy(buffer, hbm.at[0, 0], store_sem.at[kind]).wait()

    high_all = z_all * count
    kinds = []
    spots = ((hid.at[0], hid.at[1]), (rows, grad_expert))
    for le in range(local_experts):
        for dz in range(z_all):
            keeper = spots[le][dz // 2]
            r = slice(dz * count, (dz + 1) * count)
            kinds += [
                (rows_hbm.at[le, dz], gate_up_w.at[le, r]),
                (grad_gate_up_hbm.at[le, dz], gate_up_w.at[le, slice(high_all + dz * count, high_all + (dz + 1) * count)]),
                (grad_out_hbm.at[le, dz], down_w.at[le, r]),
                (activated_hbm.at[le, dz], keeper.at[:, slice((dz % 2) * half, (dz % 2 + 1) * half)]),
            ]
    backs = [pltpu.make_async_copy(a, b, back_sem.at[n]) for n, (a, b) in enumerate(kinds)]
    for b in backs:
        b.start()
    contract = (((0,), (0,)), ((), ()))

    def out_copy(slot, hbm, le, m):
        return pltpu.make_async_copy(
            ups.at[slot], hbm.at[le, pl.ds(pl.multiple_of(m * length, length), length)], out_sem.at[slot]
        )

    for le in range(local_experts):
        for b in backs[4 * z_all * le : 4 * z_all * (le + 1)]:
            b.wait()

        def up_weight(m, carry):
            slot = lax.rem(m, 2)
            if le == 0:
                pl.when(m > 1)(out_copy(slot, grad_up_w_hbm, le, m).wait)
            else:
                out_copy(slot, grad_up_w_hbm, le, m).wait()
            left = gate_up_w[le, :high_all, cols(m, length)]
            for n in range(twice // tile):
                c = slice(n * tile, (n + 1) * tile)
                ups[slot, :, c] = lax.dot_general(
                    left, gate_up_w[le, high_all : 2 * high_all, c], contract, preferred_element_type=f32
                ).astype(bf16)
            out_copy(slot, grad_up_w_hbm, le, m).start()
            return carry

        lax.fori_loop(0, width // length, up_weight, 0)

        def down_weight(m, carry):
            slot = lax.rem(m, 2)
            out_copy(slot, grad_down_w_hbm, le, m).wait()
            for n in range(width // tile):
                c = slice(n * tile, (n + 1) * tile)
                total = jnp.zeros((length, tile), f32)
                for dz in range(z_all):
                    left = spots[le][dz // 2][
                        :, pl.ds(pl.multiple_of((dz % 2) * half + m * length, length), length)
                    ]
                    total = total + lax.dot_general(
                        left, down_w[le, dz * count : (dz + 1) * count, c], contract, preferred_element_type=f32
                    )
                ups[slot, :, c] = total.astype(bf16)
            out_copy(slot, grad_down_w_hbm, le, m).start()
            return carry

        lax.fori_loop(0, half // length, down_weight, 0)
    for slot in range(2):
        out_copy(slot, grad_down_w_hbm, 0, 0).wait()
    for dx in range(mix_slots):
        mix_copy(0, dx).wait()
    finish(0, True)

    def total(c, carry):
        grad_ref[at(c), :] = own_part[0, at(c), :].astype(f32)
        for d in (1, 2, 3):
            q_copy(d, c).wait_recv()
            grad_ref[at(c), :] = grad_ref[at(c), :] + z_landed[d - 1, at(c), :].astype(f32)
        return carry

    lax.fori_loop(0, MOE_CHUNKS, total, 0)

    for k in (2, 1):
        for dx in range(1, x_all):
            m_copy(k, dx).wait()
    for c in column_copies:
        c.wait()
    for dx in range(1, x_all):
        p_sent(dx)
    for d in range(1, z_all):
        whole = own_part.at[d]
        copy(whole, whole, qs.at[d - 1], qr.at[d - 1, 0], peer(-d, 0)).wait_send()
    for dz, dx in others:
        r_copy(dz, dx).wait_send()
        r_copy(dz, dx).wait_recv()

    def sent(c, carry):
        for d in range(1, z_all):
            z_copy(d, c).wait_send()
            for dx in range(1, x_all):
                f_copy(d, dx, c).wait_send()
        for d in range(1, x_all):
            x_copy(d, c).wait_send()
        return carry

    lax.fori_loop(0, MOE_CHUNKS, sent, 0)


def moe_layer(
    hidden, upstream_all, place, router_weight, gate_up_weight, down_weight, first, second, expert_group, shard_group,
    capacity, name_id,
):
    f32, bf16 = jnp.float32, jnp.bfloat16
    length, width = hidden.shape
    local_experts, _, twice = gate_up_weight.shape
    half = twice // 2
    experts_all = router_weight.shape[1]
    x_all = expert_group // 4
    count = x_all * capacity
    dma = pltpu.SemaphoreType.DMA
    x1 = max(x_all - 1, 1)
    place_t = place.transpose(0, 1, 3, 2)
    spare = (-local_experts) % 8
    place = jnp.pad(place, ((0, 0), (0, 0), (0, spare), (0, 0)), constant_values=-1.0)
    any_spec = pl.BlockSpec(memory_space=pl.ANY)
    vmem_spec = pl.BlockSpec(memory_space=pltpu.VMEM)
    out = pl.pallas_call(
        functools.partial(moe_kernel, (x_all, capacity, shard_group // 2)),
        out_shape=[
            jax.ShapeDtypeStruct((local_experts, 4, count, width), bf16),
            jax.ShapeDtypeStruct((local_experts, 4, count, half), bf16),
            jax.ShapeDtypeStruct((local_experts, 4, count, width), bf16),
            jax.ShapeDtypeStruct((local_experts, 4, count, twice), bf16),
            jax.ShapeDtypeStruct((length, width), f32),
            jax.ShapeDtypeStruct((expert_group, 8, length), f32),
            jax.ShapeDtypeStruct((2, shard_group, length, width // shard_group), bf16),
            jax.ShapeDtypeStruct(gate_up_weight.shape, bf16),
            jax.ShapeDtypeStruct(down_weight.shape, bf16),
            jax.ShapeDtypeStruct((2, x1, length, width), bf16),
            jax.ShapeDtypeStruct((4, x_all, length, width), bf16),
            jax.ShapeDtypeStruct((4, x1, length, width), bf16),
        ]
        + [jax.ShapeDtypeStruct((length, width), bf16)] * (4 * x_all),
        in_specs=[any_spec, any_spec, vmem_spec, vmem_spec, vmem_spec, vmem_spec, any_spec, any_spec, any_spec, any_spec],
        out_specs=[any_spec] * 4 + [vmem_spec, vmem_spec] + [any_spec] * (6 + 4 * x_all),
        scratch_shapes=[
            pltpu.VMEM(gate_up_weight.shape, bf16),
            pltpu.VMEM(down_weight.shape, bf16),
            pltpu.VMEM((x_all, length, width), bf16),
            pltpu.VMEM((x_all, length, width), bf16),
            pltpu.VMEM((x_all, length, experts_all), f32),
            pltpu.VMEM((x_all, experts_all, length), f32),
            pltpu.VMEM((count, width), bf16),
            pltpu.VMEM((count, twice), f32),
            pltpu.VMEM((count, half), bf16),
            pltpu.VMEM((x_all, local_experts * capacity, width), bf16),
            pltpu.VMEM((count, width), bf16),
            pltpu.VMEM((count, twice), bf16),
            pltpu.VMEM((x_all, local_experts * capacity, width), bf16),
            pltpu.VMEM((min(2, x_all), length, width), bf16),
            pltpu.VMEM((x1, length, width), bf16),
            pltpu.VMEM((4, length, width), bf16),
            pltpu.VMEM((3, length, width), bf16),
            pltpu.VMEM((4, x_all, 8, length), f32),
            dma((2,)), dma, dma((2, x_all)), dma((4,)),
            dma((3, MOE_CHUNKS)), dma((3, MOE_CHUNKS)),
            dma((x1, MOE_CHUNKS)), dma((x1, MOE_CHUNKS)),
            dma((3, x1, MOE_CHUNKS)), dma((3, x1, MOE_CHUNKS)),
            dma((x1,)), dma((4, x1, MOE_CHUNKS)),
            dma((3,)), dma((3, MOE_CHUNKS)),
            dma((4, x_all)), dma((4, x_all)),
            dma((MOE_CHUNKS,)), dma((min(2, x_all),)),
            dma((2, shard_group - 1)), dma((2, shard_group - 1)), dma((2,)),
            dma((16 * local_experts,)), dma((2,)),
            dma((2, x1)), dma((2, x1)),
        ],
        compiler_params=pltpu.CompilerParams(
            collective_id=name_id, has_side_effects=True, vmem_limit_bytes=62 * 1024 * 1024
        ),
        cost_estimate=pl.CostEstimate(
            flops=12 * 4 * local_experts * count * width * twice, bytes_accessed=64 * 1024 * 1024,
            transcendentals=0,
        ),
    )(
        hidden, upstream_all, place, place_t, router_weight, router_weight.T, gate_up_weight, down_weight,
        first, second,
    )
    return out[4:10], out[12:]


def start_kernel(
    dims, weight_hbm, upstream_hbm, router_hbm, gains_ref, tokens_ref, routes_ref, tiles_ref,
    full_hbm, ups_hbm, router_full_hbm, gains_full_ref, place_all_ref, hidden_ref, *sems,
):
    x_all, y_all = dims
    z_all, parts = 4, 4
    (own_sem, ys, yr, rs, rr, cs, cr, fs, fr, gs, gr, zs, zr, xs, xr, us, ur, ns, nr, ps, pr, ms, mr) = sems
    f32, bf16 = jnp.float32, jnp.bfloat16
    rows = weight_hbm.shape[0]
    length = tokens_ref.shape[0]
    piece = rows // 8
    chunk = length // parts
    e = lax.axis_index("expert")
    s = lax.axis_index("shard")
    z, x = e // x_all, lax.rem(e, x_all)
    y, core = s // 2, lax.rem(s, 2)
    parity = lax.rem(z, 2)

    def expert_peer(dz, dx):
        return {"expert": lax.rem(z + dz, z_all) * x_all + lax.rem(x + dx, x_all)}

    def shard_peer(dy, flip):
        return {"shard": lax.rem(y + dy, y_all) * 2 + lax.rem(core + flip, 2)}

    beside = {"expert": (z + 1 - 2 * parity) * x_all + x}
    partner = shard_peer(0, 1)
    far = [(dz, dx) for dz in range(z_all) for dx in range(x_all) if dz + dx > 0]
    near = [(dy, flip) for dy in range(y_all) for flip in range(2) if dy + flip > 0]

    def copy(src, dst, send, recv, to):
        return pltpu.make_async_remote_copy(
            src_ref=src, dst_ref=dst, send_sem=send, recv_sem=recv, device_id=to,
            device_id_type=pl.DeviceIdType.MESH,
        )

    def piece_of(i, who):
        return jnp.where(i < 2, 4 + 2 * who + i, i - 2)

    def span(owner, k):
        return pl.ds(pl.multiple_of(owner * rows + k * piece, piece), piece)

    def y_copy(dy, i):
        k = piece_of(i, parity)
        src = weight_hbm.at[pl.ds(pl.multiple_of(k * piece, piece), piece)]
        return copy(src, full_hbm.at[span(s, k)], ys.at[dy - 1, i], yr.at[dy - 1, i], shard_peer(dy, 0))

    def owner(dy):
        return lax.rem(y - dy + y_all, y_all) * 2 + core

    def relay(dy, i):
        here = full_hbm.at[span(owner(dy), 4 + 2 * parity + i)]
        return copy(here, here, rs.at[dy - 1, i], rr.at[dy - 1, i], beside)

    def core_y(dy, i):
        here = full_hbm.at[span(owner(dy), piece_of(i, parity))]
        return copy(here, here, cs.at[dy - 1, i], cr.at[dy - 1, i], partner)

    def core_r(dy, i):
        here = full_hbm.at[span(owner(dy), 4 + 2 * (1 - parity) + i)]
        return copy(here, here, fs.at[dy - 1, i], fr.at[dy - 1, i], partner)

    whole = pl.ds(pl.multiple_of(s * rows, rows), rows)
    core_own = copy(weight_hbm, full_hbm.at[whole], gs, gr, partner)

    def at(c):
        return pl.ds(pl.multiple_of(c * chunk, chunk), chunk)

    def z_copy(d, c):
        return copy(upstream_hbm.at[at(c)], ups_hbm.at[d, 0, at(c)], zs.at[d - 1, c], zr.at[d - 1, c], expert_peer(d, 0))

    def x_copy(d):
        return copy(upstream_hbm, ups_hbm.at[0, d], xs.at[d - 1], xr.at[d - 1], expert_peer(0, d))

    def u_copy(dz, dx, c):
        return copy(
            ups_hbm.at[dz, 0, at(c)], ups_hbm.at[dz, dx, at(c)],
            us.at[dz - 1, dx - 1, c], ur.at[dz - 1, dx - 1, c], expert_peer(0, dx),
        )

    def router_copy(n, p):
        return copy(router_hbm, router_full_hbm.at[whole], ns.at[n], nr.at[n], shard_peer(*p))

    def gains_copy(n, p):
        return copy(gains_ref, gains_full_ref.at[s], ms.at[n], mr.at[n], shard_peer(*p))

    def place_copy(n, p):
        return copy(place_all_ref.at[0, 0], place_all_ref.at[p[0], p[1]], ps.at[n], pr.at[n], expert_peer(*p))

    barrier = pltpu.get_barrier_semaphore()
    peers = [expert_peer(*p) for p in far] + [shard_peer(*p) for p in near]
    for peer in peers:
        pl.semaphore_signal(barrier, inc=1, device_id=peer, device_id_type=pl.DeviceIdType.MESH)
    pl.semaphore_wait(barrier, len(peers))

    own = [
        pltpu.make_async_copy(weight_hbm, full_hbm.at[whole], own_sem.at[0]),
        pltpu.make_async_copy(upstream_hbm, ups_hbm.at[0, 0], own_sem.at[1]),
        pltpu.make_async_copy(router_hbm, router_full_hbm.at[whole], own_sem.at[2]),
    ]
    for n, p in enumerate(near):
        gains_copy(n, p).start()
        router_copy(n, p).start()
    for i in range(2):
        for dy in range(1, y_all):
            y_copy(dy, i).start()
    for d in range(1, x_all):
        x_copy(d).start()
    for d in (1, 3, 2):
        for c in range(parts):
            z_copy(d, c).start()
    core_own.start()
    for o in own:
        o.start()

    count = place_all_ref.shape[2]
    ids = lax.broadcasted_iota(jnp.int32, (count, length), 0)
    chosen = jnp.zeros((count, length), f32)
    for k in range(TOP):
        chosen = jnp.where(routes_ref[k : k + 1, :] == ids, 1.0, chosen)
    before = lax.broadcasted_iota(jnp.int32, (length, length), 0)
    after = lax.broadcasted_iota(jnp.int32, (length, length), 1)
    earlier = jnp.where(before < after, 1.0, 0.0).astype(bf16)
    rank = jnp.dot(chosen.astype(bf16), earlier, preferred_element_type=f32)
    limit = (tiles_ref[...] * TILE).astype(f32)
    place_all_ref[0, 0] = jnp.where((chosen > 0.5) & (rank < limit), rank, -1.0)
    for n, p in enumerate(far):
        place_copy(n, p).start()

    gains_full_ref[s] = gains_ref[...]
    for n, p in enumerate(near):
        gains_copy(n, p).wait_recv()
    keep = gains_ref.shape[1]
    tall = 64

    def norm(t, carry):
        r = pl.ds(pl.multiple_of(t * tall, tall), tall)
        values = tokens_ref[r, :].astype(f32)
        scale = lax.rsqrt(jnp.mean(values * values, axis=1, keepdims=True) + epsilon)
        for j in range(2 * y_all):
            c = slice(j * keep, (j + 1) * keep)
            gain = gains_full_ref[j, 0:1, :].astype(f32)
            hidden_ref[r, c] = (values[:, c] * scale * gain).astype(bf16)
        return carry

    lax.fori_loop(0, length // tall, norm, 0)

    def forward(events):
        for d, c in events:
            z_copy(d, c).wait_recv()
            for dx in range(1, x_all):
                u_copy(d, dx, c).start()

    order = {
        0: [(1, 0)], 1: [(1, 1), (1, 2)], 2: [(1, 3), (3, 0), (3, 1)], 3: [(3, 2), (3, 3), (2, 0)],
        4: [(2, 1), (2, 2), (2, 3)], 5: [],
    }
    for i in range(6):
        for dy in range(1, y_all):
            y_copy(dy, i).wait_recv()
            if i < 2:
                relay(dy, i).start()
            core_y(dy, i).start()
            if i < 4:
                y_copy(dy, i + 2).start()
        forward(order[i])
        if i in (3, 4):
            for dy in range(1, y_all):
                here = full_hbm.at[span(owner(dy), 4 + 2 * (1 - parity) + i - 3)]
                copy(here, here, rs.at[dy - 1, i - 3], rr.at[dy - 1, i - 3], beside).wait_recv()
                core_r(dy, i - 3).start()

    for o in own:
        o.wait()
    core_own.wait()
    for n, p in enumerate(near):
        gains_copy(n, p).wait_send()
        router_copy(n, p).wait()
    for n, p in enumerate(far):
        place_copy(n, p).wait()
    for d in range(1, x_all):
        x_copy(d).wait()
    for dy in range(1, y_all):
        for i in range(6):
            y_copy(dy, i).wait_send()
            core_y(dy, i).wait()
        for i in range(2):
            relay(dy, i).wait_send()
            core_r(dy, i).wait()
    for d in range(1, z_all):
        for c in range(parts):
            z_copy(d, c).wait_send()
            for dx in range(1, x_all):
                u_copy(d, dx, c).wait()


def start_layer(weight, upstream, router, gains, tokens, routes, tile_counts, expert_group, shard_group, name_id):
    f32, bf16 = jnp.float32, jnp.bfloat16
    length, width = tokens.shape
    x_all, y_all = expert_group // 4, shard_group // 2
    experts_all = tile_counts.shape[0]
    dma = pltpu.SemaphoreType.DMA
    y1, x1 = max(y_all - 1, 1), max(x_all - 1, 1)
    any_spec = pl.BlockSpec(memory_space=pl.ANY)
    vmem_spec = pl.BlockSpec(memory_space=pltpu.VMEM)
    return pl.pallas_call(
        functools.partial(start_kernel, (x_all, y_all)),
        out_shape=[
            jax.ShapeDtypeStruct((weight.shape[0] * shard_group, weight.shape[1]), bf16),
            jax.ShapeDtypeStruct((4, x_all, length, width), bf16),
            jax.ShapeDtypeStruct((router.shape[0] * shard_group, router.shape[1]), bf16),
            jax.ShapeDtypeStruct((shard_group, *gains.shape), bf16),
            jax.ShapeDtypeStruct((4, x_all, experts_all, length), f32),
            jax.ShapeDtypeStruct((length, width), bf16),
        ],
        in_specs=[any_spec] * 3 + [vmem_spec] * 4,
        out_specs=[any_spec] * 3 + [vmem_spec] * 3,
        scratch_shapes=[
            dma((3,)),
            dma((y1, 6)), dma((y1, 6)),
            dma((y1, 2)), dma((y1, 2)),
            dma((y1, 6)), dma((y1, 6)),
            dma((y1, 2)), dma((y1, 2)),
            dma, dma,
            dma((3, 4)), dma((3, 4)),
            dma((x1,)), dma((x1,)),
            dma((3, x1, 4)), dma((3, x1, 4)),
            dma((shard_group - 1,)), dma((shard_group - 1,)),
            dma((expert_group - 1,)), dma((expert_group - 1,)),
            dma((shard_group - 1,)), dma((shard_group - 1,)),
        ],
        compiler_params=pltpu.CompilerParams(
            collective_id=name_id, has_side_effects=True, vmem_limit_bytes=32 * 1024 * 1024
        ),
        cost_estimate=pl.CostEstimate(
            flops=16 * length * width, bytes_accessed=64 * 1024 * 1024, transcendentals=0
        ),
    )(weight, upstream, router, gains, tokens, routes.T, tile_counts[:, None])


def body(
    tokens,
    cotangent,
    segments,
    routes,
    tile_counts,
    norm_one,
    norm_query,
    norm_key,
    norm_two,
    qkv_weight,
    out_weight,
    router_weight,
    gate_up_weight,
    down_weight,
):
    f32, bf16 = jnp.float32, jnp.bfloat16
    length, model_width = tokens.shape
    experts_all = tile_counts.shape[0]
    local_experts = gate_up_weight.shape[0]
    expert_group = lax.axis_size("expert")
    shard_group = lax.axis_size("shard")
    capacity = length * TOP // (experts_all * TILE) * TILE
    score_scale = HEAD_DIM ** (-0.5)
    own_expert = lax.axis_index("expert")
    own_shard = lax.axis_index("shard")
    z_all = z_size(expert_group)
    x_all = expert_group // z_all

    gain_rows = jnp.stack([norm_one, norm_query, norm_key, norm_two])
    gain_rows = jnp.pad(gain_rows, ((0, 12), (0, 0)))
    qkv_full, upstream_all, router_full, gains, place_all, hidden_one = start_layer(
        qkv_weight,
        cotangent,
        router_weight,
        gain_rows,
        tokens,
        routes,
        tile_counts,
        expert_group,
        shard_group,
        3,
    )
    out_own, gains = lax.optimization_barrier((out_weight, gains))
    out_full = lax.all_gather(out_own, "shard", axis=0, tiled=True)
    gains = gains.transpose(1, 0, 2).reshape(gains.shape[1], model_width).astype(f32)
    gain_one, gain_query, gain_key, gain_two = gains[0], gains[1], gains[2], gains[3]
    place_own = lax.dynamic_slice_in_dim(
        place_all, own_expert * local_experts, local_experts, axis=2
    )
    position = jnp.arange(length, dtype=jnp.int32)

    inputs = tokens.astype(f32)
    _, first_pull = jax.vjp(rms_scale, inputs, gain_one)
    projected = jnp.dot(hidden_one, qkv_full, preferred_element_type=f32)
    cosine, sine_table = rotary_tables(length)

    def query_key_local(raw_query, raw_key, query_gain, key_gain):
        return query_key(raw_query, raw_key, query_gain, key_gain, cosine, sine_table)

    rotated, rotary_pull = jax.vjp(
        query_key_local,
        projected[:, :model_width],
        projected[:, model_width : 2 * model_width],
        gain_query,
        gain_key,
    )
    query_low = rotated[0].astype(bf16)
    key_low = rotated[1].astype(bf16)
    value_low = projected[:, 2 * model_width :].astype(bf16).reshape(length, HEADS, HEAD_DIM)
    allowed = (position[:, None] >= position[None, :]) & (
        segments[0][:, None] == segments[0][None, :]
    )
    masked = jnp.where(
        allowed[None],
        jnp.einsum("qhd,khd->hqk", query_low, key_low, preferred_element_type=f32) * score_scale,
        -1e30,
    )
    probs = softmax_rows(masked)
    probs_low = probs.astype(bf16)
    attended_low = (
        jnp.einsum("hqk,khd->qhd", probs_low, value_low, preferred_element_type=f32)
        .reshape(length, model_width)
        .astype(bf16)
    )
    middle = inputs + jnp.dot(attended_low, out_full, preferred_element_type=f32)
    scaled_two, second_pull = jax.vjp(rms_scale, middle, gain_two)
    hidden_two = scaled_two.astype(bf16)
    router = softmax_rows(jnp.dot(hidden_two, router_full, preferred_element_type=f32))
    done, mixture_parts = moe_layer(
        hidden_two,
        upstream_all,
        place_own,
        router_full,
        gate_up_weight,
        down_weight,
        attended_low,
        hidden_one,
        expert_group,
        shard_group,
        capacity,
        2,
    )
    grad_rows_sum, grad_router, columns, grad_gate_up_full, grad_down_full, came = done
    columns = columns.reshape(2, shard_group * length, -1).swapaxes(1, 2)
    grad_router = grad_router[:, :local_experts].reshape(experts_all, length).T
    grad_gate_up_weight = lax.psum_scatter(
        grad_gate_up_full, "shard", scatter_dimension=1, tiled=True
    ).astype(f32)
    grad_down_weight = lax.psum_scatter(
        grad_down_full, "shard", scatter_dimension=2, tiled=True
    ).astype(f32)

    parts = dict(enumerate(mixture_parts))

    def slot(values, *names):
        held = lax.optimization_barrier((values, [parts[n] for n in names]))
        parts.update(zip(names, held[1], strict=True))
        return held[0]

    def group(dz):
        return [dz * x_all + dx for dx in range(x_all)]

    upstream = cotangent.astype(f32)
    grad_logits = (
        router * (grad_router - jnp.sum(router * grad_router, axis=-1, keepdims=True))
    ).astype(bf16)
    grad_hidden_two = grad_rows_sum + jnp.einsum(
        "te,de->td", grad_logits, router_full, preferred_element_type=f32
    )
    grad_middle_norm, grad_gain_two = second_pull(grad_hidden_two)
    grad_middle = upstream + grad_middle_norm
    two, one = (
        (mixture_parts[dz * x_all].astype(f32) + jnp.sum(came[dz - 1].astype(f32), axis=0)).astype(bf16)
        for dz in (2, 1)
    )
    halves = [two[: length // 2], two[length // 2 :]]
    halves[0] = back_along_z(halves[0], 2, expert_group)
    three = sum_over_x(parts, 3, expert_group).astype(bf16)
    grad_middle, halves, three = slot((grad_middle, halves, three), *group(0))
    halves[1] = back_along_z(halves[1], 2, expert_group)
    here = sum_over_x(parts, 0, expert_group)
    grad_branch_low = grad_middle.astype(bf16)
    grad_attended_low = (
        jnp.einsum("te,de->td", grad_branch_low, out_full, preferred_element_type=f32)
        .astype(bf16)
        .reshape(length, HEADS, HEAD_DIM)
    )
    grad_attended_low, halves, one, here = slot((grad_attended_low, halves, one, here))
    one = back_along_z(one, 1, expert_group)
    grad_probs = jnp.einsum(
        "qhd,khd->hqk", grad_attended_low, value_low, preferred_element_type=f32
    )
    grad_scores_low = (
        probs * (grad_probs - jnp.sum(probs * grad_probs, axis=-1, keepdims=True))
    ).astype(bf16)
    grad_scores_low, one, three = slot((grad_scores_low, one, three))
    three = back_along_z(three, 3, expert_group)
    grad_queries = (
        jnp.einsum("hqk,khd->qhd", grad_scores_low, key_low, preferred_element_type=f32)
        * score_scale
    )
    grad_keys = (
        jnp.einsum("hqk,qhd->khd", grad_scores_low, query_low, preferred_element_type=f32)
        * score_scale
    )
    grad_values = jnp.einsum(
        "hqk,qhd->khd", probs_low, grad_attended_low, preferred_element_type=f32
    )
    grad_raw_query, grad_raw_key, grad_gain_query, grad_gain_key = rotary_pull(
        (grad_queries, grad_keys)
    )
    grad_projected_low = jnp.concatenate(
        [grad_raw_query, grad_raw_key, grad_values.reshape(length, model_width)], axis=-1
    ).astype(bf16)
    grad_hidden_one = jnp.einsum(
        "te,de->td", grad_projected_low, qkv_full, preferred_element_type=f32
    )
    grad_inputs_norm, grad_gain_one = first_pull(grad_hidden_one)
    grad_tokens = grad_middle + grad_inputs_norm

    grad_router_part = jnp.einsum("td,te->ed", hidden_two, grad_logits, preferred_element_type=f32)
    small = jnp.concatenate(
        [
            grad_router_part,
            jnp.stack([grad_gain_one, grad_gain_query, grad_gain_key, grad_gain_two]),
            jnp.zeros((-(experts_all + 4) % 8, model_width), f32),
        ],
        axis=0,
    )
    keep = norm_one.shape[0]
    small = jnp.stack(
        [
            lax.dynamic_slice_in_dim(
                small,
                (((own_shard // 2 + dy) % (shard_group // 2)) * 2 + (own_shard % 2 + flip) % 2) * keep,
                keep,
                axis=1,
            )
            for dy in range(shard_group // 2)
            for flip in range(2)
        ]
    )

    grads_low = jnp.concatenate([grad_branch_low, grad_projected_low], axis=1)
    grads_low, three = slot((grads_low, three))
    mixture = sum((a.astype(f32) for a in (one, jnp.concatenate(halves), three)), here)
    block_out = (middle + mixture).astype(bf16)
    grad_rows_kept, small = summed_rows(
        columns, grads_low, model_width, small, expert_group, shard_group, z_all, 256, 2, 1
    )
    grad_out_weight = grad_rows_kept[:, :model_width].astype(f32)
    grad_qkv_weight = grad_rows_kept[:, model_width:].astype(f32)
    return (
        block_out,
        grad_tokens,
        small[experts_all],
        small[experts_all + 1],
        small[experts_all + 2],
        small[experts_all + 3],
        grad_qkv_weight,
        grad_out_weight,
        small[:experts_all].T,
        grad_gate_up_weight,
        grad_down_weight,
    )


def solution(mesh):
    return jax.shard_map(
        body,
        mesh=mesh,
        in_specs=(
            P(("expert", "shard"), None),
            P(("expert", "shard"), None),
            P(("expert", "shard"), None),
            P(("expert", "shard"), None),
            P(),
            P("shard"),
            P("shard"),
            P("shard"),
            P("shard"),
            P("shard", None),
            P("shard", None),
            P("shard", None),
            P("expert", None, None),
            P("expert", None, None),
        ),
        out_specs=(
            P(("expert", "shard"), None),
            P(("expert", "shard"), None),
            P("shard"),
            P("shard"),
            P("shard"),
            P("shard"),
            P("shard", None),
            P("shard", None),
            P("shard", None),
            P("expert", "shard", None),
            P("expert", None, "shard"),
        ),
        check_vma=False,
    )
```

```python
import functools

import jax
import jax.numpy as jnp
from jax import lax
from jax.experimental import pallas as pl
from jax.experimental.pallas import tpu as pltpu
from jax.sharding import PartitionSpec as P

HEADS = 16
HEAD_DIM = 128
TOP = 8
TILE = 8


epsilon = 1e-05
rope_base = 10000.0


def rms_scale(values, scale_gain):
    return (
        values * lax.rsqrt(jnp.mean(values * values, axis=-1, keepdims=True) + epsilon) * scale_gain
    )


def rotary_tables(length):
    half_dim = HEAD_DIM // 2
    position = jnp.arange(length, dtype=jnp.float32)[:, None]
    frequency = rope_base ** (-jnp.arange(half_dim, dtype=jnp.float32) * 2.0 / HEAD_DIM)
    angles = position * frequency[None, :]
    angles = jnp.concatenate([angles, angles], axis=-1)
    return (jnp.cos(angles)[:, None, :], jnp.sin(angles)[:, None, :])


def rotate(vectors, cosine, sine_table):
    half_dim = vectors.shape[-1] // 2
    turned = jnp.concatenate([-vectors[..., half_dim:], vectors[..., :half_dim]], axis=-1)
    return vectors * cosine + turned * sine_table


def query_key(raw_query, raw_key, query_gain, key_gain, cosine, sine_table):
    length = raw_query.shape[0]
    queries = rms_scale(raw_query, query_gain).reshape(length, HEADS, HEAD_DIM)
    keys_rot = rms_scale(raw_key, key_gain).reshape(length, HEADS, HEAD_DIM)
    return (rotate(queries, cosine, sine_table), rotate(keys_rot, cosine, sine_table))


def swiglu(gate_up):
    half_dim = gate_up.shape[-1] // 2
    gate_part = gate_up[..., :half_dim]
    return gate_part / (1.0 + jnp.exp(-gate_part)) * gate_up[..., half_dim:]


def softmax_rows(logits):
    largest = jnp.max(logits, axis=-1, keepdims=True)
    raised = jnp.exp(logits - largest)
    return raised / jnp.sum(raised, axis=-1, keepdims=True)


def z_size(expert_group):
    return 4 if expert_group % 4 == 0 else 1


def shift(values, expert_group, dz, dx):
    z_all = z_size(expert_group)
    x_all = expert_group // z_all
    pairs = [
        (i, ((i // x_all + dz) % z_all) * x_all + (i % x_all + dx) % x_all)
        for i in range(expert_group)
    ]
    return lax.ppermute(values, "expert", pairs)


def gather_expert(block, expert_group):
    z_all = z_size(expert_group)
    x_all = expert_group // z_all
    rows = [block] + [shift(block, expert_group, dz, 0) for dz in range(1, z_all)]
    return [
        rows[dz] if dx == 0 else shift(rows[dz], expert_group, 0, dx)
        for dz in range(z_all)
        for dx in range(x_all)
    ]


def sum_over_x(parts, dz, expert_group):
    x_all = expert_group // z_size(expert_group)
    total = parts[dz * x_all].astype(jnp.float32)
    for dx in range(1, x_all):
        total = total + shift(parts[dz * x_all + dx], expert_group, 0, -dx).astype(jnp.float32)
    return total


def back_along_z(total, dz, expert_group):
    return shift(total, expert_group, -dz, 0)


def tail_kernel(
    dims, grads_ref, columns_ref, small_ref, out_ref, small_out_ref,
    gall, xsend, xrecv, zsend, zrecv, acc, fin, group_small, own_small, all_small, *sems
):
    steps, width, x_all, z_all, y_all, lag, first_steps = dims
    (gs_s, gs_r, es_s, es_r) = sems[14:]
    (y_s, y_r, core_s, core_r, fwd_s, fwd_r, x_s, x_r, z_s, z_r, zb_s, zb_r, xb_s, xb_r) = sems[:14]
    f32, bf16 = jnp.float32, jnp.bfloat16
    length = grads_ref.shape[0]
    rows = columns_ref.shape[1]
    block = rows // (x_all * z_all)
    half = z_all * block
    e = lax.axis_index("expert")
    s = lax.axis_index("shard")
    z, x = e // x_all, lax.rem(e, x_all)
    y, core = s // 2, lax.rem(s, 2)

    def y_peer(d):
        return {"shard": lax.rem(y + d, y_all) * 2 + core}

    partner = {"shard": y * 2 + (1 - core)}

    def x_peer(d):
        return {"expert": z * x_all + lax.rem(x + d, x_all)}

    def z_peer(d):
        return {"expert": lax.rem(z + d, z_all) * x_all + x}

    def copy(src, dst, send, recv, peer):
        return pltpu.make_async_remote_copy(
            src_ref=src, dst_ref=dst, send_sem=send, recv_sem=recv, device_id=peer,
            device_id_type=pl.DeviceIdType.MESH,
        )

    def cols(c):
        return pl.ds(pl.multiple_of(c * width, width), width)

    def y_copy(d, c):
        return copy(grads_ref.at[:, cols(c)], gall.at[2 * d - 1, c], y_s.at[d - 1], y_r.at[d - 1, c], y_peer(d))

    def core_copy(c):
        return copy(grads_ref.at[:, cols(c)], gall.at[0, c], core_s.at[0], core_r.at[c], partner)

    def fwd_copy(d, c):
        return copy(gall.at[2 * d - 1, c], gall.at[2 * d, c], fwd_s.at[d - 1], fwd_r.at[d - 1, c], partner)

    def x_copy(d, c):
        return copy(xsend.at[d - 1, c], xrecv.at[d - 1, c], x_s.at[d - 1], x_r.at[d - 1, c], x_peer(d))

    def z_copy(d, c):
        return copy(zsend.at[d - 1, c], zrecv.at[d - 1, c], z_s.at[d - 1], z_r.at[d - 1, c], z_peer(d))

    def zb_copy(d, c):
        here = fin.at[c, pl.ds(pl.multiple_of((x * z_all + z) * block, block), block)]
        return copy(here, here, zb_s.at[d - 1], zb_r.at[d - 1, c], z_peer(d))

    def xb_copy(d, c):
        here = fin.at[c, pl.ds(pl.multiple_of(x * half, half), half)]
        return copy(here, here, xb_s.at[d - 1], xb_r.at[d - 1, c], x_peer(d))

    near = [(d, flip) for d in range(y_all) for flip in range(2) if d + flip > 0]
    far = [(dz, dx) for dz in range(z_all) for dx in range(x_all) if dz + dx > 0]

    def near_peer(d, flip):
        return {"shard": lax.rem(y + d, y_all) * 2 + lax.rem(core + flip, 2)}

    def far_peer(dz, dx):
        return {"expert": lax.rem(z + dz, z_all) * x_all + lax.rem(x + dx, x_all)}

    def near_small(d, flip):
        j = 2 * d + flip
        return copy(small_ref.at[j], group_small.at[j - 1], gs_s.at[j - 1], gs_r.at[j - 1], near_peer(d, flip))

    def far_small(dz, dx):
        i = dz * x_all + dx
        return copy(own_small, all_small.at[i - 1], es_s.at[i - 1], es_r.at[i - 1], far_peer(dz, dx))

    barrier = pltpu.get_barrier_semaphore()
    peers = [near_peer(*p) for p in near] + [far_peer(*p) for p in far]
    for peer in peers:
        pl.semaphore_signal(barrier, inc=1, device_id=peer, device_id_type=pl.DeviceIdType.MESH)
    pl.semaphore_wait(barrier, len(peers))

    for p in near:
        near_small(*p).start()

    def first(c, carry):
        for d in range(1, y_all):
            y_copy(d, c).start()
        core_copy(c).start()
        return carry

    lax.fori_loop(0, steps, first, 0)
    slots = acc.shape[0]

    def step(t, carry):
        def stage(k, body):
            c = t - k * lag
            pl.when((c >= 0) & (c < steps))(lambda: body(c))

        @functools.partial(stage, 5)
        def _(c):
            for d in range(1, x_all):
                xb_copy(d, c).wait_recv()
            out_ref[:, cols(c)] = fin[c]

        @functools.partial(stage, 4)
        def _(c):
            for d in range(1, z_all):
                zb_copy(d, c).wait_recv()
            for d in range(1, x_all):
                xb_copy(d, c).start()

        @functools.partial(stage, 3)
        def _(c):
            slot = lax.rem(c, slots)
            total = acc[slot, pl.ds(pl.multiple_of(z * block, block), block), :]
            for d in range(1, z_all):
                z_copy(d, c).wait_recv()
                total = total + zrecv[d - 1, c].astype(f32)
            fin[c, pl.ds(pl.multiple_of((x * z_all + z) * block, block), block), :] = total.astype(bf16)
            for d in range(1, z_all):
                zb_copy(d, c).start()

        @functools.partial(stage, 2)
        def _(c):
            slot = lax.rem(c, slots)
            total = acc[slot]
            for d in range(1, x_all):
                x_copy(d, c).wait_recv()
                total = total + xrecv[d - 1, c].astype(f32)
            acc[slot] = total
            for d in range(1, z_all):
                there = lax.rem(z + d, z_all)
                zsend[d - 1, c] = acc[slot, pl.ds(pl.multiple_of(there * block, block), block), :].astype(bf16)
                z_copy(d, c).start()

        @functools.partial(stage, 1)
        def _(c):
            core_copy(c).wait_recv()
            for d in range(1, y_all):
                fwd_copy(d, c).wait_recv()
            kind = (c >= first_steps).astype(jnp.int32)
            others = gall[:, c].reshape((2 * y_all - 1) * length, width)
            mine = grads_ref[:, cols(c)]

            def product(there):
                at = pl.ds(pl.multiple_of(there * half, half), half)
                return jnp.dot(columns_ref[kind, at, :length], mine, preferred_element_type=f32) + jnp.dot(
                    columns_ref[kind, at, length:], others, preferred_element_type=f32
                )

            for d in range(1, x_all):
                xsend[d - 1, c] = product(lax.rem(x + d, x_all)).astype(bf16)
                x_copy(d, c).start()
            acc[lax.rem(c, slots)] = product(x)

        @functools.partial(stage, 0)
        def _(c):
            for d in range(1, y_all):
                y_copy(d, c).wait_recv()
                fwd_copy(d, c).start()

        @pl.when(t == 2)
        def _():
            total = small_ref[0]
            for j, p in enumerate(near):
                near_small(*p).wait_recv()
                total = total + group_small[j]
            own_small[...] = total
            for p in far:
                far_small(*p).start()

        return carry

    lax.fori_loop(0, steps + 5 * lag, step, 0)
    total = own_small[...]
    for i, p in enumerate(far):
        far_small(*p).wait_recv()
        total = total + all_small[i]
    small_out_ref[...] = total
    for p in near:
        near_small(*p).wait_send()
    for p in far:
        far_small(*p).wait_send()

    for d in range(1, y_all):
        copy(grads_ref, grads_ref, y_s.at[d - 1], y_r.at[d - 1, 0], y_peer(d)).wait_send()
        whole = gall.at[2 * d - 1]
        copy(whole, whole, fwd_s.at[d - 1], fwd_r.at[d - 1, 0], partner).wait_send()
    copy(grads_ref, grads_ref, core_s.at[0], core_r.at[0], partner).wait_send()
    for d in range(1, x_all):
        whole = xsend.at[d - 1]
        copy(whole, whole, x_s.at[d - 1], x_r.at[d - 1, 0], x_peer(d)).wait_send()
        copy(whole, whole, xb_s.at[d - 1], xb_r.at[d - 1, 0], x_peer(d)).wait_send()
    for d in range(1, z_all):
        whole = zsend.at[d - 1]
        copy(whole, whole, z_s.at[d - 1], z_r.at[d - 1, 0], z_peer(d)).wait_send()
        copy(whole, whole, zb_s.at[d - 1], zb_r.at[d - 1, 0], z_peer(d)).wait_send()


def summed_rows(columns, grads, first_total, small, expert_group, shard_group, z_all, width, lag, name_id):
    x_all, y_all = expert_group // z_all, shard_group // 2
    length, total = grads.shape
    rows = columns.shape[1]
    steps = total // width
    block = rows // expert_group
    half = z_all * block
    bf16 = jnp.bfloat16
    dma = pltpu.SemaphoreType.DMA
    n1 = max(y_all - 1, 1)
    x1 = max(x_all - 1, 1)
    z1 = max(z_all - 1, 1)
    slots = min(steps, 2 * lag + 1)
    return pl.pallas_call(
        functools.partial(tail_kernel, (steps, width, x_all, z_all, y_all, lag, first_total // width)),
        out_shape=[
            jax.ShapeDtypeStruct((rows, total), bf16),
            jax.ShapeDtypeStruct(small.shape[1:], jnp.float32),
        ],
        in_specs=[pl.BlockSpec(memory_space=pltpu.VMEM)] * 3,
        out_specs=[pl.BlockSpec(memory_space=pltpu.VMEM)] * 2,
        scratch_shapes=[
            pltpu.VMEM((shard_group - 1, steps, length, width), bf16),
            pltpu.VMEM((x1, steps, half, width), bf16),
            pltpu.VMEM((x1, steps, half, width), bf16),
            pltpu.VMEM((z1, steps, block, width), bf16),
            pltpu.VMEM((z1, steps, block, width), bf16),
            pltpu.VMEM((slots, half, width), jnp.float32),
            pltpu.VMEM((steps, rows, width), bf16),
            pltpu.VMEM((shard_group - 1, *small.shape[1:]), jnp.float32),
            pltpu.VMEM(small.shape[1:], jnp.float32),
            pltpu.VMEM((expert_group - 1, *small.shape[1:]), jnp.float32),
            dma((n1,)), dma((n1, steps)),
            dma((1,)), dma((steps,)),
            dma((n1,)), dma((n1, steps)),
            dma((x1,)), dma((x1, steps)),
            dma((z1,)), dma((z1, steps)),
            dma((z1,)), dma((z1, steps)),
            dma((x1,)), dma((x1, steps)),
            dma((shard_group - 1,)), dma((shard_group - 1,)),
            dma((expert_group - 1,)), dma((expert_group - 1,)),
        ],
        compiler_params=pltpu.CompilerParams(
            collective_id=name_id, has_side_effects=True, vmem_limit_bytes=60 * 1024 * 1024
        ),
        cost_estimate=pl.CostEstimate(
            flops=2 * rows * length * shard_group * total, bytes_accessed=16 * 1024 * 1024, transcendentals=0
        ),
    )(grads, columns, small)


MOE_CHUNKS = 4


def moe_kernel(
    dims, hidden_hbm, upstream_hbm, place_ref, place_t_ref, router_ref, router_t_ref, gate_up_hbm, down_hbm,
    first_hbm, second_hbm, rows_hbm, activated_hbm, grad_out_hbm, grad_gate_up_hbm, grad_ref, grad_router_ref, columns_hbm, found_hbm, summed_hbm,
    *rest,
):
    x_all, capacity, y_all = dims
    mixture_hbm = rest[: 4 * x_all]
    (
    gate_up_w, down_w, hid, ups, prob, prob_t, rows, gate_up, activated, out_rows, grad_expert, grad_gate_up, grad_rows,
    mix_stage, part_stage, own_part, z_landed, router_stage,
    w_sem, own_sem, load_sem, store_sem, zs, zr, xs, xr, fs, fr, ps, pr, qs, qr, rs, rr, lsem, mix_sem, cs, cr, own_c,
    ) = rest[4 * x_all :]
    z_all = 4
    f32, bf16 = jnp.float32, jnp.bfloat16
    length, width = hidden_hbm.shape
    local_experts, _, twice = gate_up_w.shape
    half = twice // 2
    tile = min(512, half)
    narrow = min(256, half)
    chunk = length // MOE_CHUNKS
    e = lax.axis_index("expert")
    z, x = e // x_all, lax.rem(e, x_all)

    def peer(dz, dx):
        return {"expert": lax.rem(z + dz + 4 * z_all, z_all) * x_all + lax.rem(x + dx + 4 * x_all, x_all)}

    def copy(src, dst, send, recv, to):
        return pltpu.make_async_remote_copy(
            src_ref=src, dst_ref=dst, send_sem=send, recv_sem=recv, device_id=to,
            device_id_type=pl.DeviceIdType.MESH,
        )

    def at(c):
        return pl.ds(pl.multiple_of(c * chunk, chunk), chunk)

    def z_copy(d, c):
        return copy(hidden_hbm.at[at(c)], found_hbm.at[d, 0, at(c)], zs.at[d - 1, c], zr.at[d - 1, c], peer(d, 0))

    def x_copy(d, c):
        return copy(hidden_hbm.at[at(c)], found_hbm.at[0, d, at(c)], xs.at[d - 1, c], xr.at[d - 1, c], peer(0, d))

    def f_copy(dz, dx, c):
        return copy(
            found_hbm.at[dz, 0, at(c)], found_hbm.at[dz, dx, at(c)],
            fs.at[dz - 1, dx - 1, c], fr.at[dz - 1, dx - 1, c], peer(0, dx),
        )

    def p_copy(dz, dx, c):
        return copy(
            part_stage.at[dx - 1, at(c)], summed_hbm.at[dz, dx - 1, at(c)],
            ps.at[dx - 1], pr.at[dz, dx - 1, c], peer(0, -dx),
        )

    def p_sent(dx):
        whole = part_stage.at[dx - 1]
        copy(whole, whole, ps.at[dx - 1], pr.at[0, dx - 1, 0], peer(0, -dx)).wait_send()

    def q_copy(dz, c):
        return copy(
            own_part.at[dz, at(c)], z_landed.at[dz - 1, at(c)], qs.at[dz - 1], qr.at[dz - 1, c], peer(-dz, 0)
        )

    def r_copy(dz, dx):
        return copy(
            router_stage.at[dz, dx], grad_router_ref.at[e], rs.at[dz, dx], rr.at[dz, dx], peer(-dz, -dx)
        )

    def cols(n, w):
        return pl.ds(pl.multiple_of(n * w, w), w)

    barrier = pltpu.get_barrier_semaphore()
    others = [(dz, dx) for dz in range(z_all) for dx in range(x_all) if dz + dx > 0]
    near = [(dy, flip) for dy in range(y_all) for flip in range(2) if dy + flip > 0]
    shard = lax.axis_index("shard")

    def near_at(dy, flip):
        return lax.rem(shard // 2 + dy, y_all) * 2 + lax.rem(lax.rem(shard, 2) + flip, 2)

    for dz, dx in others:
        pl.semaphore_signal(barrier, inc=1, device_id=peer(dz, dx), device_id_type=pl.DeviceIdType.MESH)
    for dy, flip in near:
        pl.semaphore_signal(
            barrier, inc=1, device_id={"shard": near_at(dy, flip)}, device_id_type=pl.DeviceIdType.MESH
        )
    pl.semaphore_wait(barrier, len(others) + len(near))

    keep = columns_hbm.shape[3]

    def column_copy(kind, source, dy, flip):
        j = 2 * dy + flip
        there = near_at(dy, flip)
        src = source.at[:, pl.ds(pl.multiple_of(there * keep, keep), keep)]
        if j == 0:
            return pltpu.make_async_copy(src, columns_hbm.at[kind, 0], own_c.at[kind])
        return copy(src, columns_hbm.at[kind, j], cs.at[kind, j - 1], cr.at[kind, j - 1], {"shard": there})

    column_copies = [
        column_copy(kind, source, dy, flip)
        for kind, source in enumerate((first_hbm, second_hbm))
        for dy, flip in [(0, 0)] + near
    ]
    own = pltpu.make_async_copy(hidden_hbm, found_hbm.at[0, 0], own_sem)
    own.start()
    weights = [
        pltpu.make_async_copy(gate_up_hbm, gate_up_w, w_sem.at[0]),
        pltpu.make_async_copy(down_hbm, down_w, w_sem.at[1]),
    ]
    for w in weights:
        w.start()

    def send_own(c, carry):
        for d in range(1, x_all):
            x_copy(d, c).start()
        return carry

    for d in (1, 2, 3):

        def send_z(c, carry):
            z_copy(d, c).start()
            return carry

        lax.fori_loop(0, MOE_CHUNKS, send_z, 0)

    for c in column_copies:
        c.start()

    def events(first, last):
        def one(k, carry):
            @pl.when(k < last)
            def _():
                j = k // MOE_CHUNKS
                c = lax.rem(k, MOE_CHUNKS)
                d = 1 + j
                z_copy(d, c).wait_recv()
                for dx in range(1, x_all):
                    f_copy(d, dx, c).start()

            return carry

        lax.fori_loop(first, first + MOE_CHUNKS, one, 0)

    def own_slots(le):
        return pl.ds(pl.multiple_of(le * capacity, capacity), capacity)

    def finish(dz, last):
        def load(c):
            return pltpu.make_async_copy(summed_hbm.at[dz, dx - 1, at(c)], mix_stage.at[0, at(c)], lsem.at[c])

        def add(c):
            load(c).wait()
            own_part[dz, at(c), :] = (
                own_part[dz, at(c), :].astype(f32) + mix_stage[0, at(c), :].astype(f32)
            ).astype(bf16)
            if dx == x_all - 1:
                if not last:
                    q_copy(dz, c).start()

        def arrive(c, carry):
            p_copy(dz, dx, c).wait_recv()
            load(c).start()
            if last:
                add(c)
            return carry

        def rest(c, carry):
            add(c)
            return carry

        for dx in range(1, x_all):
            lax.fori_loop(0, MOE_CHUNKS, arrive, 0)
            if not last:
                lax.fori_loop(0, MOE_CHUNKS, rest, 0)

    mix_slots = mix_stage.shape[0]

    def mix_copy(dz, dx):
        slot = dx % mix_slots
        return pltpu.make_async_copy(mix_stage.at[slot], mixture_hbm[dz * x_all + dx], mix_sem.at[slot])

    def pieces(p):
        return 4 + sum(n * (p >= k).astype(jnp.int32) for k, n in enumerate((1, 1, 1, 1, 1, 2, 1, 0)))

    def group_at(g):
        return lax.rem(g + 1, z_all)

    slot_row = lax.broadcasted_iota(jnp.int32, (capacity, length), 0).astype(f32)
    slot_col = lax.broadcasted_iota(jnp.int32, (length, local_experts * capacity), 1).astype(f32)
    own.wait()
    events(0, 4)
    lax.fori_loop(0, MOE_CHUNKS, send_own, 0)

    def load_upstream(dz):
        return [pltpu.make_async_copy(upstream_hbm.at[dz, dx], ups.at[dx], load_sem.at[1, dx]) for dx in range(x_all)]

    for load in load_upstream(1):
        load.start()

    def group(g, carry):
        dz = group_at(g)

        def arrive(c, inner):
            for dx in range(1, x_all):

                @pl.when(dz == 0)
                def _():
                    x_copy(dx, c).wait_recv()

                @pl.when(dz > 0)
                def _():
                    f_copy(dz, dx, c).wait_recv()

            return inner

        lax.fori_loop(0, MOE_CHUNKS, arrive, 0)
        loads = []
        for dx in range(x_all):
            loads.append(pltpu.make_async_copy(found_hbm.at[dz, dx], hid.at[dx], load_sem.at[0, dx]))
        for load in loads:
            load.start()
        for load in loads + load_upstream(dz):
            load.wait()
        pl.when(g == 0)(lambda: [w.wait() for w in weights] and None)

        for dx in range(x_all):
            logits = jnp.dot(hid[dx], router_ref[...], preferred_element_type=f32)
            raised = jnp.exp(logits - jnp.max(logits, axis=1, keepdims=True))
            prob[dx] = raised / jnp.sum(raised, axis=1, keepdims=True)
            logits = lax.dot_general(
                router_t_ref[...], hid[dx], (((1,), (1,)), ((), ())), preferred_element_type=f32
            )
            raised = jnp.exp(logits - jnp.max(logits, axis=0, keepdims=True))
            prob_t[dx] = raised / jnp.sum(raised, axis=0, keepdims=True)
            router_stage[dz, dx] = jnp.zeros(router_stage.shape[2:], f32)

        def store(kind, buffer, hbm, le):
            return pltpu.make_async_copy(buffer, hbm.at[le, dz], store_sem.at[kind])

        def expert(le, inner):
            @pl.when(g + le > 0)
            def _():
                store(0, rows, rows_hbm, le).wait()
                store(1, activated, activated_hbm, le).wait()
                store(2, grad_expert, grad_out_hbm, le).wait()
                store(3, grad_gate_up, grad_gate_up_hbm, le).wait()

            chosen = [place_ref[dz, dx, pl.ds(le, 1), :] == slot_row for dx in range(x_all)]
            chosen_low = [c.astype(f32).astype(bf16) for c in chosen]

            def dispatch(n, c0):
                c = cols(n, tile)
                for dx in range(x_all):
                    rows[dx * capacity : (dx + 1) * capacity, c] = jnp.dot(
                        chosen_low[dx], hid[dx, :, c], preferred_element_type=f32
                    ).astype(bf16)
                return c0

            lax.fori_loop(0, width // tile, dispatch, 0, unroll=True)
            store(0, rows, rows_hbm, le).start()

            def up_step(n, c0):
                c = cols(n, tile)
                gate_up[:, c] = jnp.dot(rows[...], gate_up_w[le, :, c], preferred_element_type=f32)
                return c0

            lax.fori_loop(0, twice // tile, up_step, 0, unroll=True)

            def act_step(n, c0):
                gate = gate_up[:, cols(n, narrow)]
                up = gate_up[:, pl.ds(pl.multiple_of(half + n * narrow, narrow), narrow)]
                activated[:, cols(n, narrow)] = (gate / (1.0 + jnp.exp(-gate)) * up).astype(bf16)
                return c0

            lax.fori_loop(0, half // narrow, act_step, 0, unroll=True)
            store(1, activated, activated_hbm, le).start()

            def down_step(n, c0):
                c = cols(n, tile)
                result = jnp.dot(activated[...], down_w[le, :, c], preferred_element_type=f32)
                for dx in range(x_all):
                    r = slice(dx * capacity, (dx + 1) * capacity)
                    out_rows[dx, own_slots(le), c] = result[r].astype(bf16)
                return c0

            lax.fori_loop(0, width // tile, down_step, 0, unroll=True)

            events(pieces(4 * g + 2 * le - 1), pieces(4 * g + 2 * le))

            mine = e * local_experts + le
            weight_rows = [
                jnp.sum(jnp.where(chosen[dx], prob_t[dx, pl.ds(mine, 1), :], 0.0), axis=1, keepdims=True)
                for dx in range(x_all)
            ]

            def grad_step(n, totals):
                c = cols(n, tile)
                new = []
                for dx in range(x_all):
                    r = slice(dx * capacity, (dx + 1) * capacity)
                    up_rows = jnp.dot(chosen_low[dx], ups[dx, :, c], preferred_element_type=f32)
                    grad_expert[r, c] = (weight_rows[dx] * up_rows).astype(bf16)
                    new.append(
                        totals[dx]
                        + jnp.sum(up_rows * out_rows[dx, own_slots(le), c].astype(f32), axis=1, keepdims=True)
                    )
                return tuple(new)

            totals = lax.fori_loop(
                0, width // tile, grad_step, tuple(jnp.zeros((capacity, 1), f32) for _ in range(x_all)),
                unroll=True,
            )
            store(2, grad_expert, grad_out_hbm, le).start()
            for dx in range(x_all):
                router_stage[dz, dx, pl.ds(le, 1), :] = jnp.sum(
                    jnp.where(chosen[dx], totals[dx], 0.0), axis=0, keepdims=True
                )

            def back_step(n, c0):
                ga = lax.dot_general(
                    grad_expert[...], down_w[le, cols(n, narrow), :], (((1,), (1,)), ((), ())),
                    preferred_element_type=f32,
                )
                gate = gate_up[:, cols(n, narrow)]
                c_up = pl.ds(pl.multiple_of(half + n * narrow, narrow), narrow)
                up = gate_up[:, c_up]
                sg = 1.0 / (1.0 + jnp.exp(-gate))
                grad_gate_up[:, cols(n, narrow)] = (ga * up * sg * (1.0 + gate * (1.0 - sg))).astype(bf16)
                grad_gate_up[:, c_up] = (ga * (gate * sg)).astype(bf16)
                return c0

            lax.fori_loop(0, half // narrow, back_step, 0, unroll=True)
            store(3, grad_gate_up, grad_gate_up_hbm, le).start()

            def row_step(n, c0):
                result = lax.dot_general(
                    grad_gate_up[...], gate_up_w[le, cols(n, narrow), :], (((1,), (1,)), ((), ())),
                    preferred_element_type=f32,
                )
                for dx in range(x_all):
                    r = slice(dx * capacity, (dx + 1) * capacity)
                    grad_rows[dx, own_slots(le), cols(n, narrow)] = result[r].astype(bf16)
                return c0

            lax.fori_loop(0, width // narrow, row_step, 0, unroll=True)
            events(pieces(4 * g + 2 * le), pieces(4 * g + 2 * le + 1))

            @pl.when((le == 0) & (g > 0))
            def _():
                for dx in range(mix_slots):
                    mix_copy(0, dx).wait()
                finish(group_at(g - 1), False)

            return inner

        assert local_experts == 2
        lax.fori_loop(0, local_experts, expert, 0)

        @pl.when(g < z_all - 1)
        def _():
            for load in load_upstream(group_at(g + 1)):
                load.start()

        def stages():
            for dx in range(1, x_all):
                p_sent(dx)

        pl.when(g > 0)(stages)
        for dx in range(x_all):
            weight = jnp.zeros(slot_col.shape, f32)
            mask = jnp.zeros(slot_col.shape, f32)
            lane = lax.broadcasted_iota(jnp.int32, prob.shape[1:], 1)
            for le in range(local_experts):
                spot = place_t_ref[dz, dx, :, le : le + 1]
                here = jnp.where(spot < 0.0, -1.0, spot + le * capacity) == slot_col
                p = jnp.sum(jnp.where(lane == e * local_experts + le, prob[dx], 0.0), axis=1, keepdims=True)
                weight = jnp.where(here, p, weight)
                mask = jnp.where(here, 1.0, mask)
            low = mask.astype(bf16)
            high = weight.astype(bf16)
            remainder = (weight - high.astype(f32)).astype(bf16)

            if dx >= mix_slots:
                mix_copy(0, dx).wait()

            def combine(n, c0):
                c = cols(n, tile)
                mix = jnp.dot(high, out_rows[dx, :, c], preferred_element_type=f32) + jnp.dot(
                    remainder, out_rows[dx, :, c], preferred_element_type=f32
                )
                grad = jnp.dot(low, grad_rows[dx, :, c], preferred_element_type=f32)
                mix_stage[dx % mix_slots, :, c] = mix.astype(bf16)
                if dx == 0:
                    own_part[dz, :, c] = grad.astype(bf16)
                else:
                    part_stage[dx - 1, :, c] = grad.astype(bf16)
                return c0

            lax.fori_loop(0, width // tile, combine, 0, unroll=True)
            for k in range(z_all):
                pl.when(dz == k)(mix_copy(k, dx).start)
            if dx > 0:
                for c in range(MOE_CHUNKS):
                    p_copy(dz, dx, c).start()
                r_copy(dz, dx).start()
            else:

                @pl.when(dz > 0)
                def _():
                    r_copy(dz, 0).start()

                @pl.when(dz == 0)
                def _():
                    grad_router_ref[e] = router_stage[0, 0]

        return carry

    lax.fori_loop(0, z_all, group, 0)
    for dx in range(mix_slots):
        mix_copy(0, dx).wait()
    finish(0, True)

    def total(c, carry):
        grad_ref[at(c), :] = own_part[0, at(c), :].astype(f32)
        for d in (1, 2, 3):
            q_copy(d, c).wait_recv()
            grad_ref[at(c), :] = grad_ref[at(c), :] + z_landed[d - 1, at(c), :].astype(f32)
        return carry

    lax.fori_loop(0, MOE_CHUNKS, total, 0)

    for c in column_copies:
        c.wait()
    for kind, buffer, hbm in (
        (0, rows, rows_hbm), (1, activated, activated_hbm), (2, grad_expert, grad_out_hbm),
        (3, grad_gate_up, grad_gate_up_hbm),
    ):
        pltpu.make_async_copy(buffer, hbm.at[0, 0], store_sem.at[kind]).wait()
    for dx in range(1, x_all):
        p_sent(dx)
    for d in range(1, z_all):
        whole = own_part.at[d]
        copy(whole, whole, qs.at[d - 1], qr.at[d - 1, 0], peer(-d, 0)).wait_send()
    for dz, dx in others:
        r_copy(dz, dx).wait_send()
        r_copy(dz, dx).wait_recv()

    def sent(c, carry):
        for d in range(1, z_all):
            z_copy(d, c).wait_send()
            for dx in range(1, x_all):
                f_copy(d, dx, c).wait_send()
        for d in range(1, x_all):
            x_copy(d, c).wait_send()
        return carry

    lax.fori_loop(0, MOE_CHUNKS, sent, 0)


def moe_layer(
    hidden, upstream_all, place, router_weight, gate_up_weight, down_weight, first, second, expert_group, shard_group,
    capacity, name_id,
):
    f32, bf16 = jnp.float32, jnp.bfloat16
    length, width = hidden.shape
    local_experts, _, twice = gate_up_weight.shape
    half = twice // 2
    experts_all = router_weight.shape[1]
    x_all = expert_group // 4
    count = x_all * capacity
    dma = pltpu.SemaphoreType.DMA
    x1 = max(x_all - 1, 1)
    place_t = place.transpose(0, 1, 3, 2)
    spare = (-local_experts) % 8
    place = jnp.pad(place, ((0, 0), (0, 0), (0, spare), (0, 0)), constant_values=-1.0)
    any_spec = pl.BlockSpec(memory_space=pl.ANY)
    vmem_spec = pl.BlockSpec(memory_space=pltpu.VMEM)
    out = pl.pallas_call(
        functools.partial(moe_kernel, (x_all, capacity, shard_group // 2)),
        out_shape=[
            jax.ShapeDtypeStruct((local_experts, 4, count, width), bf16),
            jax.ShapeDtypeStruct((local_experts, 4, count, half), bf16),
            jax.ShapeDtypeStruct((local_experts, 4, count, width), bf16),
            jax.ShapeDtypeStruct((local_experts, 4, count, twice), bf16),
            jax.ShapeDtypeStruct((length, width), f32),
            jax.ShapeDtypeStruct((expert_group, 8, length), f32),
            jax.ShapeDtypeStruct((2, shard_group, length, width // shard_group), bf16),
            jax.ShapeDtypeStruct((4, x_all, length, width), bf16),
            jax.ShapeDtypeStruct((4, x1, length, width), bf16),
        ]
        + [jax.ShapeDtypeStruct((length, width), bf16)] * (4 * x_all),
        in_specs=[any_spec, any_spec, vmem_spec, vmem_spec, vmem_spec, vmem_spec, any_spec, any_spec, any_spec, any_spec],
        out_specs=[any_spec] * 4 + [vmem_spec, vmem_spec] + [any_spec] * (3 + 4 * x_all),
        scratch_shapes=[
            pltpu.VMEM(gate_up_weight.shape, bf16),
            pltpu.VMEM(down_weight.shape, bf16),
            pltpu.VMEM((x_all, length, width), bf16),
            pltpu.VMEM((x_all, length, width), bf16),
            pltpu.VMEM((x_all, length, experts_all), f32),
            pltpu.VMEM((x_all, experts_all, length), f32),
            pltpu.VMEM((count, width), bf16),
            pltpu.VMEM((count, twice), f32),
            pltpu.VMEM((count, half), bf16),
            pltpu.VMEM((x_all, local_experts * capacity, width), bf16),
            pltpu.VMEM((count, width), bf16),
            pltpu.VMEM((count, twice), bf16),
            pltpu.VMEM((x_all, local_experts * capacity, width), bf16),
            pltpu.VMEM((min(2, x_all), length, width), bf16),
            pltpu.VMEM((x1, length, width), bf16),
            pltpu.VMEM((4, length, width), bf16),
            pltpu.VMEM((3, length, width), bf16),
            pltpu.VMEM((4, x_all, 8, length), f32),
            dma((2,)), dma, dma((2, x_all)), dma((4,)),
            dma((3, MOE_CHUNKS)), dma((3, MOE_CHUNKS)),
            dma((x1, MOE_CHUNKS)), dma((x1, MOE_CHUNKS)),
            dma((3, x1, MOE_CHUNKS)), dma((3, x1, MOE_CHUNKS)),
            dma((x1,)), dma((4, x1, MOE_CHUNKS)),
            dma((3,)), dma((3, MOE_CHUNKS)),
            dma((4, x_all)), dma((4, x_all)),
            dma((MOE_CHUNKS,)), dma((min(2, x_all),)),
            dma((2, shard_group - 1)), dma((2, shard_group - 1)), dma((2,)),
        ],
        compiler_params=pltpu.CompilerParams(
            collective_id=name_id, has_side_effects=True, vmem_limit_bytes=62 * 1024 * 1024
        ),
        cost_estimate=pl.CostEstimate(
            flops=12 * 4 * local_experts * count * width * twice, bytes_accessed=64 * 1024 * 1024,
            transcendentals=0,
        ),
    )(
        hidden, upstream_all, place, place_t, router_weight, router_weight.T, gate_up_weight, down_weight,
        first, second,
    )
    return out[:7], out[9:]


def start_kernel(
    dims, weight_hbm, upstream_hbm, router_hbm, gains_ref, tokens_ref, routes_ref, tiles_ref,
    full_hbm, ups_hbm, router_full_hbm, gains_full_ref, place_all_ref, hidden_ref, *sems,
):
    x_all, y_all = dims
    z_all, parts = 4, 4
    (own_sem, ys, yr, rs, rr, cs, cr, fs, fr, gs, gr, zs, zr, xs, xr, us, ur, ns, nr, ps, pr, ms, mr) = sems
    f32, bf16 = jnp.float32, jnp.bfloat16
    rows = weight_hbm.shape[0]
    length = tokens_ref.shape[0]
    piece = rows // 8
    chunk = length // parts
    e = lax.axis_index("expert")
    s = lax.axis_index("shard")
    z, x = e // x_all, lax.rem(e, x_all)
    y, core = s // 2, lax.rem(s, 2)
    parity = lax.rem(z, 2)

    def expert_peer(dz, dx):
        return {"expert": lax.rem(z + dz, z_all) * x_all + lax.rem(x + dx, x_all)}

    def shard_peer(dy, flip):
        return {"shard": lax.rem(y + dy, y_all) * 2 + lax.rem(core + flip, 2)}

    beside = {"expert": (z + 1 - 2 * parity) * x_all + x}
    partner = shard_peer(0, 1)
    far = [(dz, dx) for dz in range(z_all) for dx in range(x_all) if dz + dx > 0]
    near = [(dy, flip) for dy in range(y_all) for flip in range(2) if dy + flip > 0]

    def copy(src, dst, send, recv, to):
        return pltpu.make_async_remote_copy(
            src_ref=src, dst_ref=dst, send_sem=send, recv_sem=recv, device_id=to,
            device_id_type=pl.DeviceIdType.MESH,
        )

    def piece_of(i, who):
        return jnp.where(i < 2, 4 + 2 * who + i, i - 2)

    def span(owner, k):
        return pl.ds(pl.multiple_of(owner * rows + k * piece, piece), piece)

    def y_copy(dy, i):
        k = piece_of(i, parity)
        src = weight_hbm.at[pl.ds(pl.multiple_of(k * piece, piece), piece)]
        return copy(src, full_hbm.at[span(s, k)], ys.at[dy - 1, i], yr.at[dy - 1, i], shard_peer(dy, 0))

    def owner(dy):
        return lax.rem(y - dy + y_all, y_all) * 2 + core

    def relay(dy, i):
        here = full_hbm.at[span(owner(dy), 4 + 2 * parity + i)]
        return copy(here, here, rs.at[dy - 1, i], rr.at[dy - 1, i], beside)

    def core_y(dy, i):
        here = full_hbm.at[span(owner(dy), piece_of(i, parity))]
        return copy(here, here, cs.at[dy - 1, i], cr.at[dy - 1, i], partner)

    def core_r(dy, i):
        here = full_hbm.at[span(owner(dy), 4 + 2 * (1 - parity) + i)]
        return copy(here, here, fs.at[dy - 1, i], fr.at[dy - 1, i], partner)

    whole = pl.ds(pl.multiple_of(s * rows, rows), rows)
    core_own = copy(weight_hbm, full_hbm.at[whole], gs, gr, partner)

    def at(c):
        return pl.ds(pl.multiple_of(c * chunk, chunk), chunk)

    def z_copy(d, c):
        return copy(upstream_hbm.at[at(c)], ups_hbm.at[d, 0, at(c)], zs.at[d - 1, c], zr.at[d - 1, c], expert_peer(d, 0))

    def x_copy(d):
        return copy(upstream_hbm, ups_hbm.at[0, d], xs.at[d - 1], xr.at[d - 1], expert_peer(0, d))

    def u_copy(dz, dx, c):
        return copy(
            ups_hbm.at[dz, 0, at(c)], ups_hbm.at[dz, dx, at(c)],
            us.at[dz - 1, dx - 1, c], ur.at[dz - 1, dx - 1, c], expert_peer(0, dx),
        )

    def router_copy(n, p):
        return copy(router_hbm, router_full_hbm.at[whole], ns.at[n], nr.at[n], shard_peer(*p))

    def gains_copy(n, p):
        return copy(gains_ref, gains_full_ref.at[s], ms.at[n], mr.at[n], shard_peer(*p))

    def place_copy(n, p):
        return copy(place_all_ref.at[0, 0], place_all_ref.at[p[0], p[1]], ps.at[n], pr.at[n], expert_peer(*p))

    barrier = pltpu.get_barrier_semaphore()
    peers = [expert_peer(*p) for p in far] + [shard_peer(*p) for p in near]
    for peer in peers:
        pl.semaphore_signal(barrier, inc=1, device_id=peer, device_id_type=pl.DeviceIdType.MESH)
    pl.semaphore_wait(barrier, len(peers))

    own = [
        pltpu.make_async_copy(weight_hbm, full_hbm.at[whole], own_sem.at[0]),
        pltpu.make_async_copy(upstream_hbm, ups_hbm.at[0, 0], own_sem.at[1]),
        pltpu.make_async_copy(router_hbm, router_full_hbm.at[whole], own_sem.at[2]),
    ]
    for n, p in enumerate(near):
        gains_copy(n, p).start()
        router_copy(n, p).start()
    for i in range(2):
        for dy in range(1, y_all):
            y_copy(dy, i).start()
    for d in range(1, x_all):
        x_copy(d).start()
    for d in (1, 3, 2):
        for c in range(parts):
            z_copy(d, c).start()
    core_own.start()
    for o in own:
        o.start()

    count = place_all_ref.shape[2]
    ids = lax.broadcasted_iota(jnp.int32, (count, length), 0)
    chosen = jnp.zeros((count, length), f32)
    for k in range(TOP):
        chosen = jnp.where(routes_ref[k : k + 1, :] == ids, 1.0, chosen)
    before = lax.broadcasted_iota(jnp.int32, (length, length), 0)
    after = lax.broadcasted_iota(jnp.int32, (length, length), 1)
    earlier = jnp.where(before < after, 1.0, 0.0).astype(bf16)
    rank = jnp.dot(chosen.astype(bf16), earlier, preferred_element_type=f32)
    limit = (tiles_ref[...] * TILE).astype(f32)
    place_all_ref[0, 0] = jnp.where((chosen > 0.5) & (rank < limit), rank, -1.0)
    for n, p in enumerate(far):
        place_copy(n, p).start()

    gains_full_ref[s] = gains_ref[...]
    for n, p in enumerate(near):
        gains_copy(n, p).wait_recv()
    keep = gains_ref.shape[1]
    tall = 64

    def norm(t, carry):
        r = pl.ds(pl.multiple_of(t * tall, tall), tall)
        values = tokens_ref[r, :].astype(f32)
        scale = lax.rsqrt(jnp.mean(values * values, axis=1, keepdims=True) + epsilon)
        for j in range(2 * y_all):
            c = slice(j * keep, (j + 1) * keep)
            gain = gains_full_ref[j, 0:1, :].astype(f32)
            hidden_ref[r, c] = (values[:, c] * scale * gain).astype(bf16)
        return carry

    lax.fori_loop(0, length // tall, norm, 0)

    def forward(events):
        for d, c in events:
            z_copy(d, c).wait_recv()
            for dx in range(1, x_all):
                u_copy(d, dx, c).start()

    order = {
        0: [(1, 0)], 1: [(1, 1), (1, 2)], 2: [(1, 3), (3, 0), (3, 1)], 3: [(3, 2), (3, 3), (2, 0)],
        4: [(2, 1), (2, 2), (2, 3)], 5: [],
    }
    for i in range(6):
        for dy in range(1, y_all):
            y_copy(dy, i).wait_recv()
            if i < 2:
                relay(dy, i).start()
            core_y(dy, i).start()
            if i < 4:
                y_copy(dy, i + 2).start()
        forward(order[i])
        if i in (3, 4):
            for dy in range(1, y_all):
                here = full_hbm.at[span(owner(dy), 4 + 2 * (1 - parity) + i - 3)]
                copy(here, here, rs.at[dy - 1, i - 3], rr.at[dy - 1, i - 3], beside).wait_recv()
                core_r(dy, i - 3).start()

    for o in own:
        o.wait()
    core_own.wait()
    for n, p in enumerate(near):
        gains_copy(n, p).wait_send()
        router_copy(n, p).wait()
    for n, p in enumerate(far):
        place_copy(n, p).wait()
    for d in range(1, x_all):
        x_copy(d).wait()
    for dy in range(1, y_all):
        for i in range(6):
            y_copy(dy, i).wait_send()
            core_y(dy, i).wait()
        for i in range(2):
            relay(dy, i).wait_send()
            core_r(dy, i).wait()
    for d in range(1, z_all):
        for c in range(parts):
            z_copy(d, c).wait_send()
            for dx in range(1, x_all):
                u_copy(d, dx, c).wait()


def start_layer(weight, upstream, router, gains, tokens, routes, tile_counts, expert_group, shard_group, name_id):
    f32, bf16 = jnp.float32, jnp.bfloat16
    length, width = tokens.shape
    x_all, y_all = expert_group // 4, shard_group // 2
    experts_all = tile_counts.shape[0]
    dma = pltpu.SemaphoreType.DMA
    y1, x1 = max(y_all - 1, 1), max(x_all - 1, 1)
    any_spec = pl.BlockSpec(memory_space=pl.ANY)
    vmem_spec = pl.BlockSpec(memory_space=pltpu.VMEM)
    return pl.pallas_call(
        functools.partial(start_kernel, (x_all, y_all)),
        out_shape=[
            jax.ShapeDtypeStruct((weight.shape[0] * shard_group, weight.shape[1]), bf16),
            jax.ShapeDtypeStruct((4, x_all, length, width), bf16),
            jax.ShapeDtypeStruct((router.shape[0] * shard_group, router.shape[1]), bf16),
            jax.ShapeDtypeStruct((shard_group, *gains.shape), bf16),
            jax.ShapeDtypeStruct((4, x_all, experts_all, length), f32),
            jax.ShapeDtypeStruct((length, width), bf16),
        ],
        in_specs=[any_spec] * 3 + [vmem_spec] * 4,
        out_specs=[any_spec] * 3 + [vmem_spec] * 3,
        scratch_shapes=[
            dma((3,)),
            dma((y1, 6)), dma((y1, 6)),
            dma((y1, 2)), dma((y1, 2)),
            dma((y1, 6)), dma((y1, 6)),
            dma((y1, 2)), dma((y1, 2)),
            dma, dma,
            dma((3, 4)), dma((3, 4)),
            dma((x1,)), dma((x1,)),
            dma((3, x1, 4)), dma((3, x1, 4)),
            dma((shard_group - 1,)), dma((shard_group - 1,)),
            dma((expert_group - 1,)), dma((expert_group - 1,)),
            dma((shard_group - 1,)), dma((shard_group - 1,)),
        ],
        compiler_params=pltpu.CompilerParams(
            collective_id=name_id, has_side_effects=True, vmem_limit_bytes=32 * 1024 * 1024
        ),
        cost_estimate=pl.CostEstimate(
            flops=16 * length * width, bytes_accessed=64 * 1024 * 1024, transcendentals=0
        ),
    )(weight, upstream, router, gains, tokens, routes.T, tile_counts[:, None])


def body(
    tokens,
    cotangent,
    segments,
    routes,
    tile_counts,
    norm_one,
    norm_query,
    norm_key,
    norm_two,
    qkv_weight,
    out_weight,
    router_weight,
    gate_up_weight,
    down_weight,
):
    f32, bf16 = jnp.float32, jnp.bfloat16
    length, model_width = tokens.shape
    experts_all = tile_counts.shape[0]
    local_experts = gate_up_weight.shape[0]
    expert_group = lax.axis_size("expert")
    shard_group = lax.axis_size("shard")
    capacity = length * TOP // (experts_all * TILE) * TILE
    score_scale = HEAD_DIM ** (-0.5)
    own_expert = lax.axis_index("expert")
    own_shard = lax.axis_index("shard")
    z_all = z_size(expert_group)
    x_all = expert_group // z_all

    gain_rows = jnp.stack([norm_one, norm_query, norm_key, norm_two])
    gain_rows = jnp.pad(gain_rows, ((0, 12), (0, 0)))
    qkv_full, upstream_all, router_full, gains, place_all, hidden_one = start_layer(
        qkv_weight,
        cotangent,
        router_weight,
        gain_rows,
        tokens,
        routes,
        tile_counts,
        expert_group,
        shard_group,
        3,
    )
    out_own, gains = lax.optimization_barrier((out_weight, gains))
    out_full = lax.all_gather(out_own, "shard", axis=0, tiled=True)
    gains = gains.transpose(1, 0, 2).reshape(gains.shape[1], model_width).astype(f32)
    gain_one, gain_query, gain_key, gain_two = gains[0], gains[1], gains[2], gains[3]
    place_own = lax.dynamic_slice_in_dim(
        place_all, own_expert * local_experts, local_experts, axis=2
    )
    position = jnp.arange(length, dtype=jnp.int32)

    inputs = tokens.astype(f32)
    _, first_pull = jax.vjp(rms_scale, inputs, gain_one)
    projected = jnp.dot(hidden_one, qkv_full, preferred_element_type=f32)
    cosine, sine_table = rotary_tables(length)

    def query_key_local(raw_query, raw_key, query_gain, key_gain):
        return query_key(raw_query, raw_key, query_gain, key_gain, cosine, sine_table)

    rotated, rotary_pull = jax.vjp(
        query_key_local,
        projected[:, :model_width],
        projected[:, model_width : 2 * model_width],
        gain_query,
        gain_key,
    )
    query_low = rotated[0].astype(bf16)
    key_low = rotated[1].astype(bf16)
    value_low = projected[:, 2 * model_width :].astype(bf16).reshape(length, HEADS, HEAD_DIM)
    allowed = (position[:, None] >= position[None, :]) & (
        segments[0][:, None] == segments[0][None, :]
    )
    masked = jnp.where(
        allowed[None],
        jnp.einsum("qhd,khd->hqk", query_low, key_low, preferred_element_type=f32) * score_scale,
        -1e30,
    )
    probs = softmax_rows(masked)
    probs_low = probs.astype(bf16)
    attended_low = (
        jnp.einsum("hqk,khd->qhd", probs_low, value_low, preferred_element_type=f32)
        .reshape(length, model_width)
        .astype(bf16)
    )
    middle = inputs + jnp.dot(attended_low, out_full, preferred_element_type=f32)
    scaled_two, second_pull = jax.vjp(rms_scale, middle, gain_two)
    hidden_two = scaled_two.astype(bf16)
    router = softmax_rows(jnp.dot(hidden_two, router_full, preferred_element_type=f32))
    row_count = expert_group * capacity
    done, mixture_parts = moe_layer(
        hidden_two,
        upstream_all,
        place_own,
        router_full,
        gate_up_weight,
        down_weight,
        attended_low,
        hidden_one,
        expert_group,
        shard_group,
        capacity,
        2,
    )
    columns = done[6].reshape(2, shard_group * length, -1).swapaxes(1, 2)
    expert_rows, activated, grad_expert, grad_gate_up_low = (
        a.reshape(local_experts, row_count, a.shape[-1]) for a in done[:4]
    )
    grad_rows_sum = done[4]
    grad_router = done[5][:, :local_experts].reshape(experts_all, length).T
    parts = dict(enumerate(mixture_parts))

    def slot(values, *names):
        held = lax.optimization_barrier((values, [parts[n] for n in names]))
        parts.update(zip(names, held[1], strict=True))
        return held[0]

    def group(dz):
        return [dz * x_all + dx for dx in range(x_all)]

    upstream = cotangent.astype(f32)
    grad_logits = (
        router * (grad_router - jnp.sum(router * grad_router, axis=-1, keepdims=True))
    ).astype(bf16)
    grad_hidden_two = grad_rows_sum + jnp.einsum(
        "te,de->td", grad_logits, router_full, preferred_element_type=f32
    )
    grad_middle_norm, grad_gain_two = second_pull(grad_hidden_two)
    grad_middle = upstream + grad_middle_norm
    two = sum_over_x(parts, 2, expert_group).astype(bf16)
    grad_middle, expert_rows, two = slot((grad_middle, expert_rows, two), *group(1))
    halves = [two[: length // 2], two[length // 2 :]]
    halves[0] = back_along_z(halves[0], 2, expert_group)
    one = sum_over_x(parts, 1, expert_group).astype(bf16)
    grad_gate_up_full = jnp.einsum(
        "erd,erf->edf", expert_rows, grad_gate_up_low, preferred_element_type=f32
    ).astype(bf16)
    grad_middle, grad_gate_up_full, activated, halves, one = slot(
        (grad_middle, grad_gate_up_full, activated, halves, one), *group(3)
    )
    grad_gate_up_weight = lax.psum_scatter(
        grad_gate_up_full, "shard", scatter_dimension=1, tiled=True
    ).astype(f32)
    halves[1] = back_along_z(halves[1], 2, expert_group)
    three = sum_over_x(parts, 3, expert_group).astype(bf16)
    grad_down_full = jnp.einsum(
        "erf,erd->efd", activated, grad_expert, preferred_element_type=f32
    ).astype(bf16)
    grad_middle, grad_down_full, halves, one, three = slot(
        (grad_middle, grad_down_full, halves, one, three), *group(0)
    )
    grad_down_weight = lax.psum_scatter(
        grad_down_full, "shard", scatter_dimension=2, tiled=True
    ).astype(f32)
    one = back_along_z(one, 1, expert_group)
    here = sum_over_x(parts, 0, expert_group)
    grad_branch_low = grad_middle.astype(bf16)
    grad_attended_low = (
        jnp.einsum("te,de->td", grad_branch_low, out_full, preferred_element_type=f32)
        .astype(bf16)
        .reshape(length, HEADS, HEAD_DIM)
    )
    grad_probs = jnp.einsum(
        "qhd,khd->hqk", grad_attended_low, value_low, preferred_element_type=f32
    )
    grad_scores_low = (
        probs * (grad_probs - jnp.sum(probs * grad_probs, axis=-1, keepdims=True))
    ).astype(bf16)
    grad_scores_low, one, here, three = slot((grad_scores_low, one, here, three))
    three = back_along_z(three, 3, expert_group)
    grad_queries = (
        jnp.einsum("hqk,khd->qhd", grad_scores_low, key_low, preferred_element_type=f32)
        * score_scale
    )
    grad_keys = (
        jnp.einsum("hqk,qhd->khd", grad_scores_low, query_low, preferred_element_type=f32)
        * score_scale
    )
    grad_values = jnp.einsum(
        "hqk,qhd->khd", probs_low, grad_attended_low, preferred_element_type=f32
    )
    grad_raw_query, grad_raw_key, grad_gain_query, grad_gain_key = rotary_pull(
        (grad_queries, grad_keys)
    )
    grad_projected_low = jnp.concatenate(
        [grad_raw_query, grad_raw_key, grad_values.reshape(length, model_width)], axis=-1
    ).astype(bf16)
    grad_hidden_one = jnp.einsum(
        "te,de->td", grad_projected_low, qkv_full, preferred_element_type=f32
    )
    grad_inputs_norm, grad_gain_one = first_pull(grad_hidden_one)
    grad_tokens = grad_middle + grad_inputs_norm

    grad_router_part = jnp.einsum("td,te->ed", hidden_two, grad_logits, preferred_element_type=f32)
    small = jnp.concatenate(
        [
            grad_router_part,
            jnp.stack([grad_gain_one, grad_gain_query, grad_gain_key, grad_gain_two]),
            jnp.zeros((-(experts_all + 4) % 8, model_width), f32),
        ],
        axis=0,
    )
    keep = norm_one.shape[0]
    small = jnp.stack(
        [
            lax.dynamic_slice_in_dim(
                small,
                (((own_shard // 2 + dy) % (shard_group // 2)) * 2 + (own_shard % 2 + flip) % 2) * keep,
                keep,
                axis=1,
            )
            for dy in range(shard_group // 2)
            for flip in range(2)
        ]
    )

    grads_low = jnp.concatenate([grad_branch_low, grad_projected_low], axis=1)
    grads_low, three = slot((grads_low, three))
    mixture = sum((a.astype(f32) for a in (one, jnp.concatenate(halves), three)), here)
    block_out = (middle + mixture).astype(bf16)
    grad_rows_kept, small = summed_rows(
        columns, grads_low, model_width, small, expert_group, shard_group, z_all, 256, 3, 1
    )
    grad_out_weight = grad_rows_kept[:, :model_width].astype(f32)
    grad_qkv_weight = grad_rows_kept[:, model_width:].astype(f32)
    return (
        block_out,
        grad_tokens,
        small[experts_all],
        small[experts_all + 1],
        small[experts_all + 2],
        small[experts_all + 3],
        grad_qkv_weight,
        grad_out_weight,
        small[:experts_all].T,
        grad_gate_up_weight,
        grad_down_weight,
    )


def solution(mesh):
    return jax.shard_map(
        body,
        mesh=mesh,
        in_specs=(
            P(("expert", "shard"), None),
            P(("expert", "shard"), None),
            P(("expert", "shard"), None),
            P(("expert", "shard"), None),
            P(),
            P("shard"),
            P("shard"),
            P("shard"),
            P("shard"),
            P("shard", None),
            P("shard", None),
            P("shard", None),
            P("expert", None, None),
            P("expert", None, None),
        ),
        out_specs=(
            P(("expert", "shard"), None),
            P(("expert", "shard"), None),
            P("shard"),
            P("shard"),
            P("shard"),
            P("shard"),
            P("shard", None),
            P("shard", None),
            P("shard", None),
            P("expert", "shard", None),
            P("expert", None, "shard"),
        ),
        check_vma=False,
    )
```
